128 devices in a mesh: dp: 8 (over x, core), tensor: 16 (over z, y).
Axes of the slice: x: 4, y: 4, z: 4, core: 2. Of those that a mesh axis runs over, the one named last changes fastest.
Arguments:
- block_input: bfloat16 [16384, 1024], P(('dp', 'tensor')), may hold values from -6 to 6
- attn_gain: bfloat16 [1024], replicated, may hold values from 0.5 to 1.5
- w_query: bfloat16 [1024, 1024], P(None, 'tensor'), may hold values from -0.75 to 0.75
- w_keyval: bfloat16 [1024, 1024], replicated, may hold values from -0.5 to 0.5
- w_out: bfloat16 [1024, 1024], P('tensor'), may hold values from -3 to 3
- ffn_gain: bfloat16 [1024], replicated, may hold values from 0.5 to 1.5
- w_router: bfloat16 [1024, 32], replicated, may hold values from -0.09375 to 0.09375
- w_gateup: bfloat16 [32, 1024, 1024], P('tensor'), may hold values from -0.1875 to 0.1875
- w_down: bfloat16 [32, 512, 1024], P('tensor'), may hold values from -6 to 6
- routes: int32 [16384, 8], P(('dp', 'tensor')), may hold values from 0 to 31, all different within a row; in each aligned block of 128 rows (0 to 127, 128 to 255, ...) at most 64 rows name the same one
- cotangent: bfloat16 [16384, 1024], P(('dp', 'tensor')), may hold values from -6 to 6
Outputs:
- block_out: bfloat16 [16384, 1024], P(('dp', 'tensor'))
- grad_input: float32 [16384, 1024], P(('dp', 'tensor'))
- grad_attn_gain: float32 [1024], replicated
- grad_query: float32 [1024, 1024], P(None, 'tensor')
- grad_keyval: float32 [1024, 1024], replicated
- grad_out_proj: float32 [1024, 1024], P('tensor')
- grad_ffn_gain: float32 [1024], replicated
- grad_router: float32 [1024, 32], replicated
- grad_gateup: float32 [32, 1024, 1024], P('tensor')
- grad_down: float32 [32, 512, 1024], P('tensor')
The draws below stay inside these ranges and needn't reach their ends.
Inputs may be any that keep to these rules, and one draw needn't show every extreme that they name: `routes`: each row names 8 different experts. Among the rows of one device no expert is named by more than 64 rows, and in every draw some expert is named by exactly 64 rows of some device.
All inputs are finite; a program needn't handle non-finite values.
Results may differ from the reference program's by a relative error of at most 0.028.
Values may be sent and summed in bfloat16 or wider, within the bound.
A program may use at most 128 MiB of HBM per device.

```python
import math
import jax
import jax.numpy as jnp
import numpy as np
from jax import lax

D = 1024
HEADS = 16
KV_HEADS = 8
HD = 64
FF = 512
EXPERTS = 32
TOP = 8
TOK_DEV = 128
LEN = 2048
TOKENS = 16384
CAP = 64
N_DP = 8
N_TENSOR = 16


def steps_of(key, shape, cuts, least, top_value):
    loudness, own = 1.0, jax.random.fold_in(key, 6)
    for dim, parts in cuts:
        draws = jnp.exp(jax.random.uniform(jax.random.fold_in(own, dim), (parts,), jnp.float32, least / len(cuts), top_value / len(cuts)))
        loudness = loudness * jnp.repeat(draws, shape[dim] // parts).reshape([-1 if axis == dim else 1 for axis in range(len(shape))])
    return loudness


def assign_block(stream_key, own, number, rows, amount, top, bound, slope):
    order = jax.random.permutation(stream_key, amount)
    packed, common = shares(amount, rows * top, bound, slope, True), shares(amount, rows * top, bound, slope, False)
    places = jnp.arange(amount)

    def named(lengths, offset_by):
        used = int((lengths > 0).sum())
        fixed = max(1, used // 4)
        moved = fixed + (places - fixed + offset_by * (used - fixed)) % max(1, amount - fixed)
        return jnp.zeros((amount,), jnp.int32).at[order[jnp.where(places < fixed, places, moved)]].set(jnp.asarray(lengths, jnp.int32))

    lengths = jnp.where(number % 4 == 0, named(packed, number // 4), named(common, number - number // 4 - 1))
    mixed = jax.random.permutation(jax.random.fold_in(own, 3), amount)
    donor, sink = mixed[0:amount // 2 * 2:2], mixed[1:amount // 2 * 2:2]
    room = jnp.minimum(lengths[donor] - 1, bound - lengths[sink]) // 2
    room = jnp.where((donor == order[0]) | (sink == order[0]) | (lengths[sink] == 0), 0, jnp.maximum(room, 0))
    moved = jax.random.randint(jax.random.fold_in(own, 4), (amount // 2,), 0, 1 << 20) % (room + 1)
    lengths = lengths.at[donor].add(-moved).at[sink].add(moved)
    members = jnp.searchsorted(jnp.cumsum(lengths), jnp.arange(rows * top), side="right").astype(jnp.int32)
    grid = members.reshape(top, rows).T
    grid = grid[jax.random.permutation(jax.random.fold_in(own, 1), rows)]
    offset_by = jax.random.randint(jax.random.fold_in(own, 2), (rows, 1), 0, top)
    return jnp.take_along_axis(grid, (jnp.arange(top)[None, :] + offset_by) % top, axis=1)


def shares(count, total, reach, skew, full):
    weights = [(1 << 20) // math.isqrt(standing ** skew) + 1 for standing in range(1, count + 1)]
    largest = reach if full else min(reach, max(-(-total // count), total * weights[0] // sum(weights)))
    least = 1 if total - largest >= count - 1 else 0
    counts, rest = [largest] + [least] * (count - 1), total - largest - least * (count - 1)
    while rest > 0:
        free = [i for i in range(1, count) if counts[i] < largest] or [i for i in range(1, count) if counts[i] < reach]
        whole, left = sum([weights[i] for i in free]), rest
        for i in free:
            addition = min(reach - counts[i], max(1, left * weights[i] // whole), rest)
            counts[i] = counts[i] + addition
            rest = rest - addition
    return np.array(counts)


def noise(rng, dims, spread, most, cuts=(), held_as=jnp.bfloat16):
    drawn = spread * jax.random.normal(rng, dims, jnp.float32)
    if cuts:
        drawn = drawn * steps_of(rng, dims, cuts, -0.22, 0.18)
    return jnp.clip(drawn, -most, most).astype(held_as)


def setup_inputs(seed: int = 0) -> dict:
    seeds = jax.random.split(jax.random.key(seed), 12)
    block_input = noise(seeds[0], (TOKENS, D), 1.0, 6.0, ((0, 128),))
    attn_gain = jnp.clip(1.0 + 0.1 * jax.random.normal(seeds[1], (D,), jnp.float32), 0.5, 1.5).astype(jnp.bfloat16)
    w_query = noise(seeds[2], (D, HEADS * HD), (D // 16) ** -0.5, 0.75, ((1, 16),))
    w_keyval = noise(seeds[3], (D, 2 * KV_HEADS * HD), (D // 8) ** -0.5, 0.5)
    w_out = noise(seeds[4], (HEADS * HD, D), 4 ** -0.5, 3.0, ((0, 16),))
    ffn_gain = jnp.clip(1.0 + 0.1 * jax.random.normal(seeds[5], (D,), jnp.float32), 0.5, 1.5).astype(jnp.bfloat16)
    w_router = noise(seeds[6], (D, EXPERTS), (4 * D) ** -0.5, 0.09375)
    w_gateup = noise(seeds[7], (EXPERTS, D, 2 * FF), D ** -0.5, 0.1875, ((0, 16),))
    w_down = noise(seeds[8], (EXPERTS, FF, D), 1 ** -0.5, 6.0, ((0, 16),))
    routes_keys = jax.random.split(jax.random.fold_in(seeds[9], 1), TOKENS // TOK_DEV)
    routes_turns = jax.random.permutation(jax.random.fold_in(seeds[9], 3), TOKENS // TOK_DEV)
    routes = jax.vmap(lambda own, number: assign_block(jax.random.fold_in(seeds[9], 2), own, number, TOK_DEV, EXPERTS, TOP, CAP, 1))(routes_keys, routes_turns).reshape((TOKENS, TOP))
    cotangent = noise(seeds[10], (TOKENS, D), 1.0, 6.0, ((0, 128),))
    return {"block_input": block_input, "attn_gain": attn_gain, "w_query": w_query, "w_keyval": w_keyval, "w_out": w_out, "ffn_gain": ffn_gain, "w_router": w_router, "w_gateup": w_gateup, "w_down": w_down, "routes": routes, "cotangent": cotangent}


ATTN_SCALE = 0.015625
RES_SCALE = 0.22
EPSILON = 1e-06
ROPE_BASE = 10000.0

@jax.custom_vjp
def low(v):
    return lax.optimization_barrier(v.astype(jnp.bfloat16)).astype(jnp.float32)

@jax.custom_vjp
def low_back(v):
    return v

def low_keep(v):
    return (low(v), None)

def low_pass(kept, grad):
    return (grad,)

def back_keep(v):
    return (v, None)

def back_low(kept, grad):
    return (low(grad),)
low.defvjp(low_keep, low_pass)
low_back.defvjp(back_keep, back_low)

def rms_norm(values, gain):
    return values * lax.rsqrt(lax.optimization_barrier(jnp.mean(values * values, axis=-1, keepdims=True)) + EPSILON) * gain

def rope_tables(length, width):
    half_width = width // 2
    inverse = ROPE_BASE ** (-(jnp.arange(half_width, dtype=jnp.float32) * 2.0) / width)
    angles = jnp.arange(length, dtype=jnp.float32)[:, None] * inverse[None, :]
    return (jnp.cos(angles), jnp.sin(angles))

def rotate(values, cosine, sine_table, direction):
    half_width = values.shape[-1] // 2
    shape_out = (values.shape[0],) + (1,) * (values.ndim - 2) + (half_width,)
    cosine = cosine.reshape(shape_out)
    sine_table = sine_table.reshape(shape_out) * direction
    first = values[..., :half_width]
    second = values[..., half_width:]
    return jnp.concatenate([first * cosine - second * sine_table, second * cosine + first * sine_table], axis=-1)

def head_tables():
    per_group = HEADS // N_TENSOR
    group_ratio = HEADS // KV_HEADS
    kv_count = max(1, per_group // group_ratio)
    key_cols = []
    local_heads = []
    for group_id in range(N_TENSOR):
        first_head = group_id * per_group // group_ratio
        head_ids = list(range(first_head, first_head + kv_count))
        key_part = [head_id * HD + column for head_id in head_ids for column in range(HD)]
        value_part = [KV_HEADS * HD + head_id * HD + column for head_id in head_ids for column in range(HD)]
        key_cols.append(key_part + value_part)
        local_heads.append([(group_id * per_group + member) // group_ratio - first_head for member in range(per_group)])
    return (np.array(key_cols, np.int32), np.array(local_heads, np.int32), kv_count)

def slot_tables(routes):
    devices = N_DP * N_TENSOR
    per_device = routes.reshape(devices, TOK_DEV * TOP)
    onehot = (per_device[:, :, None] == jnp.arange(EXPERTS, dtype=jnp.int32)[None, None, :]).astype(jnp.int32)
    running = jnp.cumsum(onehot, axis=1) - 1
    slot_index = lax.optimization_barrier(jnp.sum(running * onehot, axis=2))
    sources = jnp.arange(devices, dtype=jnp.int32)[:, None]
    destination = (per_device * devices + sources) * CAP + slot_index
    pair_ids = jnp.arange(TOKENS * TOP, dtype=jnp.int32)
    owners = jnp.full((EXPERTS * devices * CAP,), TOKENS, jnp.int32).at[destination.reshape(-1)].set(pair_ids // TOP)
    return (owners.reshape(EXPERTS, devices * CAP), destination.reshape(TOKENS, TOP))

def reference(block_input, attn_gain, w_query, w_keyval, w_out, ffn_gain, w_router, w_gateup, w_down, routes, cotangent):
    highest = lax.Precision.HIGHEST
    key_cols, local_heads, kv_count = head_tables()
    per_group = HEADS // N_TENSOR
    group_of = np.arange(HEADS) // per_group
    local_of = local_heads.reshape(-1)
    owners, destination = slot_tables(routes)
    block_rows = min(512, LEN)
    blocks = LEN // block_rows
    cosine, sine_table = rope_tables(LEN, HD)

    def attend_block(queries, key_heads, value_heads, first_row):
        scores = low_back(jnp.einsum('hqd,hkd->hqk', queries, key_heads, precision=highest) * ATTN_SCALE)
        positions = first_row + jnp.arange(block_rows, dtype=jnp.int32)
        allowed = jnp.arange(LEN, dtype=jnp.int32)[None, :] <= positions[:, None]
        scores = jnp.where(allowed[None], scores, -1e+30)
        weights = jax.nn.softmax(scores, axis=-1)
        return jnp.einsum('hqk,hkd->hqd', low(weights), value_heads, precision=highest)
    checked_block = jax.checkpoint(attend_block)

    def attention(normed, query_weight, pair_weight, out_weight):
        queries = low_back(jnp.dot(normed, query_weight, precision=highest)).reshape(LEN, HEADS, HD)
        pairs = low_back(jnp.einsum('ld,dgc->lgc', normed, pair_weight, precision=highest))
        key_rows = pairs[..., :kv_count * HD].reshape(LEN, N_TENSOR, kv_count, HD)
        value_rows = pairs[..., kv_count * HD:].reshape(LEN, N_TENSOR, kv_count, HD)
        queries = low(rotate(queries, cosine, sine_table, 1.0)).transpose(1, 0, 2)
        key_heads = low(rotate(key_rows, cosine, sine_table, 1.0))[:, group_of, local_of].transpose(1, 0, 2)
        value_heads = low(value_rows)[:, group_of, local_of].transpose(1, 0, 2)
        query_blocks = queries.reshape(HEADS, blocks, block_rows, HD).transpose(1, 0, 2, 3)
        starts = jnp.arange(blocks, dtype=jnp.int32) * block_rows

        def run_block(operands):
            return checked_block(operands[0], key_heads, value_heads, operands[1])
        context = lax.map(run_block, (query_blocks, starts))
        context = context.transpose(0, 2, 1, 3).reshape(LEN, HEADS * HD)
        context = low_back(low(context))
        return low_back(jnp.dot(context, out_weight, precision=highest))

    def forward(inputs, gain_one, query_weight, keyval_weight, out_weight, gain_two, router_weight, gateup_weight, down_weight):
        normed = low(rms_norm(inputs, gain_one)).reshape(N_DP, LEN, HD * 0 + D)
        pair_weight = keyval_weight[:, key_cols]

        def one_sequence(sequence):
            return attention(sequence, query_weight, pair_weight, out_weight)
        attended = lax.map(one_sequence, normed).reshape(TOKENS, D)
        residual = inputs + RES_SCALE * attended
        normed_two = low(rms_norm(residual, gain_two))
        logits = low_back(jnp.dot(normed_two, router_weight, precision=highest))
        gate_weights = jax.nn.softmax(jnp.take_along_axis(logits, routes, axis=1), axis=-1)
        padded = jnp.concatenate([normed_two, jnp.zeros((1, D), jnp.float32)], axis=0)

        def expert(operands):
            owner_rows, gate_up, down_proj = operands
            arrived = low_back(padded[owner_rows])
            activations = low_back(jnp.dot(arrived, gate_up, precision=highest))
            hidden = low(jax.nn.silu(activations[:, :FF]) * activations[:, FF:])
            return low_back(low(jnp.dot(hidden, down_proj, precision=highest)))
        outputs = lax.map(jax.checkpoint(expert), (owners, gateup_weight, down_weight)).reshape(-1, D)
        combined = jnp.zeros((TOKENS, D), jnp.float32)
        for choice_index in range(TOP):
            combined = combined + gate_weights[:, choice_index:choice_index + 1] * outputs[destination[:, choice_index]]
        return residual + RES_SCALE * combined
    params = (block_input.astype(jnp.float32), attn_gain.astype(jnp.float32), w_query.astype(jnp.float32), w_keyval.astype(jnp.float32), w_out.astype(jnp.float32), ffn_gain.astype(jnp.float32), w_router.astype(jnp.float32), w_gateup.astype(jnp.float32), w_down.astype(jnp.float32))
    result, pullback = jax.vjp(forward, *params)
    grads = pullback(cotangent.astype(jnp.float32))
    return (result.astype(jnp.bfloat16), grads[0], grads[1], grads[2], grads[3], grads[4], grads[5], grads[6], grads[7], grads[8])
```

```python
import jax
import jax.numpy as jnp
import numpy as np
from jax import lax
from jax.experimental import pallas as pl
from jax.experimental.pallas import tpu as pltpu
from jax.sharding import PartitionSpec as P

HEADS = 16
KV_HEADS = 8
HD = 64
EXPERTS = 32
TOP = 8
CAP = 64
ATTN_SCALE = 0.015625
RES_SCALE = 0.22
EPSILON = 1e-06
ROPE_BASE = 10000.0
F32 = jnp.float32
BF16 = jnp.bfloat16
Q_ROWS = 256


def rms_scale(values):
    return lax.rsqrt(jnp.mean(values * values, axis=-1, keepdims=True) + EPSILON)


def norm_back(values, scale, gain, grad_normed):
    grad_scaled = grad_normed * gain
    grad_gain = jnp.sum(grad_normed * values * scale, axis=0)
    inner = jnp.mean(grad_scaled * values, axis=-1, keepdims=True)
    return (scale * (grad_scaled - values * scale * scale * inner), grad_gain)


def rope_tables(length, width):
    half_width = width // 2
    inverse = ROPE_BASE ** (-(jnp.arange(half_width, dtype=F32) * 2.0) / width)
    angles = jnp.arange(length, dtype=F32)[None, :] * inverse[:, None]
    return (jnp.cos(angles), jnp.sin(angles))


def rotate(first, second, cosine, sine):
    return first * cosine - second * sine, second * cosine + first * sine


def dot(a, b, dims):
    return lax.dot_general(a, b, ((dims[0], dims[1]), ((), ())), preferred_element_type=F32)


def causal(rows):
    key = lax.broadcasted_iota(jnp.int32, (rows, rows), 0)
    query = lax.broadcasted_iota(jnp.int32, (rows, rows), 1)
    return key <= query


RING = 4
MESH_ID = pl.DeviceIdType.MESH


def whole():
    return pl.BlockSpec(memory_space=pltpu.VMEM)


def anywhere():
    return pl.BlockSpec(memory_space=pl.ANY)


def position():
    rank = lax.axis_index("tensor")
    return lax.div(rank, RING), lax.rem(rank, RING)


def shifted(pos, axis, by):
    moved = lax.rem(pos[axis] + (by + RING), RING)
    return (moved, pos[1]) if axis == 0 else (pos[0], moved)


def joined(pos):
    return pos[0] * RING + pos[1]


def greet(tensor_peers, dp_peers=()):
    dp, rank = lax.axis_index("dp"), lax.axis_index("tensor")
    sem = pltpu.get_barrier_semaphore()
    peers = [(dp, p) for p in tensor_peers] + [(p, rank) for p in dp_peers]
    for peer in peers:
        pl.semaphore_signal(sem, inc=1, device_id=peer, device_id_type=MESH_ID)
    pl.semaphore_wait(sem, len(peers))


def neighbours():
    pos = position()
    return [joined(shifted(pos, axis, by)) for axis in (0, 1) for by in (1, -1)]


def others(axis, count):
    return [lax.rem(lax.axis_index(axis) + r, count) for r in range(1, count)]


def torus_messages(half, rows):
    primary, secondary = (0, 1) if half == 0 else (1, 0)
    h, q = rows // 2, rows // 4
    full = (half * h, h)
    part = {1: (half * h, q), -1: (half * h + q, q)}
    out = []
    for d in (1, -1):
        out.append((0, ("p1", d), None, full, (0, 0), primary, d))
        out.append((0, ("s1", 0, d), None, full, (0, 0), secondary, d))
        out.append((1, ("p2", d), ("p1", d), part[d], (-d, 0), primary, d))
        for e in (1, -1):
            out.append((1, ("s1", -d, e), ("p1", d), full, (-d, 0), secondary, e))
    for e in (1, -1):
        out.append((2, ("s2", 0, e), ("s1", 0, e), part[e], (0, -e), secondary, e))
        for d in (1, -1):
            out.append((3, ("s1", ("o", d), e), ("p2", d), part[d], (2, 0), secondary, e))
            out.append((4, ("s2", d, e), ("s1", d, e), part[e], (d, -e), secondary, e))
        out.append((5, ("s2", "o", e), ("s1", ("o", e), e), part[e], (2, -e), secondary, e))
    return out


class Torus:
    COUNT = 44
    STAGES = 6

    def __init__(self, rows):
        self.rows = rows
        self.pos = position()
        self.dp = lax.axis_index("dp")
        self.messages, self.children, self.place, order, used = {}, {}, {}, [], 0
        for half in (0, 1):
            for at, (stage, key, needs, piece, offset, axis, way) in enumerate(torus_messages(half, rows)):
                key = (half, key)
                needs = None if needs is None else (half, needs)
                self.messages[key] = (len(order), stage, needs, piece, offset, axis, way)
                self.children.setdefault(needs, []).append(key)
                self.place[key] = used
                used += piece[1]
                order.append((stage, at, half, key))
        self.landing_rows = used
        self.order = [entry[3] for entry in sorted(order, key=lambda entry: entry[:3])]

    def block(self, key, pos):
        half, offset = key[0], self.messages[key][4]
        primary, secondary = (0, 1) if half == 0 else (1, 0)
        return joined(shifted(shifted(pos, primary, offset[0]), secondary, offset[1]))

    def sender(self, key):
        _, _, _, _, _, axis, way = self.messages[key]
        return shifted(self.pos, axis, -way)

    def receiver(self, key):
        _, _, _, _, _, axis, way = self.messages[key]
        return shifted(self.pos, axis, way)


class Gather(Torus):
    def __init__(self, buf, send, recv):
        super().__init__(buf.shape[1])
        self.buf, self.send, self.recv = buf, send, recv
        self.arrived = set()

    def copy(self, key, incoming):
        number, (first, count) = self.messages[key][0], self.messages[key][3]
        at = self.sender(key) if incoming else self.pos
        ref = self.buf.at[self.block(key, at), pl.ds(first, count)]
        return pltpu.make_async_remote_copy(
            src_ref=ref, dst_ref=ref, send_sem=self.send.at[number], recv_sem=self.recv.at[number],
            device_id=(self.dp, joined(at if incoming else self.receiver(key))), device_id_type=MESH_ID,
        )

    def arrive(self, key):
        if key not in self.arrived:
            self.arrived.add(key)
            self.copy(key, True).wait_recv()

    def stage(self, number):
        for key in self.order:
            _, stage, needs, *_ = self.messages[key]
            if stage == number:
                if needs is not None:
                    self.arrive(needs)
                self.copy(key, False).start()

    def arrive_stage(self, number):
        for key in self.order:
            if self.messages[key][1] == number:
                self.arrive(key)

    def finish(self):
        for key in self.order:
            self.arrive(key)
        for key in self.order:
            self.copy(key, False).wait_send()


class Scatter(Torus):
    def __init__(self, parts, landing, send, recv):
        super().__init__(parts.shape[1])
        self.parts, self.landing, self.send, self.recv = parts, landing, send, recv

    def copy(self, key):
        number, (first, count) = self.messages[key][0], self.messages[key][3]
        at = self.sender(key)
        return pltpu.make_async_remote_copy(
            src_ref=self.parts.at[self.block(key, at), pl.ds(first, count)],
            dst_ref=self.landing.at[pl.ds(self.place[key], count)],
            send_sem=self.send.at[number], recv_sem=self.recv.at[number],
            device_id=(self.dp, joined(at)), device_id_type=MESH_ID,
        )

    def landed(self, key):
        count = self.messages[key][3][1]
        self.copy(key).wait_recv()
        return self.landing[pl.ds(self.place[key], count), :].astype(F32)

    def stage(self, number):
        for key in reversed(self.order):
            if self.messages[key][1] == number:
                pieces = {}
                for child in self.children.get(key, []):
                    pieces.setdefault(self.messages[child][3], []).append(child)
                for (first, count), children in pieces.items():
                    at = (self.block(children[0], self.pos), pl.ds(first, count))
                    self.parts[at] = sum((self.landed(c) for c in children), self.parts[at].astype(F32)).astype(self.parts.dtype)
                self.copy(key).start()

    def result(self):
        out = []
        for half in (0, 1):
            children = [c for c in self.children[None] if c[0] == half]
            first, count = self.messages[children[0]][3]
            own = self.parts[joined(self.pos), pl.ds(first, count)].astype(F32)
            out.append(sum((self.landed(c) for c in children), own))
        return out

    def finish(self):
        for key in self.order:
            self.copy(key).wait_send()


class Exchange:
    def __init__(self, source, target, send, recv, axis="tensor", same=False):
        self.source, self.target, self.send, self.recv, self.axis, self.same = source, target, send, recv, axis, same
        self.count = target.shape[0]
        self.rank = lax.axis_index(axis)

    def device(self, to):
        if self.axis == "tensor":
            return (lax.axis_index("dp"), to)
        return (to, lax.axis_index("tensor"))

    def copy(self, r):
        to = lax.rem(self.rank + r, self.count)
        return pltpu.make_async_remote_copy(
            src_ref=self.source if self.same else self.source.at[to],
            dst_ref=self.target.at[self.rank], send_sem=self.send.at[r - 1],
            recv_sem=self.recv.at[r - 1], device_id=self.device(to), device_id_type=MESH_ID,
        )

    def start(self):
        for r in range(1, self.count):
            self.copy(r).start()

    def arrive(self):
        for r in range(1, self.count):
            origin = lax.rem(self.rank + self.count - r, self.count)
            pltpu.make_async_remote_copy(
                src_ref=self.target.at[origin], dst_ref=self.target.at[origin], send_sem=self.send.at[r - 1],
                recv_sem=self.recv.at[r - 1], device_id=self.device(origin), device_id_type=MESH_ID,
            ).wait_recv()

    def sent(self):
        for r in range(1, self.count):
            self.copy(r).wait_send()


def pair_sems(count):
    return [pltpu.SemaphoreType.DMA((count,))] * 2


def call(kernel, name, number, out_shape, in_specs, out_specs, scratch, limit, flops=0, bytes_accessed=0):
    return pl.pallas_call(
        kernel, out_shape=out_shape, in_specs=in_specs, out_specs=out_specs, scratch_shapes=scratch,
        compiler_params=pltpu.CompilerParams(collective_id=number, has_side_effects=True, vmem_limit_bytes=limit << 20),
        cost_estimate=pl.CostEstimate(flops=flops, bytes_accessed=bytes_accessed, transcendentals=0),
        name=name,
    )


def forward_kernel(
    x_ref, gain_ref, query_ref, keyval_ref, out_w_ref, cot_ref, cosine_ref, sine_ref,
    normed_out, qkv_out, wide_ref, log_ref, context_ref, query_all, out_all, cot_all,
    buf, query_t, local_w, pair_w, qkv, key_rows, context_parts,
    sems_a, sems_b, sems_c, sems_d, sems_e, local_sems,
):
    tokens, width = x_ref.shape
    rank = lax.axis_index("tensor")
    z, y = position()
    half = HD // 2
    pair_copies = []
    for part in range(2):
        column = pl.multiple_of(part * KV_HEADS * HD + z * 2 * HD, 2 * HD)
        copy = pltpu.make_async_copy(keyval_ref.at[:, pl.ds(column, 2 * HD)], pair_w.at[part], local_sems.at[part])
        copy.start()
        pair_copies.append(copy)
    own_cot = pltpu.make_async_copy(cot_ref, cot_all.at[rank], local_sems.at[2])
    own_cot.start()
    own_out = pltpu.make_async_copy(out_w_ref, out_all.at[rank], local_sems.at[3])
    own_out.start()
    inputs = x_ref[...].astype(F32)
    buf[rank] = (inputs * rms_scale(inputs) * gain_ref[...].astype(F32)).astype(BF16)
    greet(others("tensor", RING * RING))
    main = Gather(buf, *sems_a)
    main.stage(0)
    query_t[...] = query_ref[...].T
    own_query = pltpu.make_async_copy(query_t, query_all.at[rank], local_sems.at[4])
    own_query.start()
    for copy in pair_copies:
        copy.wait()
    odd = lax.rem(lax.div(rank, 2), 2)
    local_w[:HD] = query_t[...]
    for part in range(2):
        tall = pair_w[part].T.astype(F32)
        local_w[HD * (part + 1) : HD * (part + 2)] = jnp.where(odd == 0, tall[:HD], tall[HD:]).astype(BF16)
    pos = main.pos

    def project(dz, dy):
        block = joined(shifted(shifted(pos, 0, dz), 1, dy))
        columns = pl.ds(pl.multiple_of(block * tokens, tokens), tokens)
        made = dot(local_w[...], buf[block], ((1,), (1,)))
        cosine, sine = cosine_ref[:, columns], sine_ref[:, columns]
        rows = []
        for first in (0, HD):
            rows += rotate(made[first : first + half], made[first + half : first + HD], cosine, sine)
        rows.append(made[2 * HD :])
        qkv[:, columns] = jnp.concatenate(rows, axis=0).astype(BF16)

    project(0, 0)
    main.stage(1)
    main.stage(2)
    main.arrive_stage(0)
    for offset in ((0, 1), (0, 3), (1, 0), (3, 0)):
        project(*offset)
    main.stage(3)
    main.stage(4)
    own_out.wait()
    own_query.wait()
    own_cot.wait()
    back = [Gather(out_all, *sems_b), Gather(query_all, *sems_c), Gather(cot_all, *sems_d)]
    main.arrive_stage(1)
    main.arrive_stage(2)
    for offset in ((1, 1), (1, 3), (3, 1), (3, 3), (2, 0), (0, 2)):
        project(*offset)
    main.stage(5)
    for other in back:
        other.stage(0)
    main.arrive_stage(3)
    main.arrive_stage(4)
    for offset in ((2, 1), (2, 3), (1, 2), (3, 2)):
        project(*offset)
    main.arrive_stage(5)
    project(2, 2)
    normed_copy = pltpu.make_async_copy(buf, normed_out, local_sems.at[5])
    normed_copy.start()
    qkv_copy = pltpu.make_async_copy(qkv, qkv_out, local_sems.at[6])
    qkv_copy.start()
    key_rows[...] = qkv[HD : 2 * HD].T
    swap = Exchange(context_parts, context_ref, *sems_e)
    todo = [(other, stage) for stage in range(1, 6) for other in back]
    attend(qkv, key_rows, wide_ref, log_ref, context_parts, tokens, todo)
    swap.start()
    context_ref[rank] = context_parts[rank]
    for other, stage in todo:
        other.stage(stage)
    swap.arrive()
    for other in back:
        other.finish()
    main.finish()
    swap.sent()
    normed_copy.wait()
    qkv_copy.wait()


def attend(qkv, key_rows, wide_ref, log_ref, parts_ref, tokens, todo):
    length = qkv.shape[1]
    allowed = causal(Q_ROWS)
    query, value = slice(0, HD), slice(2 * HD, 3 * HD)
    for block in range(length // Q_ROWS):
        first = block * Q_ROWS
        columns = slice(first, first + Q_ROWS)
        scaled = qkv[query, columns] * ATTN_SCALE
        near = dot(key_rows[columns, :], scaled, ((1,), (0,)))
        near = jnp.where(allowed, near, -1e30)
        largest = jnp.max(near, axis=0, keepdims=True)
        if block:
            far = dot(key_rows[:first, :], scaled, ((1,), (0,)))
            largest = jnp.maximum(largest, jnp.max(far, axis=0, keepdims=True))
        near = jnp.exp(near - largest)
        total = jnp.sum(near, axis=0, keepdims=True)
        context = dot(qkv[value, columns], near.astype(BF16), ((1,), (0,)))
        if block:
            far = jnp.exp(far - largest)
            total = total + jnp.sum(far, axis=0, keepdims=True)
            context = context + dot(qkv[value, :first], far.astype(BF16), ((1,), (0,)))
        context = context / total
        wide_ref[:, columns] = context
        log_ref[:, columns] = largest + jnp.log(total)
        low = context.astype(BF16)
        for part in range(Q_ROWS // tokens):
            parts_ref[first // tokens + part] = low[:, part * tokens : (part + 1) * tokens]
        for _ in range(min(len(todo), 1 if block >= 3 else 0)):
            other, stage = todo.pop(0)
            other.stage(stage)


def forward(x, gain, w_query, w_keyval, w_out, cotangent, cosine, sine):
    tokens, width = x.shape
    count = RING * RING
    length = tokens * count

    def kernel(*refs):
        plain, sems = refs[:-11], refs[-11:]
        forward_kernel(*plain, *[sems[2 * i : 2 * i + 2] for i in range(5)], sems[10])

    shape = jax.ShapeDtypeStruct
    return call(
        kernel, "forward", 1,
        (
            shape((count, tokens, width), BF16), shape((3 * HD, length), BF16), shape((HD, length), F32),
            shape((1, length), F32), shape((count, HD, tokens), BF16), shape((count, HD, width), BF16),
            shape((count, HD, width), BF16), shape((count, tokens, width), BF16),
        ),
        [whole(), whole(), whole(), anywhere(), anywhere(), anywhere(), whole(), whole()],
        [anywhere(), anywhere(), whole(), whole(), whole(), anywhere(), anywhere(), anywhere()],
        [
            pltpu.VMEM((count, tokens, width), BF16), pltpu.VMEM((HD, width), BF16), pltpu.VMEM((3 * HD, width), BF16),
            pltpu.VMEM((2, width, 2 * HD), BF16), pltpu.VMEM((3 * HD, length), BF16), pltpu.VMEM((length, HD), BF16),
            pltpu.VMEM((count, HD, tokens), BF16),
            *(pair_sems(Torus.COUNT) * 4), *pair_sems(count - 1), pltpu.SemaphoreType.DMA((8,)),
        ],
        48, flops=2 * length * (3 * HD * width + length * HD * 2), bytes_accessed=20 << 20,
    )(x, gain.reshape(1, width), w_query, w_keyval, w_out, cotangent, cosine, sine)


def middle_kernel(x_ref, context_ref, out_all_ref, gain_ref, residual_ref, normed_ref, all_ref, buf, send, recv, sem):
    rank = lax.axis_index("tensor")
    attention = dot(context_ref[...], out_all_ref[...], ((0,), (0,)))
    residual = x_ref[...].astype(F32) + RES_SCALE * attention
    residual_ref[...] = residual
    normed = (residual * rms_scale(residual) * gain_ref[...].astype(F32)).astype(BF16)
    normed_ref[...] = normed
    buf[rank] = normed
    greet(neighbours())
    gather = Gather(buf, send, recv)
    for stage in range(6):
        gather.stage(stage)
    gather.finish()
    copy = pltpu.make_async_copy(buf, all_ref, sem)
    copy.start()
    copy.wait()


def middle(x, context, out_all, gain):
    tokens, width = x.shape
    count = RING * RING
    shape = jax.ShapeDtypeStruct
    return call(
        middle_kernel, "middle", 2,
        (shape((tokens, width), F32), shape((tokens, width), BF16), shape((count, tokens, width), BF16)),
        [whole()] * 4, [whole(), whole(), anywhere()],
        [pltpu.VMEM((count, tokens, width), BF16), *pair_sems(Torus.COUNT), pltpu.SemaphoreType.DMA],
        32, flops=2 * tokens * width * width, bytes_accessed=12 << 20,
    )(x, context.reshape(HEADS * HD, tokens), out_all.reshape(HEADS * HD, width), gain.reshape(1, width))


def scatter_kernel(first_ref, second_ref, small_ref, first_out, second_out, small_out, one, two, land_one, land_two, *sems):
    rank = lax.axis_index("tensor")
    sems, local = sems[:-1], sems[-1]
    copies = [pltpu.make_async_copy(a, b, local.at[i]) for i, (a, b) in enumerate(((first_ref, one), (second_ref, two)))]
    for copy in copies:
        copy.start()
    greet(others("tensor", RING * RING))
    swap = Exchange(small_ref, small_out, sems[4], sems[5])
    swap.start()
    small_out[rank] = small_ref[rank]
    sums = [Scatter(one, land_one, sems[0], sems[1]), Scatter(two, land_two, sems[2], sems[3])]
    for copy, each in zip(copies, sums):
        copy.wait()
        each.stage(5)
        each.stage(4)
    for stage in (3, 2, 1, 0):
        for each in sums:
            each.stage(stage)
    for each, out in zip(sums, (first_out, second_out)):
        rows = out.shape[0] // 2
        for half, value in enumerate(each.result()):
            out[half * rows : (half + 1) * rows] = value
        each.finish()
    swap.arrive()
    swap.sent()


def scatter_two(first, second, small):
    count, tokens, width = first.shape
    shape = jax.ShapeDtypeStruct
    part = pltpu.VMEM((count, tokens, width), BF16)
    land = pltpu.VMEM(((count - 1) * tokens, width), BF16)
    return call(
        scatter_kernel, "scatter_two", 3,
        (shape((tokens, width), F32), shape((tokens, width), F32), shape(small.shape, F32)),
        [anywhere(), anywhere(), whole()], [whole()] * 3,
        [part, part, land, land, *(pair_sems(Torus.COUNT) * 2), *pair_sems(count - 1), pltpu.SemaphoreType.DMA((2,))],
        40, flops=1 << 24, bytes_accessed=20 << 20,
    )(first, second, small)


def backward_kernel(
    qkv_ref, grad_ref, wide_ref, log_ref, cosine_ref, sine_ref, normed_ref, context_ref, grad_att_ref,
    out_ref, weight_ref, sum_ref,
    grad_parts, parts_out, grad, query_rows, key_rows, value_rows, grad_rows, grad_query, grad_key, grad_value,
    normed, wide_grad, out_parts, out_land,
    send_a, recv_a, send_b, recv_b, send_c, recv_c, local,
):
    count, _, tokens = grad_ref.shape
    length = count * tokens
    rank = lax.axis_index("tensor")
    copy = pltpu.make_async_copy(normed_ref, normed, local)
    copy.start()
    greet(others("tensor", count))
    swap = Exchange(grad_ref, grad_parts, send_a, recv_a)
    swap.start()
    query, key, value = slice(0, HD), slice(HD, 2 * HD), slice(2 * HD, 3 * HD)
    query_rows[...] = qkv_ref[query].T
    key_rows[...] = qkv_ref[key].T
    value_rows[...] = qkv_ref[value].T
    scatter = Scatter(out_parts, out_land, send_c, recv_c)
    grad_att = grad_att_ref[...]
    for part in range(count):
        out_parts[part] = dot(context_ref[part], grad_att, ((1,), (0,))).astype(BF16)
    grad_parts[rank] = grad_ref[rank]
    swap.arrive()
    scatter.stage(5)
    scatter.stage(4)
    for part in range(count):
        grad[:, part * tokens : (part + 1) * tokens] = grad_parts[part]
    grad_rows[...] = grad[...].T
    allowed = causal(Q_ROWS)
    blocks = length // Q_ROWS
    for block in reversed(range(blocks)):
        first = block * Q_ROWS
        columns = slice(first, first + Q_ROWS)
        scaled = qkv_ref[query, columns] * ATTN_SCALE
        logs = log_ref[:, columns]
        grad_block = grad[:, columns]
        inner = jnp.sum(grad_block.astype(F32) * wide_ref[:, columns], axis=0, keepdims=True)
        total = jnp.zeros((HD, Q_ROWS), F32)
        spans = [(columns, True)]
        if block:
            spans.append((slice(0, first), False))
        for keys, near in spans:
            weights = jnp.exp(dot(key_rows[keys, :], scaled, ((1,), (0,))) - logs)
            if near:
                weights = jnp.where(allowed, weights, 0.0)
            grad_weights = dot(value_rows[keys, :], grad_block, ((1,), (0,)))
            grad_scores = (weights * (grad_weights - inner)).astype(BF16)
            total = total + dot(qkv_ref[key, keys], grad_scores, ((1,), (0,)))
            key_part = dot(grad_scores, query_rows[columns, :], ((1,), (0,)))
            value_part = dot(weights.astype(BF16), grad_rows[columns, :], ((1,), (0,)))
            if block == blocks - 1:
                grad_key[keys, :] = key_part
                grad_value[keys, :] = value_part
            else:
                grad_key[keys, :] += key_part
                grad_value[keys, :] += value_part
        grad_query[:, columns] = total * ATTN_SCALE
    half = HD // 2
    cosine, sine = cosine_ref[...], -sine_ref[...]
    for place, wide in enumerate((grad_query[...], grad_key[...].T * ATTN_SCALE)):
        rows = rotate(wide[:half], wide[half:], cosine, sine)
        wide_grad[place * HD : (place + 1) * HD] = jnp.concatenate(rows, axis=0).astype(BF16)
    wide_grad[2 * HD :] = grad_value[...].T.astype(BF16)
    for part in range(count):
        parts_out[part] = wide_grad[:, part * tokens : (part + 1) * tokens]
    back = Exchange(parts_out, out_ref, send_b, recv_b)
    back.start()
    out_ref[rank] = parts_out[rank]
    copy.wait()
    for stage in (3, 2, 1, 0):
        scatter.stage(stage)
    weight_ref[...] = dot(wide_grad[...], normed[...], ((1,), (0,)))
    rows = sum_ref.shape[0] // 2
    for place, value_half in enumerate(scatter.result()):
        sum_ref[place * rows : (place + 1) * rows] = value_half
    back.arrive()
    back.sent()
    swap.sent()
    scatter.finish()


def backward(qkv, grad_context, wide, logs, cosine, sine, normed, context, grad_att):
    count, _, tokens = grad_context.shape
    length, width = normed.shape
    shape = jax.ShapeDtypeStruct
    low = pltpu.VMEM((length, HD), BF16)
    return call(
        backward_kernel, "backward", 4,
        (shape((count, 3 * HD, tokens), BF16), shape((3 * HD, width), F32), shape((HD, width), F32)),
        [whole()] * 6 + [anywhere()] + [whole()] * 2, [whole()] * 3,
        [
            pltpu.VMEM((count, HD, tokens), BF16), pltpu.VMEM((count, 3 * HD, tokens), BF16), pltpu.VMEM((HD, length), BF16),
            low, low, low, low,
            pltpu.VMEM((HD, length), F32), pltpu.VMEM((length, HD), F32), pltpu.VMEM((length, HD), F32),
            pltpu.VMEM((length, width), BF16), pltpu.VMEM((3 * HD, length), BF16),
            pltpu.VMEM((count, HD, width), BF16), pltpu.VMEM(((count - 1) * HD, width), BF16),
            *pair_sems(count - 1), *pair_sems(count - 1), *pair_sems(Torus.COUNT), pltpu.SemaphoreType.DMA,
        ],
        48, flops=2 * length * length * HD * 5, bytes_accessed=12 << 20,
    )(qkv, grad_context, wide, logs, cosine, sine, normed, context, grad_att)


SMALL = 384


def finish_kernel(
    weight_ref, out_sum_ref, small_ref, query_ref, out_ref, keyval_ref, small_out,
    give, pair_land, mine, land, summed, small_parts, small_land, small_sum, small_dp, gather_buf,
    send_p, recv_p, send_s, recv_s, send_a, recv_a, send_b, recv_b, send_c, recv_c, send_d, recv_d, send_e, recv_e,
):
    count = RING * RING
    rank, dp = lax.axis_index("tensor"), lax.axis_index("dp")
    dps = land.shape[0]
    odd = lax.rem(rank, 2)
    partner = rank + 1 - 2 * odd
    width = weight_ref.shape[1]
    column = width // dps
    give[...] = weight_ref[pl.ds(pl.multiple_of(HD + HD * (1 - odd), HD), HD), :].astype(BF16)
    for i in range(count):
        small_parts[i, :, :256] = small_ref[8 * (i // 4) : 8 * (i // 4) + 8, 256 * (i % 4) : 256 * (i % 4) + 256]
        small_parts[i, :, 256:] = small_ref[32:40, 128 * (i // 2) : 128 * (i // 2) + 128]
    greet(others("tensor", count), others("dp", dps))
    swap = pltpu.make_async_remote_copy(
        src_ref=give, dst_ref=pair_land, send_sem=send_p, recv_sem=recv_p, device_id=(dp, partner), device_id_type=MESH_ID
    )
    swap.start()
    small = Exchange(small_parts, small_land, send_s, recv_s)
    small.start()
    small_land[rank] = small_parts[rank]
    lists = [weight_ref[:HD], out_sum_ref[...]]
    swap.wait_recv()
    lists.append(weight_ref[pl.ds(pl.multiple_of(HD + HD * odd, HD), HD), :] + pair_land[...].astype(F32))
    for j, rows in enumerate(lists):
        low = rows.astype(BF16)
        for i in range(dps):
            mine[i, j * HD : (j + 1) * HD] = low[:, i * column : (i + 1) * column]
    first = Exchange(mine, land, send_a, recv_a, "dp")
    first.start()
    land[dp] = mine[dp]
    small.arrive()
    small_sum[...] = jnp.sum(small_land[...], axis=0)
    second_small = Exchange(small_sum, small_dp, send_c, recv_c, "dp", same=True)
    second_small.start()
    small_dp[dp] = small_sum[...]
    first.arrive()
    own = jnp.sum(land[...].astype(F32), axis=0).astype(BF16)
    summed[dp] = own
    second = Exchange(summed.at[dp], summed, send_b, recv_b, "dp", same=True)
    second.start()
    second_small.arrive()
    second_small.sent()
    small_sum[...] = jnp.sum(small_dp[...], axis=0)
    third_small = Exchange(small_sum, small_out, send_d, recv_d, same=True)
    third_small.start()
    small_out[rank] = small_sum[...]
    second.arrive()
    for i in range(dps):
        columns = slice(i * column, (i + 1) * column)
        query_ref[:, columns] = summed[i, :HD]
        out_ref[:, columns] = summed[i, HD : 2 * HD]
        gather_buf[rank, :, columns] = summed[i, 2 * HD :]
    gather = Gather(gather_buf, send_e, recv_e)
    for stage in range(6):
        gather.stage(stage)
    gather.finish()
    for i in range(count):
        base = (i % 2) * KV_HEADS * HD + (i // 2) * HD
        keyval_ref[base : base + HD, :] = gather_buf[i]
    third_small.arrive()
    swap.wait_send()
    for each in (small, first, second, third_small):
        each.sent()


def finish(weight, out_sum, small, dps):
    width = weight.shape[1]
    count = RING * RING
    column = width // dps
    shape = jax.ShapeDtypeStruct
    small_shape = (8, SMALL)
    return call(
        finish_kernel, "finish", 5,
        (shape((HD, width), BF16), shape((HD, width), BF16), shape((count * HD, width), BF16), shape((count, *small_shape), F32)),
        [whole()] * 3, [whole()] * 4,
        [
            pltpu.VMEM((HD, width), BF16), pltpu.VMEM((HD, width), BF16), pltpu.VMEM((dps, 3 * HD, column), BF16),
            pltpu.VMEM((dps, 3 * HD, column), BF16), pltpu.VMEM((dps, 3 * HD, column), BF16),
            pltpu.VMEM((count, *small_shape), F32), pltpu.VMEM((count, *small_shape), F32), pltpu.VMEM(small_shape, F32),
            pltpu.VMEM((dps, *small_shape), F32), pltpu.VMEM((count, HD, width), BF16),
            pltpu.SemaphoreType.DMA, pltpu.SemaphoreType.DMA, *pair_sems(count - 1), *pair_sems(dps - 1), *pair_sems(dps - 1),
            *pair_sems(dps - 1), *pair_sems(count - 1), *pair_sems(Torus.COUNT),
        ],
        40, flops=1 << 24, bytes_accessed=10 << 20,
    )(weight, out_sum, small)


def shards(
    block_input, attn_gain, w_query, w_keyval, w_out, ffn_gain, w_router, w_gateup, w_down, routes, cotangent,
):
    devices = lax.axis_size("tensor")
    rank = lax.axis_index("tensor")
    tokens, width = block_input.shape
    length = tokens * devices
    local = w_gateup.shape[0]
    hidden_width = w_down.shape[1]

    routes_all = lax.all_gather(routes.T, "tensor", axis=0)
    cosine, sine = rope_tables(length, HD)
    normed_one_all, qkv, wide_out, logs, context, query_all, out_all, cotangent_all = forward(
        block_input, attn_gain, w_query, w_keyval, w_out, cotangent, cosine, sine
    )
    residual, normed_two, normed_two_all = middle(block_input, context, out_all, ffn_gain)
    query_all = query_all.reshape(HEADS * HD, width)
    out_all = out_all.reshape(HEADS * HD, width)

    ids = jnp.arange(EXPERTS, dtype=jnp.int32)
    named = jnp.any(routes_all[:, :, None, :] == ids[None, None, :, None], axis=1)

    def gates_of(normed, mask):
        logits = jnp.where(mask, dot(w_router, normed, ((0,), (1,))), -1e30)
        powers = jnp.where(mask, jnp.exp(logits - jnp.max(logits, axis=0, keepdims=True)), 0.0)
        return powers / jnp.sum(powers, axis=0, keepdims=True)

    own_named = lax.dynamic_index_in_dim(named, rank, 0, keepdims=False)
    own_gates = gates_of(normed_two, own_named)
    wide_named = named.transpose(1, 0, 2).reshape(EXPERTS, length)
    gates = gates_of(normed_two_all.reshape(length, width), wide_named)
    gates = lax.dynamic_slice_in_dim(gates, rank * local, local, 0).reshape(local, devices, tokens).transpose(1, 0, 2)
    mine = lax.dynamic_slice_in_dim(named, rank * local, local, 1)
    upper = jnp.asarray(np.triu(np.ones((tokens, tokens), np.float32), 1), BF16)
    place = jnp.einsum("set,tu->seu", mine.astype(BF16), upper, preferred_element_type=F32)
    slots = jnp.arange(CAP, dtype=F32)
    onehot = (place[:, :, None, :] == slots[None, None, :, None]) & mine[:, :, None, :]
    pick = onehot.astype(BF16).reshape(devices, local * CAP, tokens)
    slot_gates = jnp.sum(jnp.where(onehot, gates[:, :, None, :], 0.0), axis=3, keepdims=True)

    arrived = jnp.einsum("sct,std->scd", pick, normed_two_all, preferred_element_type=F32).astype(BF16)
    arrived = arrived.reshape(devices, local, CAP, width)
    grad_slots = jnp.einsum("sct,std->scd", pick, cotangent_all, preferred_element_type=F32)
    grad_slots = RES_SCALE * grad_slots.reshape(devices, local, CAP, width)
    grad_arrived = (slot_gates * grad_slots).astype(BF16)
    activations = jnp.einsum("secd,edf->secf", arrived, w_gateup, preferred_element_type=F32)
    gate_part = activations[..., :hidden_width]
    up_part = activations[..., hidden_width:]
    gate_sigmoid = jax.nn.sigmoid(gate_part)
    hidden = (gate_part * gate_sigmoid * up_part).astype(BF16)
    produced = jnp.einsum("secf,efd->secd", hidden, w_down, preferred_element_type=F32).astype(BF16)
    grad_hidden = jnp.einsum("secd,efd->secf", grad_arrived, w_down, preferred_element_type=F32)
    grad_gate = grad_hidden * up_part * gate_sigmoid * (1.0 + gate_part * (1.0 - gate_sigmoid))
    grad_up = grad_hidden * gate_part * gate_sigmoid
    grad_acts = jnp.concatenate([grad_gate, grad_up], axis=-1).astype(BF16)
    grad_rows = jnp.einsum("secf,edf->secd", grad_acts, w_gateup, preferred_element_type=F32).astype(BF16)
    slot_grads = jnp.sum(grad_slots * produced.astype(F32), axis=3, keepdims=True)
    grad_gates = jnp.sum(jnp.where(onehot, slot_grads, 0.0), axis=2)
    weighted = (slot_gates * produced.astype(F32)).astype(BF16).reshape(devices, local * CAP, width)
    combined_part = jnp.einsum("sct,scd->std", pick, weighted, preferred_element_type=F32).astype(BF16)
    grad_part = jnp.einsum("sct,scd->std", pick, grad_rows.reshape(devices, local * CAP, width), preferred_element_type=F32).astype(BF16)
    grad_w_down = jnp.einsum("secf,secd->efd", hidden, grad_arrived, preferred_element_type=F32)
    grad_w_gateup = jnp.einsum("secd,secf->edf", arrived, grad_acts, preferred_element_type=F32)
    grad_w_gateup, grad_w_down = lax.psum((grad_w_gateup.astype(BF16), grad_w_down.astype(BF16)), "dp")

    padded = jnp.concatenate([grad_gates, jnp.zeros((devices, 8 - local, tokens), F32)], axis=1)
    grad_back, combined, own_grads = scatter_two(grad_part, combined_part, padded)
    block_out = (residual + RES_SCALE * combined).astype(BF16)
    own_grads = own_grads[:, :local].reshape(EXPERTS, tokens)
    grad_logits = own_gates * (own_grads - jnp.sum(own_gates * own_grads, axis=0, keepdims=True))
    grad_logits = grad_logits.astype(BF16)
    grad_router = dot(grad_logits, normed_two, ((1,), (0,)))
    grad_normed_two = dot(grad_logits, w_router, ((0,), (1,))) + grad_back
    gain_two = ffn_gain.astype(F32)
    grad_residual_norm, grad_gain_two = norm_back(residual, rms_scale(residual), gain_two, grad_normed_two)
    grad_residual = cotangent.astype(F32) + grad_residual_norm
    grad_attention = (RES_SCALE * grad_residual).astype(BF16)

    grad_context = dot(out_all, grad_attention, ((1,), (1,))).astype(BF16).reshape(HEADS, HD, tokens)
    back, grad_w, grad_out_sum = backward(
        qkv, grad_context, wide_out, logs, cosine, sine, normed_one_all.reshape(length, width), context, grad_attention
    )
    share = HEADS // KV_HEADS
    back = back.reshape(HEADS, 3, HD, tokens)
    back_pairs = jnp.sum(back[:, 1:].reshape(KV_HEADS, share, 2, HD, tokens).astype(F32), axis=1).astype(BF16)
    back_pairs = back_pairs.transpose(1, 0, 2, 3).reshape(2 * KV_HEADS * HD, tokens)
    grad_normed_one = dot(back[:, 0].reshape(HEADS * HD, tokens), query_all, ((0,), (0,))) + dot(
        back_pairs, w_keyval, ((0,), (1,))
    )
    inputs = block_input.astype(F32)
    grad_input_norm, grad_gain_one = norm_back(inputs, rms_scale(inputs), attn_gain.astype(F32), grad_normed_one)
    grad_input = grad_residual + grad_input_norm

    small = jnp.concatenate([grad_router, grad_gain_two[None], grad_gain_one[None], jnp.zeros((6, width), F32)], axis=0)
    grad_query_w, grad_w_out, grad_keyval, small = finish(grad_w, grad_out_sum, small, lax.axis_size("dp"))
    routers = small[:, :, :256].reshape(4, 4, 8, 256).transpose(0, 2, 1, 3).reshape(EXPERTS, width)
    gains = small[::2, :2, 256:].transpose(1, 0, 2).reshape(2, width)
    return (
        block_out,
        grad_input,
        gains[1],
        grad_query_w.astype(F32).T,
        grad_keyval.astype(F32).T,
        grad_w_out.astype(F32),
        gains[0],
        routers.T,
        grad_w_gateup.astype(F32),
        grad_w_down.astype(F32),
    )


def solution(mesh):
    rows = P(("dp", "tensor"), None)
    in_specs = (
        rows, P(), P(None, "tensor"), P(), P("tensor", None), P(), P(),
        P("tensor", None, None), P("tensor", None, None), rows, rows,
    )
    out_specs = (
        rows, rows, P(), P(None, "tensor"), P(), P("tensor", None), P(), P(),
        P("tensor", None, None), P("tensor", None, None),
    )
    return jax.shard_map(shards, mesh=mesh, in_specs=in_specs, out_specs=out_specs, check_vma=False)
```

```python
import jax
import jax.numpy as jnp
import numpy as np
from jax import lax
from jax.experimental import pallas as pl
from jax.experimental.pallas import tpu as pltpu
from jax.sharding import PartitionSpec as P

HEADS = 16
KV_HEADS = 8
HD = 64
EXPERTS = 32
TOP = 8
CAP = 64
ATTN_SCALE = 0.015625
RES_SCALE = 0.22
EPSILON = 1e-06
ROPE_BASE = 10000.0
F32 = jnp.float32
BF16 = jnp.bfloat16
Q_ROWS = 256


def rms_scale(values):
    return lax.rsqrt(jnp.mean(values * values, axis=-1, keepdims=True) + EPSILON)


def norm_back(values, scale, gain, grad_normed):
    grad_scaled = grad_normed * gain
    grad_gain = jnp.sum(grad_normed * values * scale, axis=0)
    inner = jnp.mean(grad_scaled * values, axis=-1, keepdims=True)
    return (scale * (grad_scaled - values * scale * scale * inner), grad_gain)


def rope_tables(length, width):
    half_width = width // 2
    inverse = ROPE_BASE ** (-(jnp.arange(half_width, dtype=F32) * 2.0) / width)
    angles = jnp.arange(length, dtype=F32)[None, :] * inverse[:, None]
    return (jnp.cos(angles), jnp.sin(angles))


def rotate(first, second, cosine, sine):
    return first * cosine - second * sine, second * cosine + first * sine


def dot(a, b, dims):
    return lax.dot_general(a, b, ((dims[0], dims[1]), ((), ())), preferred_element_type=F32)


def causal(rows):
    key = lax.broadcasted_iota(jnp.int32, (rows, rows), 0)
    query = lax.broadcasted_iota(jnp.int32, (rows, rows), 1)
    return key <= query


RING = 4
MESH_ID = pl.DeviceIdType.MESH


def whole():
    return pl.BlockSpec(memory_space=pltpu.VMEM)


def anywhere():
    return pl.BlockSpec(memory_space=pl.ANY)


def position():
    rank = lax.axis_index("tensor")
    return lax.div(rank, RING), lax.rem(rank, RING)


def shifted(pos, axis, by):
    moved = lax.rem(pos[axis] + (by + RING), RING)
    return (moved, pos[1]) if axis == 0 else (pos[0], moved)


def joined(pos):
    return pos[0] * RING + pos[1]


def greet(tensor_peers, dp_peers=()):
    dp, rank = lax.axis_index("dp"), lax.axis_index("tensor")
    sem = pltpu.get_barrier_semaphore()
    peers = [(dp, p) for p in tensor_peers] + [(p, rank) for p in dp_peers]
    for peer in peers:
        pl.semaphore_signal(sem, inc=1, device_id=peer, device_id_type=MESH_ID)
    pl.semaphore_wait(sem, len(peers))


def neighbours():
    pos = position()
    return [joined(shifted(pos, axis, by)) for axis in (0, 1) for by in (1, -1)]


def others(axis, count):
    return [lax.rem(lax.axis_index(axis) + r, count) for r in range(1, count)]


def torus_messages(half, rows):
    primary, secondary = (0, 1) if half == 0 else (1, 0)
    h, q = rows // 2, rows // 4
    full = (half * h, h)
    part = {1: (half * h, q), -1: (half * h + q, q)}
    out = []
    for d in (1, -1):
        out.append((0, ("p1", d), None, full, (0, 0), primary, d))
        out.append((0, ("s1", 0, d), None, full, (0, 0), secondary, d))
        out.append((1, ("p2", d), ("p1", d), part[d], (-d, 0), primary, d))
        for e in (1, -1):
            out.append((1, ("s1", -d, e), ("p1", d), full, (-d, 0), secondary, e))
    for e in (1, -1):
        out.append((2, ("s2", 0, e), ("s1", 0, e), part[e], (0, -e), secondary, e))
        for d in (1, -1):
            out.append((3, ("s1", ("o", d), e), ("p2", d), part[d], (2, 0), secondary, e))
            out.append((4, ("s2", d, e), ("s1", d, e), part[e], (d, -e), secondary, e))
        out.append((5, ("s2", "o", e), ("s1", ("o", e), e), part[e], (2, -e), secondary, e))
    return out


class Torus:
    COUNT = 44
    STAGES = 6

    def __init__(self, rows):
        self.rows = rows
        self.pos = position()
        self.dp = lax.axis_index("dp")
        self.messages, self.children, self.place, order, used = {}, {}, {}, [], 0
        for half in (0, 1):
            for at, (stage, key, needs, piece, offset, axis, way) in enumerate(torus_messages(half, rows)):
                key = (half, key)
                needs = None if needs is None else (half, needs)
                self.messages[key] = (len(order), stage, needs, piece, offset, axis, way)
                self.children.setdefault(needs, []).append(key)
                self.place[key] = used
                used += piece[1]
                order.append((stage, at, half, key))
        self.landing_rows = used
        self.order = [entry[3] for entry in sorted(order, key=lambda entry: entry[:3])]

    def block(self, key, pos):
        half, offset = key[0], self.messages[key][4]
        primary, secondary = (0, 1) if half == 0 else (1, 0)
        return joined(shifted(shifted(pos, primary, offset[0]), secondary, offset[1]))

    def sender(self, key):
        _, _, _, _, _, axis, way = self.messages[key]
        return shifted(self.pos, axis, -way)

    def receiver(self, key):
        _, _, _, _, _, axis, way = self.messages[key]
        return shifted(self.pos, axis, way)


class Gather(Torus):
    def __init__(self, buf, send, recv):
        super().__init__(buf.shape[1])
        self.buf, self.send, self.recv = buf, send, recv
        self.arrived = set()

    def copy(self, key, incoming):
        number, (first, count) = self.messages[key][0], self.messages[key][3]
        at = self.sender(key) if incoming else self.pos
        ref = self.buf.at[self.block(key, at), pl.ds(first, count)]
        return pltpu.make_async_remote_copy(
            src_ref=ref, dst_ref=ref, send_sem=self.send.at[number], recv_sem=self.recv.at[number],
            device_id=(self.dp, joined(at if incoming else self.receiver(key))), device_id_type=MESH_ID,
        )

    def arrive(self, key):
        if key not in self.arrived:
            self.arrived.add(key)
            self.copy(key, True).wait_recv()

    def stage(self, number):
        for key in self.order:
            _, stage, needs, *_ = self.messages[key]
            if stage == number:
                if needs is not None:
                    self.arrive(needs)
                self.copy(key, False).start()

    def arrive_stage(self, number):
        for key in self.order:
            if self.messages[key][1] == number:
                self.arrive(key)

    def finish(self):
        for key in self.order:
            self.arrive(key)
        for key in self.order:
            self.copy(key, False).wait_send()


class Scatter(Torus):
    def __init__(self, parts, landing, send, recv):
        super().__init__(parts.shape[1])
        self.parts, self.landing, self.send, self.recv = parts, landing, send, recv

    def copy(self, key):
        number, (first, count) = self.messages[key][0], self.messages[key][3]
        at = self.sender(key)
        return pltpu.make_async_remote_copy(
            src_ref=self.parts.at[self.block(key, at), pl.ds(first, count)],
            dst_ref=self.landing.at[pl.ds(self.place[key], count)],
            send_sem=self.send.at[number], recv_sem=self.recv.at[number],
            device_id=(self.dp, joined(at)), device_id_type=MESH_ID,
        )

    def landed(self, key):
        count = self.messages[key][3][1]
        self.copy(key).wait_recv()
        return self.landing[pl.ds(self.place[key], count), :].astype(F32)

    def stage(self, number):
        for key in reversed(self.order):
            if self.messages[key][1] == number:
                pieces = {}
                for child in self.children.get(key, []):
                    pieces.setdefault(self.messages[child][3], []).append(child)
                for (first, count), children in pieces.items():
                    at = (self.block(children[0], self.pos), pl.ds(first, count))
                    self.parts[at] = sum((self.landed(c) for c in children), self.parts[at].astype(F32)).astype(self.parts.dtype)
                self.copy(key).start()

    def result(self):
        out = []
        for half in (0, 1):
            children = [c for c in self.children[None] if c[0] == half]
            first, count = self.messages[children[0]][3]
            own = self.parts[joined(self.pos), pl.ds(first, count)].astype(F32)
            out.append(sum((self.landed(c) for c in children), own))
        return out

    def finish(self):
        for key in self.order:
            self.copy(key).wait_send()


class Exchange:
    def __init__(self, source, target, send, recv, axis="tensor", same=False):
        self.source, self.target, self.send, self.recv, self.axis, self.same = source, target, send, recv, axis, same
        self.count = target.shape[0]
        self.rank = lax.axis_index(axis)

    def device(self, to):
        if self.axis == "tensor":
            return (lax.axis_index("dp"), to)
        return (to, lax.axis_index("tensor"))

    def copy(self, r):
        to = lax.rem(self.rank + r, self.count)
        return pltpu.make_async_remote_copy(
            src_ref=self.source if self.same else self.source.at[to],
            dst_ref=self.target.at[self.rank], send_sem=self.send.at[r - 1],
            recv_sem=self.recv.at[r - 1], device_id=self.device(to), device_id_type=MESH_ID,
        )

    def start(self):
        for r in range(1, self.count):
            self.copy(r).start()

    def arrive(self):
        for r in range(1, self.count):
            origin = lax.rem(self.rank + self.count - r, self.count)
            pltpu.make_async_remote_copy(
                src_ref=self.target.at[origin], dst_ref=self.target.at[origin], send_sem=self.send.at[r - 1],
                recv_sem=self.recv.at[r - 1], device_id=self.device(origin), device_id_type=MESH_ID,
            ).wait_recv()

    def sent(self):
        for r in range(1, self.count):
            self.copy(r).wait_send()


def pair_sems(count):
    return [pltpu.SemaphoreType.DMA((count,))] * 2


def call(kernel, name, number, out_shape, in_specs, out_specs, scratch, limit, flops=0, bytes_accessed=0):
    return pl.pallas_call(
        kernel, out_shape=out_shape, in_specs=in_specs, out_specs=out_specs, scratch_shapes=scratch,
        compiler_params=pltpu.CompilerParams(collective_id=number, has_side_effects=True, vmem_limit_bytes=limit << 20),
        cost_estimate=pl.CostEstimate(flops=flops, bytes_accessed=bytes_accessed, transcendentals=0),
        name=name,
    )


def forward_kernel(
    x_ref, gain_ref, gain_two_ref, query_ref, keyval_ref, out_w_ref, cot_ref, cosine_ref, sine_ref, routes_ref,
    normed_out, qkv_out, wide_ref, log_ref, context_ref, query_all, out_out, cot_all, routes_all, residual_ref, normed_two_ref,
    buf, query_t, local_w, pair_w, qkv, key_rows, context_parts, out_all,
    sems_a, sems_b, sems_c, sems_d, sems_e, sems_f, local_sems,
):
    tokens, width = x_ref.shape
    rank = lax.axis_index("tensor")
    z, y = position()
    half = HD // 2
    pair_copies = []
    for part in range(2):
        column = pl.multiple_of(part * KV_HEADS * HD + z * 2 * HD, 2 * HD)
        copy = pltpu.make_async_copy(keyval_ref.at[:, pl.ds(column, 2 * HD)], pair_w.at[part], local_sems.at[part])
        copy.start()
        pair_copies.append(copy)
    own_cot = pltpu.make_async_copy(cot_ref, cot_all.at[rank], local_sems.at[2])
    own_cot.start()
    own_out = pltpu.make_async_copy(out_w_ref, out_all.at[rank], local_sems.at[3])
    own_out.start()
    inputs = x_ref[...].astype(F32)
    buf[rank] = (inputs * rms_scale(inputs) * gain_ref[...].astype(F32)).astype(BF16)
    greet(others("tensor", RING * RING))
    main = Gather(buf, *sems_a)
    main.stage(0)
    tell = Exchange(routes_ref, routes_all, *sems_f, same=True)
    tell.start()
    routes_all[rank] = routes_ref[...]
    query_t[...] = query_ref[...].T
    own_query = pltpu.make_async_copy(query_t, query_all.at[rank], local_sems.at[4])
    own_query.start()
    for copy in pair_copies:
        copy.wait()
    odd = lax.rem(lax.div(rank, 2), 2)
    local_w[:HD] = query_t[...]
    for part in range(2):
        tall = pair_w[part].T.astype(F32)
        local_w[HD * (part + 1) : HD * (part + 2)] = jnp.where(odd == 0, tall[:HD], tall[HD:]).astype(BF16)
    pos = main.pos

    def project(dz, dy):
        block = joined(shifted(shifted(pos, 0, dz), 1, dy))
        columns = pl.ds(pl.multiple_of(block * tokens, tokens), tokens)
        made = dot(local_w[...], buf[block], ((1,), (1,)))
        cosine, sine = cosine_ref[:, columns], sine_ref[:, columns]
        rows = []
        for first in (0, HD):
            rows += rotate(made[first : first + half], made[first + half : first + HD], cosine, sine)
        rows.append(made[2 * HD :])
        qkv[:, columns] = jnp.concatenate(rows, axis=0).astype(BF16)

    project(0, 0)
    main.stage(1)
    main.stage(2)
    main.arrive_stage(0)
    for offset in ((0, 1), (0, 3), (1, 0), (3, 0)):
        project(*offset)
    main.stage(3)
    main.stage(4)
    own_out.wait()
    own_query.wait()
    own_cot.wait()
    back = [Gather(out_all, *sems_b), Gather(query_all, *sems_c), Gather(cot_all, *sems_d)]
    main.arrive_stage(1)
    main.arrive_stage(2)
    for offset in ((1, 1), (1, 3), (3, 1), (3, 3), (2, 0), (0, 2)):
        project(*offset)
    main.stage(5)
    for other in back:
        other.stage(0)
    main.arrive_stage(3)
    main.arrive_stage(4)
    for offset in ((2, 1), (2, 3), (1, 2), (3, 2)):
        project(*offset)
    main.arrive_stage(5)
    project(2, 2)
    normed_copy = pltpu.make_async_copy(buf, normed_out, local_sems.at[5])
    normed_copy.start()
    qkv_copy = pltpu.make_async_copy(qkv, qkv_out, local_sems.at[6])
    qkv_copy.start()
    key_rows[...] = qkv[HD : 2 * HD].T
    swap = Exchange(context_parts, context_ref, *sems_e)
    todo = [(other, stage) for stage in range(1, 6) for other in back]
    attend(qkv, key_rows, wide_ref, log_ref, context_parts, tokens, todo)
    swap.start()
    context_ref[rank] = context_parts[rank]
    for other, stage in todo:
        other.stage(stage)
    tell.arrive()
    back[0].finish()
    out_copy = pltpu.make_async_copy(out_all, out_out, local_sems.at[7])
    out_copy.start()
    swap.arrive()
    context = context_ref[...].reshape(HEADS * HD, tokens)
    attention = dot(context, out_all[...].reshape(HEADS * HD, width), ((0,), (0,)))
    residual = x_ref[...].astype(F32) + RES_SCALE * attention
    residual_ref[...] = residual
    normed_two_ref[...] = (residual * rms_scale(residual) * gain_two_ref[...].astype(F32)).astype(BF16)
    for other in back[1:]:
        other.finish()
    main.finish()
    swap.sent()
    tell.sent()
    out_copy.wait()
    normed_copy.wait()
    qkv_copy.wait()


def attend(qkv, key_rows, wide_ref, log_ref, parts_ref, tokens, todo):
    length = qkv.shape[1]
    allowed = causal(Q_ROWS)
    query, value = slice(0, HD), slice(2 * HD, 3 * HD)
    for block in range(length // Q_ROWS):
        first = block * Q_ROWS
        columns = slice(first, first + Q_ROWS)
        scaled = qkv[query, columns] * ATTN_SCALE
        near = dot(key_rows[columns, :], scaled, ((1,), (0,)))
        near = jnp.where(allowed, near, -1e30)
        largest = jnp.max(near, axis=0, keepdims=True)
        if block:
            far = dot(key_rows[:first, :], scaled, ((1,), (0,)))
            largest = jnp.maximum(largest, jnp.max(far, axis=0, keepdims=True))
        near = jnp.exp(near - largest)
        total = jnp.sum(near, axis=0, keepdims=True)
        context = dot(qkv[value, columns], near.astype(BF16), ((1,), (0,)))
        if block:
            far = jnp.exp(far - largest)
            total = total + jnp.sum(far, axis=0, keepdims=True)
            context = context + dot(qkv[value, :first], far.astype(BF16), ((1,), (0,)))
        context = context / total
        wide_ref[:, columns] = context
        log_ref[:, columns] = largest + jnp.log(total)
        low = context.astype(BF16)
        for part in range(Q_ROWS // tokens):
            parts_ref[first // tokens + part] = low[:, part * tokens : (part + 1) * tokens]
        for _ in range(min(len(todo), 1 if block >= 3 else 0)):
            other, stage = todo.pop(0)
            other.stage(stage)


def forward(x, gain, gain_two, w_query, w_keyval, w_out, cotangent, cosine, sine, routes):
    tokens, width = x.shape
    count = RING * RING
    length = tokens * count

    def kernel(*refs):
        plain, sems = refs[:-13], refs[-13:]
        forward_kernel(*plain, *[sems[2 * i : 2 * i + 2] for i in range(6)], sems[12])

    shape = jax.ShapeDtypeStruct
    return call(
        kernel, "forward", 1,
        (
            shape((count, tokens, width), BF16), shape((3 * HD, length), BF16), shape((HD, length), F32),
            shape((1, length), F32), shape((count, HD, tokens), BF16), shape((count, HD, width), BF16),
            shape((count, HD, width), BF16), shape((count, tokens, width), BF16),
            shape((count, *routes.shape), jnp.int32), shape((tokens, width), F32), shape((tokens, width), BF16),
        ),
        [whole(), whole(), whole(), whole(), anywhere(), anywhere(), anywhere(), whole(), whole(), whole()],
        [anywhere(), anywhere(), whole(), whole(), whole(), anywhere(), anywhere(), anywhere(), whole(), whole(), whole()],
        [
            pltpu.VMEM((count, tokens, width), BF16), pltpu.VMEM((HD, width), BF16), pltpu.VMEM((3 * HD, width), BF16),
            pltpu.VMEM((2, width, 2 * HD), BF16), pltpu.VMEM((3 * HD, length), BF16), pltpu.VMEM((length, HD), BF16),
            pltpu.VMEM((count, HD, tokens), BF16), pltpu.VMEM((count, HD, width), BF16),
            *(pair_sems(Torus.COUNT) * 4), *pair_sems(count - 1), *pair_sems(count - 1), pltpu.SemaphoreType.DMA((8,)),
        ],
        48, flops=2 * length * (3 * HD * width + length * HD * 2), bytes_accessed=20 << 20,
    )(x, gain.reshape(1, width), gain_two.reshape(1, width), w_query, w_keyval, w_out, cotangent, cosine, sine, routes)


GROUPS = (
    ((0, 0), (0, 1), (0, 3), (1, 0), (3, 0)),
    ((1, 1), (1, 3), (3, 1), (3, 3), (2, 0), (0, 2)),
    ((2, 1), (2, 3), (1, 2), (3, 2), (2, 2)),
)
MOST = 6 * CAP
CHUNK = 32


def expert_kernel(
    normed_ref, residual_ref, cot_own_ref, gain_ref, router_ref, routes_ref, cot_ref, gateup_ref, down_ref, out_w_ref,
    grad_gateup_out, grad_down_out, combined_out, grad_residual_ref, grad_att_ref, small_ref, grad_context_ref,
    buf, cot, gateup, down, out_w, pick, gate_cols, arrived, grad_acts, grad_arrived, hidden, grad_slots,
    acts, grad_hidden, produced, grad_rows, parts, combined, landing, stage_w, notes, told, own_gates,
    send_a, recv_a, send_b, recv_b, send_c, recv_c, local, store,
):
    tokens, width = normed_ref.shape
    count = RING * RING
    local_experts, ff = down.shape[0], down.shape[1]
    rank = lax.axis_index("tensor")
    buf[rank] = normed_ref[...]
    loads = [pltpu.make_async_copy(a, b, local.at[i]) for i, (a, b) in enumerate(((gateup_ref, gateup), (down_ref, down), (cot_ref, cot), (out_w_ref, out_w)))]
    for load in loads:
        load.start()
    greet(others("tensor", count))
    gather = Gather(buf, send_a, recv_a)
    gather.stage(0)
    router = router_ref[...]
    ids = lax.broadcasted_iota(jnp.int32, (EXPERTS, tokens), 0)
    slot_ids = lax.broadcasted_iota(jnp.int32, (CAP, tokens), 0).astype(F32)
    before = lax.broadcasted_iota(jnp.int32, (tokens, tokens), 0) < lax.broadcasted_iota(jnp.int32, (tokens, tokens), 1)
    upper = jnp.where(before, 1.0, 0.0).astype(BF16)
    pos = gather.pos

    def named_of(block):
        routes = routes_ref[block]
        hits = ids == routes[0:1]
        for k in range(1, TOP):
            hits = hits | (ids == routes[k : k + 1])
        return hits

    def gates_of(normed, named):
        logits = jnp.where(named, dot(router, normed, ((1,), (1,))), -1e30)
        powers = jnp.where(named, jnp.exp(logits - jnp.max(logits, axis=0, keepdims=True)), 0.0)
        return powers / jnp.sum(powers, axis=0, keepdims=True)

    @pl.loop(0, count)
    def _(block):
        named = jnp.where(named_of(block), 1.0, 0.0)
        places = dot(named.astype(BF16), upper, ((1,), (0,)))
        for e in range(local_experts):
            mine = ids == rank * local_experts + e
            hit = jnp.sum(jnp.where(mine, named, 0.0), axis=0, keepdims=True)
            at = jnp.sum(jnp.where(mine, places, 0.0), axis=0, keepdims=True)
            at = jnp.where(hit > 0.5, at, -1.0)
            pick[block, e * CAP : (e + 1) * CAP] = jnp.where(slot_ids == at, 1.0, 0.0).astype(BF16)

    gather.stage(1)
    gather.stage(2)
    for load in loads:
        load.wait()

    def work(group, base):
        rows = len(group) * CAP
        blocks = [joined(shifted(shifted(pos, 0, dz), 1, dy)) for dz, dy in group]
        for i, block in enumerate(blocks):
            normed = buf[block]
            gates = gates_of(normed, named_of(block))
            if group[i] == (0, 0):
                own_gates[...] = gates
            chosen = pick[block]
            picked = dot(chosen, normed, ((1,), (0,))).astype(BF16)
            slots = dot(chosen, cot[block], ((1,), (0,)))
            for e in range(local_experts):
                rows_e = slice(e * CAP, (e + 1) * CAP)
                gate = jnp.sum(jnp.where(ids == rank * local_experts + e, gates, 0.0), axis=0, keepdims=True)
                column = jnp.sum(chosen[rows_e].astype(F32) * gate, axis=1, keepdims=True)
                gate_cols[e, i * CAP : (i + 1) * CAP] = column
                arrived[e, base + i * CAP : base + (i + 1) * CAP] = picked[rows_e]
                grad_slots[e, i * CAP : (i + 1) * CAP] = slots[rows_e].astype(BF16)
                grad_arrived[e, base + i * CAP : base + (i + 1) * CAP] = (column * (RES_SCALE * slots[rows_e])).astype(BF16)

        @pl.loop(0, local_experts)
        def _(e):
            acts[:rows] = dot(arrived[e, base : base + rows], gateup[e], ((1,), (0,)))
            grad_hidden[:rows] = dot(grad_arrived[e, base : base + rows], down[e], ((1,), (1,)))

            @pl.loop(0, rows // CHUNK)
            def _(c):
                at = pl.ds(pl.multiple_of(c * CHUNK, CHUNK), CHUNK)
                out = pl.ds(pl.multiple_of(base + c * CHUNK, CHUNK), CHUNK)
                gate, up = acts[at, :ff], acts[at, ff:]
                sigmoid = 1.0 / (1.0 + jnp.exp(-gate))
                silu = gate * sigmoid
                back = grad_hidden[at]
                hidden[e, out] = (silu * up).astype(BF16)
                grad_acts[e, out, :ff] = (back * up * sigmoid * (1.0 + gate * (1.0 - sigmoid))).astype(BF16)
                grad_acts[e, out, ff:] = (back * silu).astype(BF16)

            produced[e, :rows] = dot(hidden[e, base : base + rows], down[e], ((1,), (0,))).astype(BF16)
            grad_rows[e, :rows] = dot(grad_acts[e, base : base + rows], gateup[e], ((1,), (1,))).astype(BF16)

        for i, block in enumerate(blocks):
            at = slice(i * CAP, (i + 1) * CAP)
            chosen = pick[block]
            back = jnp.concatenate([grad_rows[e, at] for e in range(local_experts)], axis=0)
            parts[block] = dot(chosen, back, ((0,), (0,))).astype(BF16)
            weighted = []
            for e in range(local_experts):
                made = produced[e, at].astype(F32)
                weighted.append((gate_cols[e, at] * made).astype(BF16))
                column = RES_SCALE * jnp.sum(made * grad_slots[e, at].astype(F32), axis=1, keepdims=True)
                hits = chosen[e * CAP : (e + 1) * CAP].astype(F32)
                notes[block, e : e + 1] = jnp.sum(hits * column, axis=0, keepdims=True)
            combined[block] = dot(chosen, jnp.concatenate(weighted, axis=0), ((0,), (0,))).astype(BF16)

    gather.arrive_stage(0)
    work(GROUPS[0], 0)
    gather.stage(3)
    gather.stage(4)
    gather.arrive_stage(1)
    gather.arrive_stage(2)
    base = len(GROUPS[0]) * CAP
    work(GROUPS[1], base)
    gather.stage(5)
    for stage in (3, 4, 5):
        gather.arrive_stage(stage)
    base += len(GROUPS[1]) * CAP
    work(GROUPS[2], base)

    scatter = Scatter(parts, landing, send_b, recv_b)
    scatter.stage(5)
    scatter.stage(4)
    swap = Exchange(notes, told, send_c, recv_c)
    swap.start()
    told[rank] = notes[rank]
    combined_copy = pltpu.make_async_copy(combined, combined_out, local.at[4])
    combined_copy.start()
    strip = stage_w.shape[1]
    jobs = []
    for e in range(local_experts):
        jobs += [(arrived, grad_acts, grad_gateup_out, e, first) for first in range(0, width, strip)]
        jobs += [(hidden, grad_arrived, grad_down_out, e, first) for first in range(0, ff, strip)]
    stores = []

    def weights(number):
        left, right, out, e, first = jobs[number]
        slot = number % 2
        if number >= 2:
            stores[number - 2].wait()
        stage_w[slot] = dot(left[e, :, first : first + strip], right[e], ((0,), (0,))).astype(BF16)
        copy = pltpu.make_async_copy(stage_w.at[slot], out.at[e, pl.ds(first, strip)], store.at[slot])
        copy.start()
        stores.append(copy)

    plan = {3: 4, 2: 2, 1: 4, 0: 2}
    number = 0
    for stage in (3, 2, 1, 0):
        for _ in range(plan[stage]):
            if number < len(jobs):
                weights(number)
                number += 1
        scatter.stage(stage)
    while number < len(jobs):
        weights(number)
        number += 1
    swap.arrive()
    gates = own_gates[...]
    grads = jnp.concatenate([told[i, :local_experts] for i in range(count)], axis=0)
    grad_logits = (gates * (grads - jnp.sum(gates * grads, axis=0, keepdims=True))).astype(BF16)
    normed = normed_ref[...]
    small_ref[...] = jnp.zeros_like(small_ref)
    small_ref[:EXPERTS] = dot(grad_logits, normed, ((1,), (0,)))
    from_router = dot(grad_logits, router, ((0,), (0,)))
    gain = gain_ref[...].astype(F32)
    half = tokens // 2
    grad_gain = jnp.zeros((1, width), F32)
    for place, back in enumerate(scatter.result()):
        at = slice(place * half, (place + 1) * half)
        residual = residual_ref[at]
        scale = rms_scale(residual)
        grad_normed = from_router[at] + back
        grad_norm, part = norm_back(residual, scale, gain, grad_normed)
        grad_gain = grad_gain + part[None]
        grad_residual = cot_own_ref[at].astype(F32) + grad_norm
        grad_residual_ref[at] = grad_residual
        grad_att_ref[at] = (RES_SCALE * grad_residual).astype(BF16)
    small_ref[EXPERTS : EXPERTS + 1] = grad_gain
    grad_context_ref[...] = dot(out_w[...].reshape(HEADS * HD, width), grad_att_ref[...], ((1,), (1,))).astype(BF16).reshape(HEADS, HD, tokens)
    scatter.finish()
    gather.finish()
    swap.sent()
    for copy in stores[-2:]:
        copy.wait()
    combined_copy.wait()


def experts(normed, residual, cot_own, gain, router, routes_all, cot_all, w_gateup, w_down, out_all):
    tokens, width = normed.shape
    count = RING * RING
    local_experts, ff = w_down.shape[:2]
    shape = jax.ShapeDtypeStruct
    vmem = pltpu.VMEM
    rows = count * CAP
    return call(
        expert_kernel, "experts", 2,
        (
            shape(w_gateup.shape, BF16), shape(w_down.shape, BF16), shape((count, tokens, width), BF16),
            shape((tokens, width), F32), shape((tokens, width), BF16), shape((EXPERTS + 8, width), F32),
            shape((HEADS, HD, tokens), BF16),
        ),
        [whole()] * 6 + [anywhere()] * 4, [anywhere()] * 3 + [whole()] * 4,
        [
            vmem((count, tokens, width), BF16), vmem((count, tokens, width), BF16), vmem(w_gateup.shape, BF16),
            vmem(w_down.shape, BF16), vmem((HEADS, HD, width), BF16), vmem((count, local_experts * CAP, tokens), BF16),
            vmem((local_experts, MOST, 1), F32), vmem((local_experts, rows, width), BF16),
            vmem((local_experts, rows, 2 * ff), BF16), vmem((local_experts, rows, width), BF16),
            vmem((local_experts, rows, ff), BF16), vmem((local_experts, MOST, width), BF16),
            vmem((MOST, 2 * ff), F32), vmem((MOST, ff), F32), vmem((local_experts, MOST, width), BF16),
            vmem((local_experts, MOST, width), BF16), vmem((count, tokens, width), BF16), vmem((count, tokens, width), BF16),
            vmem(((count - 1) * tokens, width), BF16), vmem((2, 256, width), BF16), vmem((count, 8, tokens), F32),
            vmem((count, 8, tokens), F32), vmem((EXPERTS, tokens), F32),
            *pair_sems(Torus.COUNT), *pair_sems(Torus.COUNT), *pair_sems(count - 1),
            pltpu.SemaphoreType.DMA((5,)), pltpu.SemaphoreType.DMA((2,)),
        ],
        62, flops=2 * 9 * rows * width * ff * local_experts, bytes_accessed=30 << 20,
    )(normed, residual, cot_own, gain.reshape(1, width), router, routes_all, cot_all, w_gateup, w_down, out_all)


def backward_kernel(
    qkv_ref, grad_ref, wide_ref, log_ref, cosine_ref, sine_ref, normed_ref, context_ref, grad_att_ref, combined_ref, residual_ref,
    out_ref, weight_ref, sum_ref, block_ref,
    grad_parts, parts_out, grad, query_rows, key_rows, value_rows, grad_rows, grad_query, grad_key, grad_value,
    normed, wide_grad, out_parts, out_land, combined, combined_land,
    send_a, recv_a, send_b, recv_b, send_c, recv_c, send_d, recv_d, local,
):
    count, _, tokens = grad_ref.shape
    length = count * tokens
    rank = lax.axis_index("tensor")
    copy = pltpu.make_async_copy(normed_ref, normed, local.at[0])
    copy.start()
    load = pltpu.make_async_copy(combined_ref, combined, local.at[1])
    load.start()
    greet(others("tensor", count))
    swap = Exchange(grad_ref, grad_parts, send_a, recv_a)
    swap.start()
    query, key, value = slice(0, HD), slice(HD, 2 * HD), slice(2 * HD, 3 * HD)
    query_rows[...] = qkv_ref[query].T
    key_rows[...] = qkv_ref[key].T
    value_rows[...] = qkv_ref[value].T
    scatter = Scatter(out_parts, out_land, send_c, recv_c)
    grad_att = grad_att_ref[...]
    for part in range(count):
        out_parts[part] = dot(context_ref[part], grad_att, ((1,), (0,))).astype(BF16)
    grad_parts[rank] = grad_ref[rank]
    swap.arrive()
    scatter.stage(5)
    scatter.stage(4)
    load.wait()
    combine = Scatter(combined, combined_land, send_d, recv_d)
    combine.stage(5)
    combine.stage(4)
    plan = {1: (scatter, 3), 2: (combine, 3), 3: (scatter, 2), 4: (combine, 2), 5: (scatter, 1), 7: (combine, 1)}
    for part in range(count):
        grad[:, part * tokens : (part + 1) * tokens] = grad_parts[part]
    grad_rows[...] = grad[...].T
    allowed = causal(Q_ROWS)
    blocks = length // Q_ROWS
    for block in reversed(range(blocks)):
        first = block * Q_ROWS
        columns = slice(first, first + Q_ROWS)
        scaled = qkv_ref[query, columns] * ATTN_SCALE
        logs = log_ref[:, columns]
        grad_block = grad[:, columns]
        inner = jnp.sum(grad_block.astype(F32) * wide_ref[:, columns], axis=0, keepdims=True)
        total = jnp.zeros((HD, Q_ROWS), F32)
        spans = [(columns, True)]
        if block:
            spans.append((slice(0, first), False))
        for keys, near in spans:
            weights = jnp.exp(dot(key_rows[keys, :], scaled, ((1,), (0,))) - logs)
            if near:
                weights = jnp.where(allowed, weights, 0.0)
            grad_weights = dot(value_rows[keys, :], grad_block, ((1,), (0,)))
            grad_scores = (weights * (grad_weights - inner)).astype(BF16)
            total = total + dot(qkv_ref[key, keys], grad_scores, ((1,), (0,)))
            key_part = dot(grad_scores, query_rows[columns, :], ((1,), (0,)))
            value_part = dot(weights.astype(BF16), grad_rows[columns, :], ((1,), (0,)))
            if block == blocks - 1:
                grad_key[keys, :] = key_part
                grad_value[keys, :] = value_part
            else:
                grad_key[keys, :] += key_part
                grad_value[keys, :] += value_part
        grad_query[:, columns] = total * ATTN_SCALE
        if blocks - 1 - block in plan:
            each, stage = plan[blocks - 1 - block]
            each.stage(stage)
    half = HD // 2
    cosine, sine = cosine_ref[...], -sine_ref[...]
    for place, wide in enumerate((grad_query[...], grad_key[...].T * ATTN_SCALE)):
        rows = rotate(wide[:half], wide[half:], cosine, sine)
        wide_grad[place * HD : (place + 1) * HD] = jnp.concatenate(rows, axis=0).astype(BF16)
    wide_grad[2 * HD :] = grad_value[...].T.astype(BF16)
    for part in range(count):
        parts_out[part] = wide_grad[:, part * tokens : (part + 1) * tokens]
    back = Exchange(parts_out, out_ref, send_b, recv_b)
    back.start()
    out_ref[rank] = parts_out[rank]
    copy.wait()
    scatter.stage(0)
    combine.stage(0)
    weight_ref[...] = dot(wide_grad[...], normed[...], ((1,), (0,)))
    rows = sum_ref.shape[0] // 2
    for place, value_half in enumerate(scatter.result()):
        sum_ref[place * rows : (place + 1) * rows] = value_half
    rows = block_ref.shape[0] // 2
    for place, value_half in enumerate(combine.result()):
        at = slice(place * rows, (place + 1) * rows)
        block_ref[at] = (residual_ref[at] + RES_SCALE * value_half).astype(BF16)
    back.arrive()
    back.sent()
    swap.sent()
    scatter.finish()
    combine.finish()


def backward(qkv, grad_context, wide, logs, cosine, sine, normed, context, grad_att, combined, residual):
    count, _, tokens = grad_context.shape
    length, width = normed.shape
    shape = jax.ShapeDtypeStruct
    low = pltpu.VMEM((length, HD), BF16)
    return call(
        backward_kernel, "backward", 4,
        (shape((count, 3 * HD, tokens), BF16), shape((3 * HD, width), F32), shape((HD, width), F32), shape((tokens, width), BF16)),
        [whole()] * 6 + [anywhere()] + [whole()] * 2 + [anywhere(), whole()], [whole()] * 4,
        [
            pltpu.VMEM((count, HD, tokens), BF16), pltpu.VMEM((count, 3 * HD, tokens), BF16), pltpu.VMEM((HD, length), BF16),
            low, low, low, low,
            pltpu.VMEM((HD, length), F32), pltpu.VMEM((length, HD), F32), pltpu.VMEM((length, HD), F32),
            pltpu.VMEM((length, width), BF16), pltpu.VMEM((3 * HD, length), BF16),
            pltpu.VMEM((count, HD, width), BF16), pltpu.VMEM(((count - 1) * HD, width), BF16),
            pltpu.VMEM((count, tokens, width), BF16), pltpu.VMEM(((count - 1) * tokens, width), BF16),
            *pair_sems(count - 1), *pair_sems(count - 1), *pair_sems(Torus.COUNT), *pair_sems(Torus.COUNT),
            pltpu.SemaphoreType.DMA((2,)),
        ],
        56, flops=2 * length * length * HD * 5, bytes_accessed=12 << 20,
    )(qkv, grad_context, wide, logs, cosine, sine, normed, context, grad_att, combined, residual)


SMALL = 384


def finish_kernel(
    weight_ref, out_sum_ref, small_ref, query_ref, out_ref, keyval_ref, small_out,
    give, pair_land, mine, land, summed, small_parts, small_land, small_sum, small_dp, gather_buf,
    send_p, recv_p, send_s, recv_s, send_a, recv_a, send_b, recv_b, send_c, recv_c, send_d, recv_d, send_e, recv_e,
):
    count = RING * RING
    rank, dp = lax.axis_index("tensor"), lax.axis_index("dp")
    dps = land.shape[0]
    odd = lax.rem(rank, 2)
    partner = rank + 1 - 2 * odd
    width = weight_ref.shape[1]
    column = width // dps
    give[...] = weight_ref[pl.ds(pl.multiple_of(HD + HD * (1 - odd), HD), HD), :].astype(BF16)
    for i in range(count):
        small_parts[i, :, :256] = small_ref[8 * (i // 4) : 8 * (i // 4) + 8, 256 * (i % 4) : 256 * (i % 4) + 256]
        small_parts[i, :, 256:] = small_ref[32:40, 128 * (i // 2) : 128 * (i // 2) + 128]
    greet(others("tensor", count), others("dp", dps))
    swap = pltpu.make_async_remote_copy(
        src_ref=give, dst_ref=pair_land, send_sem=send_p, recv_sem=recv_p, device_id=(dp, partner), device_id_type=MESH_ID
    )
    swap.start()
    small = Exchange(small_parts, small_land, send_s, recv_s)
    small.start()
    small_land[rank] = small_parts[rank]
    lists = [weight_ref[:HD], out_sum_ref[...]]
    swap.wait_recv()
    lists.append(weight_ref[pl.ds(pl.multiple_of(HD + HD * odd, HD), HD), :] + pair_land[...].astype(F32))
    for j, rows in enumerate(lists):
        low = rows.astype(BF16)
        for i in range(dps):
            mine[i, j * HD : (j + 1) * HD] = low[:, i * column : (i + 1) * column]
    first = Exchange(mine, land, send_a, recv_a, "dp")
    first.start()
    land[dp] = mine[dp]
    small.arrive()
    small_sum[...] = jnp.sum(small_land[...], axis=0)
    second_small = Exchange(small_sum, small_dp, send_c, recv_c, "dp", same=True)
    second_small.start()
    small_dp[dp] = small_sum[...]
    first.arrive()
    own = jnp.sum(land[...].astype(F32), axis=0).astype(BF16)
    summed[dp] = own
    second = Exchange(summed.at[dp], summed, send_b, recv_b, "dp", same=True)
    second.start()
    second_small.arrive()
    second_small.sent()
    small_sum[...] = jnp.sum(small_dp[...], axis=0)
    third_small = Exchange(small_sum, small_out, send_d, recv_d, same=True)
    third_small.start()
    small_out[rank] = small_sum[...]
    second.arrive()
    for i in range(dps):
        columns = slice(i * column, (i + 1) * column)
        query_ref[:, columns] = summed[i, :HD]
        out_ref[:, columns] = summed[i, HD : 2 * HD]
        gather_buf[rank, :, columns] = summed[i, 2 * HD :]
    gather = Gather(gather_buf, send_e, recv_e)
    for stage in range(6):
        gather.stage(stage)
    gather.finish()
    for i in range(count):
        base = (i % 2) * KV_HEADS * HD + (i // 2) * HD
        keyval_ref[base : base + HD, :] = gather_buf[i]
    third_small.arrive()
    swap.wait_send()
    for each in (small, first, second, third_small):
        each.sent()


def finish(weight, out_sum, small, dps):
    width = weight.shape[1]
    count = RING * RING
    column = width // dps
    shape = jax.ShapeDtypeStruct
    small_shape = (8, SMALL)
    return call(
        finish_kernel, "finish", 5,
        (shape((HD, width), BF16), shape((HD, width), BF16), shape((count * HD, width), BF16), shape((count, *small_shape), F32)),
        [whole()] * 3, [whole()] * 4,
        [
            pltpu.VMEM((HD, width), BF16), pltpu.VMEM((HD, width), BF16), pltpu.VMEM((dps, 3 * HD, column), BF16),
            pltpu.VMEM((dps, 3 * HD, column), BF16), pltpu.VMEM((dps, 3 * HD, column), BF16),
            pltpu.VMEM((count, *small_shape), F32), pltpu.VMEM((count, *small_shape), F32), pltpu.VMEM(small_shape, F32),
            pltpu.VMEM((dps, *small_shape), F32), pltpu.VMEM((count, HD, width), BF16),
            pltpu.SemaphoreType.DMA, pltpu.SemaphoreType.DMA, *pair_sems(count - 1), *pair_sems(dps - 1), *pair_sems(dps - 1),
            *pair_sems(dps - 1), *pair_sems(count - 1), *pair_sems(Torus.COUNT),
        ],
        40, flops=1 << 24, bytes_accessed=10 << 20,
    )(weight, out_sum, small)


def shards(
    block_input, attn_gain, w_query, w_keyval, w_out, ffn_gain, w_router, w_gateup, w_down, routes, cotangent,
):
    devices = lax.axis_size("tensor")
    tokens, width = block_input.shape
    length = tokens * devices

    cosine, sine = rope_tables(length, HD)
    normed_one_all, qkv, wide_out, logs, context, query_all, out_all, cotangent_all, routes_all, residual, normed_two = forward(
        block_input, attn_gain, ffn_gain, w_query, w_keyval, w_out, cotangent, cosine, sine, routes.T
    )
    query_all = query_all.reshape(HEADS * HD, width)
    grad_w_gateup, grad_w_down, combined, grad_residual, grad_attention, small, grad_context = experts(
        normed_two, residual, cotangent, ffn_gain, w_router.T, routes_all, cotangent_all, w_gateup, w_down, out_all
    )
    grad_w_gateup, grad_w_down = lax.psum((grad_w_gateup, grad_w_down), "dp")
    back, grad_w, grad_out_sum, block_out = backward(
        qkv, grad_context, wide_out, logs, cosine, sine, normed_one_all.reshape(length, width), context, grad_attention,
        combined, residual,
    )
    share = HEADS // KV_HEADS
    back = back.reshape(HEADS, 3, HD, tokens)
    back_pairs = jnp.sum(back[:, 1:].reshape(KV_HEADS, share, 2, HD, tokens).astype(F32), axis=1).astype(BF16)
    back_pairs = back_pairs.transpose(1, 0, 2, 3).reshape(2 * KV_HEADS * HD, tokens)
    grad_normed_one = dot(back[:, 0].reshape(HEADS * HD, tokens), query_all, ((0,), (0,))) + dot(
        back_pairs, w_keyval, ((0,), (1,))
    )
    inputs = block_input.astype(F32)
    grad_input_norm, grad_gain_one = norm_back(inputs, rms_scale(inputs), attn_gain.astype(F32), grad_normed_one)
    grad_input = grad_residual + grad_input_norm

    small = lax.dynamic_update_slice(small, grad_gain_one[None], (EXPERTS + 1, 0))
    grad_query_w, grad_w_out, grad_keyval, small = finish(grad_w, grad_out_sum, small, lax.axis_size("dp"))
    routers = small[:, :, :256].reshape(4, 4, 8, 256).transpose(0, 2, 1, 3).reshape(EXPERTS, width)
    gains = small[::2, :2, 256:].transpose(1, 0, 2).reshape(2, width)
    return (
        block_out,
        grad_input,
        gains[1],
        grad_query_w.astype(F32).T,
        grad_keyval.astype(F32).T,
        grad_w_out.astype(F32),
        gains[0],
        routers.T,
        grad_w_gateup.astype(F32),
        grad_w_down.astype(F32),
    )


def solution(mesh):
    rows = P(("dp", "tensor"), None)
    in_specs = (
        rows, P(), P(None, "tensor"), P(), P("tensor", None), P(), P(),
        P("tensor", None, None), P("tensor", None, None), rows, rows,
    )
    out_specs = (
        rows, rows, P(), P(None, "tensor"), P(), P("tensor", None), P(), P(),
        P("tensor", None, None), P("tensor", None, None),
    )
    return jax.shard_map(shards, mesh=mesh, in_specs=in_specs, out_specs=out_specs, check_vma=False)
```

```python
import jax
import jax.numpy as jnp
import numpy as np
from jax import lax
from jax.experimental import pallas as pl
from jax.experimental.pallas import tpu as pltpu
from jax.sharding import PartitionSpec as P

HEADS = 16
KV_HEADS = 8
HD = 64
EXPERTS = 32
TOP = 8
CAP = 64
ATTN_SCALE = 0.015625
RES_SCALE = 0.22
EPSILON = 1e-06
ROPE_BASE = 10000.0
F32 = jnp.float32
BF16 = jnp.bfloat16
Q_ROWS = 256


def rms_scale(values):
    return lax.rsqrt(jnp.mean(values * values, axis=-1, keepdims=True) + EPSILON)


def norm_back(values, scale, gain, grad_normed):
    grad_scaled = grad_normed * gain
    grad_gain = jnp.sum(grad_normed * values * scale, axis=0)
    inner = jnp.mean(grad_scaled * values, axis=-1, keepdims=True)
    return (scale * (grad_scaled - values * scale * scale * inner), grad_gain)


def rope_tables(length, width):
    half_width = width // 2
    inverse = ROPE_BASE ** (-(np.arange(half_width) * 2.0) / width)
    angles = np.arange(length)[None, :] * inverse[:, None]
    return (jnp.asarray(np.cos(angles), F32), jnp.asarray(np.sin(angles), F32))


def rotate(first, second, cosine, sine):
    return first * cosine - second * sine, second * cosine + first * sine


def dot(a, b, dims):
    return lax.dot_general(a, b, ((dims[0], dims[1]), ((), ())), preferred_element_type=F32)


def causal(rows):
    key = lax.broadcasted_iota(jnp.int32, (rows, rows), 0)
    query = lax.broadcasted_iota(jnp.int32, (rows, rows), 1)
    return key <= query


RING = 4
MESH_ID = pl.DeviceIdType.MESH


def whole():
    return pl.BlockSpec(memory_space=pltpu.VMEM)


def anywhere():
    return pl.BlockSpec(memory_space=pl.ANY)


def position():
    rank = lax.axis_index("tensor")
    return lax.div(rank, RING), lax.rem(rank, RING)


def shifted(pos, axis, by):
    moved = lax.rem(pos[axis] + (by + RING), RING)
    return (moved, pos[1]) if axis == 0 else (pos[0], moved)


def joined(pos):
    return pos[0] * RING + pos[1]


def greet(tensor_peers, dp_peers=()):
    dp, rank = lax.axis_index("dp"), lax.axis_index("tensor")
    sem = pltpu.get_barrier_semaphore()
    peers = [(dp, p) for p in tensor_peers] + [(p, rank) for p in dp_peers]
    for peer in peers:
        pl.semaphore_signal(sem, inc=1, device_id=peer, device_id_type=MESH_ID)
    pl.semaphore_wait(sem, len(peers))


def neighbours():
    pos = position()
    return [joined(shifted(pos, axis, by)) for axis in (0, 1) for by in (1, -1)]


def others(axis, count):
    return [lax.rem(lax.axis_index(axis) + r, count) for r in range(1, count)]


def torus_messages(half, rows):
    primary, secondary = (0, 1) if half == 0 else (1, 0)
    h, q = rows // 2, rows // 4
    full = (half * h, h)
    part = {1: (half * h, q), -1: (half * h + q, q)}
    out = []
    for d in (1, -1):
        out.append((0, ("p1", d), None, full, (0, 0), primary, d))
        out.append((0, ("s1", 0, d), None, full, (0, 0), secondary, d))
        out.append((1, ("p2", d), ("p1", d), part[d], (-d, 0), primary, d))
        for e in (1, -1):
            out.append((1, ("s1", -d, e), ("p1", d), full, (-d, 0), secondary, e))
    for e in (1, -1):
        out.append((2, ("s2", 0, e), ("s1", 0, e), part[e], (0, -e), secondary, e))
        for d in (1, -1):
            out.append((3, ("s1", ("o", d), e), ("p2", d), part[d], (2, 0), secondary, e))
            out.append((4, ("s2", d, e), ("s1", d, e), part[e], (d, -e), secondary, e))
        out.append((5, ("s2", "o", e), ("s1", ("o", e), e), part[e], (2, -e), secondary, e))
    return out


class Torus:
    COUNT = 44
    STAGES = 6

    def __init__(self, rows):
        self.rows = rows
        self.pos = position()
        self.dp = lax.axis_index("dp")
        self.messages, self.children, self.place, order, used = {}, {}, {}, [], 0
        for half in (0, 1):
            for at, (stage, key, needs, piece, offset, axis, way) in enumerate(torus_messages(half, rows)):
                key = (half, key)
                needs = None if needs is None else (half, needs)
                self.messages[key] = (len(order), stage, needs, piece, offset, axis, way)
                self.children.setdefault(needs, []).append(key)
                self.place[key] = used
                used += piece[1]
                order.append((stage, at, half, key))
        self.landing_rows = used
        self.order = [entry[3] for entry in sorted(order, key=lambda entry: entry[:3])]

    def block(self, key, pos):
        half, offset = key[0], self.messages[key][4]
        primary, secondary = (0, 1) if half == 0 else (1, 0)
        return joined(shifted(shifted(pos, primary, offset[0]), secondary, offset[1]))

    def sender(self, key):
        _, _, _, _, _, axis, way = self.messages[key]
        return shifted(self.pos, axis, -way)

    def receiver(self, key):
        _, _, _, _, _, axis, way = self.messages[key]
        return shifted(self.pos, axis, way)


class Gather(Torus):
    def __init__(self, buf, send, recv):
        super().__init__(buf.shape[1])
        self.buf, self.send, self.recv = buf, send, recv
        self.arrived = set()

    def copy(self, key, incoming):
        number, (first, count) = self.messages[key][0], self.messages[key][3]
        at = self.sender(key) if incoming else self.pos
        ref = self.buf.at[self.block(key, at), pl.ds(first, count)]
        return pltpu.make_async_remote_copy(
            src_ref=ref, dst_ref=ref, send_sem=self.send.at[number], recv_sem=self.recv.at[number],
            device_id=(self.dp, joined(at if incoming else self.receiver(key))), device_id_type=MESH_ID,
        )

    def arrive(self, key):
        if key not in self.arrived:
            self.arrived.add(key)
            self.copy(key, True).wait_recv()

    def stage(self, number):
        for key in self.order:
            _, stage, needs, *_ = self.messages[key]
            if stage == number:
                if needs is not None:
                    self.arrive(needs)
                self.copy(key, False).start()

    def arrive_stage(self, number):
        for key in self.order:
            if self.messages[key][1] == number:
                self.arrive(key)

    def finish(self):
        for key in self.order:
            self.arrive(key)
        for key in self.order:
            self.copy(key, False).wait_send()


class Scatter(Torus):
    def __init__(self, parts, landing, send, recv):
        super().__init__(parts.shape[1])
        self.parts, self.landing, self.send, self.recv = parts, landing, send, recv

    def copy(self, key):
        number, (first, count) = self.messages[key][0], self.messages[key][3]
        at = self.sender(key)
        return pltpu.make_async_remote_copy(
            src_ref=self.parts.at[self.block(key, at), pl.ds(first, count)],
            dst_ref=self.landing.at[pl.ds(self.place[key], count)],
            send_sem=self.send.at[number], recv_sem=self.recv.at[number],
            device_id=(self.dp, joined(at)), device_id_type=MESH_ID,
        )

    def landed(self, key):
        count = self.messages[key][3][1]
        self.copy(key).wait_recv()
        return self.landing[pl.ds(self.place[key], count), :].astype(F32)

    def stage(self, number):
        for key in reversed(self.order):
            if self.messages[key][1] == number:
                pieces = {}
                for child in self.children.get(key, []):
                    pieces.setdefault(self.messages[child][3], []).append(child)
                for (first, count), children in pieces.items():
                    at = (self.block(children[0], self.pos), pl.ds(first, count))
                    self.parts[at] = sum((self.landed(c) for c in children), self.parts[at].astype(F32)).astype(self.parts.dtype)
                self.copy(key).start()

    def result(self):
        out = []
        for half in (0, 1):
            children = [c for c in self.children[None] if c[0] == half]
            first, count = self.messages[children[0]][3]
            own = self.parts[joined(self.pos), pl.ds(first, count)].astype(F32)
            out.append(sum((self.landed(c) for c in children), own))
        return out

    def finish(self):
        for key in self.order:
            self.copy(key).wait_send()


class Exchange:
    def __init__(self, source, target, send, recv, axis="tensor", same=False):
        self.source, self.target, self.send, self.recv, self.axis, self.same = source, target, send, recv, axis, same
        self.count = target.shape[0]
        self.rank = lax.axis_index(axis)

    def device(self, to):
        if self.axis == "tensor":
            return (lax.axis_index("dp"), to)
        return (to, lax.axis_index("tensor"))

    def copy(self, r):
        to = lax.rem(self.rank + r, self.count)
        return pltpu.make_async_remote_copy(
            src_ref=self.source if self.same else self.source.at[to],
            dst_ref=self.target.at[self.rank], send_sem=self.send.at[r - 1],
            recv_sem=self.recv.at[r - 1], device_id=self.device(to), device_id_type=MESH_ID,
        )

    def start(self):
        for r in range(1, self.count):
            self.copy(r).start()

    def arrive(self):
        for r in range(1, self.count):
            origin = lax.rem(self.rank + self.count - r, self.count)
            pltpu.make_async_remote_copy(
                src_ref=self.target.at[origin], dst_ref=self.target.at[origin], send_sem=self.send.at[r - 1],
                recv_sem=self.recv.at[r - 1], device_id=self.device(origin), device_id_type=MESH_ID,
            ).wait_recv()

    def sent(self):
        for r in range(1, self.count):
            self.copy(r).wait_send()


def pair_sems(count):
    return [pltpu.SemaphoreType.DMA((count,))] * 2


def call(kernel, name, number, out_shape, in_specs, out_specs, scratch, limit, flops=0, bytes_accessed=0):
    return pl.pallas_call(
        kernel, out_shape=out_shape, in_specs=in_specs, out_specs=out_specs, scratch_shapes=scratch,
        compiler_params=pltpu.CompilerParams(collective_id=number, has_side_effects=True, vmem_limit_bytes=limit << 20),
        cost_estimate=pl.CostEstimate(flops=flops, bytes_accessed=bytes_accessed, transcendentals=0),
        name=name,
    )


def loads(pairs, sems):
    copies = [pltpu.make_async_copy(a, b, sems.at[i]) for i, (a, b) in enumerate(pairs)]
    for copy in copies:
        copy.start()
    return copies


class Replicas:
    COUNT = RING * RING - 1 + 9

    def __init__(self, own, buf, send, recv, local):
        self.own, self.buf, self.send, self.recv = own, buf, send, recv
        self.keep = pltpu.make_async_copy(*[ref.at[:, self.columns_of(buf)] for ref in (own, buf.at[lax.axis_index("tensor")])], local)
        self.rank, self.dp = lax.axis_index("tensor"), lax.axis_index("dp")
        self.x, self.core = lax.div(self.dp, 2), lax.rem(self.dp, 2)
        self.blocks = buf.shape[0]
        self.share = buf.shape[2] // (2 * RING)

    @staticmethod
    def columns_of(buf):
        share = buf.shape[2] // (2 * RING)
        return pl.ds(pl.multiple_of(lax.axis_index("dp") * share, share), share)

    def member(self, dx, other):
        core = 1 - self.core if other else self.core
        return lax.rem(self.x + dx + RING, RING) * 2 + core

    def columns(self, member):
        return pl.ds(pl.multiple_of(member * self.share, self.share), self.share)

    def piece(self, member, part):
        first, count = {0: (0, self.blocks), 1: (0, self.blocks // 2), -1: (self.blocks // 2, self.blocks // 2)}[part]
        return self.buf.at[pl.ds(first, count), :, self.columns(member)]

    def copy(self, number, ref, device):
        return pltpu.make_async_remote_copy(
            src_ref=ref, dst_ref=ref, send_sem=self.send.at[number], recv_sem=self.recv.at[number],
            device_id=device, device_id_type=MESH_ID,
        )

    def first(self):
        count = self.blocks
        self.outgoing = []
        self.keep.start()
        for r in range(1, count):
            self.outgoing.append(pltpu.make_async_remote_copy(
                src_ref=self.own.at[:, self.columns(self.dp)], dst_ref=self.buf.at[self.rank, :, self.columns(self.dp)],
                send_sem=self.send.at[r - 1], recv_sem=self.recv.at[r - 1],
                device_id=(self.dp, lax.rem(self.rank + r, count)), device_id_type=MESH_ID,
            ))
            self.outgoing[-1].start()

    def go(self, number, member, part, dx, other):
        self.outgoing.append(self.copy(self.blocks - 1 + number, self.piece(member, part), (self.member(dx, other), self.rank)))
        self.outgoing[-1].start()

    def come(self, number, member, part):
        self.copy(self.blocks - 1 + number, self.piece(member, part), (self.dp, self.rank)).wait_recv()

    def second(self):
        for r in range(1, self.blocks):
            ref = self.buf.at[lax.rem(self.rank + self.blocks - r, self.blocks), :, self.columns(self.dp)]
            self.copy(r - 1, ref, (self.dp, self.rank)).wait_recv()
        self.keep.wait()
        self.go(0, self.dp, 0, 1, False)
        self.go(1, self.dp, 0, -1, False)
        self.go(4, self.dp, 0, 0, True)

    def third(self):
        for number, way in ((0, 1), (1, -1)):
            member = self.member(-way, False)
            self.come(number, member, 0)
            self.go(2 + number, member, way, way, False)
            self.go(5 + number, member, 0, 0, True)

    def fourth(self):
        for number, way in ((0, 1), (1, -1)):
            member = self.member(2, False)
            self.come(2 + number, member, way)
            self.go(7 + number, member, way, 0, True)

    def finish(self):
        self.come(4, self.member(0, True), 0)
        for number, way in ((0, 1), (1, -1)):
            self.come(5 + number, self.member(-way, True), 0)
            self.come(7 + number, self.member(2, True), way)
        for copy in self.outgoing:
            copy.wait_send()


def near_members():
    x, core = lax.div(lax.axis_index("dp"), 2), lax.rem(lax.axis_index("dp"), 2)
    return [lax.rem(x + 1, RING) * 2 + core, lax.rem(x + RING - 1, RING) * 2 + core, x * 2 + 1 - core]


def forward_kernel(
    x_in, gain_in, gain_two_in, query_in, keyval_ref, out_w_ref, cot_ref, cosine_in, sine_in, routes_in,
    normed_out, qkv_out, wide_ref, log_ref, context_ref, weights_out, cot_all, routes_all, residual_ref, normed_two_ref,
    x_ref, gain_ref, gain_two_ref, cosine_ref, sine_ref,
    buf, weights, own_w, local_w, pair_w, qkv, key_rows, context_parts,
    sems_a, sems_b, sems_d, sems_e, sems_f, local_sems, load_sems,
):
    tokens, width = x_ref.shape
    rank = lax.axis_index("tensor")
    z, y = position()
    half = HD // 2
    copies = loads(
        [
            (x_in, x_ref), (gain_in, gain_ref), (out_w_ref, own_w.at[:HD]), (query_in, own_w.at[HD:]),
            (routes_in, routes_all.at[rank]), (cosine_in, cosine_ref), (sine_in, sine_ref), (gain_two_in, gain_two_ref),
        ],
        load_sems,
    )
    pair_copies = []
    for part in range(2):
        column = pl.multiple_of(part * KV_HEADS * HD + z * 2 * HD, 2 * HD)
        copy = pltpu.make_async_copy(keyval_ref.at[:, pl.ds(column, 2 * HD)], pair_w.at[part], local_sems.at[part])
        copy.start()
        pair_copies.append(copy)
    own_cot = pltpu.make_async_copy(cot_ref, cot_all.at[rank], local_sems.at[2])
    own_cot.start()
    copies[0].wait()
    copies[1].wait()
    inputs = x_ref[...].astype(F32)
    buf[rank] = (inputs * rms_scale(inputs) * gain_ref[...].reshape(1, width).astype(F32)).astype(BF16)
    greet(others("tensor", RING * RING), near_members())
    main = Gather(buf, *sems_a)
    main.stage(0)
    for copy in copies[2:5]:
        copy.wait()
    replicas = Replicas(own_w, weights, *sems_b, local_sems.at[3])
    replicas.first()
    tell = Exchange(routes_all.at[rank], routes_all, *sems_f, same=True)
    tell.start()
    for copy in pair_copies + copies[5:]:
        copy.wait()
    odd = lax.rem(lax.div(rank, 2), 2)
    local_w[:HD] = own_w[HD:]
    for part in range(2):
        tall = pair_w[part].T.astype(F32)
        local_w[HD * (part + 1) : HD * (part + 2)] = jnp.where(odd == 0, tall[:HD], tall[HD:]).astype(BF16)
    pos = main.pos

    def project(dz, dy):
        block = joined(shifted(shifted(pos, 0, dz), 1, dy))
        columns = pl.ds(pl.multiple_of(block * tokens, tokens), tokens)
        made = dot(local_w[...], buf[block], ((1,), (1,)))
        cosine, sine = cosine_ref[:, columns], sine_ref[:, columns]
        rows = []
        for first in (0, HD):
            rows += rotate(made[first : first + half], made[first + half : first + HD], cosine, sine)
        rows.append(made[2 * HD :])
        qkv[:, columns] = jnp.concatenate(rows, axis=0).astype(BF16)

    project(0, 0)
    main.stage(1)
    main.stage(2)
    replicas.second()
    main.arrive_stage(0)
    for offset in ((0, 1), (0, 3), (1, 0), (3, 0)):
        project(*offset)
    main.stage(3)
    main.stage(4)
    own_cot.wait()
    back = Gather(cot_all, *sems_d)
    main.arrive_stage(1)
    main.arrive_stage(2)
    for offset in ((1, 1), (1, 3), (3, 1), (3, 3), (2, 0), (0, 2)):
        project(*offset)
    main.stage(5)
    back.stage(0)
    main.arrive_stage(3)
    main.arrive_stage(4)
    replicas.third()
    for offset in ((2, 1), (2, 3), (1, 2), (3, 2)):
        project(*offset)
    main.arrive_stage(5)
    project(2, 2)
    normed_copy = pltpu.make_async_copy(buf, normed_out, local_sems.at[5])
    normed_copy.start()
    qkv_copy = pltpu.make_async_copy(qkv, qkv_out, local_sems.at[6])
    qkv_copy.start()
    key_rows[...] = qkv[HD : 2 * HD].T
    swap = Exchange(context_parts, context_ref, *sems_e)
    todo = {2: [lambda: back.stage(1)], 3: [lambda: back.stage(2)], 5: [replicas.fourth], 6: [lambda: back.stage(3)]}
    attend(qkv, key_rows, wide_ref, log_ref, context_parts, tokens, todo)
    swap.start()
    context_ref[rank] = context_parts[rank]
    back.stage(4)
    back.stage(5)
    replicas.finish()
    weights_copy = pltpu.make_async_copy(weights, weights_out, local_sems.at[7])
    weights_copy.start()
    tell.arrive()
    swap.arrive()
    context = context_ref[...].reshape(HEADS * HD, tokens)
    attention = dot(context, weights[:, :HD].reshape(HEADS * HD, width), ((0,), (0,)))
    residual = x_ref[...].astype(F32) + RES_SCALE * attention
    residual_ref[...] = residual
    normed_two_ref[...] = (residual * rms_scale(residual) * gain_two_ref[...].reshape(1, width).astype(F32)).astype(BF16)
    back.finish()
    main.finish()
    swap.sent()
    tell.sent()
    normed_copy.wait()
    qkv_copy.wait()
    weights_copy.wait()


def attend(qkv, key_rows, wide_ref, log_ref, parts_ref, tokens, todo):
    length = qkv.shape[1]
    allowed = causal(Q_ROWS)
    query, value = slice(0, HD), slice(2 * HD, 3 * HD)
    for block in range(length // Q_ROWS):
        first = block * Q_ROWS
        columns = slice(first, first + Q_ROWS)
        scaled = qkv[query, columns] * ATTN_SCALE
        near = dot(key_rows[columns, :], scaled, ((1,), (0,)))
        near = jnp.where(allowed, near, -1e30)
        largest = jnp.max(near, axis=0, keepdims=True)
        if block:
            far = dot(key_rows[:first, :], scaled, ((1,), (0,)))
            largest = jnp.maximum(largest, jnp.max(far, axis=0, keepdims=True))
        near = jnp.exp(near - largest)
        total = jnp.sum(near, axis=0, keepdims=True)
        context = dot(qkv[value, columns], near.astype(BF16), ((1,), (0,)))
        if block:
            far = jnp.exp(far - largest)
            total = total + jnp.sum(far, axis=0, keepdims=True)
            context = context + dot(qkv[value, :first], far.astype(BF16), ((1,), (0,)))
        context = context / total
        wide_ref[:, columns] = context
        log_ref[:, columns] = largest + jnp.log(total)
        low = context.astype(BF16)
        for part in range(Q_ROWS // tokens):
            parts_ref[first // tokens + part] = low[:, part * tokens : (part + 1) * tokens]
        for task in todo.get(block, ()):
            task()


def forward(x, gain, gain_two, w_query, w_keyval, w_out, cotangent, cosine, sine, routes):
    tokens, width = x.shape
    count = RING * RING
    length = tokens * count

    def kernel(*refs):
        plain, sems = refs[:-12], refs[-12:]
        forward_kernel(*plain, *[sems[2 * i : 2 * i + 2] for i in range(5)], sems[10], sems[11])

    shape = jax.ShapeDtypeStruct
    vmem = pltpu.VMEM
    return call(
        kernel, "forward", 1,
        (
            shape((count, tokens, width), BF16), shape((3 * HD, length), BF16), shape((HD, length), F32),
            shape((1, length), F32), shape((count, HD, tokens), BF16), shape((count, 2 * HD, width), BF16),
            shape((count, tokens, width), BF16),
            shape((count, *routes.shape), jnp.int32), shape((tokens, width), F32), shape((tokens, width), BF16),
        ),
        [anywhere()] * 10,
        [anywhere(), anywhere(), whole(), whole(), whole(), anywhere(), anywhere(), whole(), whole(), whole()],
        [
            vmem(x.shape, BF16), vmem(gain.shape, BF16), vmem(gain.shape, BF16), vmem(cosine.shape, F32), vmem(sine.shape, F32),
            vmem((count, tokens, width), BF16), vmem((count, 2 * HD, width), BF16), vmem((2 * HD, width), BF16), vmem((3 * HD, width), BF16),
            vmem((2, width, 2 * HD), BF16), vmem((3 * HD, length), BF16), vmem((length, HD), BF16),
            vmem((count, HD, tokens), BF16),
            *pair_sems(Torus.COUNT), *pair_sems(Replicas.COUNT), *pair_sems(Torus.COUNT),
            *pair_sems(count - 1), *pair_sems(count - 1), pltpu.SemaphoreType.DMA((8,)), pltpu.SemaphoreType.DMA((8,)),
        ],
        48, flops=2 * length * (3 * HD * width + length * HD * 2), bytes_accessed=20 << 20,
    )(x, gain, gain_two, w_query, w_keyval, w_out, cotangent, cosine, sine, routes)


GROUPS = (
    ((0, 0), (0, 1), (0, 3), (1, 0), (3, 0)),
    ((1, 1), (1, 3), (3, 1), (3, 3), (2, 0), (0, 2)),
    ((2, 1), (2, 3), (1, 2), (3, 2), (2, 2)),
)
MOST = 6 * CAP
CHUNK = 32


def expert_kernel(
    normed_in, residual_in, gain_in, router_in, routes_in, cot_ref, gateup_ref, down_ref, out_w_ref,
    grad_gateup_out, grad_down_out, combined_out, grad_residual_ref, grad_att_ref, small_ref, grad_context_ref,
    normed_ref, residual_ref, gain_ref, router_ref, routes_ref,
    buf, cot, gateup, down, out_w, pick, gate_cols, arrived, grad_acts, grad_arrived, hidden, grad_slots,
    acts, grad_hidden, produced, grad_rows, parts, combined, landing, stage_w, notes, told, own_gates,
    send_a, recv_a, send_b, recv_b, send_c, recv_c, local, store, early,
):
    tokens, width = normed_ref.shape
    count = RING * RING
    local_experts, ff = down.shape[0], down.shape[1]
    rank = lax.axis_index("tensor")
    first = loads(
        [
            (normed_in, buf.at[rank]), (router_in, router_ref), (routes_in, routes_ref),
            (normed_in, normed_ref), (residual_in, residual_ref), (gain_in, gain_ref),
        ],
        early,
    )
    late = loads([(gateup_ref, gateup), (down_ref, down), (cot_ref, cot), (out_w_ref.at[:, :HD], out_w)], local)
    greet(others("tensor", count))
    first[0].wait()
    gather = Gather(buf, send_a, recv_a)
    gather.stage(0)
    for load in first[1:]:
        load.wait()
    router = router_ref[...]
    ids = lax.broadcasted_iota(jnp.int32, (EXPERTS, tokens), 0)
    slot_ids = lax.broadcasted_iota(jnp.int32, (CAP, tokens), 0).astype(F32)
    before = lax.broadcasted_iota(jnp.int32, (tokens, tokens), 0) < lax.broadcasted_iota(jnp.int32, (tokens, tokens), 1)
    upper = jnp.where(before, 1.0, 0.0).astype(BF16)
    pos = gather.pos

    def named_of(block):
        routes = routes_ref[block]
        hits = ids == routes[0:1]
        for k in range(1, TOP):
            hits = hits | (ids == routes[k : k + 1])
        return hits

    def gates_of(normed, named):
        logits = jnp.where(named, dot(router, normed, ((1,), (1,))), -1e30)
        powers = jnp.where(named, jnp.exp(logits - jnp.max(logits, axis=0, keepdims=True)), 0.0)
        return powers / jnp.sum(powers, axis=0, keepdims=True)

    @pl.loop(0, count)
    def _(block):
        named = jnp.where(named_of(block), 1.0, 0.0)
        places = dot(named.astype(BF16), upper, ((1,), (0,)))
        for e in range(local_experts):
            mine = ids == rank * local_experts + e
            hit = jnp.sum(jnp.where(mine, named, 0.0), axis=0, keepdims=True)
            at = jnp.sum(jnp.where(mine, places, 0.0), axis=0, keepdims=True)
            at = jnp.where(hit > 0.5, at, -1.0)
            pick[block, e * CAP : (e + 1) * CAP] = jnp.where(slot_ids == at, 1.0, 0.0).astype(BF16)

    gather.stage(1)
    gather.stage(2)
    for load in late:
        load.wait()

    def work(group, base):
        rows = len(group) * CAP
        blocks = [joined(shifted(shifted(pos, 0, dz), 1, dy)) for dz, dy in group]
        for i, block in enumerate(blocks):
            normed = buf[block]
            gates = gates_of(normed, named_of(block))
            if group[i] == (0, 0):
                own_gates[...] = gates
            chosen = pick[block]
            picked = dot(chosen, normed, ((1,), (0,))).astype(BF16)
            slots = dot(chosen, cot[block], ((1,), (0,)))
            for e in range(local_experts):
                rows_e = slice(e * CAP, (e + 1) * CAP)
                gate = jnp.sum(jnp.where(ids == rank * local_experts + e, gates, 0.0), axis=0, keepdims=True)
                column = jnp.sum(chosen[rows_e].astype(F32) * gate, axis=1, keepdims=True)
                gate_cols[e, i * CAP : (i + 1) * CAP] = column
                arrived[e, base + i * CAP : base + (i + 1) * CAP] = picked[rows_e]
                grad_slots[e, i * CAP : (i + 1) * CAP] = slots[rows_e].astype(BF16)
                grad_arrived[e, base + i * CAP : base + (i + 1) * CAP] = (column * (RES_SCALE * slots[rows_e])).astype(BF16)

        @pl.loop(0, local_experts)
        def _(e):
            acts[:rows] = dot(arrived[e, base : base + rows], gateup[e], ((1,), (0,)))
            grad_hidden[:rows] = dot(grad_arrived[e, base : base + rows], down[e], ((1,), (1,)))

            @pl.loop(0, rows // CHUNK)
            def _(c):
                at = pl.ds(pl.multiple_of(c * CHUNK, CHUNK), CHUNK)
                out = pl.ds(pl.multiple_of(base + c * CHUNK, CHUNK), CHUNK)
                gate, up = acts[at, :ff], acts[at, ff:]
                sigmoid = 1.0 / (1.0 + jnp.exp(-gate))
                silu = gate * sigmoid
                back = grad_hidden[at]
                hidden[e, out] = (silu * up).astype(BF16)
                grad_acts[e, out, :ff] = (back * up * sigmoid * (1.0 + gate * (1.0 - sigmoid))).astype(BF16)
                grad_acts[e, out, ff:] = (back * silu).astype(BF16)

            produced[e, :rows] = dot(hidden[e, base : base + rows], down[e], ((1,), (0,))).astype(BF16)
            grad_rows[e, :rows] = dot(grad_acts[e, base : base + rows], gateup[e], ((1,), (1,))).astype(BF16)

        for i, block in enumerate(blocks):
            at = slice(i * CAP, (i + 1) * CAP)
            chosen = pick[block]
            back = jnp.concatenate([grad_rows[e, at] for e in range(local_experts)], axis=0)
            parts[block] = dot(chosen, back, ((0,), (0,))).astype(BF16)
            weighted = []
            for e in range(local_experts):
                made = produced[e, at].astype(F32)
                weighted.append((gate_cols[e, at] * made).astype(BF16))
                column = RES_SCALE * jnp.sum(made * grad_slots[e, at].astype(F32), axis=1, keepdims=True)
                hits = chosen[e * CAP : (e + 1) * CAP].astype(F32)
                notes[block, e : e + 1] = jnp.sum(hits * column, axis=0, keepdims=True)
            combined[block] = dot(chosen, jnp.concatenate(weighted, axis=0), ((0,), (0,))).astype(BF16)

    gather.arrive_stage(0)
    work(GROUPS[0], 0)
    gather.stage(3)
    gather.stage(4)
    gather.arrive_stage(1)
    gather.arrive_stage(2)
    base = len(GROUPS[0]) * CAP
    work(GROUPS[1], base)
    gather.stage(5)
    for stage in (3, 4, 5):
        gather.arrive_stage(stage)
    base += len(GROUPS[1]) * CAP
    work(GROUPS[2], base)

    scatter = Scatter(parts, landing, send_b, recv_b)
    scatter.stage(5)
    scatter.stage(4)
    swap = Exchange(notes, told, send_c, recv_c)
    swap.start()
    told[rank] = notes[rank]
    combined_copy = pltpu.make_async_copy(combined, combined_out, local.at[4])
    combined_copy.start()
    strip = stage_w.shape[1]
    jobs = []
    for e in range(local_experts):
        jobs += [(arrived, grad_acts, grad_gateup_out, e, first) for first in range(0, width, strip)]
        jobs += [(hidden, grad_arrived, grad_down_out, e, first) for first in range(0, ff, strip)]
    stores = []

    def weights(number):
        left, right, out, e, first = jobs[number]
        slot = number % 2
        if number >= 2:
            stores[number - 2].wait()
        stage_w[slot] = dot(left[e, :, first : first + strip], right[e], ((0,), (0,))).astype(BF16)
        copy = pltpu.make_async_copy(stage_w.at[slot], out.at[e, pl.ds(first, strip)], store.at[slot])
        copy.start()
        stores.append(copy)

    plan = {3: 4, 2: 2, 1: 4, 0: 2}
    number = 0
    for stage in (3, 2, 1, 0):
        for _ in range(plan[stage]):
            if number < len(jobs):
                weights(number)
                number += 1
        scatter.stage(stage)
    while number < len(jobs):
        weights(number)
        number += 1
    swap.arrive()
    gates = own_gates[...]
    grads = jnp.concatenate([told[i, :local_experts] for i in range(count)], axis=0)
    grad_logits = (gates * (grads - jnp.sum(gates * grads, axis=0, keepdims=True))).astype(BF16)
    normed = normed_ref[...]
    small_ref[...] = jnp.zeros_like(small_ref)
    small_ref[:EXPERTS] = dot(grad_logits, normed, ((1,), (0,)))
    from_router = dot(grad_logits, router, ((0,), (0,)))
    gain = gain_ref[...].reshape(1, width).astype(F32)
    half = tokens // 2
    grad_gain = jnp.zeros((1, width), F32)
    for place, back in enumerate(scatter.result()):
        at = slice(place * half, (place + 1) * half)
        residual = residual_ref[at]
        scale = rms_scale(residual)
        grad_normed = from_router[at] + back
        grad_norm, part = norm_back(residual, scale, gain, grad_normed)
        grad_gain = grad_gain + part[None]
        grad_residual = cot[rank, at].astype(F32) + grad_norm
        grad_residual_ref[at] = grad_residual
        grad_att_ref[at] = (RES_SCALE * grad_residual).astype(BF16)
    small_ref[EXPERTS : EXPERTS + 1] = grad_gain
    grad_context_ref[...] = dot(out_w[...].reshape(HEADS * HD, width), grad_att_ref[...], ((1,), (1,))).astype(BF16).reshape(HEADS, HD, tokens)
    scatter.finish()
    gather.finish()
    swap.sent()
    for copy in stores[-2:]:
        copy.wait()
    combined_copy.wait()


def experts(normed, residual, gain, router, routes_all, cot_all, w_gateup, w_down, weights):
    tokens, width = normed.shape
    count = RING * RING
    local_experts, ff = w_down.shape[:2]
    shape = jax.ShapeDtypeStruct
    vmem = pltpu.VMEM
    rows = count * CAP
    return call(
        expert_kernel, "experts", 2,
        (
            shape(w_gateup.shape, BF16), shape(w_down.shape, BF16), shape((count, tokens, width), BF16),
            shape((tokens, width), F32), shape((tokens, width), BF16), shape((EXPERTS + 8, width), F32),
            shape((HEADS, HD, tokens), BF16),
        ),
        [anywhere()] * 9, [anywhere()] * 3 + [whole()] * 4,
        [
            vmem(normed.shape, BF16), vmem(residual.shape, F32), vmem(gain.shape, BF16), vmem(router.shape, BF16), vmem(routes_all.shape, jnp.int32),
            vmem((count, tokens, width), BF16), vmem((count, tokens, width), BF16), vmem(w_gateup.shape, BF16),
            vmem(w_down.shape, BF16), vmem((HEADS, HD, width), BF16), vmem((count, local_experts * CAP, tokens), BF16),
            vmem((local_experts, MOST, 1), F32), vmem((local_experts, rows, width), BF16),
            vmem((local_experts, rows, 2 * ff), BF16), vmem((local_experts, rows, width), BF16),
            vmem((local_experts, rows, ff), BF16), vmem((local_experts, MOST, width), BF16),
            vmem((MOST, 2 * ff), F32), vmem((MOST, ff), F32), vmem((local_experts, MOST, width), BF16),
            vmem((local_experts, MOST, width), BF16), vmem((count, tokens, width), BF16), vmem((count, tokens, width), BF16),
            vmem(((count - 1) * tokens, width), BF16), vmem((2, 256, width), BF16), vmem((count, 8, tokens), F32),
            vmem((count, 8, tokens), F32), vmem((EXPERTS, tokens), F32),
            *pair_sems(Torus.COUNT), *pair_sems(Torus.COUNT), *pair_sems(count - 1),
            pltpu.SemaphoreType.DMA((5,)), pltpu.SemaphoreType.DMA((2,)), pltpu.SemaphoreType.DMA((6,)),
        ],
        62, flops=2 * 9 * rows * width * ff * local_experts, bytes_accessed=30 << 20,
    )(normed, residual, gain, router, routes_all, cot_all, w_gateup, w_down, weights)


def backward_kernel(
    qkv_in, grad_in, wide_in, log_in, cosine_in, sine_in, normed_ref, context_in, grad_att_in, combined_ref, residual_in,
    out_ref, weight_ref, sum_ref, block_ref,
    qkv_ref, grad_ref, wide_ref, log_ref, cosine_ref, sine_ref, context_ref, grad_att_ref, residual_ref,
    grad_parts, parts_out, grad, query_rows, key_rows, value_rows, grad_rows, grad_query, grad_key, grad_value,
    normed, wide_grad, out_parts, out_land, combined, combined_land,
    send_a, recv_a, send_b, recv_b, send_c, recv_c, send_d, recv_d, local, early,
):
    count, _, tokens = grad_ref.shape
    length = count * tokens
    rank = lax.axis_index("tensor")
    copy = pltpu.make_async_copy(normed_ref, normed, local.at[0])
    copy.start()
    load = pltpu.make_async_copy(combined_ref, combined, local.at[1])
    load.start()
    first_loads = loads(
        [
            (grad_in, grad_ref), (qkv_in, qkv_ref), (context_in, context_ref), (grad_att_in, grad_att_ref), (wide_in, wide_ref),
            (log_in, log_ref), (cosine_in, cosine_ref), (sine_in, sine_ref), (residual_in, residual_ref),
        ],
        early,
    )
    greet(others("tensor", count))
    first_loads[0].wait()
    swap = Exchange(grad_ref, grad_parts, send_a, recv_a)
    swap.start()
    for each in first_loads[1:]:
        each.wait()
    query, key, value = slice(0, HD), slice(HD, 2 * HD), slice(2 * HD, 3 * HD)
    query_rows[...] = qkv_ref[query].T
    key_rows[...] = qkv_ref[key].T
    value_rows[...] = qkv_ref[value].T
    scatter = Scatter(out_parts, out_land, send_c, recv_c)
    grad_att = grad_att_ref[...]
    for part in range(count):
        out_parts[part] = dot(context_ref[part], grad_att, ((1,), (0,))).astype(BF16)
    grad_parts[rank] = grad_ref[rank]
    swap.arrive()
    scatter.stage(5)
    scatter.stage(4)
    load.wait()
    combine = Scatter(combined, combined_land, send_d, recv_d)
    combine.stage(5)
    combine.stage(4)
    plan = {1: (scatter, 3), 2: (combine, 3), 3: (scatter, 2), 4: (combine, 2), 5: (scatter, 1), 7: (combine, 1)}
    for part in range(count):
        grad[:, part * tokens : (part + 1) * tokens] = grad_parts[part]
    grad_rows[...] = grad[...].T
    allowed = causal(Q_ROWS)
    blocks = length // Q_ROWS
    for block in reversed(range(blocks)):
        first = block * Q_ROWS
        columns = slice(first, first + Q_ROWS)
        scaled = qkv_ref[query, columns] * ATTN_SCALE
        logs = log_ref[:, columns]
        grad_block = grad[:, columns]
        inner = jnp.sum(grad_block.astype(F32) * wide_ref[:, columns], axis=0, keepdims=True)
        total = jnp.zeros((HD, Q_ROWS), F32)
        spans = [(columns, True)]
        if block:
            spans.append((slice(0, first), False))
        for keys, near in spans:
            weights = jnp.exp(dot(key_rows[keys, :], scaled, ((1,), (0,))) - logs)
            if near:
                weights = jnp.where(allowed, weights, 0.0)
            grad_weights = dot(value_rows[keys, :], grad_block, ((1,), (0,)))
            grad_scores = (weights * (grad_weights - inner)).astype(BF16)
            total = total + dot(qkv_ref[key, keys], grad_scores, ((1,), (0,)))
            key_part = dot(grad_scores, query_rows[columns, :], ((1,), (0,)))
            value_part = dot(weights.astype(BF16), grad_rows[columns, :], ((1,), (0,)))
            if block == blocks - 1:
                grad_key[keys, :] = key_part
                grad_value[keys, :] = value_part
            else:
                grad_key[keys, :] += key_part
                grad_value[keys, :] += value_part
        grad_query[:, columns] = total * ATTN_SCALE
        if blocks - 1 - block in plan:
            each, stage = plan[blocks - 1 - block]
            each.stage(stage)
    half = HD // 2
    cosine, sine = cosine_ref[...], -sine_ref[...]
    for place, wide in enumerate((grad_query[...], grad_key[...].T * ATTN_SCALE)):
        rows = rotate(wide[:half], wide[half:], cosine, sine)
        wide_grad[place * HD : (place + 1) * HD] = jnp.concatenate(rows, axis=0).astype(BF16)
    wide_grad[2 * HD :] = grad_value[...].T.astype(BF16)
    for part in range(count):
        parts_out[part] = wide_grad[:, part * tokens : (part + 1) * tokens]
    back = Exchange(parts_out, out_ref, send_b, recv_b)
    back.start()
    out_ref[rank] = parts_out[rank]
    copy.wait()
    scatter.stage(0)
    combine.stage(0)
    weight_ref[...] = dot(wide_grad[...], normed[...], ((1,), (0,)))
    rows = sum_ref.shape[0] // 2
    for place, value_half in enumerate(scatter.result()):
        sum_ref[place * rows : (place + 1) * rows] = value_half
    rows = block_ref.shape[0] // 2
    for place, value_half in enumerate(combine.result()):
        at = slice(place * rows, (place + 1) * rows)
        block_ref[at] = (residual_ref[at] + RES_SCALE * value_half).astype(BF16)
    back.arrive()
    back.sent()
    swap.sent()
    scatter.finish()
    combine.finish()


def backward(qkv, grad_context, wide, logs, cosine, sine, normed, context, grad_att, combined, residual):
    count, _, tokens = grad_context.shape
    length, width = normed.shape
    shape = jax.ShapeDtypeStruct
    low = pltpu.VMEM((length, HD), BF16)
    return call(
        backward_kernel, "backward", 4,
        (shape((count, 3 * HD, tokens), BF16), shape((3 * HD, width), F32), shape((HD, width), F32), shape((tokens, width), BF16)),
        [anywhere()] * 11, [whole()] * 4,
        [
            pltpu.VMEM(qkv.shape, BF16), pltpu.VMEM(grad_context.shape, BF16), pltpu.VMEM(wide.shape, F32), pltpu.VMEM(logs.shape, F32),
            pltpu.VMEM(cosine.shape, F32), pltpu.VMEM(sine.shape, F32), pltpu.VMEM(context.shape, BF16),
            pltpu.VMEM(grad_att.shape, BF16), pltpu.VMEM(residual.shape, F32),
            pltpu.VMEM((count, HD, tokens), BF16), pltpu.VMEM((count, 3 * HD, tokens), BF16), pltpu.VMEM((HD, length), BF16),
            low, low, low, low,
            pltpu.VMEM((HD, length), F32), pltpu.VMEM((length, HD), F32), pltpu.VMEM((length, HD), F32),
            pltpu.VMEM((length, width), BF16), pltpu.VMEM((3 * HD, length), BF16),
            pltpu.VMEM((count, HD, width), BF16), pltpu.VMEM(((count - 1) * HD, width), BF16),
            pltpu.VMEM((count, tokens, width), BF16), pltpu.VMEM(((count - 1) * tokens, width), BF16),
            *pair_sems(count - 1), *pair_sems(count - 1), *pair_sems(Torus.COUNT), *pair_sems(Torus.COUNT),
            pltpu.SemaphoreType.DMA((2,)), pltpu.SemaphoreType.DMA((9,)),
        ],
        56, flops=2 * length * length * HD * 5, bytes_accessed=12 << 20,
    )(qkv, grad_context, wide, logs, cosine, sine, normed, context, grad_att, combined, residual)


SMALL = 384


def finish_kernel(
    weight_ref, out_sum_ref, small_ref, query_ref, out_ref, keyval_ref, small_out,
    give, pair_land, mine, land, summed, small_parts, small_land, small_sum, small_dp, gather_buf,
    send_p, recv_p, send_s, recv_s, send_a, recv_a, send_b, recv_b, send_c, recv_c, send_d, recv_d, send_e, recv_e,
):
    count = RING * RING
    rank, dp = lax.axis_index("tensor"), lax.axis_index("dp")
    dps = land.shape[0]
    odd = lax.rem(rank, 2)
    partner = rank + 1 - 2 * odd
    width = weight_ref.shape[1]
    column = width // dps
    give[...] = weight_ref[pl.ds(pl.multiple_of(HD + HD * (1 - odd), HD), HD), :].astype(BF16)
    for i in range(count):
        small_parts[i, :, :256] = small_ref[8 * (i // 4) : 8 * (i // 4) + 8, 256 * (i % 4) : 256 * (i % 4) + 256]
        small_parts[i, :, 256:] = small_ref[32:40, 128 * (i // 2) : 128 * (i // 2) + 128]
    greet(others("tensor", count), others("dp", dps))
    swap = pltpu.make_async_remote_copy(
        src_ref=give, dst_ref=pair_land, send_sem=send_p, recv_sem=recv_p, device_id=(dp, partner), device_id_type=MESH_ID
    )
    swap.start()
    small = Exchange(small_parts, small_land, send_s, recv_s)
    small.start()
    small_land[rank] = small_parts[rank]
    lists = [weight_ref[:HD], out_sum_ref[...]]
    swap.wait_recv()
    lists.append(weight_ref[pl.ds(pl.multiple_of(HD + HD * odd, HD), HD), :] + pair_land[...].astype(F32))
    for j, rows in enumerate(lists):
        low = rows.astype(BF16)
        for i in range(dps):
            mine[i, j * HD : (j + 1) * HD] = low[:, i * column : (i + 1) * column]
    first = Exchange(mine, land, send_a, recv_a, "dp")
    first.start()
    land[dp] = mine[dp]
    small.arrive()
    small_sum[...] = jnp.sum(small_land[...], axis=0)
    second_small = Exchange(small_sum, small_dp, send_c, recv_c, "dp", same=True)
    second_small.start()
    small_dp[dp] = small_sum[...]
    first.arrive()
    own = jnp.sum(land[...].astype(F32), axis=0).astype(BF16)
    summed[dp] = own
    second = Exchange(summed.at[dp], summed, send_b, recv_b, "dp", same=True)
    second.start()
    second_small.arrive()
    second_small.sent()
    small_sum[...] = jnp.sum(small_dp[...], axis=0)
    third_small = Exchange(small_sum, small_out, send_d, recv_d, same=True)
    third_small.start()
    small_out[rank] = small_sum[...]
    second.arrive()
    for i in range(dps):
        columns = slice(i * column, (i + 1) * column)
        query_ref[:, columns] = summed[i, :HD]
        out_ref[:, columns] = summed[i, HD : 2 * HD]
        gather_buf[rank, :, columns] = summed[i, 2 * HD :]
    gather = Gather(gather_buf, send_e, recv_e)
    for stage in range(6):
        gather.stage(stage)
    gather.finish()
    for i in range(count):
        base = (i % 2) * KV_HEADS * HD + (i // 2) * HD
        keyval_ref[base : base + HD, :] = gather_buf[i]
    third_small.arrive()
    swap.wait_send()
    for each in (small, first, second, third_small):
        each.sent()


def finish(weight, out_sum, small, dps):
    width = weight.shape[1]
    count = RING * RING
    column = width // dps
    shape = jax.ShapeDtypeStruct
    small_shape = (8, SMALL)
    return call(
        finish_kernel, "finish", 5,
        (shape((HD, width), BF16), shape((HD, width), BF16), shape((count * HD, width), BF16), shape((count, *small_shape), F32)),
        [whole()] * 3, [whole()] * 4,
        [
            pltpu.VMEM((HD, width), BF16), pltpu.VMEM((HD, width), BF16), pltpu.VMEM((dps, 3 * HD, column), BF16),
            pltpu.VMEM((dps, 3 * HD, column), BF16), pltpu.VMEM((dps, 3 * HD, column), BF16),
            pltpu.VMEM((count, *small_shape), F32), pltpu.VMEM((count, *small_shape), F32), pltpu.VMEM(small_shape, F32),
            pltpu.VMEM((dps, *small_shape), F32), pltpu.VMEM((count, HD, width), BF16),
            pltpu.SemaphoreType.DMA, pltpu.SemaphoreType.DMA, *pair_sems(count - 1), *pair_sems(dps - 1), *pair_sems(dps - 1),
            *pair_sems(dps - 1), *pair_sems(count - 1), *pair_sems(Torus.COUNT),
        ],
        40, flops=1 << 24, bytes_accessed=10 << 20,
    )(weight, out_sum, small)


def widen_kernel(gateup_ref, down_ref, keyval_ref, gateup_out, down_out, keyval_out):
    gateup_out[...] = gateup_ref[...].astype(F32)
    down_out[...] = down_ref[...].astype(F32)
    keyval_out[...] = keyval_ref[...].T.astype(F32)


def widen(gateup, down, keyval):
    steps = 8
    experts_here, width, wide = gateup.shape
    ff = down.shape[1]
    per = steps // experts_here
    pairs = keyval.shape[0]
    shape = jax.ShapeDtypeStruct
    gateup_spec = pl.BlockSpec((1, width // per, wide), lambda i: (i // per, i % per, 0))
    down_spec = pl.BlockSpec((1, ff // per, width), lambda i: (i // per, i % per, 0))
    return pl.pallas_call(
        widen_kernel, grid=(steps,),
        out_shape=(shape(gateup.shape, F32), shape(down.shape, F32), shape((width, pairs), F32)),
        in_specs=[gateup_spec, down_spec, pl.BlockSpec((pairs, width // steps), lambda i: (0, i))],
        out_specs=[gateup_spec, down_spec, pl.BlockSpec((width // steps, pairs), lambda i: (i, 0))],
        compiler_params=pltpu.CompilerParams(vmem_limit_bytes=60 << 20),
        name="widen",
    )(gateup, down, keyval)


def shards(
    block_input, attn_gain, w_query, w_keyval, w_out, ffn_gain, w_router, w_gateup, w_down, routes, cotangent,
):
    devices = lax.axis_size("tensor")
    tokens, width = block_input.shape
    length = tokens * devices

    cosine, sine = rope_tables(length, HD)
    normed_one_all, qkv, wide_out, logs, context, weights, cotangent_all, routes_all, residual, normed_two = forward(
        block_input, attn_gain, ffn_gain, w_query.T, w_keyval, w_out, cotangent, cosine, sine, routes.T
    )
    grad_w_gateup, grad_w_down, combined, grad_residual, grad_attention, small, grad_context = experts(
        normed_two, residual, ffn_gain, w_router.T, routes_all, cotangent_all, w_gateup, w_down, weights
    )
    grad_w_gateup, grad_w_down = lax.psum((grad_w_gateup, grad_w_down), "dp")
    back, grad_w, grad_out_sum, block_out = backward(
        qkv, grad_context, wide_out, logs, cosine, sine, normed_one_all.reshape(length, width), context, grad_attention,
        combined, residual,
    )
    share = HEADS // KV_HEADS
    back = back.reshape(HEADS, 3, HD, tokens)
    back_pairs = jnp.sum(back[:, 1:].reshape(KV_HEADS, share, 2, HD, tokens).astype(F32), axis=1).astype(BF16)
    back_pairs = back_pairs.transpose(1, 0, 2, 3).reshape(2 * KV_HEADS * HD, tokens)
    grad_normed_one = dot(back[:, 0].reshape(HEADS * HD, tokens), weights[:, HD:].reshape(HEADS * HD, width), ((0,), (0,))) + dot(
        back_pairs, w_keyval, ((0,), (1,))
    )
    inputs = block_input.astype(F32)
    grad_input_norm, grad_gain_one = norm_back(inputs, rms_scale(inputs), attn_gain.astype(F32), grad_normed_one)
    grad_input = grad_residual + grad_input_norm

    small = lax.dynamic_update_slice(small, grad_gain_one[None], (EXPERTS + 1, 0))
    grad_query_w, grad_w_out, grad_keyval, small = finish(grad_w, grad_out_sum, small, lax.axis_size("dp"))
    grad_w_gateup, grad_w_down, grad_keyval = widen(grad_w_gateup, grad_w_down, grad_keyval)
    routers = small[:, :, :256].reshape(4, 4, 8, 256).transpose(0, 2, 1, 3).reshape(EXPERTS, width)
    gains = small[::2, :2, 256:].transpose(1, 0, 2).reshape(2, width)
    return (
        block_out,
        grad_input,
        gains[1],
        grad_query_w.astype(F32).T,
        grad_keyval,
        grad_w_out.astype(F32),
        gains[0],
        routers.T,
        grad_w_gateup,
        grad_w_down,
    )


def solution(mesh):
    rows = P(("dp", "tensor"), None)
    in_specs = (
        rows, P(), P(None, "tensor"), P(), P("tensor", None), P(), P(),
        P("tensor", None, None), P("tensor", None, None), rows, rows,
    )
    out_specs = (
        rows, rows, P(), P(None, "tensor"), P(), P("tensor", None), P(), P(),
        P("tensor", None, None), P("tensor", None, None),
    )
    return jax.shard_map(shards, mesh=mesh, in_specs=in_specs, out_specs=out_specs, check_vma=False)
```

```python
import jax
import jax.numpy as jnp
import numpy as np
from jax import lax
from jax.experimental import pallas as pl
from jax.experimental.pallas import tpu as pltpu
from jax.sharding import PartitionSpec as P

HEADS = 16
KV_HEADS = 8
HD = 64
EXPERTS = 32
TOP = 8
CAP = 64
ATTN_SCALE = 0.015625
RES_SCALE = 0.22
EPSILON = 1e-06
ROPE_BASE = 10000.0
F32 = jnp.float32
BF16 = jnp.bfloat16
Q_ROWS = 256


def rms_scale(values):
    return lax.rsqrt(jnp.mean(values * values, axis=-1, keepdims=True) + EPSILON)


def norm_back(values, scale, gain, grad_normed):
    grad_scaled = grad_normed * gain
    grad_gain = jnp.sum(grad_normed * values * scale, axis=0)
    inner = jnp.mean(grad_scaled * values, axis=-1, keepdims=True)
    return (scale * (grad_scaled - values * scale * scale * inner), grad_gain)


def rope_tables(length, width):
    half_width = width // 2
    inverse = ROPE_BASE ** (-(np.arange(half_width) * 2.0) / width)
    angles = np.arange(length)[None, :] * inverse[:, None]
    return (jnp.asarray(np.cos(angles), F32), jnp.asarray(np.sin(angles), F32))


def rotate(first, second, cosine, sine):
    return first * cosine - second * sine, second * cosine + first * sine


def dot(a, b, dims):
    return lax.dot_general(a, b, ((dims[0], dims[1]), ((), ())), preferred_element_type=F32)


def causal(rows):
    key = lax.broadcasted_iota(jnp.int32, (rows, rows), 0)
    query = lax.broadcasted_iota(jnp.int32, (rows, rows), 1)
    return key <= query


RING = 4
MESH_ID = pl.DeviceIdType.MESH


def whole():
    return pl.BlockSpec(memory_space=pltpu.VMEM)


def anywhere():
    return pl.BlockSpec(memory_space=pltpu.HBM)


def position():
    rank = lax.axis_index("tensor")
    return lax.div(rank, RING), lax.rem(rank, RING)


def shifted(pos, axis, by):
    moved = lax.rem(pos[axis] + (by + RING), RING)
    return (moved, pos[1]) if axis == 0 else (pos[0], moved)


def joined(pos):
    return pos[0] * RING + pos[1]


def greet(tensor_peers, dp_peers=()):
    dp, rank = lax.axis_index("dp"), lax.axis_index("tensor")
    sem = pltpu.get_barrier_semaphore()
    peers = [(dp, p) for p in tensor_peers] + [(p, rank) for p in dp_peers]
    for peer in peers:
        pl.semaphore_signal(sem, inc=1, device_id=peer, device_id_type=MESH_ID)
    pl.semaphore_wait(sem, len(peers))


def neighbours():
    pos = position()
    return [joined(shifted(pos, axis, by)) for axis in (0, 1) for by in (1, -1)]


def others(axis, count):
    return [lax.rem(lax.axis_index(axis) + r, count) for r in range(1, count)]


def torus_messages(half, rows):
    primary, secondary = (0, 1) if half == 0 else (1, 0)
    h, q = rows // 2, rows // 4
    full = (half * h, h)
    part = {1: (half * h, q), -1: (half * h + q, q)}
    out = []
    for d in (1, -1):
        out.append((0, ("p1", d), None, full, (0, 0), primary, d))
        out.append((0, ("s1", 0, d), None, full, (0, 0), secondary, d))
        out.append((1, ("p2", d), ("p1", d), part[d], (-d, 0), primary, d))
        for e in (1, -1):
            out.append((1, ("s1", -d, e), ("p1", d), full, (-d, 0), secondary, e))
    for e in (1, -1):
        out.append((2, ("s2", 0, e), ("s1", 0, e), part[e], (0, -e), secondary, e))
        for d in (1, -1):
            out.append((3, ("s1", ("o", d), e), ("p2", d), part[d], (2, 0), secondary, e))
            out.append((4, ("s2", d, e), ("s1", d, e), part[e], (d, -e), secondary, e))
        out.append((5, ("s2", "o", e), ("s1", ("o", e), e), part[e], (2, -e), secondary, e))
    return out


class Torus:
    COUNT = 44
    STAGES = 6

    def __init__(self, rows):
        self.rows = rows
        self.pos = position()
        self.dp = lax.axis_index("dp")
        self.messages, self.children, self.place, order, used = {}, {}, {}, [], 0
        for half in (0, 1):
            for at, (stage, key, needs, piece, offset, axis, way) in enumerate(torus_messages(half, rows)):
                key = (half, key)
                needs = None if needs is None else (half, needs)
                self.messages[key] = (len(order), stage, needs, piece, offset, axis, way)
                self.children.setdefault(needs, []).append(key)
                self.place[key] = used
                used += piece[1]
                order.append((stage, at, half, key))
        self.landing_rows = used
        self.order = [entry[3] for entry in sorted(order, key=lambda entry: entry[:3])]

    def block(self, key, pos):
        half, offset = key[0], self.messages[key][4]
        primary, secondary = (0, 1) if half == 0 else (1, 0)
        return joined(shifted(shifted(pos, primary, offset[0]), secondary, offset[1]))

    def sender(self, key):
        _, _, _, _, _, axis, way = self.messages[key]
        return shifted(self.pos, axis, -way)

    def receiver(self, key):
        _, _, _, _, _, axis, way = self.messages[key]
        return shifted(self.pos, axis, way)


class Gather(Torus):
    def __init__(self, buf, send, recv):
        super().__init__(buf.shape[1])
        self.buf, self.send, self.recv = buf, send, recv
        self.arrived = set()

    def copy(self, key, incoming):
        number, (first, count) = self.messages[key][0], self.messages[key][3]
        at = self.sender(key) if incoming else self.pos
        ref = self.buf.at[self.block(key, at), pl.ds(first, count)]
        return pltpu.make_async_remote_copy(
            src_ref=ref, dst_ref=ref, send_sem=self.send.at[number], recv_sem=self.recv.at[number],
            device_id=(self.dp, joined(at if incoming else self.receiver(key))), device_id_type=MESH_ID,
        )

    def arrive(self, key):
        if key not in self.arrived:
            self.arrived.add(key)
            self.copy(key, True).wait_recv()

    def stage(self, number):
        for key in self.order:
            _, stage, needs, *_ = self.messages[key]
            if stage == number:
                if needs is not None:
                    self.arrive(needs)
                self.copy(key, False).start()

    def arrive_stage(self, number):
        for key in self.order:
            if self.messages[key][1] == number:
                self.arrive(key)

    def finish(self):
        for key in self.order:
            self.arrive(key)
        for key in self.order:
            self.copy(key, False).wait_send()


class Scatter(Torus):
    def __init__(self, parts, landing, send, recv):
        super().__init__(parts.shape[1])
        self.parts, self.landing, self.send, self.recv = parts, landing, send, recv

    def copy(self, key):
        number, (first, count) = self.messages[key][0], self.messages[key][3]
        at = self.sender(key)
        return pltpu.make_async_remote_copy(
            src_ref=self.parts.at[self.block(key, at), pl.ds(first, count)],
            dst_ref=self.landing.at[pl.ds(self.place[key], count)],
            send_sem=self.send.at[number], recv_sem=self.recv.at[number],
            device_id=(self.dp, joined(at)), device_id_type=MESH_ID,
        )

    def landed(self, key):
        count = self.messages[key][3][1]
        self.copy(key).wait_recv()
        return self.landing[pl.ds(self.place[key], count), :].astype(F32)

    def stage(self, number):
        for key in reversed(self.order):
            if self.messages[key][1] == number:
                pieces = {}
                for child in self.children.get(key, []):
                    pieces.setdefault(self.messages[child][3], []).append(child)
                for (first, count), children in pieces.items():
                    at = (self.block(children[0], self.pos), pl.ds(first, count))
                    self.parts[at] = sum((self.landed(c) for c in children), self.parts[at].astype(F32)).astype(self.parts.dtype)
                self.copy(key).start()

    def result(self):
        out = []
        for half in (0, 1):
            children = [c for c in self.children[None] if c[0] == half]
            first, count = self.messages[children[0]][3]
            own = self.parts[joined(self.pos), pl.ds(first, count)].astype(F32)
            out.append(sum((self.landed(c) for c in children), own))
        return out

    def finish(self):
        for key in self.order:
            self.copy(key).wait_send()


class Exchange:
    def __init__(self, source, target, send, recv, axis="tensor", same=False):
        self.source, self.target, self.send, self.recv, self.axis, self.same = source, target, send, recv, axis, same
        self.count = target.shape[0]
        self.rank = lax.axis_index(axis)

    def device(self, to):
        if self.axis == "tensor":
            return (lax.axis_index("dp"), to)
        return (to, lax.axis_index("tensor"))

    def copy(self, r):
        to = lax.rem(self.rank + r, self.count)
        return pltpu.make_async_remote_copy(
            src_ref=self.source if self.same else self.source.at[to],
            dst_ref=self.target.at[self.rank], send_sem=self.send.at[r - 1],
            recv_sem=self.recv.at[r - 1], device_id=self.device(to), device_id_type=MESH_ID,
        )

    def start(self):
        for r in range(1, self.count):
            self.copy(r).start()

    def arrive(self):
        for r in range(1, self.count):
            origin = lax.rem(self.rank + self.count - r, self.count)
            pltpu.make_async_remote_copy(
                src_ref=self.target.at[origin], dst_ref=self.target.at[origin], send_sem=self.send.at[r - 1],
                recv_sem=self.recv.at[r - 1], device_id=self.device(origin), device_id_type=MESH_ID,
            ).wait_recv()

    def sent(self):
        for r in range(1, self.count):
            self.copy(r).wait_send()


def pair_sems(count):
    return [pltpu.SemaphoreType.DMA((count,))] * 2


def call(kernel, name, number, out_shape, in_specs, out_specs, scratch, limit, flops=0, bytes_accessed=0):
    return pl.pallas_call(
        kernel, out_shape=out_shape, in_specs=in_specs, out_specs=out_specs, scratch_shapes=scratch,
        compiler_params=pltpu.CompilerParams(collective_id=number, has_side_effects=True, vmem_limit_bytes=limit << 10),
        cost_estimate=pl.CostEstimate(flops=flops, bytes_accessed=bytes_accessed, transcendentals=0),
        name=name,
    )


def loads(pairs, sems):
    copies = [pltpu.make_async_copy(a, b, sems.at[i]) for i, (a, b) in enumerate(pairs)]
    for copy in copies:
        copy.start()
    return copies


class Replicas:
    COUNT = RING * RING - 1 + 9

    def __init__(self, own, buf, send, recv, local):
        self.own, self.buf, self.send, self.recv = own, buf, send, recv
        self.keep = pltpu.make_async_copy(*[ref.at[:, self.columns_of(buf)] for ref in (own, buf.at[lax.axis_index("tensor")])], local)
        self.rank, self.dp = lax.axis_index("tensor"), lax.axis_index("dp")
        self.x, self.core = lax.div(self.dp, 2), lax.rem(self.dp, 2)
        self.blocks = buf.shape[0]
        self.share = buf.shape[2] // (2 * RING)

    @staticmethod
    def columns_of(buf):
        share = buf.shape[2] // (2 * RING)
        return pl.ds(pl.multiple_of(lax.axis_index("dp") * share, share), share)

    def member(self, dx, other):
        core = 1 - self.core if other else self.core
        return lax.rem(self.x + dx + RING, RING) * 2 + core

    def columns(self, member):
        return pl.ds(pl.multiple_of(member * self.share, self.share), self.share)

    def piece(self, member, part):
        first, count = {0: (0, self.blocks), 1: (0, self.blocks // 2), -1: (self.blocks // 2, self.blocks // 2)}[part]
        return self.buf.at[pl.ds(first, count), :, self.columns(member)]

    def copy(self, number, ref, device):
        return pltpu.make_async_remote_copy(
            src_ref=ref, dst_ref=ref, send_sem=self.send.at[number], recv_sem=self.recv.at[number],
            device_id=device, device_id_type=MESH_ID,
        )

    def first(self):
        count = self.blocks
        self.outgoing = []
        self.keep.start()
        for r in range(1, count):
            self.outgoing.append(pltpu.make_async_remote_copy(
                src_ref=self.own.at[:, self.columns(self.dp)], dst_ref=self.buf.at[self.rank, :, self.columns(self.dp)],
                send_sem=self.send.at[r - 1], recv_sem=self.recv.at[r - 1],
                device_id=(self.dp, lax.rem(self.rank + r, count)), device_id_type=MESH_ID,
            ))
            self.outgoing[-1].start()

    def go(self, number, member, part, dx, other):
        self.outgoing.append(self.copy(self.blocks - 1 + number, self.piece(member, part), (self.member(dx, other), self.rank)))
        self.outgoing[-1].start()

    def come(self, number, member, part):
        self.copy(self.blocks - 1 + number, self.piece(member, part), (self.dp, self.rank)).wait_recv()

    def second(self):
        for r in range(1, self.blocks):
            ref = self.buf.at[lax.rem(self.rank + self.blocks - r, self.blocks), :, self.columns(self.dp)]
            self.copy(r - 1, ref, (self.dp, self.rank)).wait_recv()
        self.keep.wait()
        self.go(0, self.dp, 0, 1, False)
        self.go(1, self.dp, 0, -1, False)
        self.go(4, self.dp, 0, 0, True)

    def third(self):
        for number, way in ((0, 1), (1, -1)):
            member = self.member(-way, False)
            self.come(number, member, 0)
            self.go(2 + number, member, way, way, False)
            self.go(5 + number, member, 0, 0, True)

    def fourth(self):
        for number, way in ((0, 1), (1, -1)):
            member = self.member(2, False)
            self.come(2 + number, member, way)
            self.go(7 + number, member, way, 0, True)

    def finish(self):
        self.come(4, self.member(0, True), 0)
        for number, way in ((0, 1), (1, -1)):
            self.come(5 + number, self.member(-way, True), 0)
            self.come(7 + number, self.member(2, True), way)
        for copy in self.outgoing:
            copy.wait_send()


def near_members():
    x, core = lax.div(lax.axis_index("dp"), 2), lax.rem(lax.axis_index("dp"), 2)
    return [lax.rem(x + 1, RING) * 2 + core, lax.rem(x + RING - 1, RING) * 2 + core, x * 2 + 1 - core]


def forward_kernel(
    x_in, gain_in, gain_two_in, query_in, keyval_ref, out_w_ref, cot_ref, cosine_in, sine_in, routes_in,
    normed_out, qkv_out, wide_ref, log_ref, context_ref, weights_out, cot_all, routes_all, residual_ref, normed_two_ref,
    x_ref, gain_ref, gain_two_ref, cosine_ref, sine_ref,
    buf, weights, own_w, local_w, pair_w, qkv, key_rows, context_parts,
    sems_a, sems_b, sems_d, sems_e, sems_f, local_sems, load_sems,
):
    tokens, width = x_ref.shape
    rank = lax.axis_index("tensor")
    z, y = position()
    half = HD // 2
    copies = loads(
        [
            (x_in, x_ref), (gain_in, gain_ref), (out_w_ref, own_w.at[:HD]), (query_in, own_w.at[HD:]),
            (routes_in, routes_all.at[rank]), (cosine_in, cosine_ref), (sine_in, sine_ref), (gain_two_in, gain_two_ref),
        ],
        load_sems,
    )
    pair_copies = []
    for part in range(2):
        column = pl.multiple_of(part * KV_HEADS * HD + z * 2 * HD, 2 * HD)
        copy = pltpu.make_async_copy(keyval_ref.at[:, pl.ds(column, 2 * HD)], pair_w.at[part], local_sems.at[part])
        copy.start()
        pair_copies.append(copy)
    own_cot = pltpu.make_async_copy(cot_ref, cot_all.at[rank], local_sems.at[2])
    own_cot.start()
    copies[0].wait()
    copies[1].wait()
    inputs = x_ref[...].astype(F32)
    buf[rank] = (inputs * rms_scale(inputs) * gain_ref[...].reshape(1, width).astype(F32)).astype(BF16)
    greet(others("tensor", RING * RING), near_members())
    main = Gather(buf, *sems_a)
    main.stage(0)
    for copy in copies[2:5]:
        copy.wait()
    replicas = Replicas(own_w, weights, *sems_b, local_sems.at[3])
    replicas.first()
    tell = Exchange(routes_all.at[rank], routes_all, *sems_f, same=True)
    tell.start()
    for copy in pair_copies + copies[5:]:
        copy.wait()
    odd = lax.rem(lax.div(rank, 2), 2)
    local_w[:HD] = own_w[HD:]
    for part in range(2):
        tall = pair_w[part].T.astype(F32)
        local_w[HD * (part + 1) : HD * (part + 2)] = jnp.where(odd == 0, tall[:HD], tall[HD:]).astype(BF16)
    pos = main.pos

    def project(dz, dy):
        block = joined(shifted(shifted(pos, 0, dz), 1, dy))
        columns = pl.ds(pl.multiple_of(block * tokens, tokens), tokens)
        made = dot(local_w[...], buf[block], ((1,), (1,)))
        cosine, sine = cosine_ref[:, columns], sine_ref[:, columns]
        rows = []
        for first in (0, HD):
            rows += rotate(made[first : first + half], made[first + half : first + HD], cosine, sine)
        rows.append(made[2 * HD :])
        qkv[:, columns] = jnp.concatenate(rows, axis=0).astype(BF16)

    project(0, 0)
    main.stage(1)
    main.stage(2)
    replicas.second()
    main.arrive_stage(0)
    for offset in ((0, 1), (0, 3), (1, 0), (3, 0)):
        project(*offset)
    main.stage(3)
    main.stage(4)
    own_cot.wait()
    back = Gather(cot_all, *sems_d)
    main.arrive_stage(1)
    main.arrive_stage(2)
    for offset in ((1, 1), (1, 3), (3, 1), (3, 3), (2, 0), (0, 2)):
        project(*offset)
    main.stage(5)
    back.stage(0)
    main.arrive_stage(3)
    main.arrive_stage(4)
    replicas.third()
    for offset in ((2, 1), (2, 3), (1, 2), (3, 2)):
        project(*offset)
    main.arrive_stage(5)
    project(2, 2)
    normed_copy = pltpu.make_async_copy(buf, normed_out, local_sems.at[5])
    normed_copy.start()
    qkv_copy = pltpu.make_async_copy(qkv, qkv_out, local_sems.at[6])
    qkv_copy.start()
    key_rows[...] = qkv[HD : 2 * HD].T
    swap = Exchange(context_parts, context_ref, *sems_e)
    todo = {2: [lambda: back.stage(1)], 3: [lambda: back.stage(2)], 5: [replicas.fourth], 6: [lambda: back.stage(3)]}
    attend(qkv, key_rows, wide_ref, log_ref, context_parts, tokens, todo)
    swap.start()
    context_ref[rank] = context_parts[rank]
    back.stage(4)
    back.stage(5)
    replicas.finish()
    weights_copy = pltpu.make_async_copy(weights, weights_out, local_sems.at[7])
    weights_copy.start()
    tell.arrive()
    swap.arrive()
    context = context_ref[...].reshape(HEADS * HD, tokens)
    attention = dot(context, weights[:, :HD].reshape(HEADS * HD, width), ((0,), (0,)))
    residual = x_ref[...].astype(F32) + RES_SCALE * attention
    residual_ref[...] = residual
    normed_two_ref[...] = (residual * rms_scale(residual) * gain_two_ref[...].reshape(1, width).astype(F32)).astype(BF16)
    back.finish()
    main.finish()
    swap.sent()
    tell.sent()
    normed_copy.wait()
    qkv_copy.wait()
    weights_copy.wait()


def attend(qkv, key_rows, wide_ref, log_ref, parts_ref, tokens, todo):
    length = qkv.shape[1]
    allowed = causal(Q_ROWS)
    query, value = slice(0, HD), slice(2 * HD, 3 * HD)
    for block in range(length // Q_ROWS):
        first = block * Q_ROWS
        columns = slice(first, first + Q_ROWS)
        scaled = qkv[query, columns] * ATTN_SCALE
        near = dot(key_rows[columns, :], scaled, ((1,), (0,)))
        near = jnp.where(allowed, near, -1e30)
        largest = jnp.max(near, axis=0, keepdims=True)
        if block:
            far = dot(key_rows[:first, :], scaled, ((1,), (0,)))
            largest = jnp.maximum(largest, jnp.max(far, axis=0, keepdims=True))
        near = jnp.exp(near - largest)
        total = jnp.sum(near, axis=0, keepdims=True)
        context = dot(qkv[value, columns], near.astype(BF16), ((1,), (0,)))
        if block:
            far = jnp.exp(far - largest)
            total = total + jnp.sum(far, axis=0, keepdims=True)
            context = context + dot(qkv[value, :first], far.astype(BF16), ((1,), (0,)))
        context = context / total
        wide_ref[:, columns] = context
        log_ref[:, columns] = largest + jnp.log(total)
        low = context.astype(BF16)
        for part in range(Q_ROWS // tokens):
            parts_ref[first // tokens + part] = low[:, part * tokens : (part + 1) * tokens]
        for task in todo.get(block, ()):
            task()


def forward(x, gain, gain_two, w_query, w_keyval, w_out, cotangent, cosine, sine, routes):
    tokens, width = x.shape
    count = RING * RING
    length = tokens * count

    def kernel(*refs):
        plain, sems = refs[:-12], refs[-12:]
        forward_kernel(*plain, *[sems[2 * i : 2 * i + 2] for i in range(5)], sems[10], sems[11])

    shape = jax.ShapeDtypeStruct
    vmem = pltpu.VMEM
    return call(
        kernel, "forward", 1,
        (
            shape((count, tokens, width), BF16), shape((3 * HD, length), BF16), shape((HD, length), F32),
            shape((1, length), F32), shape((count, HD, tokens), BF16), shape((count, 2 * HD, width), BF16),
            shape((count, tokens, width), BF16),
            shape((count, *routes.shape), jnp.int32), shape((tokens, width), F32), shape((tokens, width), BF16),
        ),
        [anywhere()] * 10,
        [anywhere(), anywhere(), whole(), whole(), whole(), anywhere(), anywhere(), whole(), whole(), whole()],
        [
            vmem(x.shape, BF16), vmem(gain.shape, BF16), vmem(gain.shape, BF16), vmem(cosine.shape, F32), vmem(sine.shape, F32),
            vmem((count, tokens, width), BF16), vmem((count, 2 * HD, width), BF16), vmem((2 * HD, width), BF16), vmem((3 * HD, width), BF16),
            vmem((2, width, 2 * HD), BF16), vmem((3 * HD, length), BF16), vmem((length, HD), BF16),
            vmem((count, HD, tokens), BF16),
            *pair_sems(Torus.COUNT), *pair_sems(Replicas.COUNT), *pair_sems(Torus.COUNT),
            *pair_sems(count - 1), *pair_sems(count - 1), pltpu.SemaphoreType.DMA((8,)), pltpu.SemaphoreType.DMA((8,)),
        ],
        65400, flops=2 * length * (3 * HD * width + length * HD * 2), bytes_accessed=20 << 20,
    )(x, gain, gain_two, w_query, w_keyval, w_out, cotangent, cosine, sine, routes)


GROUPS = (
    ((0, 0), (0, 1), (0, 3), (1, 0), (3, 0)),
    ((1, 1), (1, 3), (3, 1), (3, 3), (2, 0), (0, 2)),
    ((2, 1), (2, 3), (1, 2), (3, 2), (2, 2)),
)
MOST = 6 * CAP
CHUNK = 32


def expert_kernel(
    normed_in, residual_in, gain_in, router_in, routes_in, cot_ref, gateup_ref, down_ref, out_w_ref,
    half_out, combined_out, grad_residual_ref, grad_att_ref, small_ref, grad_context_ref,
    normed_ref, residual_ref, gain_ref, router_ref, routes_ref,
    buf, cot, gateup, down, out_w, pick, gate_cols, arrived, grad_acts, grad_arrived, hidden, grad_slots,
    acts, grad_hidden, produced, grad_rows, parts, combined, landing, stage_w, notes, told, own_gates,
    send_a, recv_a, send_b, recv_b, send_c, recv_c, send_d, recv_d, free, local, store, early,
):
    tokens, width = normed_ref.shape
    count = RING * RING
    local_experts, ff = down.shape[0], down.shape[1]
    rank = lax.axis_index("tensor")
    first = loads(
        [
            (normed_in, buf.at[rank]), (router_in, router_ref), (routes_in, routes_ref),
            (normed_in, normed_ref), (residual_in, residual_ref), (gain_in, gain_ref),
        ],
        early,
    )
    late = loads([(gateup_ref, gateup), (down_ref, down), (cot_ref, cot), (out_w_ref.at[:, :HD], out_w)], local)
    dp = lax.axis_index("dp")
    core = lax.rem(dp, 2)
    sibling = (dp + 1 - 2 * core, rank)
    greet(others("tensor", count), [sibling[0]])
    first[0].wait()
    gather = Gather(buf, send_a, recv_a)
    gather.stage(0)
    for load in first[1:]:
        load.wait()
    router = router_ref[...]
    ids = lax.broadcasted_iota(jnp.int32, (EXPERTS, tokens), 0)
    slot_ids = lax.broadcasted_iota(jnp.int32, (CAP, tokens), 0).astype(F32)
    before = lax.broadcasted_iota(jnp.int32, (tokens, tokens), 0) < lax.broadcasted_iota(jnp.int32, (tokens, tokens), 1)
    upper = jnp.where(before, 1.0, 0.0).astype(BF16)
    pos = gather.pos

    def named_of(block):
        routes = routes_ref[block]
        hits = ids == routes[0:1]
        for k in range(1, TOP):
            hits = hits | (ids == routes[k : k + 1])
        return hits

    def gates_of(normed, named):
        logits = jnp.where(named, dot(router, normed, ((1,), (1,))), -1e30)
        powers = jnp.where(named, jnp.exp(logits - jnp.max(logits, axis=0, keepdims=True)), 0.0)
        return powers / jnp.sum(powers, axis=0, keepdims=True)

    @pl.loop(0, count)
    def _(block):
        named = jnp.where(named_of(block), 1.0, 0.0)
        places = dot(named.astype(BF16), upper, ((1,), (0,)))
        for e in range(local_experts):
            mine = ids == rank * local_experts + e
            hit = jnp.sum(jnp.where(mine, named, 0.0), axis=0, keepdims=True)
            at = jnp.sum(jnp.where(mine, places, 0.0), axis=0, keepdims=True)
            at = jnp.where(hit > 0.5, at, -1.0)
            pick[block, e * CAP : (e + 1) * CAP] = jnp.where(slot_ids == at, 1.0, 0.0).astype(BF16)

    gather.stage(1)
    gather.stage(2)
    for load in late:
        load.wait()

    def work(group, base):
        rows = len(group) * CAP
        blocks = [joined(shifted(shifted(pos, 0, dz), 1, dy)) for dz, dy in group]
        for i, block in enumerate(blocks):
            normed = buf[block]
            gates = gates_of(normed, named_of(block))
            if group[i] == (0, 0):
                own_gates[...] = gates
            chosen = pick[block]
            picked = dot(chosen, normed, ((1,), (0,))).astype(BF16)
            slots = dot(chosen, cot[block], ((1,), (0,)))
            for e in range(local_experts):
                rows_e = slice(e * CAP, (e + 1) * CAP)
                gate = jnp.sum(jnp.where(ids == rank * local_experts + e, gates, 0.0), axis=0, keepdims=True)
                column = jnp.sum(chosen[rows_e].astype(F32) * gate, axis=1, keepdims=True)
                gate_cols[e, i * CAP : (i + 1) * CAP] = column
                arrived[e, base + i * CAP : base + (i + 1) * CAP] = picked[rows_e]
                grad_slots[e, i * CAP : (i + 1) * CAP] = slots[rows_e].astype(BF16)
                grad_arrived[e, base + i * CAP : base + (i + 1) * CAP] = (column * (RES_SCALE * slots[rows_e])).astype(BF16)

        @pl.loop(0, local_experts)
        def _(e):
            acts[:rows] = dot(arrived[e, base : base + rows], gateup[e], ((1,), (0,)))
            grad_hidden[:rows] = dot(grad_arrived[e, base : base + rows], down[e], ((1,), (1,)))

            @pl.loop(0, rows // CHUNK)
            def _(c):
                at = pl.ds(pl.multiple_of(c * CHUNK, CHUNK), CHUNK)
                out = pl.ds(pl.multiple_of(base + c * CHUNK, CHUNK), CHUNK)
                gate, up = acts[at, :ff], acts[at, ff:]
                sigmoid = 1.0 / (1.0 + jnp.exp(-gate))
                silu = gate * sigmoid
                back = grad_hidden[at]
                hidden[e, out] = (silu * up).astype(BF16)
                grad_acts[e, out, :ff] = (back * up * sigmoid * (1.0 + gate * (1.0 - sigmoid))).astype(BF16)
                grad_acts[e, out, ff:] = (back * silu).astype(BF16)

            produced[e, :rows] = dot(hidden[e, base : base + rows], down[e], ((1,), (0,))).astype(BF16)
            grad_rows[e, :rows] = dot(grad_acts[e, base : base + rows], gateup[e], ((1,), (1,))).astype(BF16)

        for i, block in enumerate(blocks):
            at = slice(i * CAP, (i + 1) * CAP)
            chosen = pick[block]
            back = jnp.concatenate([grad_rows[e, at] for e in range(local_experts)], axis=0)
            parts[block] = dot(chosen, back, ((0,), (0,))).astype(BF16)
            weighted = []
            for e in range(local_experts):
                made = produced[e, at].astype(F32)
                weighted.append((gate_cols[e, at] * made).astype(BF16))
                column = RES_SCALE * jnp.sum(made * grad_slots[e, at].astype(F32), axis=1, keepdims=True)
                hits = chosen[e * CAP : (e + 1) * CAP].astype(F32)
                notes[block, e : e + 1] = jnp.sum(hits * column, axis=0, keepdims=True)
            combined[block] = dot(chosen, jnp.concatenate(weighted, axis=0), ((0,), (0,))).astype(BF16)

    gather.arrive_stage(0)
    work(GROUPS[0], 0)
    gather.stage(3)
    gather.stage(4)
    gather.arrive_stage(1)
    gather.arrive_stage(2)
    base = len(GROUPS[0]) * CAP
    work(GROUPS[1], base)
    gather.stage(5)
    for stage in (3, 4, 5):
        gather.arrive_stage(stage)
    base += len(GROUPS[1]) * CAP
    work(GROUPS[2], base)

    scatter = Scatter(parts, landing, send_b, recv_b)
    scatter.stage(5)
    scatter.stage(4)
    swap = Exchange(notes, told, send_c, recv_c)
    swap.start()
    told[rank] = notes[rank]
    combined_copy = pltpu.make_async_copy(combined, combined_out, local.at[4])
    combined_copy.start()
    own_cot = cot[rank]
    gather.finish()
    pl.semaphore_signal(free, inc=1, device_id=sibling, device_id_type=MESH_ID)
    strip = stage_w.shape[1]
    per = strip // tokens
    jobs = [(arrived, grad_acts, at) for at in range(0, width, strip)] + [(hidden, grad_arrived, at) for at in range(0, ff, strip)]
    stores, gifts = [], []

    def gift(number):
        here = pl.ds(number * per, per)
        return pltpu.make_async_remote_copy(
            src_ref=buf.at[here], dst_ref=cot.at[here], send_sem=send_d.at[number], recv_sem=recv_d.at[number],
            device_id=sibling, device_id_type=MESH_ID,
        )

    def give(number):
        left, right, at = jobs[number]
        made = dot(left[1 - core, :, at : at + strip], right[1 - core], ((0,), (0,)))
        buf[number * per : (number + 1) * per] = made.astype(BF16).reshape(per, tokens, width)
        if number == 0:
            pl.semaphore_wait(free, 1)
        gifts.append(gift(number))
        gifts[-1].start()

    def keep(number):
        left, right, at = jobs[number]
        slot = number % 2
        made = dot(left[core, :, at : at + strip], right[core], ((0,), (0,)))
        gift(number).wait_recv()
        made = made + cot[number * per : (number + 1) * per].reshape(strip, width).astype(F32)
        if number >= 2:
            stores[number - 2].wait()
        stage_w[slot] = made.astype(BF16)
        copy = pltpu.make_async_copy(stage_w.at[slot], half_out.at[pl.ds(number * strip, strip)], store.at[slot])
        copy.start()
        stores.append(copy)

    tasks = [lambda n=n: give(n) for n in range(len(jobs))] + [lambda n=n: keep(n) for n in range(len(jobs))]
    for stage, amount in ((3, 4), (2, 2), (1, 4), (0, 2)):
        for _ in range(amount):
            tasks.pop(0)()
        scatter.stage(stage)
    for task in tasks:
        task()
    swap.arrive()
    gates = own_gates[...]
    grads = jnp.concatenate([told[i, :local_experts] for i in range(count)], axis=0)
    grad_logits = (gates * (grads - jnp.sum(gates * grads, axis=0, keepdims=True))).astype(BF16)
    normed = normed_ref[...]
    small_ref[...] = jnp.zeros_like(small_ref)
    small_ref[:EXPERTS] = dot(grad_logits, normed, ((1,), (0,)))
    from_router = dot(grad_logits, router, ((0,), (0,)))
    gain = gain_ref[...].reshape(1, width).astype(F32)
    half = tokens // 2
    grad_gain = jnp.zeros((1, width), F32)
    for place, back in enumerate(scatter.result()):
        at = slice(place * half, (place + 1) * half)
        residual = residual_ref[at]
        scale = rms_scale(residual)
        grad_normed = from_router[at] + back
        grad_norm, part = norm_back(residual, scale, gain, grad_normed)
        grad_gain = grad_gain + part[None]
        grad_residual = own_cot[at].astype(F32) + grad_norm
        grad_residual_ref[at] = grad_residual
        grad_att_ref[at] = (RES_SCALE * grad_residual).astype(BF16)
    small_ref[EXPERTS : EXPERTS + 1] = grad_gain
    grad_context_ref[...] = dot(out_w[...].reshape(HEADS * HD, width), grad_att_ref[...], ((1,), (1,))).astype(BF16).reshape(HEADS, HD, tokens)
    scatter.finish()
    swap.sent()
    for copy in gifts:
        copy.wait_send()
    for copy in stores[-2:]:
        copy.wait()
    combined_copy.wait()


def experts(normed, residual, gain, router, routes_all, cot_all, w_gateup, w_down, weights):
    tokens, width = normed.shape
    count = RING * RING
    local_experts, ff = w_down.shape[:2]
    shape = jax.ShapeDtypeStruct
    vmem = pltpu.VMEM
    rows = count * CAP
    return call(
        expert_kernel, "experts", 2,
        (
            shape((width + ff, width), BF16), shape((count, tokens, width), BF16),
            shape((tokens, width), F32), shape((tokens, width), BF16), shape((EXPERTS + 8, width), F32),
            shape((HEADS, HD, tokens), BF16),
        ),
        [anywhere()] * 9, [anywhere()] * 2 + [whole()] * 4,
        [
            vmem(normed.shape, BF16), vmem(residual.shape, F32), vmem(gain.shape, BF16), vmem(router.shape, BF16), vmem(routes_all.shape, jnp.int32),
            vmem((count, tokens, width), BF16), vmem((count, tokens, width), BF16), vmem(w_gateup.shape, BF16),
            vmem(w_down.shape, BF16), vmem((HEADS, HD, width), BF16), vmem((count, local_experts * CAP, tokens), BF16),
            vmem((local_experts, MOST, 1), F32), vmem((local_experts, rows, width), BF16),
            vmem((local_experts, rows, 2 * ff), BF16), vmem((local_experts, rows, width), BF16),
            vmem((local_experts, rows, ff), BF16), vmem((local_experts, MOST, width), BF16),
            vmem((MOST, 2 * ff), F32), vmem((MOST, ff), F32), vmem((local_experts, MOST, width), BF16),
            vmem((local_experts, MOST, width), BF16), vmem((count, tokens, width), BF16), vmem((count, tokens, width), BF16),
            vmem(((count - 1) * tokens, width), BF16), vmem((2, 256, width), BF16), vmem((count, 8, tokens), F32),
            vmem((count, 8, tokens), F32), vmem((EXPERTS, tokens), F32),
            *pair_sems(Torus.COUNT), *pair_sems(Torus.COUNT), *pair_sems(count - 1),
            *pair_sems((width + ff) // 256), pltpu.SemaphoreType.REGULAR, pltpu.SemaphoreType.DMA((5,)), pltpu.SemaphoreType.DMA((2,)), pltpu.SemaphoreType.DMA((6,)),
        ],
        65400, flops=2 * 9 * rows * width * ff * local_experts, bytes_accessed=30 << 20,
    )(normed, residual, gain, router, routes_all, cot_all, w_gateup, w_down, weights)


class RingSum:
    COUNT = 13

    def __init__(self, half, near, far, total, send, recv):
        self.half, self.near, self.far, self.total, self.send, self.recv = half, near, far, total, send, recv
        self.rank, dp = lax.axis_index("tensor"), lax.axis_index("dp")
        self.x, self.core = lax.div(dp, 2), lax.rem(dp, 2)
        self.chunk = half.shape[0] // RING
        self.outgoing = []

    def device(self, dx, other=False):
        core = 1 - self.core if other else self.core
        return (lax.rem(self.x + dx + RING, RING) * 2 + core, self.rank)

    def rows(self, dx, part=0):
        at, half = lax.rem(self.x + dx + RING, RING) * self.chunk, self.chunk // 2
        at = pl.multiple_of(at + (half if part == -1 else 0), half)
        return pl.ds(at, half if part else self.chunk)

    def copy(self, number, source, target, device):
        return pltpu.make_async_remote_copy(
            src_ref=source, dst_ref=target, send_sem=self.send.at[number], recv_sem=self.recv.at[number],
            device_id=device, device_id_type=MESH_ID,
        )

    def go(self, *args):
        self.outgoing.append(self.copy(*args))
        self.outgoing[-1].start()

    def come(self, number, target):
        self.copy(number, target, target, self.device(0, True)).wait_recv()

    def first(self):
        for i, way in ((0, 1), (1, -1)):
            self.go(i, self.half.at[self.rows(2, way)], self.far.at[i], self.device(way))

    def second(self):
        for i, way in ((0, 1), (1, -1)):
            self.come(i, self.far.at[i])
            at = self.rows(way, way)
            self.half[at] = (self.half[at].astype(F32) + self.far[i].astype(F32)).astype(BF16)
            self.go(2 + i, self.half.at[self.rows(way)], self.near.at[i], self.device(way))

    def third(self):
        for i in (0, 1):
            self.come(2 + i, self.near.at[i])
        own = self.half[self.rows(0)].astype(F32) + self.near[0].astype(F32) + self.near[1].astype(F32)
        self.total[self.core, self.rows(0)] = own.astype(BF16)
        ref = self.total.at[self.core, self.rows(0)]
        for i, way in ((0, 1), (1, -1)):
            self.go(4 + i, ref, ref, self.device(way))
        self.go(8, ref, ref, self.device(0, True))

    def fourth(self):
        for i, way in ((0, 1), (1, -1)):
            ref = self.total.at[self.core, self.rows(-way)]
            self.come(4 + i, ref)
            part = self.total.at[self.core, self.rows(-way, way)]
            self.go(6 + i, part, part, self.device(way))
            self.go(9 + i, ref, ref, self.device(0, True))

    def fifth(self):
        for i, way in ((0, 1), (1, -1)):
            ref = self.total.at[self.core, self.rows(2, way)]
            self.come(6 + i, ref)
            self.go(11 + i, ref, ref, self.device(0, True))

    def finish(self):
        self.come(8, self.total.at[1 - self.core, self.rows(0)])
        for i, way in ((0, 1), (1, -1)):
            self.come(9 + i, self.total.at[1 - self.core, self.rows(-way)])
            self.come(11 + i, self.total.at[1 - self.core, self.rows(2, way)])
        for copy in self.outgoing:
            copy.wait_send()


SMALL = 384


def backward_kernel(
    qkv_in, grad_in, wide_in, log_in, cosine_in, sine_in, normed_in, context_in, grad_att_in, combined_in, residual_in, half_in,
    small_in, x_in, gain_in, grad_residual_in, weights_in, keyval_in,
    block_ref, input_ref, query_ref, out_ref, keyval_ref, small_out, gain_out, gateup_out, down_out,
    qkv_ref, grad_ref, wide_ref, log_ref, cosine_ref, sine_ref, normed, context_ref, grad_att_ref, combined, residual_ref, half,
    small_ref, x_ref, gain_ref, grad_residual_ref, query_all, keyval_all,
    grad_parts, parts_out, parts_back, grad, query_rows, key_rows, value_rows, grad_rows, grad_query, grad_key, grad_value,
    wide_grad, out_parts, out_land, combined_land, far, near, total,
    weight, give, pair_land, mine, land, summed, small_parts, small_land, small_sum, small_dp, gather_buf,
    gain_parts, gain_land, gain_sum, gain_dp, back_pairs,
    send_a, recv_a, send_b, recv_b, send_c, recv_c, send_d, recv_d, send_e, recv_e, send_f, recv_f, send_g, recv_g,
    send_h, recv_h, send_i, recv_i, send_j, recv_j, send_k, recv_k, send_l, recv_l, send_m, recv_m, send_n, recv_n,
    send_p, recv_p, sems, out_sems,
):
    count, _, tokens = grad_ref.shape
    length, width = count * tokens, normed.shape[1]
    dps = land.shape[0]
    rank, dp = lax.axis_index("tensor"), lax.axis_index("dp")
    order = (
        (grad_in, grad_ref), (half_in, half), (small_in, small_ref), (qkv_in, qkv_ref), (context_in, context_ref),
        (grad_att_in, grad_att_ref), (combined_in, combined), (wide_in, wide_ref), (log_in, log_ref), (cosine_in, cosine_ref),
        (sine_in, sine_ref), (normed_in, normed), (residual_in, residual_ref), (x_in, x_ref), (gain_in, gain_ref),
        (grad_residual_in, grad_residual_ref), (weights_in.at[:, HD:], query_all), (keyval_in, keyval_all),
    )
    copies = loads(order, sems)
    greet(others("tensor", count), others("dp", dps))
    copies[0].wait()
    swap = Exchange(grad_ref, grad_parts, send_a, recv_a)
    swap.start()
    copies[1].wait()
    ring = RingSum(half, near, far, total, send_e, recv_e)
    ring.first()
    copies[2].wait()
    for i in range(count):
        small_parts[i, :, :256] = small_ref[8 * (i // 4) : 8 * (i // 4) + 8, 256 * (i % 4) : 256 * (i % 4) + 256]
        small_parts[i, :, 256:] = small_ref[32:40, 128 * (i // 2) : 128 * (i // 2) + 128]
    small = Exchange(small_parts, small_land, send_f, recv_f)
    small.start()
    small_land[rank] = small_parts[rank]
    for copy in copies[3:]:
        copy.wait()
    query, key, value = slice(0, HD), slice(HD, 2 * HD), slice(2 * HD, 3 * HD)
    query_rows[...] = qkv_ref[query].T
    key_rows[...] = qkv_ref[key].T
    value_rows[...] = qkv_ref[value].T
    scatter = Scatter(out_parts, out_land, send_c, recv_c)
    grad_att = grad_att_ref[...]
    for part in range(count):
        out_parts[part] = dot(context_ref[part], grad_att, ((1,), (0,))).astype(BF16)
    scatter.stage(5)
    scatter.stage(4)
    combine = Scatter(combined, combined_land, send_d, recv_d)
    combine.stage(5)
    combine.stage(4)
    grad_parts[rank] = grad_ref[rank]
    swap.arrive()
    for part in range(count):
        grad[:, part * tokens : (part + 1) * tokens] = grad_parts[part]
    grad_rows[...] = grad[...].T
    small.arrive()
    small_sum[0] = jnp.sum(small_land[...], axis=0)
    second_small = Exchange(small_sum.at[0], small_dp, send_g, recv_g, "dp", same=True)
    second_small.start()
    small_dp[dp] = small_sum[0]
    allowed = causal(Q_ROWS)
    blocks = length // Q_ROWS

    def small_again():
        second_small.arrive()
        small_sum[1] = jnp.sum(small_dp[...], axis=0)
        third.start()
        small_out[rank] = small_sum[1]

    third = Exchange(small_sum.at[1], small_out, send_h, recv_h, same=True)
    plan = {
        1: [lambda: scatter.stage(3)], 2: [ring.second, lambda: scatter.stage(2)], 3: [small_again],
        4: [lambda: scatter.stage(1)], 5: [lambda: combine.stage(3)], 7: [lambda: combine.stage(2)],
    }
    for block in reversed(range(blocks)):
        first = block * Q_ROWS
        columns = slice(first, first + Q_ROWS)
        scaled = qkv_ref[query, columns] * ATTN_SCALE
        logs = log_ref[:, columns]
        grad_block = grad[:, columns]
        inner = jnp.sum(grad_block.astype(F32) * wide_ref[:, columns], axis=0, keepdims=True)
        wide_total = jnp.zeros((HD, Q_ROWS), F32)
        spans = [(columns, True)]
        if block:
            spans.append((slice(0, first), False))
        for keys, close in spans:
            weights = jnp.exp(dot(key_rows[keys, :], scaled, ((1,), (0,))) - logs)
            if close:
                weights = jnp.where(allowed, weights, 0.0)
            grad_weights = dot(value_rows[keys, :], grad_block, ((1,), (0,)))
            grad_scores = (weights * (grad_weights - inner)).astype(BF16)
            wide_total = wide_total + dot(qkv_ref[key, keys], grad_scores, ((1,), (0,)))
            key_part = dot(grad_scores, query_rows[columns, :], ((1,), (0,)))
            value_part = dot(weights.astype(BF16), grad_rows[columns, :], ((1,), (0,)))
            if block == blocks - 1:
                grad_key[keys, :] = key_part
                grad_value[keys, :] = value_part
            else:
                grad_key[keys, :] += key_part
                grad_value[keys, :] += value_part
        grad_query[:, columns] = wide_total * ATTN_SCALE
        for task in plan.get(blocks - 1 - block, ()):
            task()
    middle = HD // 2
    cosine, sine = cosine_ref[...], -sine_ref[...]
    for place, wide in enumerate((grad_query[...], grad_key[...].T * ATTN_SCALE)):
        rows = rotate(wide[:middle], wide[middle:], cosine, sine)
        wide_grad[place * HD : (place + 1) * HD] = jnp.concatenate(rows, axis=0).astype(BF16)
    wide_grad[2 * HD :] = grad_value[...].T.astype(BF16)
    for part in range(count):
        parts_out[part] = wide_grad[:, part * tokens : (part + 1) * tokens]
    back = Exchange(parts_out, parts_back, send_b, recv_b)
    back.start()
    parts_back[rank] = parts_out[rank]
    weight[...] = dot(wide_grad[...], normed[...], ((1,), (0,)))
    odd = lax.rem(rank, 2)
    give[...] = weight[pl.ds(pl.multiple_of(HD + HD * (1 - odd), HD), HD), :].astype(BF16)
    pair = pltpu.make_async_remote_copy(
        src_ref=give, dst_ref=pair_land, send_sem=send_p, recv_sem=recv_p,
        device_id=(dp, rank + 1 - 2 * odd), device_id_type=MESH_ID,
    )
    pair.start()
    scatter.stage(0)
    ring.third()
    column = width // dps
    out_sum = jnp.concatenate(scatter.result(), axis=0)
    pair.wait_recv()
    kept = weight[pl.ds(pl.multiple_of(HD + HD * odd, HD), HD), :] + pair_land[...].astype(F32)
    for j, rows in enumerate((weight[:HD], out_sum, kept)):
        low = rows.astype(BF16)
        for i in range(dps):
            mine[i, j * HD : (j + 1) * HD] = low[:, i * column : (i + 1) * column]
    dp_first = Exchange(mine, land, send_i, recv_i, "dp")
    dp_first.start()
    land[dp] = mine[dp]
    combine.stage(1)

    back.arrive()
    share = HEADS // KV_HEADS
    for head in range(KV_HEADS):
        for part in range(2):
            at = slice((part + 1) * HD, (part + 2) * HD)
            both = sum(parts_back[head * share + i, at].astype(F32) for i in range(share))
            back_pairs[part * KV_HEADS + head] = both.astype(BF16)
    queries_back = parts_back[:, :HD].reshape(HEADS * HD, tokens)
    grad_normed = dot(queries_back, query_all[...].reshape(HEADS * HD, width), ((0,), (0,)))
    grad_normed = grad_normed + dot(back_pairs[...].reshape(2 * KV_HEADS * HD, tokens), keyval_all[...], ((0,), (1,)))
    inputs = x_ref[...].astype(F32)
    grad_norm, grad_gain = norm_back(inputs, rms_scale(inputs), gain_ref[...].reshape(1, width).astype(F32), grad_normed)
    input_ref[...] = grad_residual_ref[...] + grad_norm
    grad_gain = grad_gain[None]
    gain_parts[...] = jnp.zeros_like(gain_parts)
    for i in range(count):
        gain_parts[i, :1] = grad_gain[:, 128 * (i // 2) : 128 * (i // 2) + 128]
    gain_first = Exchange(gain_parts, gain_land, send_k, recv_k)
    gain_first.start()
    gain_land[rank] = gain_parts[rank]

    dp_first.arrive()
    summed[dp] = jnp.sum(land[...].astype(F32), axis=0).astype(BF16)
    dp_second = Exchange(summed.at[dp], summed, send_j, recv_j, "dp", same=True)
    dp_second.start()
    ring.fourth()
    gain_first.arrive()
    gain_sum[0] = jnp.sum(gain_land[...], axis=0)
    gain_second = Exchange(gain_sum.at[0], gain_dp, send_l, recv_l, "dp", same=True)
    gain_second.start()
    gain_dp[dp] = gain_sum[0]
    dp_second.arrive()
    for i in range(dps):
        columns = slice(i * column, (i + 1) * column)
        query_ref[:, columns] = summed[i, :HD]
        out_ref[:, columns] = summed[i, HD : 2 * HD]
        gather_buf[rank, :, columns] = summed[i, 2 * HD :]
    gather = Gather(gather_buf, send_n, recv_n)
    gather.stage(0)
    gain_second.arrive()
    gain_sum[1] = jnp.sum(gain_dp[...], axis=0)
    gain_third = Exchange(gain_sum.at[1], gain_out, send_m, recv_m, same=True)
    gain_third.start()
    gain_out[rank] = gain_sum[1]
    gather.stage(1)
    gather.stage(2)
    combine.stage(0)
    gather.stage(3)
    gather.stage(4)
    ring.fifth()
    gather.stage(5)
    rows = block_ref.shape[0] // 2
    for place, value_half in enumerate(combine.result()):
        at = slice(place * rows, (place + 1) * rows)
        block_ref[at] = (residual_ref[at] + RES_SCALE * value_half).astype(BF16)
    ring.finish()
    outs = [
        pltpu.make_async_copy(total.at[:, pl.ds(0, width)], gateup_out, out_sems.at[0]),
        pltpu.make_async_copy(total.at[:, pl.ds(width, total.shape[1] - width)], down_out, out_sems.at[1]),
    ]
    for copy in outs:
        copy.start()
    gather.finish()
    for i in range(count):
        base = (i % 2) * KV_HEADS * HD + (i // 2) * HD
        keyval_ref[base : base + HD, :] = gather_buf[i]
    third.arrive()
    gain_third.arrive()
    pair.wait_send()
    for each in (swap, back, small, second_small, third, dp_first, dp_second, gain_first, gain_second, gain_third):
        each.sent()
    scatter.finish()
    combine.finish()
    for copy in outs:
        copy.wait()


def backward(
    qkv, grad_context, wide, logs, cosine, sine, normed, context, grad_att, combined, residual, half, small,
    x, gain, grad_residual, weights, w_keyval, dps,
):
    count, _, tokens = grad_context.shape
    length, width = normed.shape
    shape = jax.ShapeDtypeStruct
    vmem = pltpu.VMEM
    low = vmem((length, HD), BF16)
    wide_rows = vmem((length, HD), F32)
    column = width // dps
    rows = half.shape[0]
    small_shape, gain_shape = (8, SMALL), (8, 128)
    operands = (
        qkv, grad_context, wide, logs, cosine, sine, normed, context, grad_att, combined, residual, half, small,
        x, gain, grad_residual, weights, w_keyval,
    )
    held = [vmem(o.shape, o.dtype) for o in operands]
    held[16] = vmem((count, HD, width), BF16)
    three = vmem((dps, 3 * HD, column), BF16)
    return call(
        backward_kernel, "backward", 4,
        (
            shape((tokens, width), BF16), shape((tokens, width), F32), shape((HD, width), BF16), shape((HD, width), BF16),
            shape((count * HD, width), BF16), shape((count, *small_shape), F32), shape((count, *gain_shape), F32),
            shape((2, width, width), BF16), shape((2, rows - width, width), BF16),
        ),
        [anywhere()] * len(operands), [whole()] * 7 + [anywhere()] * 2,
        [
            *held,
            vmem((count, HD, tokens), BF16), vmem(qkv_parts(count, tokens), BF16), vmem(qkv_parts(count, tokens), BF16),
            vmem((HD, length), BF16), low, low, low, low, vmem((HD, length), F32), wide_rows, wide_rows,
            vmem((3 * HD, length), BF16), vmem((count, HD, width), BF16), vmem(((count - 1) * HD, width), BF16),
            vmem(((count - 1) * tokens, width), BF16), vmem((2, rows // 8, width), BF16), vmem((2, rows // 4, width), BF16),
            vmem((2, rows, width), BF16),
            vmem((3 * HD, width), F32), vmem((HD, width), BF16), vmem((HD, width), BF16), three, three, three,
            vmem((count, *small_shape), F32), vmem((count, *small_shape), F32), vmem((2, *small_shape), F32),
            vmem((dps, *small_shape), F32), vmem((count, HD, width), BF16),
            vmem((count, *gain_shape), F32), vmem((count, *gain_shape), F32), vmem((2, *gain_shape), F32),
            vmem((dps, *gain_shape), F32), vmem((2 * KV_HEADS, HD, tokens), BF16),
            *pair_sems(count - 1), *pair_sems(count - 1), *pair_sems(Torus.COUNT), *pair_sems(Torus.COUNT),
            *pair_sems(RingSum.COUNT), *pair_sems(count - 1), *pair_sems(dps - 1), *pair_sems(count - 1),
            *pair_sems(dps - 1), *pair_sems(dps - 1), *pair_sems(count - 1), *pair_sems(dps - 1), *pair_sems(count - 1),
            *pair_sems(Torus.COUNT), pltpu.SemaphoreType.DMA, pltpu.SemaphoreType.DMA,
            pltpu.SemaphoreType.DMA((len(operands),)), pltpu.SemaphoreType.DMA((2,)),
        ],
        65400, flops=2 * length * length * HD * 5, bytes_accessed=30 << 20,
    )(*operands)


def qkv_parts(count, tokens):
    return (count, 3 * HD, tokens)


def widen_kernel(gateup_ref, down_ref, keyval_ref, gateup_out, down_out, keyval_out):
    gateup_out[...] = gateup_ref[...].astype(F32)
    down_out[...] = down_ref[...].astype(F32)
    keyval_out[...] = keyval_ref[...].T.astype(F32)


def widen(gateup, down, keyval):
    steps = 8
    experts_here, width, wide = gateup.shape
    ff = down.shape[1]
    per = steps // experts_here
    pairs = keyval.shape[0]
    shape = jax.ShapeDtypeStruct
    gateup_spec = pl.BlockSpec((1, width // per, wide), lambda i: (i // per, i % per, 0))
    down_spec = pl.BlockSpec((1, ff // per, width), lambda i: (i // per, i % per, 0))
    return pl.pallas_call(
        widen_kernel, grid=(steps,),
        out_shape=(shape(gateup.shape, F32), shape(down.shape, F32), shape((width, pairs), F32)),
        in_specs=[gateup_spec, down_spec, pl.BlockSpec((pairs, width // steps), lambda i: (0, i))],
        out_specs=[gateup_spec, down_spec, pl.BlockSpec((width // steps, pairs), lambda i: (i, 0))],
        compiler_params=pltpu.CompilerParams(vmem_limit_bytes=65400 << 10),
        name="widen",
    )(gateup, down, keyval)


def shards(
    block_input, attn_gain, w_query, w_keyval, w_out, ffn_gain, w_router, w_gateup, w_down, routes, cotangent,
):
    tokens, width = block_input.shape
    length = tokens * lax.axis_size("tensor")
    cosine, sine = rope_tables(length, HD)
    normed_one_all, qkv, wide_out, logs, context, weights, cotangent_all, routes_all, residual, normed_two = forward(
        block_input, attn_gain, ffn_gain, w_query.T, w_keyval, w_out, cotangent, cosine, sine, routes.T
    )
    half, combined, grad_residual, grad_attention, small, grad_context = experts(
        normed_two, residual, ffn_gain, w_router.T, routes_all, cotangent_all, w_gateup, w_down, weights
    )
    block_out, grad_input, grad_query_w, grad_w_out, grad_keyval, small, gain_one, grad_w_gateup, grad_w_down = backward(
        qkv, grad_context, wide_out, logs, cosine, sine, normed_one_all.reshape(length, width), context, grad_attention,
        combined, residual, half, small, block_input, attn_gain, grad_residual, weights, w_keyval, lax.axis_size("dp"),
    )
    grad_w_gateup, grad_w_down, grad_keyval = widen(grad_w_gateup, grad_w_down, grad_keyval)
    routers = small[:, :, :256].reshape(4, 4, 8, 256).transpose(0, 2, 1, 3).reshape(EXPERTS, width)
    return (
        block_out,
        grad_input,
        gain_one[::2, 0].reshape(width),
        grad_query_w.astype(F32).T,
        grad_keyval,
        grad_w_out.astype(F32),
        small[::2, 0, 256:].reshape(width),
        routers.T,
        grad_w_gateup,
        grad_w_down,
    )


def solution(mesh):
    rows = P(("dp", "tensor"), None)
    in_specs = (
        rows, P(), P(None, "tensor"), P(), P("tensor", None), P(), P(),
        P("tensor", None, None), P("tensor", None, None), rows, rows,
    )
    out_specs = (
        rows, rows, P(), P(None, "tensor"), P(), P("tensor", None), P(), P(),
        P("tensor", None, None), P("tensor", None, None),
    )
    return jax.shard_map(shards, mesh=mesh, in_specs=in_specs, out_specs=out_specs, check_vma=False)
```

```python
import jax
import jax.numpy as jnp
import numpy as np
from jax import lax
from jax.experimental import pallas as pl
from jax.experimental.pallas import tpu as pltpu
from jax.sharding import PartitionSpec as P

HEADS = 16
KV_HEADS = 8
HD = 64
EXPERTS = 32
TOP = 8
CAP = 64
ATTN_SCALE = 0.015625
RES_SCALE = 0.22
EPSILON = 1e-06
ROPE_BASE = 10000.0
F32 = jnp.float32
BF16 = jnp.bfloat16
Q_ROWS = 256


def rms_scale(values):
    return lax.rsqrt(jnp.mean(values * values, axis=-1, keepdims=True) + EPSILON)


def norm_back(values, scale, gain, grad_normed):
    grad_scaled = grad_normed * gain
    grad_gain = jnp.sum(grad_normed * values * scale, axis=0)
    inner = jnp.mean(grad_scaled * values, axis=-1, keepdims=True)
    return (scale * (grad_scaled - values * scale * scale * inner), grad_gain)


def rope_tables(length, width):
    half_width = width // 2
    inverse = ROPE_BASE ** (-(np.arange(half_width) * 2.0) / width)
    angles = np.arange(length)[None, :] * inverse[:, None]
    return (jnp.asarray(np.cos(angles), F32), jnp.asarray(np.sin(angles), F32))


def rotate(first, second, cosine, sine):
    return first * cosine - second * sine, second * cosine + first * sine


def dot(a, b, dims):
    return lax.dot_general(a, b, ((dims[0], dims[1]), ((), ())), preferred_element_type=F32)


def causal(rows):
    key = lax.broadcasted_iota(jnp.int32, (rows, rows), 0)
    query = lax.broadcasted_iota(jnp.int32, (rows, rows), 1)
    return key <= query


RING = 4
MESH_ID = pl.DeviceIdType.MESH


def whole():
    return pl.BlockSpec(memory_space=pltpu.VMEM)


def anywhere():
    return pl.BlockSpec(memory_space=pltpu.HBM)


def position():
    rank = lax.axis_index("tensor")
    return lax.div(rank, RING), lax.rem(rank, RING)


def shifted(pos, axis, by):
    moved = lax.rem(pos[axis] + (by + RING), RING) if by else pos[axis]
    return (moved, pos[1]) if axis == 0 else (pos[0], moved)


def joined(pos):
    return pos[0] * RING + pos[1]


def greet(tensor_peers, dp_peers=(), more=()):
    dp, rank = lax.axis_index("dp"), lax.axis_index("tensor")
    sem = pltpu.get_barrier_semaphore()
    peers = [(dp, p) for p in tensor_peers] + [(p, rank) for p in dp_peers] + list(more)
    for peer in peers:
        pl.semaphore_signal(sem, inc=1, device_id=peer, device_id_type=MESH_ID)
    pl.semaphore_wait(sem, len(peers))


def neighbours():
    pos = position()
    return [joined(shifted(pos, axis, by)) for axis in (0, 1) for by in (1, -1)]


def others(axis, count):
    return [lax.rem(lax.axis_index(axis) + r, count) for r in range(1, count)]


def torus_messages(half, rows):
    primary, secondary = (0, 1) if half == 0 else (1, 0)
    h, q = rows // 2, rows // 4
    full = (half * h, h)
    part = {1: (half * h, q), -1: (half * h + q, q)}
    out = []
    for d in (1, -1):
        out.append((0, ("p1", d), None, full, (0, 0), primary, d))
        out.append((0, ("s1", 0, d), None, full, (0, 0), secondary, d))
        out.append((1, ("p2", d), ("p1", d), part[d], (-d, 0), primary, d))
        for e in (1, -1):
            out.append((1, ("s1", -d, e), ("p1", d), full, (-d, 0), secondary, e))
    for e in (1, -1):
        out.append((2, ("s2", 0, e), ("s1", 0, e), part[e], (0, -e), secondary, e))
        for d in (1, -1):
            out.append((3, ("s1", ("o", d), e), ("p2", d), part[d], (2, 0), secondary, e))
            out.append((4, ("s2", d, e), ("s1", d, e), part[e], (d, -e), secondary, e))
        out.append((5, ("s2", "o", e), ("s1", ("o", e), e), part[e], (2, -e), secondary, e))
    return out


class Torus:
    COUNT = 44
    STAGES = 6

    def __init__(self, rows):
        self.rows = rows
        self.pos = position()
        self.dp = lax.axis_index("dp")
        self.messages, self.children, self.place, order, used = {}, {}, {}, [], 0
        for half in (0, 1):
            for at, (stage, key, needs, piece, offset, axis, way) in enumerate(torus_messages(half, rows)):
                key = (half, key)
                needs = None if needs is None else (half, needs)
                self.messages[key] = (len(order), stage, needs, piece, offset, axis, way)
                self.children.setdefault(needs, []).append(key)
                self.place[key] = used
                used += piece[1]
                order.append((stage, at, half, key))
        self.landing_rows = used
        self.order = [entry[3] for entry in sorted(order, key=lambda entry: entry[:3])]

    def block(self, key, pos):
        half, offset = key[0], self.messages[key][4]
        primary, secondary = (0, 1) if half == 0 else (1, 0)
        return joined(shifted(shifted(pos, primary, offset[0]), secondary, offset[1]))

    def sender(self, key):
        _, _, _, _, _, axis, way = self.messages[key]
        return shifted(self.pos, axis, -way)

    def receiver(self, key):
        _, _, _, _, _, axis, way = self.messages[key]
        return shifted(self.pos, axis, way)


class Gather(Torus):
    def __init__(self, buf, send, recv):
        super().__init__(buf.shape[1])
        self.buf, self.send, self.recv = buf, send, recv
        self.arrived = set()

    def copy(self, key, incoming):
        number, (first, count) = self.messages[key][0], self.messages[key][3]
        at = self.sender(key) if incoming else self.pos
        ref = self.buf.at[self.block(key, at), pl.ds(first, count)]
        return pltpu.make_async_remote_copy(
            src_ref=ref, dst_ref=ref, send_sem=self.send.at[number], recv_sem=self.recv.at[number],
            device_id=(self.dp, joined(at if incoming else self.receiver(key))), device_id_type=MESH_ID,
        )

    def arrive(self, key):
        if key not in self.arrived:
            self.arrived.add(key)
            self.copy(key, True).wait_recv()

    def stage(self, number):
        for key in self.order:
            _, stage, needs, *_ = self.messages[key]
            if stage == number:
                if needs is not None:
                    self.arrive(needs)
                self.copy(key, False).start()

    def arrive_stage(self, number):
        for key in self.order:
            if self.messages[key][1] == number:
                self.arrive(key)

    def finish(self):
        for key in self.order:
            self.arrive(key)
        for key in self.order:
            self.copy(key, False).wait_send()


class Scatter(Torus):
    def __init__(self, parts, landing, send, recv):
        super().__init__(parts.shape[1])
        self.parts, self.landing, self.send, self.recv = parts, landing, send, recv

    def copy(self, key):
        number, (first, count) = self.messages[key][0], self.messages[key][3]
        at = self.sender(key)
        return pltpu.make_async_remote_copy(
            src_ref=self.parts.at[self.block(key, at), pl.ds(first, count)],
            dst_ref=self.landing.at[pl.ds(self.place[key], count)],
            send_sem=self.send.at[number], recv_sem=self.recv.at[number],
            device_id=(self.dp, joined(at)), device_id_type=MESH_ID,
        )

    def landed(self, key):
        count = self.messages[key][3][1]
        self.copy(key).wait_recv()
        return self.landing[pl.ds(self.place[key], count), :]

    def stage(self, number):
        for key in reversed(self.order):
            if self.messages[key][1] == number:
                pieces = {}
                for child in self.children.get(key, []):
                    pieces.setdefault(self.messages[child][3], []).append(child)
                for (first, count), children in pieces.items():
                    at = (self.block(children[0], self.pos), pl.ds(first, count))
                    self.parts[at] = sum((self.landed(c) for c in children), self.parts[at])
                self.copy(key).start()

    def result(self):
        out = []
        for half in (0, 1):
            children = [c for c in self.children[None] if c[0] == half]
            first, count = self.messages[children[0]][3]
            own = self.parts[joined(self.pos), pl.ds(first, count)].astype(F32)
            out.append(sum((self.landed(c).astype(F32) for c in children), own))
        return out

    def finish(self):
        for key in self.order:
            self.copy(key).wait_send()


class Exchange:
    def __init__(self, source, target, send, recv, axis="tensor", same=False):
        self.source, self.target, self.send, self.recv, self.axis, self.same = source, target, send, recv, axis, same
        self.count = target.shape[0]
        self.rank = lax.axis_index(axis)

    def device(self, to):
        if self.axis == "tensor":
            return (lax.axis_index("dp"), to)
        return (to, lax.axis_index("tensor"))

    def copy(self, r):
        to = lax.rem(self.rank + r, self.count)
        return pltpu.make_async_remote_copy(
            src_ref=self.source if self.same else self.source.at[to],
            dst_ref=self.target.at[self.rank], send_sem=self.send.at[r - 1],
            recv_sem=self.recv.at[r - 1], device_id=self.device(to), device_id_type=MESH_ID,
        )

    def start(self):
        for r in range(1, self.count):
            self.copy(r).start()

    def arrive(self):
        for r in range(1, self.count):
            origin = lax.rem(self.rank + self.count - r, self.count)
            pltpu.make_async_remote_copy(
                src_ref=self.target.at[origin], dst_ref=self.target.at[origin], send_sem=self.send.at[r - 1],
                recv_sem=self.recv.at[r - 1], device_id=self.device(origin), device_id_type=MESH_ID,
            ).wait_recv()

    def sent(self):
        for r in range(1, self.count):
            self.copy(r).wait_send()


def pair_sems(count):
    return [pltpu.SemaphoreType.DMA((count,))] * 2


def call(kernel, name, number, out_shape, in_specs, out_specs, scratch, limit, flops=0, bytes_accessed=0):
    return pl.pallas_call(
        kernel, out_shape=out_shape, in_specs=in_specs, out_specs=out_specs, scratch_shapes=scratch,
        compiler_params=pltpu.CompilerParams(collective_id=number, has_side_effects=True, vmem_limit_bytes=limit << 10),
        cost_estimate=pl.CostEstimate(flops=flops, bytes_accessed=bytes_accessed, transcendentals=0),
        name=name,
    )


def loads(pairs, sems):
    copies = [pltpu.make_async_copy(a, b, sems.at[i]) for i, (a, b) in enumerate(pairs)]
    for copy in copies:
        copy.start()
    return copies


class Replicas:
    COUNT = RING * RING - 1 + 9

    def __init__(self, own, buf, send, recv, local):
        self.own, self.buf, self.send, self.recv = own, buf, send, recv
        self.keep = pltpu.make_async_copy(own, buf.at[lax.axis_index("tensor"), :, self.columns_of(buf)], local)
        self.rank, self.dp = lax.axis_index("tensor"), lax.axis_index("dp")
        self.x, self.core = lax.div(self.dp, 2), lax.rem(self.dp, 2)
        self.blocks = buf.shape[0]
        self.share = buf.shape[2] // (2 * RING)

    @staticmethod
    def columns_of(buf):
        share = buf.shape[2] // (2 * RING)
        return pl.ds(pl.multiple_of(lax.axis_index("dp") * share, share), share)

    def member(self, dx, other):
        core = 1 - self.core if other else self.core
        return lax.rem(self.x + dx + RING, RING) * 2 + core

    def columns(self, member):
        return pl.ds(pl.multiple_of(member * self.share, self.share), self.share)

    def piece(self, member, part):
        first, count = {0: (0, self.blocks), 1: (0, self.blocks // 2), -1: (self.blocks // 2, self.blocks // 2)}[part]
        return self.buf.at[pl.ds(first, count), :, self.columns(member)]

    def copy(self, number, ref, device):
        return pltpu.make_async_remote_copy(
            src_ref=ref, dst_ref=ref, send_sem=self.send.at[number], recv_sem=self.recv.at[number],
            device_id=device, device_id_type=MESH_ID,
        )

    def first(self):
        count = self.blocks
        self.outgoing = []
        self.keep.start()
        for r in range(1, count):
            self.outgoing.append(pltpu.make_async_remote_copy(
                src_ref=self.own, dst_ref=self.buf.at[self.rank, :, self.columns(self.dp)],
                send_sem=self.send.at[r - 1], recv_sem=self.recv.at[r - 1],
                device_id=(self.dp, lax.rem(self.rank + r, count)), device_id_type=MESH_ID,
            ))
            self.outgoing[-1].start()

    def go(self, number, member, part, dx, other):
        self.outgoing.append(self.copy(self.blocks - 1 + number, self.piece(member, part), (self.member(dx, other), self.rank)))
        self.outgoing[-1].start()

    def come(self, number, member, part):
        self.copy(self.blocks - 1 + number, self.piece(member, part), (self.dp, self.rank)).wait_recv()

    def second(self):
        for r in range(1, self.blocks):
            ref = self.buf.at[lax.rem(self.rank + self.blocks - r, self.blocks), :, self.columns(self.dp)]
            self.copy(r - 1, ref, (self.dp, self.rank)).wait_recv()
        self.keep.wait()
        self.go(0, self.dp, 0, 1, False)
        self.go(1, self.dp, 0, -1, False)
        self.go(4, self.dp, 0, 0, True)

    def third(self):
        for number, way in ((0, 1), (1, -1)):
            member = self.member(-way, False)
            self.come(number, member, 0)
            self.go(2 + number, member, way, way, False)
            self.go(5 + number, member, 0, 0, True)

    def fourth(self):
        for number, way in ((0, 1), (1, -1)):
            member = self.member(2, False)
            self.come(2 + number, member, way)
            self.go(7 + number, member, way, 0, True)

    def finish(self):
        self.come(4, self.member(0, True), 0)
        for number, way in ((0, 1), (1, -1)):
            self.come(5 + number, self.member(-way, True), 0)
            self.come(7 + number, self.member(2, True), way)
        for copy in self.outgoing:
            copy.wait_send()


def near_members():
    x, core = lax.div(lax.axis_index("dp"), 2), lax.rem(lax.axis_index("dp"), 2)
    return [lax.rem(x + 1, RING) * 2 + core, lax.rem(x + RING - 1, RING) * 2 + core, x * 2 + 1 - core]


def forward_kernel(
    x_in, gain_in, gain_two_in, query_in, keyval_ref, out_w_ref, cot_ref, cosine_in, sine_in, routes_in,
    normed_out, qkv_out, wide_ref, log_ref, context_ref, weights_out, cot_all, routes_all, residual_ref, normed_two_ref,
    x_ref, gain_ref, gain_two_ref, cosine_ref, sine_ref,
    buf, weights, own_w, local_w, pair_w, qkv, key_rows, context_parts,
    sems_a, sems_b, sems_d, sems_e, sems_f, local_sems, load_sems,
):
    tokens, width = x_ref.shape
    rank = lax.axis_index("tensor")
    z, y = position()
    half = HD // 2
    copies = loads(
        [
            (x_in, x_ref), (gain_in, gain_ref), (out_w_ref, own_w.at[:HD]), (query_in, own_w.at[HD:]),
            (routes_in, routes_all.at[rank]), (cosine_in, cosine_ref), (sine_in, sine_ref), (gain_two_in, gain_two_ref),
        ],
        load_sems,
    )
    pair_copies = []
    for part in range(2):
        column = pl.multiple_of(part * KV_HEADS * HD + z * 2 * HD, 2 * HD)
        copy = pltpu.make_async_copy(keyval_ref.at[:, pl.ds(column, 2 * HD)], pair_w.at[part], local_sems.at[part])
        copy.start()
        pair_copies.append(copy)
    own_cot = pltpu.make_async_copy(cot_ref, cot_all.at[rank], local_sems.at[2])
    own_cot.start()
    copies[0].wait()
    copies[1].wait()
    inputs = x_ref[...].astype(F32)
    buf[rank] = (inputs * rms_scale(inputs) * gain_ref[...].reshape(1, width).astype(F32)).astype(BF16)
    greet(others("tensor", RING * RING), near_members())
    main = Gather(buf, *sems_a)
    main.stage(0)
    for copy in copies[2:5]:
        copy.wait()
    replicas = Replicas(own_w.at[:, Replicas.columns_of(weights)], weights, *sems_b, local_sems.at[3])
    replicas.first()
    tell = Exchange(routes_all.at[rank], routes_all, *sems_f, same=True)
    tell.start()
    for copy in pair_copies + copies[5:]:
        copy.wait()
    odd = lax.rem(lax.div(rank, 2), 2)
    local_w[:HD] = own_w[HD:]
    for part in range(2):
        tall = pair_w[part].T.astype(F32)
        local_w[HD * (part + 1) : HD * (part + 2)] = jnp.where(odd == 0, tall[:HD], tall[HD:]).astype(BF16)
    pos = main.pos

    def project(dz, dy):
        block = joined(shifted(shifted(pos, 0, dz), 1, dy))
        columns = pl.ds(pl.multiple_of(block * tokens, tokens), tokens)
        made = dot(local_w[...], buf[block], ((1,), (1,)))
        cosine, sine = cosine_ref[:, columns], sine_ref[:, columns]
        rows = []
        for first in (0, HD):
            rows += rotate(made[first : first + half], made[first + half : first + HD], cosine, sine)
        rows.append(made[2 * HD :])
        qkv[:, columns] = jnp.concatenate(rows, axis=0).astype(BF16)

    project(0, 0)
    main.stage(1)
    main.stage(2)
    replicas.second()
    main.arrive_stage(0)
    for offset in ((0, 1), (0, 3), (1, 0), (3, 0)):
        project(*offset)
    main.stage(3)
    main.stage(4)
    own_cot.wait()
    back = Gather(cot_all, *sems_d)
    main.arrive_stage(1)
    main.arrive_stage(2)
    for offset in ((1, 1), (1, 3), (3, 1), (3, 3), (2, 0), (0, 2)):
        project(*offset)
    main.stage(5)
    back.stage(0)
    main.arrive_stage(3)
    main.arrive_stage(4)
    replicas.third()
    for offset in ((2, 1), (2, 3), (1, 2), (3, 2)):
        project(*offset)
    main.arrive_stage(5)
    project(2, 2)
    normed_copy = pltpu.make_async_copy(buf, normed_out, local_sems.at[5])
    normed_copy.start()
    qkv_copy = pltpu.make_async_copy(qkv, qkv_out, local_sems.at[6])
    qkv_copy.start()
    key_rows[...] = qkv[HD : 2 * HD].T
    swap = Exchange(context_parts, context_ref, *sems_e)
    todo = {2: [lambda: back.stage(1)], 3: [lambda: back.stage(2)], 5: [replicas.fourth], 6: [lambda: back.stage(3)]}
    attend(qkv, key_rows, wide_ref, log_ref, context_parts, tokens, todo)
    swap.start()
    context_ref[rank] = context_parts[rank]
    back.stage(4)
    back.stage(5)
    replicas.finish()
    weights_copy = pltpu.make_async_copy(weights, weights_out, local_sems.at[7])
    weights_copy.start()
    tell.arrive()
    swap.arrive()
    context = context_ref[...].reshape(HEADS * HD, tokens)
    attention = dot(context, weights[:, :HD].reshape(HEADS * HD, width), ((0,), (0,)))
    residual = x_ref[...].astype(F32) + RES_SCALE * attention
    residual_ref[...] = residual
    normed_two_ref[...] = (residual * rms_scale(residual) * gain_two_ref[...].reshape(1, width).astype(F32)).astype(BF16)
    back.finish()
    main.finish()
    swap.sent()
    tell.sent()
    normed_copy.wait()
    qkv_copy.wait()
    weights_copy.wait()


def attend(qkv, key_rows, wide_ref, log_ref, parts_ref, tokens, todo):
    length = qkv.shape[1]
    allowed = causal(Q_ROWS)
    query, value = slice(0, HD), slice(2 * HD, 3 * HD)
    for block in range(length // Q_ROWS):
        first = block * Q_ROWS
        columns = slice(first, first + Q_ROWS)
        scaled = qkv[query, columns] * ATTN_SCALE
        near = dot(key_rows[columns, :], scaled, ((1,), (0,)))
        near = jnp.where(allowed, near, -1e30)
        largest = jnp.max(near, axis=0, keepdims=True)
        if block:
            far = dot(key_rows[:first, :], scaled, ((1,), (0,)))
            largest = jnp.maximum(largest, jnp.max(far, axis=0, keepdims=True))
        near = jnp.exp(near - largest)
        total = jnp.sum(near, axis=0, keepdims=True)
        context = dot(qkv[value, columns], near.astype(BF16), ((1,), (0,)))
        if block:
            far = jnp.exp(far - largest)
            total = total + jnp.sum(far, axis=0, keepdims=True)
            context = context + dot(qkv[value, :first], far.astype(BF16), ((1,), (0,)))
        context = context / total
        wide_ref[:, columns] = context
        log_ref[:, columns] = largest + jnp.log(total)
        low = context.astype(BF16)
        for part in range(Q_ROWS // tokens):
            parts_ref[first // tokens + part] = low[:, part * tokens : (part + 1) * tokens]
        for task in todo.get(block, ()):
            task()


def forward(x, gain, gain_two, w_query, w_keyval, w_out, cotangent, cosine, sine, routes):
    tokens, width = x.shape
    count = RING * RING
    length = tokens * count

    def kernel(*refs):
        plain, sems = refs[:-12], refs[-12:]
        forward_kernel(*plain, *[sems[2 * i : 2 * i + 2] for i in range(5)], sems[10], sems[11])

    shape = jax.ShapeDtypeStruct
    vmem = pltpu.VMEM
    return call(
        kernel, "forward", 1,
        (
            shape((count, tokens, width), BF16), shape((3 * HD, length), BF16), shape((HD, length), F32),
            shape((1, length), F32), shape((count, HD, tokens), BF16), shape((count, 2 * HD, width), BF16),
            shape((count, tokens, width), BF16),
            shape((count, *routes.shape), jnp.int32), shape((tokens, width), F32), shape((tokens, width), BF16),
        ),
        [anywhere()] * 10,
        [anywhere(), anywhere(), whole(), whole(), whole(), anywhere(), anywhere(), whole(), whole(), whole()],
        [
            vmem(x.shape, BF16), vmem(gain.shape, BF16), vmem(gain.shape, BF16), vmem(cosine.shape, F32), vmem(sine.shape, F32),
            vmem((count, tokens, width), BF16), vmem((count, 2 * HD, width), BF16), vmem((2 * HD, width), BF16), vmem((3 * HD, width), BF16),
            vmem((2, width, 2 * HD), BF16), vmem((3 * HD, length), BF16), vmem((length, HD), BF16),
            vmem((count, HD, tokens), BF16),
            *pair_sems(Torus.COUNT), *pair_sems(Replicas.COUNT), *pair_sems(Torus.COUNT),
            *pair_sems(count - 1), *pair_sems(count - 1), pltpu.SemaphoreType.DMA((8,)), pltpu.SemaphoreType.DMA((8,)),
        ],
        65400, flops=2 * length * (3 * HD * width + length * HD * 2), bytes_accessed=20 << 20,
    )(x, gain, gain_two, w_query, w_keyval, w_out, cotangent, cosine, sine, routes)


class RingSum:
    COUNT = 13

    def __init__(self, half, near, far, total, send, recv):
        self.half, self.near, self.far, self.total, self.send, self.recv = half, near, far, total, send, recv
        self.rank, dp = lax.axis_index("tensor"), lax.axis_index("dp")
        self.x, self.core = lax.div(dp, 2), lax.rem(dp, 2)
        self.chunk = (total.shape[1] if half is None else half.shape[0]) // RING
        self.outgoing = []

    def device(self, dx, other=False):
        core = 1 - self.core if other else self.core
        return (lax.rem(self.x + dx + RING, RING) * 2 + core, self.rank)

    def rows(self, dx, part=0):
        at, half = lax.rem(self.x + dx + RING, RING) * self.chunk, self.chunk // 2
        at = pl.multiple_of(at + (half if part == -1 else 0), half)
        return pl.ds(at, half if part else self.chunk)

    def copy(self, number, source, target, device):
        return pltpu.make_async_remote_copy(
            src_ref=source, dst_ref=target, send_sem=self.send.at[number], recv_sem=self.recv.at[number],
            device_id=device, device_id_type=MESH_ID,
        )

    def go(self, *args):
        self.outgoing.append(self.copy(*args))
        self.outgoing[-1].start()

    def come(self, number, target):
        self.copy(number, target, target, self.device(0, True)).wait_recv()

    def first(self):
        for i, way in ((0, 1), (1, -1)):
            self.go(i, self.half.at[self.rows(2, way)], self.far.at[i], self.device(way))

    def second(self):
        for i, way in ((0, 1), (1, -1)):
            self.come(i, self.far.at[i])
            at = self.rows(way, way)
            self.half[at, :] = self.half[at, :] + self.far[i]

    def pass_on(self):
        for i, way in ((0, 1), (1, -1)):
            self.go(2 + i, self.half.at[self.rows(way)], self.near.at[i], self.device(way))

    def own_sum(self):
        for i in (0, 1):
            self.come(2 + i, self.near.at[i])
        own = self.half[self.rows(0), :].astype(F32) + self.near[0].astype(F32) + self.near[1].astype(F32)
        return own.astype(BF16)

    def third(self):
        ref = self.total.at[self.core, self.rows(0)]
        for i, way in ((0, 1), (1, -1)):
            self.go(4 + i, ref, ref, self.device(way))
        self.go(8, ref, ref, self.device(0, True))

    def fourth(self):
        for i, way in ((0, 1), (1, -1)):
            ref = self.total.at[self.core, self.rows(-way)]
            self.come(4 + i, ref)
            part = self.total.at[self.core, self.rows(-way, way)]
            self.go(6 + i, part, part, self.device(way))
            self.go(9 + i, ref, ref, self.device(0, True))

    def fifth(self):
        for i, way in ((0, 1), (1, -1)):
            ref = self.total.at[self.core, self.rows(2, way)]
            self.come(6 + i, ref)
            self.go(11 + i, ref, ref, self.device(0, True))

    def finish(self):
        self.come(8, self.total.at[1 - self.core, self.rows(0)])
        for i, way in ((0, 1), (1, -1)):
            self.come(9 + i, self.total.at[1 - self.core, self.rows(-way)])
            self.come(11 + i, self.total.at[1 - self.core, self.rows(2, way)])
        self.sent()

    def sent(self):
        for copy in self.outgoing:
            copy.wait_send()


GROUPS = (
    ((0, 0), (0, 1), (0, 3), (1, 0), (3, 0)),
    ((1, 1), (1, 3), (3, 1), (3, 3), (2, 0), (0, 2)),
    ((2, 1), (2, 3), (1, 2), (3, 2), (2, 2)),
)
MOST = 6 * CAP
CHUNK = 32


def expert_kernel(
    normed_in, residual_in, gain_in, router_in, routes_in, cot_ref, gateup_ref, down_ref, out_w_ref,
    combined_out, chunk_out, grad_residual_ref, grad_att_ref, small_ref, grad_context_ref,
    normed_ref, residual_ref, gain_ref, router_ref, routes_ref,
    buf, cot, gateup, down, out_w, pick, gate_wide, note_wide, arrived, grad_acts, hidden, grad_slots,
    acts, grad_hidden, produced, grad_rows, parts, combined, landing, half, far, near, notes, told, own_gates, own_cot, gate_parts, gate_told,
    send_f, recv_f, send_a, recv_a, send_b, recv_b, send_c, recv_c, send_d, recv_d, send_e, recv_e, local, early,
):
    tokens, width = normed_ref.shape
    count = RING * RING
    local_experts, ff = down.shape[0], down.shape[1]
    rank = lax.axis_index("tensor")
    first = loads(
        [
            (normed_in, buf.at[rank]), (router_in, router_ref), (routes_in, routes_ref),
            (normed_in, normed_ref), (residual_in, residual_ref), (gain_in, gain_ref),
            (cot_ref.at[pl.ds(pl.multiple_of(rank * tokens, tokens), tokens)], own_cot),
        ],
        early,
    )
    late = loads([(gateup_ref, gateup), (down_ref, down), (cot_ref, cot), (out_w_ref.at[:, :HD], out_w)], local)
    dp = lax.axis_index("dp")
    core = lax.rem(dp, 2)
    sibling = (dp + 1 - 2 * core, rank)
    greet(others("tensor", count), near_members())
    first[0].wait()
    gather = Gather(buf, send_a, recv_a)
    gather.stage(0)
    for load in first[1:]:
        load.wait()
    router = router_ref[...]
    ids = lax.broadcasted_iota(jnp.int32, (EXPERTS, tokens), 0)
    slot_ids = lax.broadcasted_iota(jnp.int32, (CAP, tokens), 0).astype(F32)
    before = lax.broadcasted_iota(jnp.int32, (tokens, tokens), 0) < lax.broadcasted_iota(jnp.int32, (tokens, tokens), 1)
    upper = jnp.where(before, 1.0, 0.0).astype(BF16)
    pos = gather.pos

    def named_of(block):
        routes = routes_ref[block]
        hits = ids == routes[0:1]
        for k in range(1, TOP):
            hits = hits | (ids == routes[k : k + 1])
        return hits

    named = named_of(rank)
    logits = jnp.where(named, dot(router, normed_ref[...], ((1,), (1,))), -1e30)
    powers = jnp.where(named, jnp.exp(logits - jnp.max(logits, axis=0, keepdims=True)), 0.0)
    own_gates[...] = powers / jnp.sum(powers, axis=0, keepdims=True)
    gate_parts[...] = jnp.zeros_like(gate_parts)
    for i in range(count):
        gate_parts[i, :local_experts] = own_gates[i * local_experts : (i + 1) * local_experts]
    tell = Exchange(gate_parts, gate_told, send_f, recv_f)
    tell.start()
    gate_told[rank] = gate_parts[rank]

    groups, place = [], 0
    for group in GROUPS:
        members = []
        for dz, dy in group:
            members.append((place, joined(shifted(shifted(pos, 0, dz), 1, dy))))
            place += 1
        groups.append(members)
    every = [member for members in groups for member in members]
    pairs_of = [[members[i : i + 2] for i in range(0, len(members), 2)] for members in groups]
    wide = local_experts * CAP
    pair_number = {}
    for pairs in pairs_of:
        for pair in pairs:
            pair_number[pair[0][0]] = len(pair_number)
    for pairs in pairs_of:
        for pair in pairs:
            number = pair_number[pair[0][0]]
            if len(pair) == 2:
                pick[number, :wide, tokens:] = jnp.zeros((wide, tokens), BF16)
                pick[number, wide:, :tokens] = jnp.zeros((wide, tokens), BF16)
            for i, (_, block) in enumerate(pair):
                named = jnp.where(named_of(block), 1.0, 0.0)
                places = dot(named.astype(BF16), upper, ((1,), (0,)))
                for e in range(local_experts):
                    mine = ids == rank * local_experts + e
                    hit = jnp.sum(jnp.where(mine, named, 0.0), axis=0, keepdims=True)
                    at = jnp.sum(jnp.where(mine, places, 0.0), axis=0, keepdims=True)
                    at = jnp.where(hit > 0.5, at, -1.0)
                    first = i * wide + e * CAP
                    pick[number, first : first + CAP, i * tokens : (i + 1) * tokens] = jnp.where(slot_ids == at, 1.0, 0.0).astype(BF16)

    def chosen_of(pair):
        rows = len(pair) * wide
        return pick[pair_number[pair[0][0]], :rows, : len(pair) * tokens]

    gather.stage(1)
    gather.stage(2)
    late[2].wait()

    def spread(made, pair, target):
        for i, (at, _) in enumerate(pair):
            for e in range(local_experts):
                first = i * wide + e * CAP
                target[e, at * CAP : (at + 1) * CAP] = made[first : first + CAP]

    def joint(ref, pair, at):
        return jnp.concatenate([ref[e, i * CAP : (i + 1) * CAP] for i in at for e in range(local_experts)], axis=0)

    for pairs in pairs_of:
        for pair in pairs:
            rows = [cot[pl.ds(pl.multiple_of(block * tokens, tokens), tokens), :] for _, block in pair]
            spread(dot(chosen_of(pair), jnp.concatenate(rows, axis=0), ((1,), (0,))).astype(BF16), pair, grad_slots)
    for load in (late[0], late[1], late[3]):
        load.wait()
    tell.arrive()
    for pairs in pairs_of:
        for pair in pairs:
            for i, (at, block) in enumerate(pair):
                chosen = chosen_of(pair)[i * wide : (i + 1) * wide, i * tokens : (i + 1) * tokens].astype(F32)
                for e in range(local_experts):
                    column = jnp.sum(chosen[e * CAP : (e + 1) * CAP] * gate_told[block, e : e + 1], axis=1, keepdims=True)
                    gate_wide[e, at * CAP : (at + 1) * CAP] = jnp.broadcast_to(column, (CAP, 128))

    def work(number):
        pairs, base, rows = pairs_of[number], groups[number][0][0] * CAP, len(groups[number]) * CAP
        first = groups[number][0][0]
        for pair in pairs:
            blocks = jnp.concatenate([buf[block] for _, block in pair], axis=0)
            spread(dot(chosen_of(pair), blocks, ((1,), (0,))).astype(BF16), pair, arrived)

        @pl.loop(0, local_experts)
        def _(e):
            acts[:rows] = dot(arrived[e, base : base + rows], gateup[e], ((1,), (0,)))
            grad_hidden[:rows] = dot(grad_slots[e, base : base + rows], down[e], ((1,), (1,)))

            @pl.loop(0, rows // CHUNK)
            def _(c):
                at = pl.ds(pl.multiple_of(c * CHUNK, CHUNK), CHUNK)
                out = pl.ds(pl.multiple_of(base + c * CHUNK, CHUNK), CHUNK)
                column = gate_wide[e, out]
                note = jnp.zeros((CHUNK, 128), F32)
                for k in range(0, ff, 128):
                    gate, up = acts[at, k : k + 128], acts[at, ff + k : ff + k + 128]
                    sigmoid = 0.5 + 0.5 * jnp.tanh(0.5 * gate)
                    silu = gate * sigmoid
                    made = silu * up
                    raw = RES_SCALE * grad_hidden[at, k : k + 128]
                    note = note + made * raw
                    back = column * raw
                    hidden[e, out, k : k + 128] = (column * made).astype(BF16)
                    grad_acts[e, out, k : k + 128] = (back * up * (sigmoid + silu * (1.0 - sigmoid))).astype(BF16)
                    grad_acts[e, out, ff + k : ff + k + 128] = (back * silu).astype(BF16)
                note_wide[e, out] = note

            grad_rows[e, :rows] = dot(grad_acts[e, base : base + rows], gateup[e], ((1,), (1,))).astype(BF16)

        for pair in pairs:
            back = joint(grad_rows, pair, [at - first for at, _ in pair])
            made = dot(chosen_of(pair), back, ((0,), (0,))).astype(BF16)
            for i, (_, block) in enumerate(pair):
                parts[block] = made[i * tokens : (i + 1) * tokens]

    def outcome(number):
        pairs, base, rows = pairs_of[number], groups[number][0][0] * CAP, len(groups[number]) * CAP
        first = groups[number][0][0]

        @pl.loop(0, local_experts)
        def _(e):
            produced[e, :rows] = dot(hidden[e, base : base + rows], down[e], ((1,), (0,))).astype(BF16)

        for pair in pairs:
            chosen = chosen_of(pair)
            made = dot(chosen, joint(produced, pair, [at - first for at, _ in pair]), ((0,), (0,))).astype(BF16)
            for i, (at, block) in enumerate(pair):
                combined[block] = made[i * tokens : (i + 1) * tokens]
                for e in range(local_experts):
                    begin = i * wide + e * CAP
                    hits = chosen[begin : begin + CAP, i * tokens : (i + 1) * tokens].astype(F32)
                    column = jnp.sum(note_wide[e, at * CAP : (at + 1) * CAP], axis=1, keepdims=True)
                    notes[block, e : e + 1] = jnp.sum(hits * column, axis=0, keepdims=True)

    gather.arrive_stage(0)
    work(0)
    gather.stage(3)
    gather.stage(4)
    gather.arrive_stage(1)
    gather.arrive_stage(2)
    work(1)
    gather.stage(5)
    for stage in (3, 4, 5):
        gather.arrive_stage(stage)
    work(2)

    scatter = Scatter(parts, landing, send_b, recv_b)
    for stage in (5, 4, 2):
        scatter.stage(stage)
    quarter = (width // RING, ff // RING)
    chunk = sum(quarter)
    x = lax.div(dp, 2)
    gifts = []

    def rows_of(c):
        return pl.ds(pl.multiple_of(c * chunk, chunk), chunk)

    def gift(number, c):
        return pltpu.make_async_remote_copy(
            src_ref=cot.at[rows_of(c)], dst_ref=half.at[rows_of(c)],
            send_sem=send_d.at[number], recv_sem=recv_d.at[number], device_id=sibling, device_id_type=MESH_ID,
        )

    def made_of(e, c):
        first = pl.ds(pl.multiple_of(c * quarter[0], quarter[0]), quarter[0])
        second = pl.ds(pl.multiple_of(c * quarter[1], quarter[1]), quarter[1])
        upper_rows = dot(arrived[e, :, first], grad_acts[e], ((0,), (0,)))
        return upper_rows, RES_SCALE * dot(hidden[e, :, second], grad_slots[e], ((0,), (0,)))

    def give(number, c):
        at = c * chunk
        upper_rows, lower_rows = made_of(1 - core, c)
        cot[pl.ds(pl.multiple_of(at, quarter[1]), quarter[0]), :] = upper_rows.astype(BF16)
        cot[pl.ds(pl.multiple_of(at + quarter[0], quarter[1]), quarter[1]), :] = lower_rows.astype(BF16)
        gifts.append(gift(number, c))
        gifts[-1].start()

    def keep(number, c):
        upper_rows, lower_rows = made_of(core, c)
        gift(number, c).wait_recv()
        first = pl.ds(pl.multiple_of(c * chunk, quarter[1]), quarter[0])
        second = pl.ds(pl.multiple_of(c * chunk + quarter[0], quarter[1]), quarter[1])
        half[first, :] = (upper_rows + half[first, :].astype(F32)).astype(BF16)
        half[second, :] = (lower_rows + half[second, :].astype(F32)).astype(BF16)

    ring = RingSum(half, near, far, None, send_e, recv_e)
    order = [lax.rem(x + dx, RING) for dx in (2, 1, 3, 0)]
    for number, c in enumerate(order):
        give(number, c)
    keep(0, order[0])
    ring.first()
    scatter.stage(3)
    keep(1, order[1])
    keep(2, order[2])
    scatter.stage(1)
    keep(3, order[3])
    outcome(2)
    swap = Exchange(notes, told, send_c, recv_c)
    outcome(1)
    scatter.stage(0)
    outcome(0)
    swap.start()
    told[rank] = notes[rank]
    combined_copy = pltpu.make_async_copy(combined, combined_out, local.at[4])
    combined_copy.start()
    ring.second()
    ring.pass_on()
    swap.arrive()
    gates = own_gates[...]
    grads = jnp.concatenate([told[i, :local_experts] for i in range(count)], axis=0)
    grad_logits = (gates * (grads - jnp.sum(gates * grads, axis=0, keepdims=True))).astype(BF16)
    normed = normed_ref[...]
    small_ref[...] = jnp.zeros_like(small_ref)
    small_ref[:EXPERTS] = dot(grad_logits, normed, ((1,), (0,)))
    from_router = dot(grad_logits, router, ((0,), (0,)))
    gain = gain_ref[...].reshape(1, width).astype(F32)
    middle = tokens // 2
    grad_gain = jnp.zeros((1, width), F32)
    for place, back in enumerate(scatter.result()):
        at = slice(place * middle, (place + 1) * middle)
        residual = residual_ref[at]
        scale = rms_scale(residual)
        grad_normed = from_router[at] + back
        grad_norm, part = norm_back(residual, scale, gain, grad_normed)
        grad_gain = grad_gain + part[None]
        grad_residual = own_cot[at].astype(F32) + grad_norm
        grad_residual_ref[at] = grad_residual
        grad_att_ref[at] = (RES_SCALE * grad_residual).astype(BF16)
    small_ref[EXPERTS : EXPERTS + 1] = grad_gain
    grad_context_ref[...] = dot(out_w[...].reshape(HEADS * HD, width), grad_att_ref[...], ((1,), (1,))).astype(BF16).reshape(HEADS, HD, tokens)
    scatter.finish()
    gather.finish()
    swap.sent()
    tell.sent()
    chunk_out[...] = ring.own_sum()
    for copy in gifts:
        copy.wait_send()
    ring.sent()
    combined_copy.wait()


def experts(normed, residual, gain, router, routes_all, cot_all, w_gateup, w_down, weights):
    tokens, width = normed.shape
    count = RING * RING
    local_experts, ff = w_down.shape[:2]
    shape = jax.ShapeDtypeStruct
    vmem = pltpu.VMEM
    rows = count * CAP
    return call(
        expert_kernel, "experts", 2,
        (
            shape((count, tokens, width), BF16), shape(((width + ff) // RING, width), BF16),
            shape((tokens, width), F32), shape((tokens, width), BF16), shape((EXPERTS + 8, width), F32),
            shape((HEADS, HD, tokens), BF16),
        ),
        [anywhere()] * 9, [anywhere()] + [whole()] * 5,
        [
            vmem(normed.shape, BF16), vmem(residual.shape, F32), vmem(gain.shape, BF16), vmem(router.shape, BF16), vmem(routes_all.shape, jnp.int32),
            vmem((count, tokens, width), BF16), vmem((count * tokens, width), BF16), vmem(w_gateup.shape, BF16),
            vmem(w_down.shape, BF16), vmem((HEADS, HD, width), BF16), vmem((9, 2 * local_experts * CAP, 2 * tokens), BF16),
            vmem((local_experts, rows, 128), F32), vmem((local_experts, rows, 128), F32), vmem((local_experts, rows, width), BF16),
            vmem((local_experts, rows, 2 * ff), BF16),
            vmem((local_experts, rows, ff), BF16), vmem((local_experts, rows, width), BF16),
            vmem((MOST, 2 * ff), F32), vmem((MOST, ff), F32), vmem((local_experts, MOST, width), BF16),
            vmem((local_experts, MOST, width), BF16), vmem((count, tokens, width), BF16), vmem((count, tokens, width), BF16),
            vmem(((count - 1) * tokens, width), BF16), vmem((width + ff, width), BF16), vmem((2, (width + ff) // 8, width), BF16), vmem((2, (width + ff) // 4, width), BF16), vmem((count, 8, tokens), F32),
            vmem((count, 8, tokens), F32), vmem((EXPERTS, tokens), F32), vmem((tokens, width), BF16), vmem((count, 8, tokens), F32), vmem((count, 8, tokens), F32),
            *pair_sems(count - 1),
            *pair_sems(Torus.COUNT), *pair_sems(Torus.COUNT), *pair_sems(count - 1),
            *pair_sems(RING), *pair_sems(RingSum.COUNT), pltpu.SemaphoreType.DMA((5,)), pltpu.SemaphoreType.DMA((7,)),
        ],
        65400, flops=2 * 9 * rows * width * ff * local_experts, bytes_accessed=30 << 20,
    )(normed, residual, gain, router, routes_all, cot_all.reshape(count * tokens, width), w_gateup, w_down, weights)


SMALL = 384


def backward_kernel(
    qkv_in, grad_in, wide_in, log_in, cosine_in, sine_in, normed_in, context_in, grad_att_in, combined_in, residual_in, chunk_in,
    small_in, x_in, gain_in, grad_residual_in, weights_in, keyval_in,
    block_ref, input_ref, query_ref, out_ref, keyval_ref, small_out, gain_out, gateup_out, down_out,
    qkv_ref, grad_ref, wide_ref, log_ref, cosine_ref, sine_ref, normed, context_ref, grad_att_ref, combined, residual_ref,
    small_ref, x_ref, gain_ref, grad_residual_ref, query_all, keyval_all,
    grad_parts, parts_out, parts_back, grad, query_rows, key_rows, value_rows, grad_rows, grad_query, grad_key, grad_value,
    wide_grad, out_parts, out_land, combined_land, total,
    weight, give, pair_land, kv_own, mine, land, summed, small_parts, small_land, small_sum, small_dp, gather_buf,
    gain_sum, gain_dp, gain_land, back_pairs, out_mine, out_dp, out_all,
    send_a, recv_a, send_b, recv_b, send_c, recv_c, send_d, recv_d, send_e, recv_e, send_f, recv_f, send_g, recv_g,
    send_h, recv_h, send_i, recv_i, send_j, recv_j, send_k, recv_k, send_l, recv_l, send_n, recv_n,
    send_m, recv_m, send_q, recv_q, send_p, recv_p, sems, out_sems,
):
    count, _, tokens = grad_ref.shape
    length, width = count * tokens, normed.shape[1]
    dps = land.shape[0]
    rank, dp = lax.axis_index("tensor"), lax.axis_index("dp")
    order = (
        (grad_in, grad_ref), (chunk_in, total.at[lax.rem(dp, 2), pl.ds(pl.multiple_of(lax.div(dp, 2) * chunk_in.shape[0], chunk_in.shape[0]), chunk_in.shape[0])]), (small_in, small_ref), (qkv_in, qkv_ref), (context_in, context_ref),
        (grad_att_in, grad_att_ref), (combined_in, combined), (wide_in, wide_ref), (log_in, log_ref), (cosine_in, cosine_ref),
        (sine_in, sine_ref), (normed_in, normed), (residual_in, residual_ref), (x_in, x_ref), (gain_in, gain_ref),
        (grad_residual_in, grad_residual_ref), (weights_in.at[:, HD:], query_all), (keyval_in, keyval_all),
    )
    copies = loads(order, sems)
    odd = lax.rem(rank, 2)
    partner = rank + 1 - 2 * odd
    greet(others("tensor", count), others("dp", dps), [(p, partner) for p in others("dp", dps)])
    copies[0].wait()
    swap = Exchange(grad_ref, grad_parts, send_a, recv_a)
    swap.start()
    copies[1].wait()
    ring = RingSum(None, None, None, total, send_e, recv_e)
    ring.third()
    copies[2].wait()
    for i in range(count):
        small_parts[i, :, :256] = small_ref[8 * (i // 4) : 8 * (i // 4) + 8, 256 * (i % 4) : 256 * (i % 4) + 256]
        small_parts[i, :, 256:] = small_ref[32:40, 128 * (i // 2) : 128 * (i // 2) + 128]
    small = Exchange(small_parts, small_land, send_f, recv_f)
    small.start()
    small_land[rank] = small_parts[rank]
    copies[3].wait()
    query, key, value = slice(0, HD), slice(HD, 2 * HD), slice(2 * HD, 3 * HD)
    query_rows[...] = qkv_ref[query].T
    key_rows[...] = qkv_ref[key].T
    value_rows[...] = qkv_ref[value].T
    scatter = Scatter(out_parts, out_land, send_c, recv_c)
    copies[4].wait()
    copies[5].wait()
    grad_att = grad_att_ref[...]
    for part in range(count):
        out_parts[part] = dot(context_ref[part], grad_att, ((1,), (0,))).astype(BF16)
    for stage in (5, 4, 2):
        scatter.stage(stage)
    combine = Scatter(combined, combined_land, send_d, recv_d)
    grad_parts[rank] = grad_ref[rank]
    for copy in copies[7:11]:
        copy.wait()
    swap.arrive()
    for part in range(count):
        grad[:, part * tokens : (part + 1) * tokens] = grad_parts[part]
    grad_rows[...] = grad[...].T
    second_small = Exchange(small_sum.at[0], small_dp, send_g, recv_g, "dp", same=True)
    allowed = causal(Q_ROWS)
    blocks = length // Q_ROWS

    def combine_leaves():
        copies[6].wait()
        for stage in (5, 4, 2):
            combine.stage(stage)

    def small_dps():
        small.arrive()
        small_sum[0] = jnp.sum(small_land[...], axis=0)
        second_small.start()
        small_dp[dp] = small_sum[0]

    def small_again():
        second_small.arrive()
        small_sum[1] = jnp.sum(small_dp[...], axis=0)
        third.start()
        small_out[rank] = small_sum[1]

    third = Exchange(small_sum.at[1], small_out, send_h, recv_h, same=True)
    plan = {0: [combine_leaves], 2: [lambda: scatter.stage(3)], 3: [small_dps], 6: [lambda: scatter.stage(1)], 7: [ring.fourth]}
    for block in reversed(range(blocks)):
        first = block * Q_ROWS
        columns = slice(first, first + Q_ROWS)
        scaled = qkv_ref[query, columns] * ATTN_SCALE
        logs = log_ref[:, columns]
        grad_block = grad[:, columns]
        inner = jnp.sum(grad_block.astype(F32) * wide_ref[:, columns], axis=0, keepdims=True)
        wide_total = jnp.zeros((HD, Q_ROWS), F32)
        spans = [(columns, True)]
        if block:
            spans.append((slice(0, first), False))
        for keys, close in spans:
            weights = jnp.exp(dot(key_rows[keys, :], scaled, ((1,), (0,))) - logs)
            if close:
                weights = jnp.where(allowed, weights, 0.0)
            grad_weights = dot(value_rows[keys, :], grad_block, ((1,), (0,)))
            grad_scores = (weights * (grad_weights - inner)).astype(BF16)
            wide_total = wide_total + dot(qkv_ref[key, keys], grad_scores, ((1,), (0,)))
            key_part = dot(grad_scores, query_rows[columns, :], ((1,), (0,)))
            value_part = dot(weights.astype(BF16), grad_rows[columns, :], ((1,), (0,)))
            if block == blocks - 1:
                grad_key[keys, :] = key_part
                grad_value[keys, :] = value_part
            else:
                grad_key[keys, :] += key_part
                grad_value[keys, :] += value_part
        grad_query[:, columns] = wide_total * ATTN_SCALE
        for task in plan.get(blocks - 1 - block, ()):
            task()
    middle = HD // 2
    cosine, sine = cosine_ref[...], -sine_ref[...]
    for place, wide in enumerate((grad_query[...], grad_key[...].T * ATTN_SCALE)):
        rows = rotate(wide[:middle], wide[middle:], cosine, sine)
        wide_grad[place * HD : (place + 1) * HD] = jnp.concatenate(rows, axis=0).astype(BF16)
    wide_grad[2 * HD :] = grad_value[...].T.astype(BF16)
    for part in range(count):
        parts_out[part] = wide_grad[:, part * tokens : (part + 1) * tokens]
    back = Exchange(parts_out, parts_back, send_b, recv_b)
    back.start()
    parts_back[rank] = parts_out[rank]
    for copy in copies[11:]:
        copy.wait()
    weight[...] = dot(wide_grad[...], normed[...], ((1,), (0,)))
    column = width // dps
    kept = weight[pl.ds(pl.multiple_of(HD + HD * odd, HD), HD), :]
    for j, rows in enumerate((weight[:HD], kept)):
        low = rows.astype(BF16)
        for i in range(dps):
            mine[i, j * HD : (j + 1) * HD] = low[:, i * column : (i + 1) * column]
    dp_first = Exchange(mine, land, send_i, recv_i, "dp")
    dp_first.start()
    low = weight[pl.ds(pl.multiple_of(HD + HD * (1 - odd), HD), HD), :].astype(BF16)
    for i in range(dps):
        give[i] = low[:, i * column : (i + 1) * column]

    def across(r):
        to = lax.rem(dp + r, dps)
        return pltpu.make_async_remote_copy(
            src_ref=give.at[to], dst_ref=pair_land.at[dp], send_sem=send_p.at[r], recv_sem=recv_p.at[r],
            device_id=(to, partner), device_id_type=MESH_ID,
        )

    def across_here(r):
        at = pair_land.at[lax.rem(dp + dps - r, dps)]
        return pltpu.make_async_remote_copy(
            src_ref=at, dst_ref=at, send_sem=send_p.at[r], recv_sem=recv_p.at[r],
            device_id=(dp, partner), device_id_type=MESH_ID,
        )

    for r in range(dps):
        across(r).start()
    land[dp] = mine[dp]
    scatter.stage(0)
    small_again()
    combine.stage(3)
    out_sum = jnp.concatenate(scatter.result(), axis=0).astype(BF16)
    for i in range(dps):
        out_mine[i] = out_sum[:, i * column : (i + 1) * column]
    out_first = Exchange(out_mine, out_dp, send_m, recv_m, "dp")

    back.arrive()
    share = HEADS // KV_HEADS
    for head in range(KV_HEADS):
        for part in range(2):
            at = slice((part + 1) * HD, (part + 2) * HD)
            both = sum(parts_back[head * share + i, at].astype(F32) for i in range(share))
            back_pairs[part * KV_HEADS + head] = both.astype(BF16)
    queries_back = parts_back[:, :HD].reshape(HEADS * HD, tokens)
    grad_normed = dot(queries_back, query_all[...].reshape(HEADS * HD, width), ((0,), (0,)))
    grad_normed = grad_normed + dot(back_pairs[...].reshape(2 * KV_HEADS * HD, tokens), keyval_all[...], ((0,), (1,)))
    inputs = x_ref[...].astype(F32)
    grad_norm, grad_gain = norm_back(inputs, rms_scale(inputs), gain_ref[...].reshape(1, width).astype(F32), grad_normed)
    input_ref[...] = grad_residual_ref[...] + grad_norm
    grad_gain = grad_gain[None]
    for i in range(gain_sum.shape[1]):
        gain_sum[0, i : i + 1] = grad_gain[:, 128 * i : 128 * i + 128]

    dp_first.arrive()
    for r in range(dps):
        across_here(r).wait_recv()
    both = jnp.sum(land[...].astype(F32), axis=0)
    kv_own[...] = (both[HD:] + jnp.sum(pair_land[...].astype(F32), axis=0)).astype(BF16)
    replicas = Replicas(kv_own, gather_buf, send_n, recv_n, out_sems.at[0])
    replicas.first()
    summed[dp] = both[:HD].astype(BF16)
    dp_second = Exchange(summed.at[dp], summed, send_j, recv_j, "dp", same=True)
    dp_second.start()
    gain_first = Exchange(gain_sum.at[0], gain_dp, send_k, recv_k, "dp", same=True)
    gain_first.start()
    gain_dp[dp] = gain_sum[0]
    out_first.start()
    out_dp[dp] = out_mine[dp]
    ring.fifth()
    combine.stage(1)
    replicas.second()
    gain_first.arrive()
    gain_sum[1] = jnp.sum(gain_dp[...], axis=0)
    gain_second = Exchange(gain_sum.at[1], gain_land, send_l, recv_l, same=True)
    gain_second.start()
    gain_land[rank] = gain_sum[1]
    ring.finish()
    outs = []
    per = chunk_in.shape[0]
    for c in range(RING):
        down_rows = per - width // RING
        outs.append(pltpu.make_async_copy(total.at[:, pl.ds(c * per, width // RING)], gateup_out.at[:, pl.ds(c * (width // RING), width // RING)], out_sems.at[1 + c]))
        outs.append(pltpu.make_async_copy(total.at[:, pl.ds(c * per + width // RING, down_rows)], down_out.at[:, pl.ds(c * down_rows, down_rows)], out_sems.at[1 + RING + c]))
    for copy in outs:
        copy.start()
    out_first.arrive()
    out_all[dp] = jnp.sum(out_dp[...].astype(F32), axis=0).astype(BF16)
    out_second = Exchange(out_all.at[dp], out_all, send_q, recv_q, "dp", same=True)
    out_second.start()
    dp_second.arrive()
    for i in range(dps):
        query_ref[:, i * column : (i + 1) * column] = summed[i]
    combine.stage(0)
    replicas.third()
    replicas.fourth()
    rows = block_ref.shape[0] // 2
    for place, value_half in enumerate(combine.result()):
        at = slice(place * rows, (place + 1) * rows)
        block_ref[at] = (residual_ref[at] + RES_SCALE * value_half).astype(BF16)
    out_second.arrive()
    for i in range(dps):
        out_ref[:, i * column : (i + 1) * column] = out_all[i]
    third.arrive()
    gain_second.arrive()
    gain_out[...] = jnp.sum(gain_land[...], axis=0)
    replicas.finish()
    for i in range(count):
        base = (i % 2) * KV_HEADS * HD + (i // 2) * HD
        keyval_ref[base : base + HD, :] = gather_buf[i]
    for r in range(dps):
        across(r).wait_send()
    for each in (swap, back, small, second_small, third, dp_first, dp_second, gain_first, gain_second, out_first, out_second):
        each.sent()
    scatter.finish()
    combine.finish()
    for copy in outs:
        copy.wait()


def backward(
    qkv, grad_context, wide, logs, cosine, sine, normed, context, grad_att, combined, residual, chunk, small,
    x, gain, grad_residual, weights, w_keyval, dps,
):
    count, _, tokens = grad_context.shape
    length, width = normed.shape
    shape = jax.ShapeDtypeStruct
    vmem = pltpu.VMEM
    low = vmem((length, HD), BF16)
    wide_rows = vmem((length, HD), F32)
    column = width // dps
    rows = RING * chunk.shape[0]
    small_shape, gain_shape = (8, SMALL), (8, 128)
    operands = (
        qkv, grad_context, wide, logs, cosine, sine, normed, context, grad_att, combined, residual, chunk, small,
        x, gain, grad_residual, weights, w_keyval,
    )
    held = [vmem(o.shape, o.dtype) for o in operands]
    held[16] = vmem((count, HD, width), BF16)
    del held[11]
    three = vmem((dps, 2 * HD, column), BF16)
    return call(
        backward_kernel, "backward", 4,
        (
            shape((tokens, width), BF16), shape((tokens, width), F32), shape((HD, width), BF16), shape((HD, width), BF16),
            shape((count * HD, width), BF16), shape((count, *small_shape), F32), shape(gain_shape, F32),
            shape((2, width, width), BF16), shape((2, rows - width, width), BF16),
        ),
        [anywhere()] * len(operands), [whole()] * 7 + [anywhere()] * 2,
        [
            *held,
            vmem((count, HD, tokens), BF16), vmem(qkv_parts(count, tokens), BF16), vmem(qkv_parts(count, tokens), BF16),
            vmem((HD, length), BF16), low, low, low, low, vmem((HD, length), F32), wide_rows, wide_rows,
            vmem((3 * HD, length), BF16), vmem((count, HD, width), BF16), vmem(((count - 1) * HD, width), BF16),
            vmem(((count - 1) * tokens, width), BF16),
            vmem((2, rows, width), BF16),
            vmem((3 * HD, width), F32), vmem((dps, HD, column), BF16), vmem((dps, HD, column), BF16), vmem((HD, column), BF16),
            three, three, vmem((dps, HD, column), BF16),
            vmem((count, *small_shape), F32), vmem((count, *small_shape), F32), vmem((2, *small_shape), F32),
            vmem((dps, *small_shape), F32), vmem((count, HD, width), BF16),
            vmem((2, *gain_shape), F32), vmem((dps, *gain_shape), F32), vmem((count, *gain_shape), F32), vmem((2 * KV_HEADS, HD, tokens), BF16), *([vmem((dps, HD, column), BF16)] * 3),
            *pair_sems(count - 1), *pair_sems(count - 1), *pair_sems(Torus.COUNT), *pair_sems(Torus.COUNT),
            *pair_sems(RingSum.COUNT), *pair_sems(count - 1), *pair_sems(dps - 1), *pair_sems(count - 1),
            *pair_sems(dps - 1), *pair_sems(dps - 1), *pair_sems(dps - 1), *pair_sems(count - 1),
            *pair_sems(Replicas.COUNT), *pair_sems(dps - 1), *pair_sems(dps - 1), *pair_sems(dps),
            pltpu.SemaphoreType.DMA((len(operands),)), pltpu.SemaphoreType.DMA((1 + 2 * RING,)),
        ],
        65400, flops=2 * length * length * HD * 5, bytes_accessed=30 << 20,
    )(*operands)


def qkv_parts(count, tokens):
    return (count, 3 * HD, tokens)


def polish_kernel(
    gateup_ref, down_ref, keyval_ref, query_ref, out_ref, block_ref, input_ref, small_ref, gain_ref,
    gateup_out, down_out, keyval_out, query_out, out_out, block_out, input_out, router_out, gain_two_out, gain_one_out,
):
    gateup_out[...] = gateup_ref[...].astype(F32)
    down_out[...] = down_ref[...].astype(F32)
    keyval_out[...] = keyval_ref[...].T.astype(F32)

    @pl.when(pl.program_id(0) == 0)
    def _():
        query_out[...] = query_ref[...].astype(F32)
        out_out[...] = out_ref[...].astype(F32)
        block_out[...] = block_ref[...]
        input_out[...] = input_ref[...]
        for i in range(small_ref.shape[0]):
            router_out[8 * (i // 4) : 8 * (i // 4) + 8, 256 * (i % 4) : 256 * (i % 4) + 256] = small_ref[i, :, :256]
        for i in range(gain_two_out.shape[0]):
            gain_two_out[i : i + 1] = small_ref[2 * i, :1, 256:]
        gain_one_out[...] = gain_ref[...]


def polish(gateup, down, keyval, query, out, block, grad_input, small, gain):
    steps = 8
    experts_here, width, wide = gateup.shape
    ff = down.shape[1]
    per = steps // experts_here
    pairs = keyval.shape[0]
    shape = jax.ShapeDtypeStruct
    gateup_spec = pl.BlockSpec((1, width // per, wide), lambda i: (i // per, i % per, 0))
    down_spec = pl.BlockSpec((1, ff // per, width), lambda i: (i // per, i % per, 0))

    def once(dims):
        return pl.BlockSpec(dims, lambda i: (0,) * len(dims))

    rest = [query.shape, out.shape, block.shape, grad_input.shape]
    return pl.pallas_call(
        polish_kernel, grid=(steps,),
        out_shape=(
            shape(gateup.shape, F32), shape(down.shape, F32), shape((width, pairs), F32), shape(query.shape, F32),
            shape(out.shape, F32), shape(block.shape, BF16), shape(grad_input.shape, F32), shape((EXPERTS, width), F32),
            shape(gain.shape, F32), shape(gain.shape, F32),
        ),
        in_specs=[
            gateup_spec, down_spec, pl.BlockSpec((pairs, width // steps), lambda i: (0, i)),
            *[once(dims) for dims in rest], once(small.shape), once(gain.shape),
        ],
        out_specs=[
            gateup_spec, down_spec, pl.BlockSpec((width // steps, pairs), lambda i: (i, 0)),
            *[once(dims) for dims in rest], once((EXPERTS, width)), once(gain.shape), once(gain.shape),
        ],
        compiler_params=pltpu.CompilerParams(vmem_limit_bytes=65400 << 10),
        name="polish",
    )(gateup, down, keyval, query, out, block, grad_input, small, gain)


def shards(
    block_input, attn_gain, w_query, w_keyval, w_out, ffn_gain, w_router, w_gateup, w_down, routes, cotangent,
):
    tokens, width = block_input.shape
    length = tokens * lax.axis_size("tensor")
    cosine, sine = rope_tables(length, HD)
    normed_one_all, qkv, wide_out, logs, context, weights, cotangent_all, routes_all, residual, normed_two = forward(
        block_input, attn_gain, ffn_gain, w_query.T, w_keyval, w_out, cotangent, cosine, sine, routes.T
    )
    combined, chunk, grad_residual, grad_attention, small, grad_context = experts(
        normed_two, residual, ffn_gain, w_router.T, routes_all, cotangent_all, w_gateup, w_down, weights
    )
    block_out, grad_input, grad_query_w, grad_w_out, grad_keyval, small, gain_one, grad_w_gateup, grad_w_down = backward(
        qkv, grad_context, wide_out, logs, cosine, sine, normed_one_all.reshape(length, width), context, grad_attention,
        combined, residual, chunk, small, block_input, attn_gain, grad_residual, weights, w_keyval, lax.axis_size("dp"),
    )
    grad_w_gateup, grad_w_down, grad_keyval, grad_query_w, grad_w_out, block_out, grad_input, routers, gain_two, gain_one = polish(
        grad_w_gateup, grad_w_down, grad_keyval, grad_query_w, grad_w_out, block_out, grad_input, small, gain_one
    )
    return (
        block_out,
        grad_input,
        gain_one.reshape(width),
        grad_query_w.T,
        grad_keyval,
        grad_w_out,
        gain_two.reshape(width),
        routers.T,
        grad_w_gateup,
        grad_w_down,
    )


def solution(mesh):
    rows = P(("dp", "tensor"), None)
    in_specs = (
        rows, P(), P(None, "tensor"), P(), P("tensor", None), P(), P(),
        P("tensor", None, None), P("tensor", None, None), rows, rows,
    )
    out_specs = (
        rows, rows, P(), P(None, "tensor"), P(), P("tensor", None), P(), P(),
        P("tensor", None, None), P("tensor", None, None),
    )
    return jax.shard_map(shards, mesh=mesh, in_specs=in_specs, out_specs=out_specs, check_vma=False)
```

```python
import jax
import jax.numpy as jnp
import numpy as np
from jax import lax
from jax.experimental import pallas as pl
from jax.experimental.pallas import tpu as pltpu
from jax.sharding import PartitionSpec as P

HEADS = 16
KV_HEADS = 8
HD = 64
EXPERTS = 32
TOP = 8
CAP = 64
ATTN_SCALE = 0.015625
RES_SCALE = 0.22
EPSILON = 1e-06
ROPE_BASE = 10000.0
F32 = jnp.float32
BF16 = jnp.bfloat16
Q_ROWS = 256


def rms_scale(values):
    return lax.rsqrt(jnp.mean(values * values, axis=-1, keepdims=True) + EPSILON)


def norm_back(values, scale, gain, grad_normed):
    grad_scaled = grad_normed * gain
    grad_gain = jnp.sum(grad_normed * values * scale, axis=0)
    inner = jnp.mean(grad_scaled * values, axis=-1, keepdims=True)
    return (scale * (grad_scaled - values * scale * scale * inner), grad_gain)


def rope_tables(length, width):
    half_width = width // 2
    inverse = ROPE_BASE ** (-(np.arange(half_width) * 2.0) / width)
    angles = np.arange(length)[None, :] * inverse[:, None]
    return (jnp.asarray(np.cos(angles), F32), jnp.asarray(np.sin(angles), F32))


def rotate(first, second, cosine, sine):
    return first * cosine - second * sine, second * cosine + first * sine


def dot(a, b, dims):
    return lax.dot_general(a, b, ((dims[0], dims[1]), ((), ())), preferred_element_type=F32)


def causal(rows):
    key = lax.broadcasted_iota(jnp.int32, (rows, rows), 0)
    query = lax.broadcasted_iota(jnp.int32, (rows, rows), 1)
    return key <= query


RING = 4
MESH_ID = pl.DeviceIdType.MESH


def whole():
    return pl.BlockSpec(memory_space=pltpu.VMEM)


def anywhere():
    return pl.BlockSpec(memory_space=pltpu.HBM)


def position():
    rank = lax.axis_index("tensor")
    return lax.div(rank, RING), lax.rem(rank, RING)


def shifted(pos, axis, by):
    moved = lax.rem(pos[axis] + (by + RING), RING) if by else pos[axis]
    return (moved, pos[1]) if axis == 0 else (pos[0], moved)


def joined(pos):
    return pos[0] * RING + pos[1]


def greet(tensor_peers, dp_peers=(), more=()):
    dp, rank = lax.axis_index("dp"), lax.axis_index("tensor")
    sem = pltpu.get_barrier_semaphore()
    peers = [(dp, p) for p in tensor_peers] + [(p, rank) for p in dp_peers] + list(more)
    for peer in peers:
        pl.semaphore_signal(sem, inc=1, device_id=peer, device_id_type=MESH_ID)
    pl.semaphore_wait(sem, len(peers))


def neighbours():
    pos = position()
    return [joined(shifted(pos, axis, by)) for axis in (0, 1) for by in (1, -1)]


def others(axis, count):
    return [lax.rem(lax.axis_index(axis) + r, count) for r in range(1, count)]


def torus_messages(half, rows):
    primary, secondary = (0, 1) if half == 0 else (1, 0)
    h, q = rows // 2, rows // 4
    full = (half * h, h)
    part = {1: (half * h, q), -1: (half * h + q, q)}
    out = []
    for d in (1, -1):
        out.append((0, ("p1", d), None, full, (0, 0), primary, d))
        out.append((0, ("s1", 0, d), None, full, (0, 0), secondary, d))
        out.append((1, ("p2", d), ("p1", d), part[d], (-d, 0), primary, d))
        for e in (1, -1):
            out.append((1, ("s1", -d, e), ("p1", d), full, (-d, 0), secondary, e))
    for e in (1, -1):
        out.append((2, ("s2", 0, e), ("s1", 0, e), part[e], (0, -e), secondary, e))
        for d in (1, -1):
            out.append((3, ("s1", ("o", d), e), ("p2", d), part[d], (2, 0), secondary, e))
            out.append((4, ("s2", d, e), ("s1", d, e), part[e], (d, -e), secondary, e))
        out.append((5, ("s2", "o", e), ("s1", ("o", e), e), part[e], (2, -e), secondary, e))
    return out


class Torus:
    COUNT = 44
    STAGES = 6

    def __init__(self, rows):
        self.rows = rows
        self.pos = position()
        self.dp = lax.axis_index("dp")
        self.messages, self.children, self.place, order, used = {}, {}, {}, [], 0
        for half in (0, 1):
            for at, (stage, key, needs, piece, offset, axis, way) in enumerate(torus_messages(half, rows)):
                key = (half, key)
                needs = None if needs is None else (half, needs)
                self.messages[key] = (len(order), stage, needs, piece, offset, axis, way)
                self.children.setdefault(needs, []).append(key)
                self.place[key] = used
                used += piece[1]
                order.append((stage, at, half, key))
        self.landing_rows = used
        self.order = [entry[3] for entry in sorted(order, key=lambda entry: entry[:3])]

    def block(self, key, pos):
        half, offset = key[0], self.messages[key][4]
        primary, secondary = (0, 1) if half == 0 else (1, 0)
        return joined(shifted(shifted(pos, primary, offset[0]), secondary, offset[1]))

    def sender(self, key):
        _, _, _, _, _, axis, way = self.messages[key]
        return shifted(self.pos, axis, -way)

    def receiver(self, key):
        _, _, _, _, _, axis, way = self.messages[key]
        return shifted(self.pos, axis, way)


class Gather(Torus):
    def __init__(self, buf, send, recv):
        self.flat = len(buf.shape) == 2
        super().__init__(buf.shape[0] // (RING * RING) if self.flat else buf.shape[1])
        self.buf, self.send, self.recv = buf, send, recv
        self.arrived = set()

    def piece(self, block, first, count):
        if self.flat:
            return self.buf.at[pl.ds(pl.multiple_of(block * self.rows + first, self.rows // 4), count)]
        return self.buf.at[block, pl.ds(first, count)]

    def copy(self, key, incoming):
        number, (first, count) = self.messages[key][0], self.messages[key][3]
        at = self.sender(key) if incoming else self.pos
        ref = self.piece(self.block(key, at), first, count)
        return pltpu.make_async_remote_copy(
            src_ref=ref, dst_ref=ref, send_sem=self.send.at[number], recv_sem=self.recv.at[number],
            device_id=(self.dp, joined(at if incoming else self.receiver(key))), device_id_type=MESH_ID,
        )

    def arrive(self, key):
        if key not in self.arrived:
            self.arrived.add(key)
            self.copy(key, True).wait_recv()

    def stage(self, number):
        for key in self.order:
            _, stage, needs, *_ = self.messages[key]
            if stage == number:
                if needs is not None:
                    self.arrive(needs)
                self.copy(key, False).start()

    def arrive_stage(self, number):
        for key in self.order:
            if self.messages[key][1] == number:
                self.arrive(key)

    def finish(self):
        for key in self.order:
            self.arrive(key)
        for key in self.order:
            self.copy(key, False).wait_send()


class Scatter(Torus):
    def __init__(self, parts, landing, send, recv):
        super().__init__(parts.shape[1])
        self.parts, self.landing, self.send, self.recv = parts, landing, send, recv

    def copy(self, key):
        number, (first, count) = self.messages[key][0], self.messages[key][3]
        at = self.sender(key)
        return pltpu.make_async_remote_copy(
            src_ref=self.parts.at[self.block(key, at), pl.ds(first, count)],
            dst_ref=self.landing.at[pl.ds(self.place[key], count)],
            send_sem=self.send.at[number], recv_sem=self.recv.at[number],
            device_id=(self.dp, joined(at)), device_id_type=MESH_ID,
        )

    def landed(self, key):
        count = self.messages[key][3][1]
        self.copy(key).wait_recv()
        return self.landing[pl.ds(self.place[key], count), :]

    def stage(self, number):
        for key in reversed(self.order):
            if self.messages[key][1] == number:
                pieces = {}
                for child in self.children.get(key, []):
                    pieces.setdefault(self.messages[child][3], []).append(child)
                for (first, count), children in pieces.items():
                    at = (self.block(children[0], self.pos), pl.ds(first, count))
                    self.parts[at] = sum((self.landed(c) for c in children), self.parts[at])
                self.copy(key).start()

    def result(self):
        out = []
        for half in (0, 1):
            children = [c for c in self.children[None] if c[0] == half]
            first, count = self.messages[children[0]][3]
            own = self.parts[joined(self.pos), pl.ds(first, count)].astype(F32)
            out.append(sum((self.landed(c).astype(F32) for c in children), own))
        return out

    def finish(self):
        for key in self.order:
            self.copy(key).wait_send()


class Exchange:
    def __init__(self, source, target, send, recv, axis="tensor", same=False):
        self.source, self.target, self.send, self.recv, self.axis, self.same = source, target, send, recv, axis, same
        self.count = target.shape[0]
        self.rank = lax.axis_index(axis)

    def device(self, to):
        if self.axis == "tensor":
            return (lax.axis_index("dp"), to)
        return (to, lax.axis_index("tensor"))

    def copy(self, r):
        to = lax.rem(self.rank + r, self.count)
        return pltpu.make_async_remote_copy(
            src_ref=self.source if self.same else self.source.at[to],
            dst_ref=self.target.at[self.rank], send_sem=self.send.at[r - 1],
            recv_sem=self.recv.at[r - 1], device_id=self.device(to), device_id_type=MESH_ID,
        )

    def start(self):
        for r in range(1, self.count):
            self.copy(r).start()

    def arrive(self):
        for r in range(1, self.count):
            origin = lax.rem(self.rank + self.count - r, self.count)
            pltpu.make_async_remote_copy(
                src_ref=self.target.at[origin], dst_ref=self.target.at[origin], send_sem=self.send.at[r - 1],
                recv_sem=self.recv.at[r - 1], device_id=self.device(origin), device_id_type=MESH_ID,
            ).wait_recv()

    def sent(self):
        for r in range(1, self.count):
            self.copy(r).wait_send()


def pair_sems(count):
    return [pltpu.SemaphoreType.DMA((count,))] * 2


def call(kernel, name, number, out_shape, in_specs, out_specs, scratch, limit, flops=0, bytes_accessed=0):
    return pl.pallas_call(
        kernel, out_shape=out_shape, in_specs=in_specs, out_specs=out_specs, scratch_shapes=scratch,
        compiler_params=pltpu.CompilerParams(collective_id=number, has_side_effects=True, vmem_limit_bytes=limit << 10),
        cost_estimate=pl.CostEstimate(flops=flops, bytes_accessed=bytes_accessed, transcendentals=0),
        name=name,
    )


def loads(pairs, sems):
    copies = [pltpu.make_async_copy(a, b, sems.at[i]) for i, (a, b) in enumerate(pairs)]
    for copy in copies:
        copy.start()
    return copies


class Replicas:
    COUNT = RING * RING - 1 + 9

    def __init__(self, own, buf, send, recv, local):
        self.own, self.buf, self.send, self.recv = own, buf, send, recv
        self.keep = pltpu.make_async_copy(own, buf.at[lax.axis_index("tensor"), :, self.columns_of(buf)], local)
        self.rank, self.dp = lax.axis_index("tensor"), lax.axis_index("dp")
        self.x, self.core = lax.div(self.dp, 2), lax.rem(self.dp, 2)
        self.blocks = buf.shape[0]
        self.share = buf.shape[2] // (2 * RING)

    @staticmethod
    def columns_of(buf):
        share = buf.shape[2] // (2 * RING)
        return pl.ds(pl.multiple_of(lax.axis_index("dp") * share, share), share)

    def member(self, dx, other):
        core = 1 - self.core if other else self.core
        return lax.rem(self.x + dx + RING, RING) * 2 + core

    def columns(self, member):
        return pl.ds(pl.multiple_of(member * self.share, self.share), self.share)

    def piece(self, member, part):
        first, count = {0: (0, self.blocks), 1: (0, self.blocks // 2), -1: (self.blocks // 2, self.blocks // 2)}[part]
        return self.buf.at[pl.ds(first, count), :, self.columns(member)]

    def copy(self, number, ref, device):
        return pltpu.make_async_remote_copy(
            src_ref=ref, dst_ref=ref, send_sem=self.send.at[number], recv_sem=self.recv.at[number],
            device_id=device, device_id_type=MESH_ID,
        )

    def first(self):
        count = self.blocks
        self.outgoing = []
        self.keep.start()
        for r in range(1, count):
            self.outgoing.append(pltpu.make_async_remote_copy(
                src_ref=self.own, dst_ref=self.buf.at[self.rank, :, self.columns(self.dp)],
                send_sem=self.send.at[r - 1], recv_sem=self.recv.at[r - 1],
                device_id=(self.dp, lax.rem(self.rank + r, count)), device_id_type=MESH_ID,
            ))
            self.outgoing[-1].start()

    def go(self, number, member, part, dx, other):
        self.outgoing.append(self.copy(self.blocks - 1 + number, self.piece(member, part), (self.member(dx, other), self.rank)))
        self.outgoing[-1].start()

    def come(self, number, member, part):
        self.copy(self.blocks - 1 + number, self.piece(member, part), (self.dp, self.rank)).wait_recv()

    def second(self):
        for r in range(1, self.blocks):
            ref = self.buf.at[lax.rem(self.rank + self.blocks - r, self.blocks), :, self.columns(self.dp)]
            self.copy(r - 1, ref, (self.dp, self.rank)).wait_recv()
        self.keep.wait()
        self.go(0, self.dp, 0, 1, False)
        self.go(1, self.dp, 0, -1, False)
        self.go(4, self.dp, 0, 0, True)

    def third(self):
        for number, way in ((0, 1), (1, -1)):
            member = self.member(-way, False)
            self.come(number, member, 0)
            self.go(2 + number, member, way, way, False)
            self.go(5 + number, member, 0, 0, True)

    def fourth(self):
        for number, way in ((0, 1), (1, -1)):
            member = self.member(2, False)
            self.come(2 + number, member, way)
            self.go(7 + number, member, way, 0, True)

    def finish(self):
        self.come(4, self.member(0, True), 0)
        for number, way in ((0, 1), (1, -1)):
            self.come(5 + number, self.member(-way, True), 0)
            self.come(7 + number, self.member(2, True), way)
        for copy in self.outgoing:
            copy.wait_send()


def near_members():
    x, core = lax.div(lax.axis_index("dp"), 2), lax.rem(lax.axis_index("dp"), 2)
    return [lax.rem(x + 1, RING) * 2 + core, lax.rem(x + RING - 1, RING) * 2 + core, x * 2 + 1 - core]


def attend(qkv, key_rows, wide_ref, log_ref, parts_ref, tokens, todo):
    length = qkv.shape[1]
    allowed = causal(Q_ROWS)
    query, value = slice(0, HD), slice(2 * HD, 3 * HD)
    for block in range(length // Q_ROWS):
        first = block * Q_ROWS
        columns = slice(first, first + Q_ROWS)
        scaled = qkv[query, columns] * ATTN_SCALE
        near = dot(key_rows[columns, :], scaled, ((1,), (0,)))
        near = jnp.where(allowed, near, -1e30)
        largest = jnp.max(near, axis=0, keepdims=True)
        if block:
            far = dot(key_rows[:first, :], scaled, ((1,), (0,)))
            largest = jnp.maximum(largest, jnp.max(far, axis=0, keepdims=True))
        near = jnp.exp(near - largest)
        total = jnp.sum(near, axis=0, keepdims=True)
        context = dot(qkv[value, columns], near.astype(BF16), ((1,), (0,)))
        if block:
            far = jnp.exp(far - largest)
            total = total + jnp.sum(far, axis=0, keepdims=True)
            context = context + dot(qkv[value, :first], far.astype(BF16), ((1,), (0,)))
        context = context / total
        wide_ref[:, columns] = context
        log_ref[:, columns] = largest + jnp.log(total)
        low = context.astype(BF16)
        for part in range(Q_ROWS // tokens):
            parts_ref[first // tokens + part] = low[:, part * tokens : (part + 1) * tokens]
        for task in todo.get(block, ()):
            task()


class RingSum:
    COUNT = 15

    def __init__(self, half, near, far, total, send, recv):
        self.half, self.near, self.far, self.total, self.send, self.recv = half, near, far, total, send, recv
        self.rank, dp = lax.axis_index("tensor"), lax.axis_index("dp")
        self.x, self.core = lax.div(dp, 2), lax.rem(dp, 2)
        self.chunk = total.shape[1] // RING if near is None else near.shape[1]
        self.outgoing = []

    def device(self, dx, other=False):
        core = 1 - self.core if other else self.core
        return (lax.rem(self.x + dx + RING, RING) * 2 + core, self.rank)

    def rows(self, dx, part=0):
        at, half = lax.rem(self.x + dx + RING, RING) * self.chunk, self.chunk // 2
        at = pl.multiple_of(at + (half if part == -1 else 0), half)
        return pl.ds(at, half if part else self.chunk)

    def copy(self, number, source, target, device):
        return pltpu.make_async_remote_copy(
            src_ref=source, dst_ref=target, send_sem=self.send.at[number], recv_sem=self.recv.at[number],
            device_id=device, device_id_type=MESH_ID,
        )

    def go(self, *args):
        self.outgoing.append(self.copy(*args))
        self.outgoing[-1].start()

    def come(self, number, target):
        self.copy(number, target, target, self.device(0, True)).wait_recv()

    def first(self):
        for i, way in ((0, 1), (1, -1)):
            self.go(i, self.half.at[self.rows(2, way)], self.far.at[i], self.device(way))

    def part(self, way, which):
        half = self.chunk // 2
        return self.near.at[0 if way == 1 else 1, pl.ds(0 if which == 1 else half, half)]

    def early(self):
        for i, way in ((0, 1), (1, -1)):
            self.go(13 + i, self.half.at[self.rows(way, -way)], self.part(way, -way), self.device(way))

    def second(self):
        for i, way in ((0, 1), (1, -1)):
            self.come(i, self.far.at[i])
            at = self.rows(way, way)
            self.half[at, :] = self.half[at, :] + self.far[i]
            self.go(2 + i, self.half.at[at], self.part(way, way), self.device(way))

    def own_sum(self):
        for i, way in ((0, 1), (1, -1)):
            self.come(13 + i, self.part(way, -way))
            self.come(2 + i, self.part(way, way))
        own = self.half[self.rows(0), :].astype(F32) + self.near[0].astype(F32) + self.near[1].astype(F32)
        return own.astype(BF16)

    def third(self):
        ref = self.total.at[self.core, self.rows(0)]
        for i, way in ((0, 1), (1, -1)):
            self.go(4 + i, ref, ref, self.device(way))
        self.go(8, ref, ref, self.device(0, True))

    def fourth(self):
        for i, way in ((0, 1), (1, -1)):
            ref = self.total.at[self.core, self.rows(-way)]
            self.come(4 + i, ref)
            part = self.total.at[self.core, self.rows(-way, way)]
            self.go(6 + i, part, part, self.device(way))
            self.go(9 + i, ref, ref, self.device(0, True))

    def fifth(self):
        for i, way in ((0, 1), (1, -1)):
            ref = self.total.at[self.core, self.rows(2, way)]
            self.come(6 + i, ref)
            self.go(11 + i, ref, ref, self.device(0, True))

    def finish(self):
        self.come(8, self.total.at[1 - self.core, self.rows(0)])
        for i, way in ((0, 1), (1, -1)):
            self.come(9 + i, self.total.at[1 - self.core, self.rows(-way)])
            self.come(11 + i, self.total.at[1 - self.core, self.rows(2, way)])
        self.sent()

    def sent(self):
        for copy in self.outgoing:
            copy.wait_send()


GROUPS = (
    ((0, 0), (0, 1), (0, 3), (1, 0), (3, 0)),
    ((1, 1), (1, 3), (3, 1), (3, 3), (2, 0), (0, 2)),
    ((2, 1), (2, 3), (1, 2), (3, 2), (2, 2)),
)
MOST = 6 * CAP
CHUNK = 32


def front_kernel(
    x_in, gain_in, gain_two_in, query_in, keyval_in, out_w_in, cot_in, cosine_in, sine_in, routes_in, router_in, gateup_in, down_in,
    normed_out, qkv_out, wide_ref, log_ref, context_ref, query_out, residual_ref,
    combined_out, chunk_out, grad_residual_ref, grad_att_ref, small_ref, grad_context_ref,
    x_ref, gain_one_ref, gain_two_ref, cosine_ref, sine_ref, own_w, local_w, pair_w, qkv, key_rows, context_parts,
    normed_ref, router_ref, routes_ref, own_cot,
    buf, weights, buf2, cot, gateup, down, out_w, pick, gate_wide, note_wide, arrived, grad_acts, hidden, grad_slots,
    acts, grad_hidden, grad_rows, landing, far, near, notes, told, own_gates, gate_parts, gate_told,
    sems_a, sems_b, sems_d, sems_e, sems_f, pair_a, pair_b, pair_c, pair_d, pair_e, pair_f, free, local_sems, load_sems, late_sems,
):
    combined, parts = buf, weights
    (send_a, recv_a), (send_b, recv_b), (send_c, recv_c) = pair_a, pair_b, pair_c
    (send_d, recv_d), (send_e, recv_e), (send_f, recv_f) = pair_d, pair_e, pair_f
    tokens, width = x_ref.shape
    rank = lax.axis_index("tensor")
    z, y = position()
    half = HD // 2
    copies = loads(
        [
            (x_in, x_ref), (gain_in, gain_one_ref), (out_w_in, own_w.at[:HD]), (query_in, own_w.at[HD:]),
            (routes_in, routes_ref.at[rank]), (cosine_in, cosine_ref), (sine_in, sine_ref), (gain_two_in, gain_two_ref),
            (router_in, router_ref), (cot_in, own_cot),
        ],
        load_sems,
    )
    count = RING * RING
    length = count * tokens
    local_experts, ff = down.shape[0], down.shape[1]
    late = loads([(gateup_in, gateup), (down_in, down)], late_sems)
    dp = lax.axis_index("dp")
    core = lax.rem(dp, 2)
    sibling = (dp + 1 - 2 * core, rank)
    pair_copies = []
    for part in range(2):
        column = pl.multiple_of(part * KV_HEADS * HD + z * 2 * HD, 2 * HD)
        copy = pltpu.make_async_copy(keyval_in.at[:, pl.ds(column, 2 * HD)], pair_w.at[part], local_sems.at[part])
        copy.start()
        pair_copies.append(copy)
    cot_copy = pltpu.make_async_copy(cot_in, cot.at[pl.ds(pl.multiple_of(rank * tokens, tokens), tokens)], local_sems.at[2])
    cot_copy.start()
    copies[0].wait()
    copies[1].wait()
    own_rows = pl.ds(pl.multiple_of(rank * tokens, tokens), tokens)
    inputs = x_ref[...].astype(F32)
    buf[rank] = (inputs * rms_scale(inputs) * gain_one_ref[...].reshape(1, width).astype(F32)).astype(BF16)
    greet(others("tensor", RING * RING), near_members())
    main = Gather(buf, *sems_a)
    main.stage(0)
    for copy in copies[2:5]:
        copy.wait()
    replicas = Replicas(own_w.at[:, Replicas.columns_of(weights)], weights, *sems_b, local_sems.at[3])
    replicas.first()
    tell = Exchange(routes_ref.at[rank], routes_ref, *sems_f, same=True)
    tell.start()
    for copy in pair_copies + copies[5:]:
        copy.wait()
    odd = lax.rem(lax.div(rank, 2), 2)
    local_w[:HD] = own_w[HD:]
    for part in range(2):
        tall = pair_w[part].T.astype(F32)
        local_w[HD * (part + 1) : HD * (part + 2)] = jnp.where(odd == 0, tall[:HD], tall[HD:]).astype(BF16)
    ids = lax.broadcasted_iota(jnp.int32, (EXPERTS, tokens), 0)
    slot_ids = lax.broadcasted_iota(jnp.int32, (CAP, tokens), 0).astype(F32)
    before = lax.broadcasted_iota(jnp.int32, (tokens, tokens), 0) < lax.broadcasted_iota(jnp.int32, (tokens, tokens), 1)
    upper = jnp.where(before, 1.0, 0.0).astype(BF16)
    pos = main.pos

    def named_of(block):
        routes = routes_ref[block]
        hits = ids == routes[0:1]
        for k in range(1, TOP):
            hits = hits | (ids == routes[k : k + 1])
        return hits


    groups, place = [], 0
    for group in GROUPS:
        members = []
        for dz, dy in group:
            members.append((place, joined(shifted(shifted(pos, 0, dz), 1, dy))))
            place += 1
        groups.append(members)
    every = [member for members in groups for member in members]
    pairs_of = [[members[i : i + 2] for i in range(0, len(members), 2)] for members in groups]
    wide = local_experts * CAP
    pair_number = {}
    for pairs in pairs_of:
        for pair in pairs:
            pair_number[pair[0][0]] = len(pair_number)
    def make_picks(pairs):
        for pair in pairs:
            number = pair_number[pair[0][0]]
            if len(pair) == 2:
                pick[number, :wide, tokens:] = jnp.zeros((wide, tokens), BF16)
                pick[number, wide:, :tokens] = jnp.zeros((wide, tokens), BF16)
            for i, (_, block) in enumerate(pair):
                named = jnp.where(named_of(block), 1.0, 0.0)
                places = dot(named.astype(BF16), upper, ((1,), (0,)))
                for e in range(local_experts):
                    mine = ids == rank * local_experts + e
                    hit = jnp.sum(jnp.where(mine, named, 0.0), axis=0, keepdims=True)
                    at = jnp.sum(jnp.where(mine, places, 0.0), axis=0, keepdims=True)
                    at = jnp.where(hit > 0.5, at, -1.0)
                    first = i * wide + e * CAP
                    pick[number, first : first + CAP, i * tokens : (i + 1) * tokens] = jnp.where(slot_ids == at, 1.0, 0.0).astype(BF16)


    def project(dz, dy):
        block = joined(shifted(shifted(pos, 0, dz), 1, dy))
        columns = pl.ds(pl.multiple_of(block * tokens, tokens), tokens)
        made = dot(local_w[...], buf[block], ((1,), (1,)))
        cosine, sine = cosine_ref[:, columns], sine_ref[:, columns]
        rows = []
        for first in (0, HD):
            rows += rotate(made[first : first + half], made[first + half : first + HD], cosine, sine)
        rows.append(made[2 * HD :])
        qkv[:, columns] = jnp.concatenate(rows, axis=0).astype(BF16)

    project(0, 0)
    main.stage(1)
    main.stage(2)
    replicas.second()
    main.arrive_stage(0)
    for offset in ((0, 1), (0, 3), (1, 0), (3, 0)):
        project(*offset)
    tell.arrive()
    main.stage(3)
    main.stage(4)
    make_picks(pairs_of[0])
    cot_copy.wait()
    back = Gather(cot, *sems_d)
    main.arrive_stage(1)
    main.arrive_stage(2)
    for offset in ((1, 1), (1, 3), (3, 1), (3, 3), (2, 0), (0, 2)):
        project(*offset)
    main.stage(5)
    back.stage(0)
    make_picks(pairs_of[1])
    main.arrive_stage(3)
    main.arrive_stage(4)
    replicas.third()
    for offset in ((2, 1), (2, 3), (1, 2), (3, 2)):
        project(*offset)
    main.arrive_stage(5)
    project(2, 2)
    make_picks(pairs_of[2])
    normed_copy = pltpu.make_async_copy(buf, normed_out, local_sems.at[5])
    normed_copy.start()
    qkv_copy = pltpu.make_async_copy(qkv, qkv_out, local_sems.at[6])
    qkv_copy.start()
    key_rows[...] = qkv[HD : 2 * HD].T
    swap_context = Exchange(context_parts, context_ref, *sems_e)
    todo = {2: [lambda: back.stage(1)], 3: [lambda: back.stage(2)], 5: [replicas.fourth], 6: [lambda: back.stage(3)]}
    attend(qkv, key_rows, wide_ref, log_ref, context_parts, tokens, todo)
    swap_context.start()
    context_ref[rank] = context_parts[rank]
    main.finish()
    replicas.finish()
    query_copy = pltpu.make_async_copy(weights.at[:, pl.ds(HD, HD)], query_out, local_sems.at[7])
    query_copy.start()
    out_copy = pltpu.make_async_copy(weights.at[:, pl.ds(0, HD)], out_w, local_sems.at[4])
    out_copy.start()
    back.stage(4)
    swap_context.arrive()
    back.stage(5)
    context = context_ref[...].reshape(HEADS * HD, tokens)
    attention = dot(context, weights[:, :HD].reshape(HEADS * HD, width), ((0,), (0,)))
    residual = x_ref[...].astype(F32) + RES_SCALE * attention
    residual_ref[...] = residual
    normed_ref[...] = (residual * rms_scale(residual) * gain_two_ref[...].reshape(1, width).astype(F32)).astype(BF16)
    buf2[own_rows, :] = normed_ref[...]
    gather = Gather(buf2, send_a, recv_a)
    gather.stage(0)
    router = router_ref[...]
    named = named_of(rank)
    logits = jnp.where(named, dot(router, normed_ref[...], ((1,), (1,))), -1e30)
    powers = jnp.where(named, jnp.exp(logits - jnp.max(logits, axis=0, keepdims=True)), 0.0)
    own_gates[...] = powers / jnp.sum(powers, axis=0, keepdims=True)
    gate_parts[...] = jnp.zeros_like(gate_parts)
    for i in range(count):
        gate_parts[i, :local_experts] = own_gates[i * local_experts : (i + 1) * local_experts]
    tell_gates = Exchange(gate_parts, gate_told, send_f, recv_f)
    tell_gates.start()
    gate_told[rank] = gate_parts[rank]

    def chosen_of(pair):
        rows = len(pair) * wide
        return pick[pair_number[pair[0][0]], :rows, : len(pair) * tokens]

    back.finish()

    def spread(made, pair, target):
        for i, (at, _) in enumerate(pair):
            for e in range(local_experts):
                first = i * wide + e * CAP
                target[e, at * CAP : (at + 1) * CAP] = made[first : first + CAP]

    def joint(ref, pair, at):
        return jnp.concatenate([ref[e, i * CAP : (i + 1) * CAP] for i in at for e in range(local_experts)], axis=0)

    for pairs in pairs_of:
        for pair in pairs:
            rows = [cot[pl.ds(pl.multiple_of(block * tokens, tokens), tokens), :] for _, block in pair]
            spread(dot(chosen_of(pair), jnp.concatenate(rows, axis=0), ((1,), (0,))).astype(BF16), pair, grad_slots)
    gather.stage(1)
    gather.stage(2)
    for copy in late:
        copy.wait()
    for e in range(local_experts):
        for first in range(0, count * CAP, 256):
            at = slice(first, first + 256)
            grad_hidden[e, at] = dot(grad_slots[e, at], down[e], ((1,), (1,))).astype(BF16)
    for copy in (normed_copy, qkv_copy, query_copy, out_copy):
        copy.wait()
    tell_gates.arrive()
    for pairs in pairs_of:
        for pair in pairs:
            for i, (at, block) in enumerate(pair):
                chosen = chosen_of(pair)[i * wide : (i + 1) * wide, i * tokens : (i + 1) * tokens].astype(F32)
                for e in range(local_experts):
                    column = jnp.sum(chosen[e * CAP : (e + 1) * CAP] * gate_told[block, e : e + 1], axis=1, keepdims=True)
                    gate_wide[e, at * CAP : (at + 1) * CAP] = jnp.broadcast_to(column, (CAP, 128))

    def work(number, between=()):
        pairs, base, rows = pairs_of[number], groups[number][0][0] * CAP, len(groups[number]) * CAP
        first = groups[number][0][0]
        for pair in pairs:
            blocks = jnp.concatenate([buf2[pl.ds(pl.multiple_of(block * tokens, tokens), tokens), :] for _, block in pair], axis=0)
            spread(dot(chosen_of(pair), blocks, ((1,), (0,))).astype(BF16), pair, arrived)

        def one(e):
            acts[:rows] = dot(arrived[e, base : base + rows], gateup[e], ((1,), (0,)))

            @pl.loop(0, rows // CHUNK)
            def _(c):
                at = pl.ds(pl.multiple_of(c * CHUNK, CHUNK), CHUNK)
                out = pl.ds(pl.multiple_of(base + c * CHUNK, CHUNK), CHUNK)
                column = gate_wide[e, out]
                note = jnp.zeros((CHUNK, 128), F32)
                for k in range(0, ff, 128):
                    gate, up = acts[at, k : k + 128], acts[at, ff + k : ff + k + 128]
                    sigmoid = 0.5 + 0.5 * jnp.tanh(0.5 * gate)
                    silu = gate * sigmoid
                    made = silu * up
                    raw = RES_SCALE * grad_hidden[e, out, k : k + 128].astype(F32)
                    note = note + made * raw
                    back = column * raw
                    hidden[e, out, k : k + 128] = (column * made).astype(BF16)
                    grad_acts[e, out, k : k + 128] = (back * up * (sigmoid + silu * (1.0 - sigmoid))).astype(BF16)
                    grad_acts[e, out, ff + k : ff + k + 128] = (back * silu).astype(BF16)
                note_wide[e, out] = note

            grad_rows[e, :rows] = dot(grad_acts[e, base : base + rows], gateup[e], ((1,), (1,))).astype(BF16)

        for e in range(local_experts):
            one(e)
            if e == 0:
                for task in between:
                    task()
        for pair in pairs:
            back = joint(grad_rows, pair, [at - first for at, _ in pair])
            made = dot(chosen_of(pair), back, ((0,), (0,))).astype(BF16)
            for i, (_, block) in enumerate(pair):
                parts[block] = made[i * tokens : (i + 1) * tokens]

    def outcome(number):
        pairs, base, rows = pairs_of[number], groups[number][0][0] * CAP, len(groups[number]) * CAP
        first = groups[number][0][0]

        @pl.loop(0, local_experts)
        def _(e):
            grad_rows[e, :rows] = dot(hidden[e, base : base + rows], down[e], ((1,), (0,))).astype(BF16)

        for pair in pairs:
            chosen = chosen_of(pair)
            made = dot(chosen, joint(grad_rows, pair, [at - first for at, _ in pair]), ((0,), (0,))).astype(BF16)
            for i, (at, block) in enumerate(pair):
                combined[block] = made[i * tokens : (i + 1) * tokens]

    def report(number):
        for pair in pairs_of[number]:
            chosen = chosen_of(pair)
            for i, (at, block) in enumerate(pair):
                for e in range(local_experts):
                    begin = i * wide + e * CAP
                    hits = chosen[begin : begin + CAP, i * tokens : (i + 1) * tokens].astype(F32)
                    column = jnp.sum(note_wide[e, at * CAP : (at + 1) * CAP], axis=1, keepdims=True)
                    notes[block, e : e + 1] = jnp.sum(hits * column, axis=0, keepdims=True)

    gather.arrive_stage(0)
    work(0, [lambda: gather.stage(3), lambda: gather.stage(4)])
    gather.arrive_stage(1)
    gather.arrive_stage(2)
    work(1, [lambda: gather.stage(5)])
    for stage in (3, 4, 5):
        gather.arrive_stage(stage)
    work(2)

    scatter = Scatter(parts, landing, send_b, recv_b)
    for stage in (5, 4, 2):
        scatter.stage(stage)
    gather.finish()
    pl.semaphore_signal(free, inc=1, device_id=sibling, device_id_type=MESH_ID)
    quarter = (width // RING, ff // RING)
    chunk = sum(quarter)
    x = lax.div(dp, 2)
    gifts = []

    def rows_of(c):
        return pl.ds(pl.multiple_of(c * chunk, chunk), chunk)

    def gift(number, c):
        return pltpu.make_async_remote_copy(
            src_ref=cot.at[rows_of(c)], dst_ref=buf2.at[rows_of(c)],
            send_sem=send_d.at[number], recv_sem=recv_d.at[number], device_id=sibling, device_id_type=MESH_ID,
        )

    def made_of(e, c):
        first = pl.ds(pl.multiple_of(c * quarter[0], quarter[0]), quarter[0])
        second = pl.ds(pl.multiple_of(c * quarter[1], quarter[1]), quarter[1])
        upper_rows = dot(arrived[e, :, first], grad_acts[e], ((0,), (0,)))
        return upper_rows, RES_SCALE * dot(hidden[e, :, second], grad_slots[e], ((0,), (0,)))

    def give(number, c):
        at = c * chunk
        upper_rows, lower_rows = made_of(1 - core, c)
        cot[pl.ds(pl.multiple_of(at, quarter[1]), quarter[0]), :] = upper_rows.astype(BF16)
        cot[pl.ds(pl.multiple_of(at + quarter[0], quarter[1]), quarter[1]), :] = lower_rows.astype(BF16)
        if number == 0:
            pl.semaphore_wait(free, 1)
        gifts.append(gift(number, c))
        gifts[-1].start()

    def keep(number, c):
        upper_rows, lower_rows = made_of(core, c)
        gift(number, c).wait_recv()
        first = pl.ds(pl.multiple_of(c * chunk, quarter[1]), quarter[0])
        second = pl.ds(pl.multiple_of(c * chunk + quarter[0], quarter[1]), quarter[1])
        buf2[first, :] = (upper_rows + buf2[first, :].astype(F32)).astype(BF16)
        buf2[second, :] = (lower_rows + buf2[second, :].astype(F32)).astype(BF16)

    ring = RingSum(buf2, near, far, None, send_e, recv_e)
    order = [lax.rem(x + dx, RING) for dx in (2, 1, 3, 0)]
    give(0, order[0])
    give(1, order[1])
    keep(0, order[0])
    ring.first()
    scatter.stage(3)
    for number in range(3):
        report(number)
    swap = Exchange(notes, told, send_c, recv_c)
    swap.start()
    told[rank] = notes[rank]
    give(2, order[2])
    keep(1, order[1])
    keep(2, order[2])
    ring.early()
    scatter.stage(1)
    give(3, order[3])
    keep(3, order[3])
    ring.second()
    outcome(2)
    scatter.stage(0)
    outcome(1)
    outcome(0)
    combined_copy = pltpu.make_async_copy(combined, combined_out, local_sems.at[0])
    combined_copy.start()
    swap.arrive()
    gates = own_gates[...]
    grads = jnp.concatenate([told[i, :local_experts] for i in range(count)], axis=0)
    grad_logits = (gates * (grads - jnp.sum(gates * grads, axis=0, keepdims=True))).astype(BF16)
    normed = normed_ref[...]
    small_ref[...] = jnp.zeros_like(small_ref)
    small_ref[:EXPERTS] = dot(grad_logits, normed, ((1,), (0,)))
    from_router = dot(grad_logits, router, ((0,), (0,)))
    gain = gain_two_ref[...].reshape(1, width).astype(F32)
    middle = tokens // 2
    grad_gain = jnp.zeros((1, width), F32)
    for place, back in enumerate(scatter.result()):
        at = slice(place * middle, (place + 1) * middle)
        residual = residual_ref[at]
        scale = rms_scale(residual)
        grad_normed = from_router[at] + back
        grad_norm, part = norm_back(residual, scale, gain, grad_normed)
        grad_gain = grad_gain + part[None]
        grad_residual = own_cot[at].astype(F32) + grad_norm
        grad_residual_ref[at] = grad_residual
        grad_att_ref[at] = (RES_SCALE * grad_residual).astype(BF16)
    small_ref[EXPERTS : EXPERTS + 1] = grad_gain
    grad_context_ref[...] = dot(out_w[...].reshape(HEADS * HD, width), grad_att_ref[...], ((1,), (1,))).astype(BF16).reshape(HEADS, HD, tokens)
    scatter.finish()
    swap.sent()
    swap_context.sent()
    tell.sent()
    tell_gates.sent()
    chunk_out[...] = ring.own_sum()
    for copy in gifts:
        copy.wait_send()
    ring.sent()
    combined_copy.wait()


def front(x, gain, gain_two, w_query, w_keyval, w_out, cotangent, cosine, sine, routes, router, w_gateup, w_down):
    tokens, width = x.shape
    count = RING * RING
    length = tokens * count
    local_experts, ff = w_down.shape[:2]
    rows = count * CAP
    sem_counts = (
        Torus.COUNT, Replicas.COUNT, Torus.COUNT, count - 1, count - 1,
        Torus.COUNT, Torus.COUNT, count - 1, RING, RingSum.COUNT, count - 1,
    )
    pairs = len(sem_counts)

    def kernel(*refs):
        cut = len(refs) - 2 * pairs - 4
        sems = refs[cut : cut + 2 * pairs]
        front_kernel(*refs[:cut], *[sems[2 * i : 2 * i + 2] for i in range(pairs)], *refs[cut + 2 * pairs :])

    shape = jax.ShapeDtypeStruct
    vmem = pltpu.VMEM
    block = vmem((count, tokens, width), BF16)
    flat = vmem((length, width), BF16)
    note = vmem((count, 8, tokens), F32)
    semaphores = [one for n in sem_counts for one in pair_sems(n)]
    return call(
        kernel, "front", 1,
        (
            shape((count, tokens, width), BF16), shape((3 * HD, length), BF16), shape((HD, length), F32),
            shape((1, length), F32), shape((count, HD, tokens), BF16), shape((count, HD, width), BF16), shape((tokens, width), F32),
            shape((count, tokens, width), BF16), shape(((width + ff) // RING, width), BF16),
            shape((tokens, width), F32), shape((tokens, width), BF16), shape((EXPERTS + 8, width), F32),
            shape((HEADS, HD, tokens), BF16),
        ),
        [anywhere()] * 13,
        [anywhere(), anywhere(), whole(), whole(), whole(), anywhere(), whole(), anywhere()] + [whole()] * 5,
        [
            vmem(x.shape, BF16), vmem(gain.shape, BF16), vmem(gain.shape, BF16), vmem(cosine.shape, F32), vmem(sine.shape, F32),
            vmem((2 * HD, width), BF16), vmem((3 * HD, width), BF16), vmem((2, width, 2 * HD), BF16), vmem((3 * HD, length), BF16),
            vmem((length, HD), BF16), vmem((count, HD, tokens), BF16),
            vmem(x.shape, BF16), vmem(router.shape, BF16), vmem((count, *routes.shape), jnp.int32), vmem(x.shape, BF16),
            block, block, flat, flat, vmem(w_gateup.shape, BF16), vmem(w_down.shape, BF16), vmem((HEADS, HD, width), BF16),
            vmem((9, 2 * local_experts * CAP, 2 * tokens), BF16),
            vmem((local_experts, rows, 128), F32), vmem((local_experts, rows, 128), F32), vmem((local_experts, rows, width), BF16),
            vmem((local_experts, rows, 2 * ff), BF16), vmem((local_experts, rows, ff), BF16), vmem((local_experts, rows, width), BF16),
            vmem((MOST, 2 * ff), F32), vmem((local_experts, rows, ff), BF16), vmem((local_experts, MOST, width), BF16),
            vmem(((count - 1) * tokens, width), BF16), vmem((2, (width + ff) // 8, width), BF16), vmem((2, (width + ff) // 4, width), BF16),
            note, note, vmem((EXPERTS, tokens), F32), note, note,
            *semaphores, pltpu.SemaphoreType.REGULAR, pltpu.SemaphoreType.DMA((8,)), pltpu.SemaphoreType.DMA((10,)),
            pltpu.SemaphoreType.DMA((2,)),
        ],
        65400, flops=2 * 9 * rows * width * ff * local_experts + 2 * length * (3 * HD * width + length * HD * 2), bytes_accessed=40 << 20,
    )(x, gain, gain_two, w_query, w_keyval, w_out, cotangent, cosine, sine, routes, router, w_gateup, w_down)


SMALL = 384


def backward_kernel(
    qkv_in, grad_in, wide_in, log_in, cosine_in, sine_in, normed_in, context_in, grad_att_in, combined_in, residual_in, chunk_in,
    small_in, x_in, gain_in, grad_residual_in, weights_in, keyval_in,
    block_ref, input_ref, query_ref, out_ref, keyval_ref, small_out, gain_out, gateup_out, down_out,
    qkv_ref, grad_ref, wide_ref, log_ref, cosine_ref, sine_ref, normed, context_ref, grad_att_ref, combined, residual_ref,
    small_ref, x_ref, gain_ref, grad_residual_ref, query_all, keyval_all,
    grad_parts, parts_out, parts_back, grad, query_rows, key_rows, value_rows, grad_rows, grad_query, grad_key, grad_value,
    wide_grad, out_parts, out_land, combined_land, total,
    weight, give, pair_land, kv_own, mine, land, summed, small_parts, small_land, small_sum, small_dp, gather_buf,
    gain_sum, gain_dp, gain_land, back_pairs, out_mine, out_dp, out_all,
    send_a, recv_a, send_b, recv_b, send_c, recv_c, send_d, recv_d, send_e, recv_e, send_f, recv_f, send_g, recv_g,
    send_h, recv_h, send_i, recv_i, send_j, recv_j, send_k, recv_k, send_l, recv_l, send_n, recv_n,
    send_m, recv_m, send_q, recv_q, send_p, recv_p, sems, out_sems,
):
    count, _, tokens = grad_ref.shape
    length, width = count * tokens, normed.shape[1]
    dps = land.shape[0]
    rank, dp = lax.axis_index("tensor"), lax.axis_index("dp")
    order = (
        (grad_in, grad_ref), (chunk_in, total.at[lax.rem(dp, 2), pl.ds(pl.multiple_of(lax.div(dp, 2) * chunk_in.shape[0], chunk_in.shape[0]), chunk_in.shape[0])]), (small_in, small_ref), (qkv_in, qkv_ref), (context_in, context_ref),
        (grad_att_in, grad_att_ref), (combined_in, combined), (wide_in, wide_ref), (log_in, log_ref), (cosine_in, cosine_ref),
        (sine_in, sine_ref), (normed_in, normed), (residual_in, residual_ref), (x_in, x_ref), (gain_in, gain_ref),
        (grad_residual_in, grad_residual_ref), (weights_in, query_all), (keyval_in, keyval_all),
    )
    copies = loads(order, sems)
    odd = lax.rem(rank, 2)
    partner = rank + 1 - 2 * odd
    greet(others("tensor", count), others("dp", dps), [(p, partner) for p in others("dp", dps)])
    copies[0].wait()
    swap = Exchange(grad_ref, grad_parts, send_a, recv_a)
    swap.start()
    copies[1].wait()
    ring = RingSum(None, None, None, total, send_e, recv_e)
    ring.third()
    copies[2].wait()
    for i in range(count):
        small_parts[i, :, :256] = small_ref[8 * (i // 4) : 8 * (i // 4) + 8, 256 * (i % 4) : 256 * (i % 4) + 256]
        small_parts[i, :, 256:] = small_ref[32:40, 128 * (i // 2) : 128 * (i // 2) + 128]
    small = Exchange(small_parts, small_land, send_f, recv_f)
    small.start()
    small_land[rank] = small_parts[rank]
    copies[3].wait()
    query, key, value = slice(0, HD), slice(HD, 2 * HD), slice(2 * HD, 3 * HD)
    query_rows[...] = qkv_ref[query].T
    key_rows[...] = qkv_ref[key].T
    value_rows[...] = qkv_ref[value].T
    scatter = Scatter(out_parts, out_land, send_c, recv_c)
    copies[4].wait()
    copies[5].wait()
    grad_att = grad_att_ref[...]
    for part in range(count):
        out_parts[part] = dot(context_ref[part], grad_att, ((1,), (0,))).astype(BF16)
    for stage in (5, 4, 2):
        scatter.stage(stage)
    combine = Scatter(combined, combined_land, send_d, recv_d)
    grad_parts[rank] = grad_ref[rank]
    for copy in copies[7:11]:
        copy.wait()
    swap.arrive()
    for part in range(count):
        grad[:, part * tokens : (part + 1) * tokens] = grad_parts[part]
    grad_rows[...] = grad[...].T
    second_small = Exchange(small_sum.at[0], small_dp, send_g, recv_g, "dp", same=True)
    allowed = causal(Q_ROWS)
    blocks = length // Q_ROWS

    def combine_leaves():
        copies[6].wait()
        for stage in (5, 4, 2):
            combine.stage(stage)

    def small_dps():
        small.arrive()
        small_sum[0] = jnp.sum(small_land[...], axis=0)
        second_small.start()
        small_dp[dp] = small_sum[0]

    def small_again():
        second_small.arrive()
        small_sum[1] = jnp.sum(small_dp[...], axis=0)
        third.start()
        small_out[rank] = small_sum[1]

    third = Exchange(small_sum.at[1], small_out, send_h, recv_h, same=True)
    plan = {0: [combine_leaves], 2: [lambda: scatter.stage(3)], 3: [small_dps], 6: [lambda: scatter.stage(1)], 7: [ring.fourth]}
    for block in reversed(range(blocks)):
        first = block * Q_ROWS
        columns = slice(first, first + Q_ROWS)
        scaled = qkv_ref[query, columns] * ATTN_SCALE
        logs = log_ref[:, columns]
        grad_block = grad[:, columns]
        inner = jnp.sum(grad_block.astype(F32) * wide_ref[:, columns], axis=0, keepdims=True)
        wide_total = jnp.zeros((HD, Q_ROWS), F32)
        spans = [(columns, True)]
        if block:
            spans.append((slice(0, first), False))
        for keys, close in spans:
            weights = jnp.exp(dot(key_rows[keys, :], scaled, ((1,), (0,))) - logs)
            if close:
                weights = jnp.where(allowed, weights, 0.0)
            grad_weights = dot(value_rows[keys, :], grad_block, ((1,), (0,)))
            grad_scores = (weights * (grad_weights - inner)).astype(BF16)
            wide_total = wide_total + dot(qkv_ref[key, keys], grad_scores, ((1,), (0,)))
            key_part = dot(grad_scores, query_rows[columns, :], ((1,), (0,)))
            value_part = dot(weights.astype(BF16), grad_rows[columns, :], ((1,), (0,)))
            if block == blocks - 1:
                grad_key[keys, :] = key_part
                grad_value[keys, :] = value_part
            else:
                grad_key[keys, :] += key_part
                grad_value[keys, :] += value_part
        grad_query[:, columns] = wide_total * ATTN_SCALE
        for task in plan.get(blocks - 1 - block, ()):
            task()
    middle = HD // 2
    cosine, sine = cosine_ref[...], -sine_ref[...]
    for place, wide in enumerate((grad_query[...], grad_key[...].T * ATTN_SCALE)):
        rows = rotate(wide[:middle], wide[middle:], cosine, sine)
        wide_grad[place * HD : (place + 1) * HD] = jnp.concatenate(rows, axis=0).astype(BF16)
    wide_grad[2 * HD :] = grad_value[...].T.astype(BF16)
    for part in range(count):
        parts_out[part] = wide_grad[:, part * tokens : (part + 1) * tokens]
    back = Exchange(parts_out, parts_back, send_b, recv_b)
    back.start()
    parts_back[rank] = parts_out[rank]
    for copy in copies[11:]:
        copy.wait()
    weight[...] = dot(wide_grad[...], normed[...], ((1,), (0,)))
    column = width // dps
    kept = weight[pl.ds(pl.multiple_of(HD + HD * odd, HD), HD), :]
    for j, rows in enumerate((weight[:HD], kept)):
        low = rows.astype(BF16)
        for i in range(dps):
            mine[i, j * HD : (j + 1) * HD] = low[:, i * column : (i + 1) * column]
    dp_first = Exchange(mine, land, send_i, recv_i, "dp")
    dp_first.start()
    low = weight[pl.ds(pl.multiple_of(HD + HD * (1 - odd), HD), HD), :].astype(BF16)
    for i in range(dps):
        give[i] = low[:, i * column : (i + 1) * column]

    def across(r):
        to = lax.rem(dp + r, dps)
        return pltpu.make_async_remote_copy(
            src_ref=give.at[to], dst_ref=pair_land.at[dp], send_sem=send_p.at[r], recv_sem=recv_p.at[r],
            device_id=(to, partner), device_id_type=MESH_ID,
        )

    def across_here(r):
        at = pair_land.at[lax.rem(dp + dps - r, dps)]
        return pltpu.make_async_remote_copy(
            src_ref=at, dst_ref=at, send_sem=send_p.at[r], recv_sem=recv_p.at[r],
            device_id=(dp, partner), device_id_type=MESH_ID,
        )

    for r in range(dps):
        across(r).start()
    land[dp] = mine[dp]
    scatter.stage(0)
    small_again()
    combine.stage(3)
    out_sum = jnp.concatenate(scatter.result(), axis=0).astype(BF16)
    for i in range(dps):
        out_mine[i] = out_sum[:, i * column : (i + 1) * column]
    out_first = Exchange(out_mine, out_dp, send_m, recv_m, "dp")

    back.arrive()
    share = HEADS // KV_HEADS
    for head in range(KV_HEADS):
        for part in range(2):
            at = slice((part + 1) * HD, (part + 2) * HD)
            both = sum(parts_back[head * share + i, at].astype(F32) for i in range(share))
            back_pairs[part * KV_HEADS + head] = both.astype(BF16)
    queries_back = parts_back[:, :HD].reshape(HEADS * HD, tokens)
    grad_normed = dot(queries_back, query_all[...].reshape(HEADS * HD, width), ((0,), (0,)))
    grad_normed = grad_normed + dot(back_pairs[...].reshape(2 * KV_HEADS * HD, tokens), keyval_all[...], ((0,), (1,)))
    inputs = x_ref[...].astype(F32)
    grad_norm, grad_gain = norm_back(inputs, rms_scale(inputs), gain_ref[...].reshape(1, width).astype(F32), grad_normed)
    input_ref[...] = grad_residual_ref[...] + grad_norm
    grad_gain = grad_gain[None]
    for i in range(gain_sum.shape[1]):
        gain_sum[0, i : i + 1] = grad_gain[:, 128 * i : 128 * i + 128]

    dp_first.arrive()
    for r in range(dps):
        across_here(r).wait_recv()
    both = jnp.sum(land[...].astype(F32), axis=0)
    kv_own[...] = (both[HD:] + jnp.sum(pair_land[...].astype(F32), axis=0)).astype(BF16)
    replicas = Replicas(kv_own, gather_buf, send_n, recv_n, out_sems.at[0])
    replicas.first()
    summed[dp] = both[:HD].astype(BF16)
    dp_second = Exchange(summed.at[dp], summed, send_j, recv_j, "dp", same=True)
    dp_second.start()
    gain_first = Exchange(gain_sum.at[0], gain_dp, send_k, recv_k, "dp", same=True)
    gain_first.start()
    gain_dp[dp] = gain_sum[0]
    out_first.start()
    out_dp[dp] = out_mine[dp]
    ring.fifth()
    combine.stage(1)
    replicas.second()
    gain_first.arrive()
    gain_sum[1] = jnp.sum(gain_dp[...], axis=0)
    gain_second = Exchange(gain_sum.at[1], gain_land, send_l, recv_l, same=True)
    gain_second.start()
    gain_land[rank] = gain_sum[1]
    ring.finish()
    outs = []
    per = chunk_in.shape[0]
    for c in range(RING):
        down_rows = per - width // RING
        outs.append(pltpu.make_async_copy(total.at[:, pl.ds(c * per, width // RING)], gateup_out.at[:, pl.ds(c * (width // RING), width // RING)], out_sems.at[1 + c]))
        outs.append(pltpu.make_async_copy(total.at[:, pl.ds(c * per + width // RING, down_rows)], down_out.at[:, pl.ds(c * down_rows, down_rows)], out_sems.at[1 + RING + c]))
    for copy in outs:
        copy.start()
    out_first.arrive()
    out_all[dp] = jnp.sum(out_dp[...].astype(F32), axis=0).astype(BF16)
    out_second = Exchange(out_all.at[dp], out_all, send_q, recv_q, "dp", same=True)
    out_second.start()
    dp_second.arrive()
    for i in range(dps):
        query_ref[:, i * column : (i + 1) * column] = summed[i]
    combine.stage(0)
    replicas.third()
    replicas.fourth()
    rows = block_ref.shape[0] // 2
    for place, value_half in enumerate(combine.result()):
        at = slice(place * rows, (place + 1) * rows)
        block_ref[at] = (residual_ref[at] + RES_SCALE * value_half).astype(BF16)
    out_second.arrive()
    for i in range(dps):
        out_ref[:, i * column : (i + 1) * column] = out_all[i]
    third.arrive()
    gain_second.arrive()
    gain_out[...] = jnp.sum(gain_land[...], axis=0)
    replicas.finish()
    for i in range(count):
        base = (i % 2) * KV_HEADS * HD + (i // 2) * HD
        keyval_ref[base : base + HD, :] = gather_buf[i]
    for r in range(dps):
        across(r).wait_send()
    for each in (swap, back, small, second_small, third, dp_first, dp_second, gain_first, gain_second, out_first, out_second):
        each.sent()
    scatter.finish()
    combine.finish()
    for copy in outs:
        copy.wait()


def backward(
    qkv, grad_context, wide, logs, cosine, sine, normed, context, grad_att, combined, residual, chunk, small,
    x, gain, grad_residual, weights, w_keyval, dps,
):
    count, _, tokens = grad_context.shape
    length, width = normed.shape
    shape = jax.ShapeDtypeStruct
    vmem = pltpu.VMEM
    low = vmem((length, HD), BF16)
    wide_rows = vmem((length, HD), F32)
    column = width // dps
    rows = RING * chunk.shape[0]
    small_shape, gain_shape = (8, SMALL), (8, 128)
    operands = (
        qkv, grad_context, wide, logs, cosine, sine, normed, context, grad_att, combined, residual, chunk, small,
        x, gain, grad_residual, weights, w_keyval,
    )
    held = [vmem(o.shape, o.dtype) for o in operands]
    held[16] = vmem((count, HD, width), BF16)
    del held[11]
    three = vmem((dps, 2 * HD, column), BF16)
    return call(
        backward_kernel, "backward", 4,
        (
            shape((tokens, width), BF16), shape((tokens, width), F32), shape((HD, width), BF16), shape((HD, width), BF16),
            shape((count * HD, width), BF16), shape((count, *small_shape), F32), shape(gain_shape, F32),
            shape((2, width, width), BF16), shape((2, rows - width, width), BF16),
        ),
        [anywhere()] * len(operands), [whole()] * 7 + [anywhere()] * 2,
        [
            *held,
            vmem((count, HD, tokens), BF16), vmem(qkv_parts(count, tokens), BF16), vmem(qkv_parts(count, tokens), BF16),
            vmem((HD, length), BF16), low, low, low, low, vmem((HD, length), F32), wide_rows, wide_rows,
            vmem((3 * HD, length), BF16), vmem((count, HD, width), BF16), vmem(((count - 1) * HD, width), BF16),
            vmem(((count - 1) * tokens, width), BF16),
            vmem((2, rows, width), BF16),
            vmem((3 * HD, width), F32), vmem((dps, HD, column), BF16), vmem((dps, HD, column), BF16), vmem((HD, column), BF16),
            three, three, vmem((dps, HD, column), BF16),
            vmem((count, *small_shape), F32), vmem((count, *small_shape), F32), vmem((2, *small_shape), F32),
            vmem((dps, *small_shape), F32), vmem((count, HD, width), BF16),
            vmem((2, *gain_shape), F32), vmem((dps, *gain_shape), F32), vmem((count, *gain_shape), F32), vmem((2 * KV_HEADS, HD, tokens), BF16), *([vmem((dps, HD, column), BF16)] * 3),
            *pair_sems(count - 1), *pair_sems(count - 1), *pair_sems(Torus.COUNT), *pair_sems(Torus.COUNT),
            *pair_sems(RingSum.COUNT), *pair_sems(count - 1), *pair_sems(dps - 1), *pair_sems(count - 1),
            *pair_sems(dps - 1), *pair_sems(dps - 1), *pair_sems(dps - 1), *pair_sems(count - 1),
            *pair_sems(Replicas.COUNT), *pair_sems(dps - 1), *pair_sems(dps - 1), *pair_sems(dps),
            pltpu.SemaphoreType.DMA((len(operands),)), pltpu.SemaphoreType.DMA((1 + 2 * RING,)),
        ],
        65400, flops=2 * length * length * HD * 5, bytes_accessed=30 << 20,
    )(*operands)


def qkv_parts(count, tokens):
    return (count, 3 * HD, tokens)


def polish_kernel(
    gateup_ref, down_ref, keyval_ref, query_ref, out_ref, block_ref, input_ref, small_ref, gain_ref,
    gateup_out, down_out, keyval_out, query_out, out_out, block_out, input_out, router_out, gain_two_out, gain_one_out,
):
    gateup_out[...] = gateup_ref[...].astype(F32)
    down_out[...] = down_ref[...].astype(F32)
    keyval_out[...] = keyval_ref[...].T.astype(F32)

    @pl.when(pl.program_id(0) == 0)
    def _():
        query_out[...] = query_ref[...].astype(F32)
        out_out[...] = out_ref[...].astype(F32)
        block_out[...] = block_ref[...]
        input_out[...] = input_ref[...]
        for i in range(small_ref.shape[0]):
            router_out[8 * (i // 4) : 8 * (i // 4) + 8, 256 * (i % 4) : 256 * (i % 4) + 256] = small_ref[i, :, :256]
        for i in range(gain_two_out.shape[0]):
            gain_two_out[i : i + 1] = small_ref[2 * i, :1, 256:]
        gain_one_out[...] = gain_ref[...]


def polish(gateup, down, keyval, query, out, block, grad_input, small, gain):
    steps = 8
    experts_here, width, wide = gateup.shape
    ff = down.shape[1]
    per = steps // experts_here
    pairs = keyval.shape[0]
    shape = jax.ShapeDtypeStruct
    gateup_spec = pl.BlockSpec((1, width // per, wide), lambda i: (i // per, i % per, 0))
    down_spec = pl.BlockSpec((1, ff // per, width), lambda i: (i // per, i % per, 0))

    def once(dims):
        return pl.BlockSpec(dims, lambda i: (0,) * len(dims))

    rest = [query.shape, out.shape, block.shape, grad_input.shape]
    return pl.pallas_call(
        polish_kernel, grid=(steps,),
        out_shape=(
            shape(gateup.shape, F32), shape(down.shape, F32), shape((width, pairs), F32), shape(query.shape, F32),
            shape(out.shape, F32), shape(block.shape, BF16), shape(grad_input.shape, F32), shape((EXPERTS, width), F32),
            shape(gain.shape, F32), shape(gain.shape, F32),
        ),
        in_specs=[
            gateup_spec, down_spec, pl.BlockSpec((pairs, width // steps), lambda i: (0, i)),
            *[once(dims) for dims in rest], once(small.shape), once(gain.shape),
        ],
        out_specs=[
            gateup_spec, down_spec, pl.BlockSpec((width // steps, pairs), lambda i: (i, 0)),
            *[once(dims) for dims in rest], once((EXPERTS, width)), once(gain.shape), once(gain.shape),
        ],
        compiler_params=pltpu.CompilerParams(vmem_limit_bytes=65400 << 10),
        name="polish",
    )(gateup, down, keyval, query, out, block, grad_input, small, gain)


def shards(
    block_input, attn_gain, w_query, w_keyval, w_out, ffn_gain, w_router, w_gateup, w_down, routes, cotangent,
):
    tokens, width = block_input.shape
    length = tokens * lax.axis_size("tensor")
    cosine, sine = rope_tables(length, HD)
    (
        normed_one_all, qkv, wide_out, logs, context, query_all, residual, combined, chunk, grad_residual, grad_attention, small,
        grad_context,
    ) = front(
        block_input, attn_gain, ffn_gain, w_query.T, w_keyval, w_out, cotangent, cosine, sine, routes.T, w_router.T, w_gateup, w_down
    )
    block_out, grad_input, grad_query_w, grad_w_out, grad_keyval, small, gain_one, grad_w_gateup, grad_w_down = backward(
        qkv, grad_context, wide_out, logs, cosine, sine, normed_one_all.reshape(length, width), context, grad_attention,
        combined, residual, chunk, small, block_input, attn_gain, grad_residual, query_all, w_keyval, lax.axis_size("dp"),
    )
    grad_w_gateup, grad_w_down, grad_keyval, grad_query_w, grad_w_out, block_out, grad_input, routers, gain_two, gain_one = polish(
        grad_w_gateup, grad_w_down, grad_keyval, grad_query_w, grad_w_out, block_out, grad_input, small, gain_one
    )
    return (
        block_out,
        grad_input,
        gain_one.reshape(width),
        grad_query_w.T,
        grad_keyval,
        grad_w_out,
        gain_two.reshape(width),
        routers.T,
        grad_w_gateup,
        grad_w_down,
    )


def solution(mesh):
    rows = P(("dp", "tensor"), None)
    in_specs = (
        rows, P(), P(None, "tensor"), P(), P("tensor", None), P(), P(),
        P("tensor", None, None), P("tensor", None, None), rows, rows,
    )
    out_specs = (
        rows, rows, P(), P(None, "tensor"), P(), P("tensor", None), P(), P(),
        P("tensor", None, None), P("tensor", None, None),
    )
    return jax.shard_map(shards, mesh=mesh, in_specs=in_specs, out_specs=out_specs, check_vma=False)
```

```python
import jax
import jax.numpy as jnp
import numpy as np
from jax import lax
from jax.experimental import pallas as pl
from jax.experimental.pallas import tpu as pltpu
from jax.sharding import PartitionSpec as P

HEADS = 16
KV_HEADS = 8
HD = 64
EXPERTS = 32
TOP = 8
CAP = 64
ATTN_SCALE = 0.015625
RES_SCALE = 0.22
EPSILON = 1e-06
ROPE_BASE = 10000.0
F32 = jnp.float32
BF16 = jnp.bfloat16
Q_ROWS = 256


def rms_scale(values):
    return lax.rsqrt(jnp.mean(values * values, axis=-1, keepdims=True) + EPSILON)


def norm_back(values, scale, gain, grad_normed):
    grad_scaled = grad_normed * gain
    grad_gain = jnp.sum(grad_normed * values * scale, axis=0)
    inner = jnp.mean(grad_scaled * values, axis=-1, keepdims=True)
    return (scale * (grad_scaled - values * scale * scale * inner), grad_gain)


def rope_tables(length, width):
    half_width = width // 2
    inverse = ROPE_BASE ** (-(np.arange(half_width) * 2.0) / width)
    angles = np.arange(length)[None, :] * inverse[:, None]
    return (jnp.asarray(np.cos(angles), F32), jnp.asarray(np.sin(angles), F32))


def rotate(first, second, cosine, sine):
    return first * cosine - second * sine, second * cosine + first * sine


def dot(a, b, dims):
    return lax.dot_general(a, b, ((dims[0], dims[1]), ((), ())), preferred_element_type=F32)


def causal(rows):
    key = lax.broadcasted_iota(jnp.int32, (rows, rows), 0)
    query = lax.broadcasted_iota(jnp.int32, (rows, rows), 1)
    return key <= query


RING = 4
MESH_ID = pl.DeviceIdType.MESH


def whole():
    return pl.BlockSpec(memory_space=pltpu.VMEM)


def anywhere():
    return pl.BlockSpec(memory_space=pltpu.HBM)


def position():
    rank = lax.axis_index("tensor")
    return lax.div(rank, RING), lax.rem(rank, RING)


def shifted(pos, axis, by):
    moved = lax.rem(pos[axis] + (by + RING), RING) if by else pos[axis]
    return (moved, pos[1]) if axis == 0 else (pos[0], moved)


def joined(pos):
    return pos[0] * RING + pos[1]


def greet(tensor_peers, dp_peers=(), more=()):
    dp, rank = lax.axis_index("dp"), lax.axis_index("tensor")
    sem = pltpu.get_barrier_semaphore()
    peers = [(dp, p) for p in tensor_peers] + [(p, rank) for p in dp_peers] + list(more)
    for peer in peers:
        pl.semaphore_signal(sem, inc=1, device_id=peer, device_id_type=MESH_ID)
    pl.semaphore_wait(sem, len(peers))


def neighbours():
    pos = position()
    return [joined(shifted(pos, axis, by)) for axis in (0, 1) for by in (1, -1)]


def others(axis, count):
    return [lax.rem(lax.axis_index(axis) + r, count) for r in range(1, count)]


def torus_messages(half, rows):
    primary, secondary = (0, 1) if half == 0 else (1, 0)
    h, q = rows // 2, rows // 4
    full = (half * h, h)
    part = {1: (half * h, q), -1: (half * h + q, q)}
    out = []
    for d in (1, -1):
        out.append((0, ("p1", d), None, full, (0, 0), primary, d))
        out.append((0, ("s1", 0, d), None, full, (0, 0), secondary, d))
        out.append((1, ("p2", d), ("p1", d), part[d], (-d, 0), primary, d))
        for e in (1, -1):
            out.append((1, ("s1", -d, e), ("p1", d), full, (-d, 0), secondary, e))
    for e in (1, -1):
        out.append((2, ("s2", 0, e), ("s1", 0, e), part[e], (0, -e), secondary, e))
        for d in (1, -1):
            out.append((3, ("s1", ("o", d), e), ("p2", d), part[d], (2, 0), secondary, e))
            out.append((4, ("s2", d, e), ("s1", d, e), part[e], (d, -e), secondary, e))
        out.append((5, ("s2", "o", e), ("s1", ("o", e), e), part[e], (2, -e), secondary, e))
    return out


class Torus:
    COUNT = 44
    STAGES = 6

    def __init__(self, rows):
        self.rows = rows
        self.pos = position()
        self.dp = lax.axis_index("dp")
        self.messages, self.children, self.place, order, used = {}, {}, {}, [], 0
        for half in (0, 1):
            for at, (stage, key, needs, piece, offset, axis, way) in enumerate(torus_messages(half, rows)):
                key = (half, key)
                needs = None if needs is None else (half, needs)
                self.messages[key] = (len(order), stage, needs, piece, offset, axis, way)
                self.children.setdefault(needs, []).append(key)
                self.place[key] = used
                used += piece[1]
                order.append((stage, at, half, key))
        self.landing_rows = used
        self.order = [entry[3] for entry in sorted(order, key=lambda entry: entry[:3])]

    def block(self, key, pos):
        half, offset = key[0], self.messages[key][4]
        primary, secondary = (0, 1) if half == 0 else (1, 0)
        return joined(shifted(shifted(pos, primary, offset[0]), secondary, offset[1]))

    def sender(self, key):
        _, _, _, _, _, axis, way = self.messages[key]
        return shifted(self.pos, axis, -way)

    def receiver(self, key):
        _, _, _, _, _, axis, way = self.messages[key]
        return shifted(self.pos, axis, way)


class Gather(Torus):
    def __init__(self, buf, send, recv):
        self.flat = len(buf.shape) == 2
        super().__init__(buf.shape[0] // (RING * RING) if self.flat else buf.shape[1])
        self.buf, self.send, self.recv = buf, send, recv
        self.arrived = set()

    def piece(self, block, first, count):
        if self.flat:
            return self.buf.at[pl.ds(pl.multiple_of(block * self.rows + first, self.rows // 4), count)]
        return self.buf.at[block, pl.ds(first, count)]

    def copy(self, key, incoming):
        number, (first, count) = self.messages[key][0], self.messages[key][3]
        at = self.sender(key) if incoming else self.pos
        ref = self.piece(self.block(key, at), first, count)
        return pltpu.make_async_remote_copy(
            src_ref=ref, dst_ref=ref, send_sem=self.send.at[number], recv_sem=self.recv.at[number],
            device_id=(self.dp, joined(at if incoming else self.receiver(key))), device_id_type=MESH_ID,
        )

    def arrive(self, key):
        if key not in self.arrived:
            self.arrived.add(key)
            self.copy(key, True).wait_recv()

    def stage(self, number):
        for key in self.order:
            _, stage, needs, *_ = self.messages[key]
            if stage == number:
                if needs is not None:
                    self.arrive(needs)
                self.copy(key, False).start()

    def arrive_stage(self, number):
        for key in self.order:
            if self.messages[key][1] == number:
                self.arrive(key)

    def finish(self):
        for key in self.order:
            self.arrive(key)
        for key in self.order:
            self.copy(key, False).wait_send()


class Scatter(Torus):
    def __init__(self, parts, landing, send, recv):
        super().__init__(parts.shape[1])
        self.parts, self.landing, self.send, self.recv = parts, landing, send, recv

    def copy(self, key):
        number, (first, count) = self.messages[key][0], self.messages[key][3]
        at = self.sender(key)
        return pltpu.make_async_remote_copy(
            src_ref=self.parts.at[self.block(key, at), pl.ds(first, count)],
            dst_ref=self.landing.at[pl.ds(self.place[key], count)],
            send_sem=self.send.at[number], recv_sem=self.recv.at[number],
            device_id=(self.dp, joined(at)), device_id_type=MESH_ID,
        )

    def landed(self, key):
        count = self.messages[key][3][1]
        self.copy(key).wait_recv()
        return self.landing[pl.ds(self.place[key], count), :]

    def stage(self, number):
        for key in reversed(self.order):
            if self.messages[key][1] == number:
                pieces = {}
                for child in self.children.get(key, []):
                    pieces.setdefault(self.messages[child][3], []).append(child)
                for (first, count), children in pieces.items():
                    at = (self.block(children[0], self.pos), pl.ds(first, count))
                    self.parts[at] = sum((self.landed(c) for c in children), self.parts[at])
                self.copy(key).start()

    def result(self):
        out = []
        for half in (0, 1):
            children = [c for c in self.children[None] if c[0] == half]
            first, count = self.messages[children[0]][3]
            own = self.parts[joined(self.pos), pl.ds(first, count)].astype(F32)
            out.append(sum((self.landed(c).astype(F32) for c in children), own))
        return out

    def finish(self):
        for key in self.order:
            self.copy(key).wait_send()


class Exchange:
    def __init__(self, source, target, send, recv, axis="tensor", same=False):
        self.source, self.target, self.send, self.recv, self.axis, self.same = source, target, send, recv, axis, same
        self.count = target.shape[0]
        self.rank = lax.axis_index(axis)

    def device(self, to):
        if self.axis == "tensor":
            return (lax.axis_index("dp"), to)
        return (to, lax.axis_index("tensor"))

    def copy(self, r):
        to = lax.rem(self.rank + r, self.count)
        return pltpu.make_async_remote_copy(
            src_ref=self.source if self.same else self.source.at[to],
            dst_ref=self.target.at[self.rank], send_sem=self.send.at[r - 1],
            recv_sem=self.recv.at[r - 1], device_id=self.device(to), device_id_type=MESH_ID,
        )

    def start(self):
        for r in range(1, self.count):
            self.copy(r).start()

    def arrive(self):
        for r in range(1, self.count):
            origin = lax.rem(self.rank + self.count - r, self.count)
            pltpu.make_async_remote_copy(
                src_ref=self.target.at[origin], dst_ref=self.target.at[origin], send_sem=self.send.at[r - 1],
                recv_sem=self.recv.at[r - 1], device_id=self.device(origin), device_id_type=MESH_ID,
            ).wait_recv()

    def sent(self):
        for r in range(1, self.count):
            self.copy(r).wait_send()


def pair_sems(count):
    return [pltpu.SemaphoreType.DMA((count,))] * 2


def call(kernel, name, number, out_shape, in_specs, out_specs, scratch, limit, flops=0, bytes_accessed=0):
    return pl.pallas_call(
        kernel, out_shape=out_shape, in_specs=in_specs, out_specs=out_specs, scratch_shapes=scratch,
        compiler_params=pltpu.CompilerParams(collective_id=number, has_side_effects=True, vmem_limit_bytes=limit << 10),
        cost_estimate=pl.CostEstimate(flops=flops, bytes_accessed=bytes_accessed, transcendentals=0),
        name=name,
    )


def loads(pairs, sems):
    copies = [pltpu.make_async_copy(a, b, sems.at[i]) for i, (a, b) in enumerate(pairs)]
    for copy in copies:
        copy.start()
    return copies


class Replicas:
    COUNT = RING * RING - 1 + 9

    def __init__(self, own, buf, send, recv, local):
        self.own, self.buf, self.send, self.recv = own, buf, send, recv
        self.keep = pltpu.make_async_copy(own, buf.at[lax.axis_index("tensor"), :, self.columns_of(buf)], local)
        self.rank, self.dp = lax.axis_index("tensor"), lax.axis_index("dp")
        self.x, self.core = lax.div(self.dp, 2), lax.rem(self.dp, 2)
        self.blocks = buf.shape[0]
        self.share = buf.shape[2] // (2 * RING)

    @staticmethod
    def columns_of(buf):
        share = buf.shape[2] // (2 * RING)
        return pl.ds(pl.multiple_of(lax.axis_index("dp") * share, share), share)

    def member(self, dx, other):
        core = 1 - self.core if other else self.core
        return lax.rem(self.x + dx + RING, RING) * 2 + core

    def columns(self, member):
        return pl.ds(pl.multiple_of(member * self.share, self.share), self.share)

    def piece(self, member, part):
        first, count = {0: (0, self.blocks), 1: (0, self.blocks // 2), -1: (self.blocks // 2, self.blocks // 2)}[part]
        return self.buf.at[pl.ds(first, count), :, self.columns(member)]

    def copy(self, number, ref, device):
        return pltpu.make_async_remote_copy(
            src_ref=ref, dst_ref=ref, send_sem=self.send.at[number], recv_sem=self.recv.at[number],
            device_id=device, device_id_type=MESH_ID,
        )

    def first(self):
        count = self.blocks
        self.outgoing = []
        self.keep.start()
        for r in range(1, count):
            self.outgoing.append(pltpu.make_async_remote_copy(
                src_ref=self.own, dst_ref=self.buf.at[self.rank, :, self.columns(self.dp)],
                send_sem=self.send.at[r - 1], recv_sem=self.recv.at[r - 1],
                device_id=(self.dp, lax.rem(self.rank + r, count)), device_id_type=MESH_ID,
            ))
            self.outgoing[-1].start()

    def go(self, number, member, part, dx, other):
        self.outgoing.append(self.copy(self.blocks - 1 + number, self.piece(member, part), (self.member(dx, other), self.rank)))
        self.outgoing[-1].start()

    def come(self, number, member, part):
        self.copy(self.blocks - 1 + number, self.piece(member, part), (self.dp, self.rank)).wait_recv()

    def second(self):
        for r in range(1, self.blocks):
            ref = self.buf.at[lax.rem(self.rank + self.blocks - r, self.blocks), :, self.columns(self.dp)]
            self.copy(r - 1, ref, (self.dp, self.rank)).wait_recv()
        self.keep.wait()
        self.go(0, self.dp, 0, 1, False)
        self.go(1, self.dp, 0, -1, False)
        self.go(4, self.dp, 0, 0, True)

    def third(self):
        for number, way in ((0, 1), (1, -1)):
            member = self.member(-way, False)
            self.come(number, member, 0)
            self.go(2 + number, member, way, way, False)
            self.go(5 + number, member, 0, 0, True)

    def fourth(self):
        for number, way in ((0, 1), (1, -1)):
            member = self.member(2, False)
            self.come(2 + number, member, way)
            self.go(7 + number, member, way, 0, True)

    def finish(self):
        self.come(4, self.member(0, True), 0)
        for number, way in ((0, 1), (1, -1)):
            self.come(5 + number, self.member(-way, True), 0)
            self.come(7 + number, self.member(2, True), way)
        for copy in self.outgoing:
            copy.wait_send()


def near_members():
    x, core = lax.div(lax.axis_index("dp"), 2), lax.rem(lax.axis_index("dp"), 2)
    return [lax.rem(x + 1, RING) * 2 + core, lax.rem(x + RING - 1, RING) * 2 + core, x * 2 + 1 - core]


def attend(qkv, key_rows, wide_ref, log_ref, parts_ref, tokens, todo):
    length = qkv.shape[1]
    allowed = causal(Q_ROWS)
    query, value = slice(0, HD), slice(2 * HD, 3 * HD)
    for block in range(length // Q_ROWS):
        first = block * Q_ROWS
        columns = slice(first, first + Q_ROWS)
        scaled = qkv[query, columns] * ATTN_SCALE
        near = dot(key_rows[columns, :], scaled, ((1,), (0,)))
        near = jnp.where(allowed, near, -1e30)
        largest = jnp.max(near, axis=0, keepdims=True)
        if block:
            far = dot(key_rows[:first, :], scaled, ((1,), (0,)))
            largest = jnp.maximum(largest, jnp.max(far, axis=0, keepdims=True))
        near = jnp.exp(near - largest)
        total = jnp.sum(near, axis=0, keepdims=True)
        context = dot(qkv[value, columns], near.astype(BF16), ((1,), (0,)))
        if block:
            far = jnp.exp(far - largest)
            total = total + jnp.sum(far, axis=0, keepdims=True)
            context = context + dot(qkv[value, :first], far.astype(BF16), ((1,), (0,)))
        context = context / total
        wide_ref[:, columns] = context
        log_ref[:, columns] = largest + jnp.log(total)
        low = context.astype(BF16)
        for part in range(Q_ROWS // tokens):
            parts_ref[first // tokens + part] = low[:, part * tokens : (part + 1) * tokens]
        for task in todo.get(block, ()):
            task()


class RingSum:
    COUNT = 15

    def __init__(self, half, near, far, total, send, recv):
        self.half, self.near, self.far, self.total, self.send, self.recv = half, near, far, total, send, recv
        self.rank, dp = lax.axis_index("tensor"), lax.axis_index("dp")
        self.x, self.core = lax.div(dp, 2), lax.rem(dp, 2)
        self.chunk = total.shape[1] // RING if near is None else near.shape[1]
        self.outgoing = []

    def device(self, dx, other=False):
        core = 1 - self.core if other else self.core
        return (lax.rem(self.x + dx + RING, RING) * 2 + core, self.rank)

    def rows(self, dx, part=0):
        at, half = lax.rem(self.x + dx + RING, RING) * self.chunk, self.chunk // 2
        at = pl.multiple_of(at + (half if part == -1 else 0), half)
        return pl.ds(at, half if part else self.chunk)

    def copy(self, number, source, target, device):
        return pltpu.make_async_remote_copy(
            src_ref=source, dst_ref=target, send_sem=self.send.at[number], recv_sem=self.recv.at[number],
            device_id=device, device_id_type=MESH_ID,
        )

    def go(self, *args):
        self.outgoing.append(self.copy(*args))
        self.outgoing[-1].start()

    def come(self, number, target):
        self.copy(number, target, target, self.device(0, True)).wait_recv()

    def first(self):
        for i, way in ((0, 1), (1, -1)):
            self.go(i, self.half.at[self.rows(2, way)], self.far.at[i], self.device(way))

    def part(self, way, which):
        half = self.chunk // 2
        return self.near.at[0 if way == 1 else 1, pl.ds(0 if which == 1 else half, half)]

    def early(self):
        for i, way in ((0, 1), (1, -1)):
            self.go(13 + i, self.half.at[self.rows(way, -way)], self.part(way, -way), self.device(way))

    def second(self):
        for i, way in ((0, 1), (1, -1)):
            self.come(i, self.far.at[i])
            at = self.rows(way, way)
            self.half[at, :] = self.half[at, :] + self.far[i]
            self.go(2 + i, self.half.at[at], self.part(way, way), self.device(way))

    def own_sum(self):
        for i, way in ((0, 1), (1, -1)):
            self.come(13 + i, self.part(way, -way))
            self.come(2 + i, self.part(way, way))
        own = self.half[self.rows(0), :].astype(F32) + self.near[0].astype(F32) + self.near[1].astype(F32)
        return own.astype(BF16)

    def third(self):
        ref = self.total.at[self.core, self.rows(0)]
        for i, way in ((0, 1), (1, -1)):
            self.go(4 + i, ref, ref, self.device(way))
        self.go(8, ref, ref, self.device(0, True))

    def fourth(self):
        for i, way in ((0, 1), (1, -1)):
            ref = self.total.at[self.core, self.rows(-way)]
            self.come(4 + i, ref)
            part = self.total.at[self.core, self.rows(-way, way)]
            self.go(6 + i, part, part, self.device(way))
            self.go(9 + i, ref, ref, self.device(0, True))

    def fifth(self):
        for i, way in ((0, 1), (1, -1)):
            ref = self.total.at[self.core, self.rows(2, way)]
            self.come(6 + i, ref)
            self.go(11 + i, ref, ref, self.device(0, True))

    def finish(self):
        self.come(8, self.total.at[1 - self.core, self.rows(0)])
        for i, way in ((0, 1), (1, -1)):
            self.come(9 + i, self.total.at[1 - self.core, self.rows(-way)])
            self.come(11 + i, self.total.at[1 - self.core, self.rows(2, way)])
        self.sent()

    def sent(self):
        for copy in self.outgoing:
            copy.wait_send()


GROUPS = (
    ((0, 0), (0, 1), (0, 3), (1, 0), (3, 0)),
    ((1, 1), (1, 3), (3, 1), (3, 3), (2, 0), (0, 2)),
    ((2, 1), (2, 3), (1, 2), (3, 2), (2, 2)),
)
MOST = 6 * CAP
CHUNK = 32


def front_kernel(
    x_in, gain_in, gain_two_in, query_in, keyval_in, out_w_in, cot_in, cosine_in, sine_in, routes_in, router_in, gateup_in, down_in,
    normed_out, qkv_out, wide_ref, log_ref, context_ref, query_out, residual_ref,
    combined_out, chunk_out, grad_residual_ref, grad_att_ref, small_ref, grad_context_ref,
    x_ref, gain_one_ref, gain_two_ref, cosine_ref, sine_ref, own_w, local_w, pair_w, qkv, key_rows, context_parts,
    normed_ref, router_ref, routes_ref, own_cot,
    buf, weights, buf2, cot, gateup, down, out_w, pick, gate_wide, note_wide, arrived, grad_acts, hidden, grad_slots,
    acts, grad_hidden, grad_rows, landing, far, near, notes, told, own_gates, gate_parts, gate_told,
    sems_a, sems_b, sems_c, sems_d, sems_e, sems_f, pair_a, pair_b, pair_c, pair_d, pair_e, pair_f, free, local_sems, load_sems, late_sems,
):
    combined, parts = buf, weights
    (send_a, recv_a), (send_b, recv_b), (send_c, recv_c) = pair_a, pair_b, pair_c
    (send_d, recv_d), (send_e, recv_e), (send_f, recv_f) = pair_d, pair_e, pair_f
    tokens, width = x_ref.shape
    rank = lax.axis_index("tensor")
    z, y = position()
    half = HD // 2
    copies = loads(
        [
            (x_in, x_ref), (gain_in, gain_one_ref), (out_w_in, own_w.at[:HD]), (query_in, own_w.at[HD:]),
            (routes_in, routes_ref.at[rank]), (cosine_in, cosine_ref), (sine_in, sine_ref), (gain_two_in, gain_two_ref),
            (router_in, router_ref), (cot_in, own_cot),
        ],
        load_sems,
    )
    count = RING * RING
    length = count * tokens
    local_experts, ff = down.shape[0], down.shape[1]
    late = loads([(gateup_in, gateup), (down_in, down)], late_sems)
    dp = lax.axis_index("dp")
    core = lax.rem(dp, 2)
    sibling = (dp + 1 - 2 * core, rank)
    pair_copies = []
    for part in range(2):
        column = pl.multiple_of(part * KV_HEADS * HD + z * 2 * HD, 2 * HD)
        copy = pltpu.make_async_copy(keyval_in.at[:, pl.ds(column, 2 * HD)], pair_w.at[part], local_sems.at[part])
        copy.start()
        pair_copies.append(copy)
    cot_copy = pltpu.make_async_copy(cot_in, cot.at[pl.ds(pl.multiple_of(rank * tokens, tokens), tokens)], local_sems.at[2])
    cot_copy.start()
    copies[0].wait()
    copies[1].wait()
    own_rows = pl.ds(pl.multiple_of(rank * tokens, tokens), tokens)
    inputs = x_ref[...].astype(F32)
    buf[rank] = (inputs * rms_scale(inputs) * gain_one_ref[...].reshape(1, width).astype(F32)).astype(BF16)
    greet(others("tensor", RING * RING), near_members())
    main = Gather(buf, *sems_a)
    main.stage(0)
    for copy in copies[2:5]:
        copy.wait()
    share = Replicas.columns_of(weights)
    of_out = Replicas(own_w.at[pl.ds(0, HD), share], weights.at[:, pl.ds(0, HD)], *sems_b, local_sems.at[3])
    of_query = Replicas(own_w.at[pl.ds(HD, HD), share], weights.at[:, pl.ds(HD, HD)], *sems_c, local_sems.at[1])
    of_out.first()
    tell = Exchange(routes_ref.at[rank], routes_ref, *sems_f, same=True)
    tell.start()
    for copy in pair_copies + copies[5:]:
        copy.wait()
    odd = lax.rem(lax.div(rank, 2), 2)
    local_w[:HD] = own_w[HD:]
    for part in range(2):
        tall = pair_w[part].T.astype(F32)
        local_w[HD * (part + 1) : HD * (part + 2)] = jnp.where(odd == 0, tall[:HD], tall[HD:]).astype(BF16)
    ids = lax.broadcasted_iota(jnp.int32, (EXPERTS, tokens), 0)
    slot_ids = lax.broadcasted_iota(jnp.int32, (CAP, tokens), 0).astype(F32)
    before = lax.broadcasted_iota(jnp.int32, (tokens, tokens), 0) < lax.broadcasted_iota(jnp.int32, (tokens, tokens), 1)
    upper = jnp.where(before, 1.0, 0.0).astype(BF16)
    pos = main.pos

    def named_of(block):
        routes = routes_ref[block]
        hits = ids == routes[0:1]
        for k in range(1, TOP):
            hits = hits | (ids == routes[k : k + 1])
        return hits


    groups, place = [], 0
    for group in GROUPS:
        members = []
        for dz, dy in group:
            members.append((place, joined(shifted(shifted(pos, 0, dz), 1, dy))))
            place += 1
        groups.append(members)
    every = [member for members in groups for member in members]
    pairs_of = [[members[i : i + 2] for i in range(0, len(members), 2)] for members in groups]
    wide = local_experts * CAP
    pair_number = {}
    for pairs in pairs_of:
        for pair in pairs:
            pair_number[pair[0][0]] = len(pair_number)
    def make_picks(pairs):
        for pair in pairs:
            number = pair_number[pair[0][0]]
            if len(pair) == 2:
                pick[number, :wide, tokens:] = jnp.zeros((wide, tokens), BF16)
                pick[number, wide:, :tokens] = jnp.zeros((wide, tokens), BF16)
            for i, (_, block) in enumerate(pair):
                named = jnp.where(named_of(block), 1.0, 0.0)
                places = dot(named.astype(BF16), upper, ((1,), (0,)))
                for e in range(local_experts):
                    mine = ids == rank * local_experts + e
                    hit = jnp.sum(jnp.where(mine, named, 0.0), axis=0, keepdims=True)
                    at = jnp.sum(jnp.where(mine, places, 0.0), axis=0, keepdims=True)
                    at = jnp.where(hit > 0.5, at, -1.0)
                    first = i * wide + e * CAP
                    pick[number, first : first + CAP, i * tokens : (i + 1) * tokens] = jnp.where(slot_ids == at, 1.0, 0.0).astype(BF16)


    def project(dz, dy):
        block = joined(shifted(shifted(pos, 0, dz), 1, dy))
        columns = pl.ds(pl.multiple_of(block * tokens, tokens), tokens)
        made = dot(local_w[...], buf[block], ((1,), (1,)))
        cosine, sine = cosine_ref[:, columns], sine_ref[:, columns]
        rows = []
        for first in (0, HD):
            rows += rotate(made[first : first + half], made[first + half : first + HD], cosine, sine)
        rows.append(made[2 * HD :])
        qkv[:, columns] = jnp.concatenate(rows, axis=0).astype(BF16)

    project(0, 0)
    main.stage(1)
    main.stage(2)
    of_out.second()
    of_query.first()
    main.arrive_stage(0)
    for offset in ((0, 1), (0, 3), (1, 0), (3, 0)):
        project(*offset)
    tell.arrive()
    main.stage(3)
    main.stage(4)
    make_picks(pairs_of[0])
    of_out.third()
    of_query.second()
    cot_copy.wait()
    back = Gather(cot, *sems_d)
    main.arrive_stage(1)
    main.arrive_stage(2)
    for offset in ((1, 1), (1, 3), (3, 1), (3, 3), (2, 0), (0, 2)):
        project(*offset)
    main.stage(5)
    back.stage(0)
    make_picks(pairs_of[1])
    main.arrive_stage(3)
    main.arrive_stage(4)
    of_out.fourth()
    of_query.third()
    for offset in ((2, 1), (2, 3), (1, 2), (3, 2)):
        project(*offset)
    main.arrive_stage(5)
    project(2, 2)
    make_picks(pairs_of[2])
    normed_copy = pltpu.make_async_copy(buf, normed_out, local_sems.at[5])
    normed_copy.start()
    qkv_copy = pltpu.make_async_copy(qkv, qkv_out, local_sems.at[6])
    qkv_copy.start()
    key_rows[...] = qkv[HD : 2 * HD].T
    swap_context = Exchange(context_parts, context_ref, *sems_e)
    todo = {2: [lambda: back.stage(1)], 3: [lambda: back.stage(2)], 5: [of_query.fourth], 6: [lambda: back.stage(3)]}
    attend(qkv, key_rows, wide_ref, log_ref, context_parts, tokens, todo)
    swap_context.start()
    context_ref[rank] = context_parts[rank]
    main.finish()
    of_out.finish()
    of_query.finish()
    query_copy = pltpu.make_async_copy(weights.at[:, pl.ds(HD, HD)], query_out, local_sems.at[7])
    query_copy.start()
    out_copy = pltpu.make_async_copy(weights.at[:, pl.ds(0, HD)], out_w, local_sems.at[4])
    out_copy.start()
    back.stage(4)
    swap_context.arrive()
    back.stage(5)
    context = context_ref[...].reshape(HEADS * HD, tokens)
    attention = dot(context, weights[:, :HD].reshape(HEADS * HD, width), ((0,), (0,)))
    residual = x_ref[...].astype(F32) + RES_SCALE * attention
    residual_ref[...] = residual
    normed_ref[...] = (residual * rms_scale(residual) * gain_two_ref[...].reshape(1, width).astype(F32)).astype(BF16)
    buf2[own_rows, :] = normed_ref[...]
    gather = Gather(buf2, send_a, recv_a)
    gather.stage(0)
    router = router_ref[...]
    named = named_of(rank)
    logits = jnp.where(named, dot(router, normed_ref[...], ((1,), (1,))), -1e30)
    powers = jnp.where(named, jnp.exp(logits - jnp.max(logits, axis=0, keepdims=True)), 0.0)
    own_gates[...] = powers / jnp.sum(powers, axis=0, keepdims=True)
    gate_parts[...] = jnp.zeros_like(gate_parts)
    for i in range(count):
        gate_parts[i, :local_experts] = own_gates[i * local_experts : (i + 1) * local_experts]
    tell_gates = Exchange(gate_parts, gate_told, send_f, recv_f)
    tell_gates.start()
    gate_told[rank] = gate_parts[rank]

    def chosen_of(pair):
        rows = len(pair) * wide
        return pick[pair_number[pair[0][0]], :rows, : len(pair) * tokens]

    back.finish()

    def spread(made, pair, target):
        for i, (at, _) in enumerate(pair):
            for e in range(local_experts):
                first = i * wide + e * CAP
                target[e, at * CAP : (at + 1) * CAP] = made[first : first + CAP]

    def joint(ref, pair, at):
        return jnp.concatenate([ref[e, i * CAP : (i + 1) * CAP] for i in at for e in range(local_experts)], axis=0)

    for pairs in pairs_of:
        for pair in pairs:
            rows = [cot[pl.ds(pl.multiple_of(block * tokens, tokens), tokens), :] for _, block in pair]
            spread(dot(chosen_of(pair), jnp.concatenate(rows, axis=0), ((1,), (0,))).astype(BF16), pair, grad_slots)
    gather.stage(1)
    gather.stage(2)
    for copy in late:
        copy.wait()
    for e in range(local_experts):
        for first in range(0, count * CAP, 256):
            at = slice(first, first + 256)
            grad_hidden[e, at] = dot(grad_slots[e, at], down[e], ((1,), (1,))).astype(BF16)
    for copy in (normed_copy, qkv_copy, query_copy, out_copy):
        copy.wait()
    tell_gates.arrive()
    for pairs in pairs_of:
        for pair in pairs:
            for i, (at, block) in enumerate(pair):
                chosen = chosen_of(pair)[i * wide : (i + 1) * wide, i * tokens : (i + 1) * tokens].astype(F32)
                for e in range(local_experts):
                    column = jnp.sum(chosen[e * CAP : (e + 1) * CAP] * gate_told[block, e : e + 1], axis=1, keepdims=True)
                    gate_wide[e, at * CAP : (at + 1) * CAP] = jnp.broadcast_to(column, (CAP, 128))

    def work(number, between=()):
        pairs, base, rows = pairs_of[number], groups[number][0][0] * CAP, len(groups[number]) * CAP
        first = groups[number][0][0]
        for pair in pairs:
            blocks = jnp.concatenate([buf2[pl.ds(pl.multiple_of(block * tokens, tokens), tokens), :] for _, block in pair], axis=0)
            spread(dot(chosen_of(pair), blocks, ((1,), (0,))).astype(BF16), pair, arrived)

        def one(e):
            acts[:rows] = dot(arrived[e, base : base + rows], gateup[e], ((1,), (0,)))

            @pl.loop(0, rows // CHUNK)
            def _(c):
                at = pl.ds(pl.multiple_of(c * CHUNK, CHUNK), CHUNK)
                out = pl.ds(pl.multiple_of(base + c * CHUNK, CHUNK), CHUNK)
                column = gate_wide[e, out]
                note = jnp.zeros((CHUNK, 128), F32)
                for k in range(0, ff, 128):
                    gate, up = acts[at, k : k + 128], acts[at, ff + k : ff + k + 128]
                    sigmoid = 0.5 + 0.5 * jnp.tanh(0.5 * gate)
                    silu = gate * sigmoid
                    made = silu * up
                    raw = RES_SCALE * grad_hidden[e, out, k : k + 128].astype(F32)
                    note = note + made * raw
                    back = column * raw
                    hidden[e, out, k : k + 128] = (column * made).astype(BF16)
                    grad_acts[e, out, k : k + 128] = (back * up * (sigmoid + silu * (1.0 - sigmoid))).astype(BF16)
                    grad_acts[e, out, ff + k : ff + k + 128] = (back * silu).astype(BF16)
                note_wide[e, out] = note

        for e in range(local_experts):
            one(e)
            if e == 0:
                for task in between:
                    task()
    def rows_back(number):
        pairs, base, rows = pairs_of[number], groups[number][0][0] * CAP, len(groups[number]) * CAP
        first = groups[number][0][0]
        for e in range(local_experts):
            grad_rows[e, :rows] = dot(grad_acts[e, base : base + rows], gateup[e], ((1,), (1,))).astype(BF16)
        for pair in pairs:
            back = joint(grad_rows, pair, [at - first for at, _ in pair])
            made = dot(chosen_of(pair), back, ((0,), (0,))).astype(BF16)
            for i, (_, block) in enumerate(pair):
                parts[block] = made[i * tokens : (i + 1) * tokens]

    def outcome(number):
        pairs, base, rows = pairs_of[number], groups[number][0][0] * CAP, len(groups[number]) * CAP
        first = groups[number][0][0]

        @pl.loop(0, local_experts)
        def _(e):
            grad_rows[e, :rows] = dot(hidden[e, base : base + rows], down[e], ((1,), (0,))).astype(BF16)

        for pair in pairs:
            chosen = chosen_of(pair)
            made = dot(chosen, joint(grad_rows, pair, [at - first for at, _ in pair]), ((0,), (0,))).astype(BF16)
            for i, (at, block) in enumerate(pair):
                combined[block] = made[i * tokens : (i + 1) * tokens]

    def report(number):
        for pair in pairs_of[number]:
            chosen = chosen_of(pair)
            for i, (at, block) in enumerate(pair):
                for e in range(local_experts):
                    begin = i * wide + e * CAP
                    hits = chosen[begin : begin + CAP, i * tokens : (i + 1) * tokens].astype(F32)
                    column = jnp.sum(note_wide[e, at * CAP : (at + 1) * CAP], axis=1, keepdims=True)
                    notes[block, e : e + 1] = jnp.sum(hits * column, axis=0, keepdims=True)

    gather.arrive_stage(0)
    work(0, [lambda: gather.stage(3), lambda: gather.stage(4)])
    gather.arrive_stage(1)
    gather.arrive_stage(2)
    work(1, [lambda: gather.stage(5)])
    rows_back(1)
    for stage in (3, 4, 5):
        gather.arrive_stage(stage)
    work(2)
    rows_back(2)

    gather.finish()
    pl.semaphore_signal(free, inc=1, device_id=sibling, device_id_type=MESH_ID)
    scatter = Scatter(parts, landing, send_b, recv_b)
    quarter = (width // RING, ff // RING)
    chunk = sum(quarter)
    x = lax.div(dp, 2)
    gifts = []

    def rows_of(c):
        return pl.ds(pl.multiple_of(c * chunk, chunk), chunk)

    def gift(number, c):
        return pltpu.make_async_remote_copy(
            src_ref=cot.at[rows_of(c)], dst_ref=buf2.at[rows_of(c)],
            send_sem=send_d.at[number], recv_sem=recv_d.at[number], device_id=sibling, device_id_type=MESH_ID,
        )

    def made_of(e, c):
        first = pl.ds(pl.multiple_of(c * quarter[0], quarter[0]), quarter[0])
        second = pl.ds(pl.multiple_of(c * quarter[1], quarter[1]), quarter[1])
        upper_rows = dot(arrived[e, :, first], grad_acts[e], ((0,), (0,)))
        return upper_rows, RES_SCALE * dot(hidden[e, :, second], grad_slots[e], ((0,), (0,)))

    def give(number, c):
        at = c * chunk
        upper_rows, lower_rows = made_of(1 - core, c)
        cot[pl.ds(pl.multiple_of(at, quarter[1]), quarter[0]), :] = upper_rows.astype(BF16)
        cot[pl.ds(pl.multiple_of(at + quarter[0], quarter[1]), quarter[1]), :] = lower_rows.astype(BF16)
        if number == 0:
            pl.semaphore_wait(free, 1)
        gifts.append(gift(number, c))
        gifts[-1].start()

    def keep(number, c):
        upper_rows, lower_rows = made_of(core, c)
        gift(number, c).wait_recv()
        first = pl.ds(pl.multiple_of(c * chunk, quarter[1]), quarter[0])
        second = pl.ds(pl.multiple_of(c * chunk + quarter[0], quarter[1]), quarter[1])
        buf2[first, :] = (upper_rows + buf2[first, :].astype(F32)).astype(BF16)
        buf2[second, :] = (lower_rows + buf2[second, :].astype(F32)).astype(BF16)

    ring = RingSum(buf2, near, far, None, send_e, recv_e)
    order = [lax.rem(x + dx, RING) for dx in (2, 1, 3, 0)]
    give(0, order[0])
    for stage in (5, 4, 2):
        scatter.stage(stage)
    keep(0, order[0])
    ring.first()
    scatter.stage(3)
    rows_back(0)
    give(1, order[1])
    give(2, order[2])
    keep(1, order[1])
    keep(2, order[2])
    ring.early()
    scatter.stage(1)
    for number in range(3):
        report(number)
    swap = Exchange(notes, told, send_c, recv_c)
    swap.start()
    told[rank] = notes[rank]
    give(3, order[3])
    keep(3, order[3])
    ring.second()
    outcome(2)
    scatter.stage(0)
    outcome(1)
    outcome(0)
    combined_copy = pltpu.make_async_copy(combined, combined_out, local_sems.at[0])
    combined_copy.start()
    swap.arrive()
    gates = own_gates[...]
    grads = jnp.concatenate([told[i, :local_experts] for i in range(count)], axis=0)
    grad_logits = (gates * (grads - jnp.sum(gates * grads, axis=0, keepdims=True))).astype(BF16)
    normed = normed_ref[...]
    small_ref[...] = jnp.zeros_like(small_ref)
    small_ref[:EXPERTS] = dot(grad_logits, normed, ((1,), (0,)))
    from_router = dot(grad_logits, router, ((0,), (0,)))
    gain = gain_two_ref[...].reshape(1, width).astype(F32)
    middle = tokens // 2
    grad_gain = jnp.zeros((1, width), F32)
    for place, back in enumerate(scatter.result()):
        at = slice(place * middle, (place + 1) * middle)
        residual = residual_ref[at]
        scale = rms_scale(residual)
        grad_normed = from_router[at] + back
        grad_norm, part = norm_back(residual, scale, gain, grad_normed)
        grad_gain = grad_gain + part[None]
        grad_residual = own_cot[at].astype(F32) + grad_norm
        grad_residual_ref[at] = grad_residual
        grad_att_ref[at] = (RES_SCALE * grad_residual).astype(BF16)
    small_ref[EXPERTS : EXPERTS + 1] = grad_gain
    grad_context_ref[...] = dot(out_w[...].reshape(HEADS * HD, width), grad_att_ref[...], ((1,), (1,))).astype(BF16).reshape(HEADS, HD, tokens)
    scatter.finish()
    swap.sent()
    swap_context.sent()
    tell.sent()
    tell_gates.sent()
    chunk_out[...] = ring.own_sum()
    for copy in gifts:
        copy.wait_send()
    ring.sent()
    combined_copy.wait()


def front(x, gain, gain_two, w_query, w_keyval, w_out, cotangent, cosine, sine, routes, router, w_gateup, w_down):
    tokens, width = x.shape
    count = RING * RING
    length = tokens * count
    local_experts, ff = w_down.shape[:2]
    rows = count * CAP
    sem_counts = (
        Torus.COUNT, Replicas.COUNT, Replicas.COUNT, Torus.COUNT, count - 1, count - 1,
        Torus.COUNT, Torus.COUNT, count - 1, RING, RingSum.COUNT, count - 1,
    )
    pairs = len(sem_counts)

    def kernel(*refs):
        cut = len(refs) - 2 * pairs - 4
        sems = refs[cut : cut + 2 * pairs]
        front_kernel(*refs[:cut], *[sems[2 * i : 2 * i + 2] for i in range(pairs)], *refs[cut + 2 * pairs :])

    shape = jax.ShapeDtypeStruct
    vmem = pltpu.VMEM
    block = vmem((count, tokens, width), BF16)
    flat = vmem((length, width), BF16)
    note = vmem((count, 8, tokens), F32)
    semaphores = [one for n in sem_counts for one in pair_sems(n)]
    return call(
        kernel, "front", 1,
        (
            shape((count, tokens, width), BF16), shape((3 * HD, length), BF16), shape((HD, length), F32),
            shape((1, length), F32), shape((count, HD, tokens), BF16), shape((count, HD, width), BF16), shape((tokens, width), F32),
            shape((count, tokens, width), BF16), shape(((width + ff) // RING, width), BF16),
            shape((tokens, width), F32), shape((tokens, width), BF16), shape((EXPERTS + 8, width), F32),
            shape((HEADS, HD, tokens), BF16),
        ),
        [anywhere()] * 13,
        [anywhere(), anywhere(), whole(), whole(), whole(), anywhere(), whole(), anywhere()] + [whole()] * 5,
        [
            vmem(x.shape, BF16), vmem(gain.shape, BF16), vmem(gain.shape, BF16), vmem(cosine.shape, F32), vmem(sine.shape, F32),
            vmem((2 * HD, width), BF16), vmem((3 * HD, width), BF16), vmem((2, width, 2 * HD), BF16), vmem((3 * HD, length), BF16),
            vmem((length, HD), BF16), vmem((count, HD, tokens), BF16),
            vmem(x.shape, BF16), vmem(router.shape, BF16), vmem((count, *routes.shape), jnp.int32), vmem(x.shape, BF16),
            block, block, flat, flat, vmem(w_gateup.shape, BF16), vmem(w_down.shape, BF16), vmem((HEADS, HD, width), BF16),
            vmem((9, 2 * local_experts * CAP, 2 * tokens), BF16),
            vmem((local_experts, rows, 128), F32), vmem((local_experts, rows, 128), F32), vmem((local_experts, rows, width), BF16),
            vmem((local_experts, rows, 2 * ff), BF16), vmem((local_experts, rows, ff), BF16), vmem((local_experts, rows, width), BF16),
            vmem((MOST, 2 * ff), F32), vmem((local_experts, rows, ff), BF16), vmem((local_experts, MOST, width), BF16),
            vmem(((count - 1) * tokens, width), BF16), vmem((2, (width + ff) // 8, width), BF16), vmem((2, (width + ff) // 4, width), BF16),
            note, note, vmem((EXPERTS, tokens), F32), note, note,
            *semaphores, pltpu.SemaphoreType.REGULAR, pltpu.SemaphoreType.DMA((8,)), pltpu.SemaphoreType.DMA((10,)),
            pltpu.SemaphoreType.DMA((2,)),
        ],
        65400, flops=2 * 9 * rows * width * ff * local_experts + 2 * length * (3 * HD * width + length * HD * 2), bytes_accessed=40 << 20,
    )(x, gain, gain_two, w_query, w_keyval, w_out, cotangent, cosine, sine, routes, router, w_gateup, w_down)


SMALL = 384


def backward_kernel(
    qkv_in, grad_in, wide_in, log_in, cosine_in, sine_in, normed_in, context_in, grad_att_in, combined_in, residual_in, chunk_in,
    small_in, x_in, gain_in, grad_residual_in, weights_in, keyval_in,
    block_ref, input_ref, query_ref, out_ref, keyval_ref, small_out, gain_out, gateup_out, down_out,
    qkv_ref, grad_ref, wide_ref, log_ref, cosine_ref, sine_ref, normed, context_ref, grad_att_ref, combined, residual_ref,
    small_ref, x_ref, gain_ref, grad_residual_ref, query_all, keyval_all,
    grad_parts, parts_out, parts_back, grad, query_rows, key_rows, value_rows, grad_rows, grad_query, grad_key, grad_value,
    wide_grad, out_parts, out_land, combined_land, total,
    weight, give, pair_land, kv_own, mine, land, summed, small_parts, small_land, small_sum, small_dp, gather_buf,
    gain_sum, gain_dp, gain_land, back_pairs, out_mine, out_dp, out_all,
    send_a, recv_a, send_b, recv_b, send_c, recv_c, send_d, recv_d, send_e, recv_e, send_f, recv_f, send_g, recv_g,
    send_h, recv_h, send_i, recv_i, send_j, recv_j, send_k, recv_k, send_l, recv_l, send_n, recv_n,
    send_m, recv_m, send_q, recv_q, send_p, recv_p, sems, out_sems,
):
    count, _, tokens = grad_ref.shape
    length, width = count * tokens, normed.shape[1]
    dps = land.shape[0]
    rank, dp = lax.axis_index("tensor"), lax.axis_index("dp")
    order = (
        (grad_in, grad_ref), (chunk_in, total.at[lax.rem(dp, 2), pl.ds(pl.multiple_of(lax.div(dp, 2) * chunk_in.shape[0], chunk_in.shape[0]), chunk_in.shape[0])]), (small_in, small_ref), (qkv_in, qkv_ref), (context_in, context_ref),
        (grad_att_in, grad_att_ref), (combined_in, combined), (wide_in, wide_ref), (log_in, log_ref), (cosine_in, cosine_ref),
        (sine_in, sine_ref), (normed_in, normed), (residual_in, residual_ref), (x_in, x_ref), (gain_in, gain_ref),
        (grad_residual_in, grad_residual_ref), (weights_in, query_all), (keyval_in, keyval_all),
    )
    copies = loads(order, sems)
    odd = lax.rem(rank, 2)
    partner = rank + 1 - 2 * odd
    greet(others("tensor", count), others("dp", dps), [(p, partner) for p in others("dp", dps)])
    copies[0].wait()
    swap = Exchange(grad_ref, grad_parts, send_a, recv_a)
    swap.start()
    copies[1].wait()
    ring = RingSum(None, None, None, total, send_e, recv_e)
    ring.third()
    copies[2].wait()
    for i in range(count):
        small_parts[i, :, :256] = small_ref[8 * (i // 4) : 8 * (i // 4) + 8, 256 * (i % 4) : 256 * (i % 4) + 256]
        small_parts[i, :, 256:] = small_ref[32:40, 128 * (i // 2) : 128 * (i // 2) + 128]
    small = Exchange(small_parts, small_land, send_f, recv_f)
    small.start()
    small_land[rank] = small_parts[rank]
    copies[3].wait()
    query, key, value = slice(0, HD), slice(HD, 2 * HD), slice(2 * HD, 3 * HD)
    query_rows[...] = qkv_ref[query].T
    key_rows[...] = qkv_ref[key].T
    value_rows[...] = qkv_ref[value].T
    scatter = Scatter(out_parts, out_land, send_c, recv_c)
    copies[4].wait()
    copies[5].wait()
    grad_att = grad_att_ref[...]
    for part in range(count):
        out_parts[part] = dot(context_ref[part], grad_att, ((1,), (0,))).astype(BF16)
    for stage in (5, 4, 2):
        scatter.stage(stage)
    combine = Scatter(combined, combined_land, send_d, recv_d)
    grad_parts[rank] = grad_ref[rank]
    for copy in copies[7:11]:
        copy.wait()
    swap.arrive()
    for part in range(count):
        grad[:, part * tokens : (part + 1) * tokens] = grad_parts[part]
    grad_rows[...] = grad[...].T
    second_small = Exchange(small_sum.at[0], small_dp, send_g, recv_g, "dp", same=True)
    allowed = causal(Q_ROWS)
    blocks = length // Q_ROWS

    def combine_leaves():
        copies[6].wait()
        for stage in (5, 4, 2):
            combine.stage(stage)

    def small_dps():
        small.arrive()
        small_sum[0] = jnp.sum(small_land[...], axis=0)
        second_small.start()
        small_dp[dp] = small_sum[0]

    def small_again():
        second_small.arrive()
        small_sum[1] = jnp.sum(small_dp[...], axis=0)
        third.start()
        small_out[rank] = small_sum[1]

    third = Exchange(small_sum.at[1], small_out, send_h, recv_h, same=True)
    plan = {0: [combine_leaves], 2: [lambda: scatter.stage(3)], 3: [small_dps], 6: [lambda: scatter.stage(1)], 7: [ring.fourth]}
    for block in reversed(range(blocks)):
        first = block * Q_ROWS
        columns = slice(first, first + Q_ROWS)
        scaled = qkv_ref[query, columns] * ATTN_SCALE
        logs = log_ref[:, columns]
        grad_block = grad[:, columns]
        inner = jnp.sum(grad_block.astype(F32) * wide_ref[:, columns], axis=0, keepdims=True)
        wide_total = jnp.zeros((HD, Q_ROWS), F32)
        spans = [(columns, True)]
        if block:
            spans.append((slice(0, first), False))
        for keys, close in spans:
            weights = jnp.exp(dot(key_rows[keys, :], scaled, ((1,), (0,))) - logs)
            if close:
                weights = jnp.where(allowed, weights, 0.0)
            grad_weights = dot(value_rows[keys, :], grad_block, ((1,), (0,)))
            grad_scores = (weights * (grad_weights - inner)).astype(BF16)
            wide_total = wide_total + dot(qkv_ref[key, keys], grad_scores, ((1,), (0,)))
            key_part = dot(grad_scores, query_rows[columns, :], ((1,), (0,)))
            value_part = dot(weights.astype(BF16), grad_rows[columns, :], ((1,), (0,)))
            if block == blocks - 1:
                grad_key[keys, :] = key_part
                grad_value[keys, :] = value_part
            else:
                grad_key[keys, :] += key_part
                grad_value[keys, :] += value_part
        grad_query[:, columns] = wide_total * ATTN_SCALE
        for task in plan.get(blocks - 1 - block, ()):
            task()
    middle = HD // 2
    cosine, sine = cosine_ref[...], -sine_ref[...]
    for place, wide in enumerate((grad_query[...], grad_key[...].T * ATTN_SCALE)):
        rows = rotate(wide[:middle], wide[middle:], cosine, sine)
        wide_grad[place * HD : (place + 1) * HD] = jnp.concatenate(rows, axis=0).astype(BF16)
    wide_grad[2 * HD :] = grad_value[...].T.astype(BF16)
    for part in range(count):
        parts_out[part] = wide_grad[:, part * tokens : (part + 1) * tokens]
    back = Exchange(parts_out, parts_back, send_b, recv_b)
    back.start()
    parts_back[rank] = parts_out[rank]
    for copy in copies[11:]:
        copy.wait()
    weight[...] = dot(wide_grad[...], normed[...], ((1,), (0,)))
    column = width // dps
    kept = weight[pl.ds(pl.multiple_of(HD + HD * odd, HD), HD), :]
    for j, rows in enumerate((weight[:HD], kept)):
        low = rows.astype(BF16)
        for i in range(dps):
            mine[i, j * HD : (j + 1) * HD] = low[:, i * column : (i + 1) * column]
    dp_first = Exchange(mine, land, send_i, recv_i, "dp")
    dp_first.start()
    low = weight[pl.ds(pl.multiple_of(HD + HD * (1 - odd), HD), HD), :].astype(BF16)
    for i in range(dps):
        give[i] = low[:, i * column : (i + 1) * column]

    def across(r):
        to = lax.rem(dp + r, dps)
        return pltpu.make_async_remote_copy(
            src_ref=give.at[to], dst_ref=pair_land.at[dp], send_sem=send_p.at[r], recv_sem=recv_p.at[r],
            device_id=(to, partner), device_id_type=MESH_ID,
        )

    def across_here(r):
        at = pair_land.at[lax.rem(dp + dps - r, dps)]
        return pltpu.make_async_remote_copy(
            src_ref=at, dst_ref=at, send_sem=send_p.at[r], recv_sem=recv_p.at[r],
            device_id=(dp, partner), device_id_type=MESH_ID,
        )

    for r in range(dps):
        across(r).start()
    land[dp] = mine[dp]
    scatter.stage(0)
    small_again()
    combine.stage(3)
    out_sum = jnp.concatenate(scatter.result(), axis=0).astype(BF16)
    for i in range(dps):
        out_mine[i] = out_sum[:, i * column : (i + 1) * column]
    out_first = Exchange(out_mine, out_dp, send_m, recv_m, "dp")

    back.arrive()
    share = HEADS // KV_HEADS
    for head in range(KV_HEADS):
        for part in range(2):
            at = slice((part + 1) * HD, (part + 2) * HD)
            both = sum(parts_back[head * share + i, at].astype(F32) for i in range(share))
            back_pairs[part * KV_HEADS + head] = both.astype(BF16)
    queries_back = parts_back[:, :HD].reshape(HEADS * HD, tokens)
    grad_normed = dot(queries_back, query_all[...].reshape(HEADS * HD, width), ((0,), (0,)))
    grad_normed = grad_normed + dot(back_pairs[...].reshape(2 * KV_HEADS * HD, tokens), keyval_all[...], ((0,), (1,)))
    inputs = x_ref[...].astype(F32)
    grad_norm, grad_gain = norm_back(inputs, rms_scale(inputs), gain_ref[...].reshape(1, width).astype(F32), grad_normed)
    input_ref[...] = grad_residual_ref[...] + grad_norm
    grad_gain = grad_gain[None]
    for i in range(gain_sum.shape[1]):
        gain_sum[0, i : i + 1] = grad_gain[:, 128 * i : 128 * i + 128]

    dp_first.arrive()
    for r in range(dps):
        across_here(r).wait_recv()
    both = jnp.sum(land[...].astype(F32), axis=0)
    kv_own[...] = (both[HD:] + jnp.sum(pair_land[...].astype(F32), axis=0)).astype(BF16)
    replicas = Replicas(kv_own, gather_buf, send_n, recv_n, out_sems.at[0])
    replicas.first()
    summed[dp] = both[:HD].astype(BF16)
    dp_second = Exchange(summed.at[dp], summed, send_j, recv_j, "dp", same=True)
    dp_second.start()
    gain_first = Exchange(gain_sum.at[0], gain_dp, send_k, recv_k, "dp", same=True)
    gain_first.start()
    gain_dp[dp] = gain_sum[0]
    out_first.start()
    out_dp[dp] = out_mine[dp]
    ring.fifth()
    combine.stage(1)
    replicas.second()
    gain_first.arrive()
    gain_sum[1] = jnp.sum(gain_dp[...], axis=0)
    gain_second = Exchange(gain_sum.at[1], gain_land, send_l, recv_l, same=True)
    gain_second.start()
    gain_land[rank] = gain_sum[1]
    ring.finish()
    outs = []
    per = chunk_in.shape[0]
    for c in range(RING):
        down_rows = per - width // RING
        outs.append(pltpu.make_async_copy(total.at[:, pl.ds(c * per, width // RING)], gateup_out.at[:, pl.ds(c * (width // RING), width // RING)], out_sems.at[1 + c]))
        outs.append(pltpu.make_async_copy(total.at[:, pl.ds(c * per + width // RING, down_rows)], down_out.at[:, pl.ds(c * down_rows, down_rows)], out_sems.at[1 + RING + c]))
    for copy in outs:
        copy.start()
    out_first.arrive()
    out_all[dp] = jnp.sum(out_dp[...].astype(F32), axis=0).astype(BF16)
    out_second = Exchange(out_all.at[dp], out_all, send_q, recv_q, "dp", same=True)
    out_second.start()
    dp_second.arrive()
    for i in range(dps):
        query_ref[:, i * column : (i + 1) * column] = summed[i]
    combine.stage(0)
    replicas.third()
    replicas.fourth()
    rows = block_ref.shape[0] // 2
    for place, value_half in enumerate(combine.result()):
        at = slice(place * rows, (place + 1) * rows)
        block_ref[at] = (residual_ref[at] + RES_SCALE * value_half).astype(BF16)
    out_second.arrive()
    for i in range(dps):
        out_ref[:, i * column : (i + 1) * column] = out_all[i]
    third.arrive()
    gain_second.arrive()
    gain_out[...] = jnp.sum(gain_land[...], axis=0)
    replicas.finish()
    for i in range(count):
        base = (i % 2) * KV_HEADS * HD + (i // 2) * HD
        keyval_ref[base : base + HD, :] = gather_buf[i]
    for r in range(dps):
        across(r).wait_send()
    for each in (swap, back, small, second_small, third, dp_first, dp_second, gain_first, gain_second, out_first, out_second):
        each.sent()
    scatter.finish()
    combine.finish()
    for copy in outs:
        copy.wait()


def backward(
    qkv, grad_context, wide, logs, cosine, sine, normed, context, grad_att, combined, residual, chunk, small,
    x, gain, grad_residual, weights, w_keyval, dps,
):
    count, _, tokens = grad_context.shape
    length, width = normed.shape
    shape = jax.ShapeDtypeStruct
    vmem = pltpu.VMEM
    low = vmem((length, HD), BF16)
    wide_rows = vmem((length, HD), F32)
    column = width // dps
    rows = RING * chunk.shape[0]
    small_shape, gain_shape = (8, SMALL), (8, 128)
    operands = (
        qkv, grad_context, wide, logs, cosine, sine, normed, context, grad_att, combined, residual, chunk, small,
        x, gain, grad_residual, weights, w_keyval,
    )
    held = [vmem(o.shape, o.dtype) for o in operands]
    held[16] = vmem((count, HD, width), BF16)
    del held[11]
    three = vmem((dps, 2 * HD, column), BF16)
    return call(
        backward_kernel, "backward", 4,
        (
            shape((tokens, width), BF16), shape((tokens, width), F32), shape((HD, width), BF16), shape((HD, width), BF16),
            shape((count * HD, width), BF16), shape((count, *small_shape), F32), shape(gain_shape, F32),
            shape((2, width, width), BF16), shape((2, rows - width, width), BF16),
        ),
        [anywhere()] * len(operands), [whole()] * 7 + [anywhere()] * 2,
        [
            *held,
            vmem((count, HD, tokens), BF16), vmem(qkv_parts(count, tokens), BF16), vmem(qkv_parts(count, tokens), BF16),
            vmem((HD, length), BF16), low, low, low, low, vmem((HD, length), F32), wide_rows, wide_rows,
            vmem((3 * HD, length), BF16), vmem((count, HD, width), BF16), vmem(((count - 1) * HD, width), BF16),
            vmem(((count - 1) * tokens, width), BF16),
            vmem((2, rows, width), BF16),
            vmem((3 * HD, width), F32), vmem((dps, HD, column), BF16), vmem((dps, HD, column), BF16), vmem((HD, column), BF16),
            three, three, vmem((dps, HD, column), BF16),
            vmem((count, *small_shape), F32), vmem((count, *small_shape), F32), vmem((2, *small_shape), F32),
            vmem((dps, *small_shape), F32), vmem((count, HD, width), BF16),
            vmem((2, *gain_shape), F32), vmem((dps, *gain_shape), F32), vmem((count, *gain_shape), F32), vmem((2 * KV_HEADS, HD, tokens), BF16), *([vmem((dps, HD, column), BF16)] * 3),
            *pair_sems(count - 1), *pair_sems(count - 1), *pair_sems(Torus.COUNT), *pair_sems(Torus.COUNT),
            *pair_sems(RingSum.COUNT), *pair_sems(count - 1), *pair_sems(dps - 1), *pair_sems(count - 1),
            *pair_sems(dps - 1), *pair_sems(dps - 1), *pair_sems(dps - 1), *pair_sems(count - 1),
            *pair_sems(Replicas.COUNT), *pair_sems(dps - 1), *pair_sems(dps - 1), *pair_sems(dps),
            pltpu.SemaphoreType.DMA((len(operands),)), pltpu.SemaphoreType.DMA((1 + 2 * RING,)),
        ],
        65400, flops=2 * length * length * HD * 5, bytes_accessed=30 << 20,
    )(*operands)


def qkv_parts(count, tokens):
    return (count, 3 * HD, tokens)


def polish_kernel(
    gateup_ref, down_ref, keyval_ref, query_ref, out_ref, block_ref, input_ref, small_ref, gain_ref,
    gateup_out, down_out, keyval_out, query_out, out_out, block_out, input_out, router_out, gain_two_out, gain_one_out,
):
    gateup_out[...] = gateup_ref[...].astype(F32)
    down_out[...] = down_ref[...].astype(F32)
    keyval_out[...] = keyval_ref[...].T.astype(F32)

    @pl.when(pl.program_id(0) == 0)
    def _():
        query_out[...] = query_ref[...].astype(F32)
        out_out[...] = out_ref[...].astype(F32)
        block_out[...] = block_ref[...]
        input_out[...] = input_ref[...]
        for i in range(small_ref.shape[0]):
            router_out[8 * (i // 4) : 8 * (i // 4) + 8, 256 * (i % 4) : 256 * (i % 4) + 256] = small_ref[i, :, :256]
        for i in range(gain_two_out.shape[0]):
            gain_two_out[i : i + 1] = small_ref[2 * i, :1, 256:]
        gain_one_out[...] = gain_ref[...]


def polish(gateup, down, keyval, query, out, block, grad_input, small, gain):
    steps = 4
    experts_here, width, wide = gateup.shape
    ff = down.shape[1]
    per = steps // experts_here
    pairs = keyval.shape[0]
    shape = jax.ShapeDtypeStruct
    gateup_spec = pl.BlockSpec((1, width // per, wide), lambda i: (i // per, i % per, 0))
    down_spec = pl.BlockSpec((1, ff // per, width), lambda i: (i // per, i % per, 0))

    def once(dims):
        return pl.BlockSpec(dims, lambda i: (0,) * len(dims))

    rest = [query.shape, out.shape, block.shape, grad_input.shape]
    return pl.pallas_call(
        polish_kernel, grid=(steps,),
        out_shape=(
            shape(gateup.shape, F32), shape(down.shape, F32), shape((width, pairs), F32), shape(query.shape, F32),
            shape(out.shape, F32), shape(block.shape, BF16), shape(grad_input.shape, F32), shape((EXPERTS, width), F32),
            shape(gain.shape, F32), shape(gain.shape, F32),
        ),
        in_specs=[
            gateup_spec, down_spec, pl.BlockSpec((pairs, width // steps), lambda i: (0, i)),
            *[once(dims) for dims in rest], once(small.shape), once(gain.shape),
        ],
        out_specs=[
            gateup_spec, down_spec, pl.BlockSpec((width // steps, pairs), lambda i: (i, 0)),
            *[once(dims) for dims in rest], once((EXPERTS, width)), once(gain.shape), once(gain.shape),
        ],
        compiler_params=pltpu.CompilerParams(vmem_limit_bytes=65400 << 10),
        name="polish",
    )(gateup, down, keyval, query, out, block, grad_input, small, gain)


def shards(
    block_input, attn_gain, w_query, w_keyval, w_out, ffn_gain, w_router, w_gateup, w_down, routes, cotangent,
):
    tokens, width = block_input.shape
    length = tokens * lax.axis_size("tensor")
    cosine, sine = rope_tables(length, HD)
    (
        normed_one_all, qkv, wide_out, logs, context, query_all, residual, combined, chunk, grad_residual, grad_attention, small,
        grad_context,
    ) = front(
        block_input, attn_gain, ffn_gain, w_query.T, w_keyval, w_out, cotangent, cosine, sine, routes.T, w_router.T, w_gateup, w_down
    )
    block_out, grad_input, grad_query_w, grad_w_out, grad_keyval, small, gain_one, grad_w_gateup, grad_w_down = backward(
        qkv, grad_context, wide_out, logs, cosine, sine, normed_one_all.reshape(length, width), context, grad_attention,
        combined, residual, chunk, small, block_input, attn_gain, grad_residual, query_all, w_keyval, lax.axis_size("dp"),
    )
    grad_w_gateup, grad_w_down, grad_keyval, grad_query_w, grad_w_out, block_out, grad_input, routers, gain_two, gain_one = polish(
        grad_w_gateup, grad_w_down, grad_keyval, grad_query_w, grad_w_out, block_out, grad_input, small, gain_one
    )
    return (
        block_out,
        grad_input,
        gain_one.reshape(width),
        grad_query_w.T,
        grad_keyval,
        grad_w_out,
        gain_two.reshape(width),
        routers.T,
        grad_w_gateup,
        grad_w_down,
    )


def solution(mesh):
    rows = P(("dp", "tensor"), None)
    in_specs = (
        rows, P(), P(None, "tensor"), P(), P("tensor", None), P(), P(),
        P("tensor", None, None), P("tensor", None, None), rows, rows,
    )
    out_specs = (
        rows, rows, P(), P(None, "tensor"), P(), P("tensor", None), P(), P(),
        P("tensor", None, None), P("tensor", None, None),
    )
    return jax.shard_map(shards, mesh=mesh, in_specs=in_specs, out_specs=out_specs, check_vma=False)
```

```python
import jax
import jax.numpy as jnp
import numpy as np
from jax import lax
from jax.experimental import pallas as pl
from jax.experimental.pallas import tpu as pltpu
from jax.sharding import PartitionSpec as P

HEADS = 16
KV_HEADS = 8
HD = 64
EXPERTS = 32
TOP = 8
CAP = 64
ATTN_SCALE = 0.015625
RES_SCALE = 0.22
EPSILON = 1e-06
ROPE_BASE = 10000.0
F32 = jnp.float32
BF16 = jnp.bfloat16
Q_ROWS = 256


def rms_scale(values):
    return lax.rsqrt(jnp.mean(values * values, axis=-1, keepdims=True) + EPSILON)


def norm_back(values, scale, gain, grad_normed):
    grad_scaled = grad_normed * gain
    grad_gain = jnp.sum(grad_normed * values * scale, axis=0)
    inner = jnp.mean(grad_scaled * values, axis=-1, keepdims=True)
    return (scale * (grad_scaled - values * scale * scale * inner), grad_gain)


def rope_tables(length, width):
    half_width = width // 2
    inverse = ROPE_BASE ** (-(np.arange(half_width) * 2.0) / width)
    angles = np.arange(length)[None, :] * inverse[:, None]
    return (jnp.asarray(np.cos(angles), F32), jnp.asarray(np.sin(angles), F32))


def rotate(first, second, cosine, sine):
    return first * cosine - second * sine, second * cosine + first * sine


def dot(a, b, dims):
    return lax.dot_general(a, b, ((dims[0], dims[1]), ((), ())), preferred_element_type=F32)


def causal(rows):
    key = lax.broadcasted_iota(jnp.int32, (rows, rows), 0)
    query = lax.broadcasted_iota(jnp.int32, (rows, rows), 1)
    return key <= query


RING = 4
MESH_ID = pl.DeviceIdType.MESH


def whole():
    return pl.BlockSpec(memory_space=pltpu.VMEM)


def anywhere():
    return pl.BlockSpec(memory_space=pltpu.HBM)


def position():
    rank = lax.axis_index("tensor")
    return lax.div(rank, RING), lax.rem(rank, RING)


def shifted(pos, axis, by):
    moved = lax.rem(pos[axis] + (by + RING), RING) if by else pos[axis]
    return (moved, pos[1]) if axis == 0 else (pos[0], moved)


def joined(pos):
    return pos[0] * RING + pos[1]


def greet(tensor_peers, dp_peers=(), more=()):
    dp, rank = lax.axis_index("dp"), lax.axis_index("tensor")
    sem = pltpu.get_barrier_semaphore()
    peers = [(dp, p) for p in tensor_peers] + [(p, rank) for p in dp_peers] + list(more)
    for peer in peers:
        pl.semaphore_signal(sem, inc=1, device_id=peer, device_id_type=MESH_ID)
    pl.semaphore_wait(sem, len(peers))


def neighbours():
    pos = position()
    return [joined(shifted(pos, axis, by)) for axis in (0, 1) for by in (1, -1)]


def others(axis, count):
    return [lax.rem(lax.axis_index(axis) + r, count) for r in range(1, count)]


def torus_messages(half, rows):
    primary, secondary = (0, 1) if half == 0 else (1, 0)
    h, q = rows // 2, rows // 4
    full = (half * h, h)
    part = {1: (half * h, q), -1: (half * h + q, q)}
    out = []
    for d in (1, -1):
        out.append((0, ("p1", d), None, full, (0, 0), primary, d))
        out.append((0, ("s1", 0, d), None, full, (0, 0), secondary, d))
        out.append((1, ("p2", d), ("p1", d), part[d], (-d, 0), primary, d))
        for e in (1, -1):
            out.append((1, ("s1", -d, e), ("p1", d), full, (-d, 0), secondary, e))
    for e in (1, -1):
        out.append((2, ("s2", 0, e), ("s1", 0, e), part[e], (0, -e), secondary, e))
        for d in (1, -1):
            out.append((3, ("s1", ("o", d), e), ("p2", d), part[d], (2, 0), secondary, e))
            out.append((4, ("s2", d, e), ("s1", d, e), part[e], (d, -e), secondary, e))
        out.append((5, ("s2", "o", e), ("s1", ("o", e), e), part[e], (2, -e), secondary, e))
    return out


class Torus:
    COUNT = 44
    STAGES = 6

    def __init__(self, rows):
        self.rows = rows
        self.pos = position()
        self.dp = lax.axis_index("dp")
        self.messages, self.children, self.place, order, used = {}, {}, {}, [], 0
        for half in (0, 1):
            for at, (stage, key, needs, piece, offset, axis, way) in enumerate(torus_messages(half, rows)):
                key = (half, key)
                needs = None if needs is None else (half, needs)
                self.messages[key] = (len(order), stage, needs, piece, offset, axis, way)
                self.children.setdefault(needs, []).append(key)
                self.place[key] = used
                used += piece[1]
                order.append((stage, at, half, key))
        self.landing_rows = used
        self.order = [entry[3] for entry in sorted(order, key=lambda entry: entry[:3])]

    def block(self, key, pos):
        half, offset = key[0], self.messages[key][4]
        primary, secondary = (0, 1) if half == 0 else (1, 0)
        return joined(shifted(shifted(pos, primary, offset[0]), secondary, offset[1]))

    def sender(self, key):
        _, _, _, _, _, axis, way = self.messages[key]
        return shifted(self.pos, axis, -way)

    def receiver(self, key):
        _, _, _, _, _, axis, way = self.messages[key]
        return shifted(self.pos, axis, way)


class Gather(Torus):
    def __init__(self, buf, send, recv):
        self.flat = len(buf.shape) == 2
        super().__init__(buf.shape[0] // (RING * RING) if self.flat else buf.shape[1])
        self.buf, self.send, self.recv = buf, send, recv
        self.arrived = set()

    def piece(self, block, first, count):
        if self.flat:
            return self.buf.at[pl.ds(pl.multiple_of(block * self.rows + first, self.rows // 4), count)]
        return self.buf.at[block, pl.ds(first, count)]

    def copy(self, key, incoming):
        number, (first, count) = self.messages[key][0], self.messages[key][3]
        at = self.sender(key) if incoming else self.pos
        ref = self.piece(self.block(key, at), first, count)
        return pltpu.make_async_remote_copy(
            src_ref=ref, dst_ref=ref, send_sem=self.send.at[number], recv_sem=self.recv.at[number],
            device_id=(self.dp, joined(at if incoming else self.receiver(key))), device_id_type=MESH_ID,
        )

    def arrive(self, key):
        if key not in self.arrived:
            self.arrived.add(key)
            self.copy(key, True).wait_recv()

    def stage(self, number):
        for key in self.order:
            _, stage, needs, *_ = self.messages[key]
            if stage == number:
                if needs is not None:
                    self.arrive(needs)
                self.copy(key, False).start()

    def arrive_stage(self, number):
        for key in self.order:
            if self.messages[key][1] == number:
                self.arrive(key)

    def finish(self):
        for key in self.order:
            self.arrive(key)
        for key in self.order:
            self.copy(key, False).wait_send()


class Scatter(Torus):
    def __init__(self, parts, landing, send, recv):
        super().__init__(parts.shape[1])
        self.parts, self.landing, self.send, self.recv = parts, landing, send, recv

    def copy(self, key):
        number, (first, count) = self.messages[key][0], self.messages[key][3]
        at = self.sender(key)
        return pltpu.make_async_remote_copy(
            src_ref=self.parts.at[self.block(key, at), pl.ds(first, count)],
            dst_ref=self.landing.at[pl.ds(self.place[key], count)],
            send_sem=self.send.at[number], recv_sem=self.recv.at[number],
            device_id=(self.dp, joined(at)), device_id_type=MESH_ID,
        )

    def landed(self, key):
        count = self.messages[key][3][1]
        self.copy(key).wait_recv()
        return self.landing[pl.ds(self.place[key], count), :]

    def stage(self, number):
        for key in reversed(self.order):
            if self.messages[key][1] == number:
                pieces = {}
                for child in self.children.get(key, []):
                    pieces.setdefault(self.messages[child][3], []).append(child)
                for (first, count), children in pieces.items():
                    at = (self.block(children[0], self.pos), pl.ds(first, count))
                    self.parts[at] = sum((self.landed(c) for c in children), self.parts[at])
                self.copy(key).start()

    def result(self):
        out = []
        for half in (0, 1):
            children = [c for c in self.children[None] if c[0] == half]
            first, count = self.messages[children[0]][3]
            own = self.parts[joined(self.pos), pl.ds(first, count)].astype(F32)
            out.append(sum((self.landed(c).astype(F32) for c in children), own))
        return out

    def finish(self):
        for key in self.order:
            self.copy(key).wait_send()


class Exchange:
    def __init__(self, source, target, send, recv, axis="tensor", same=False):
        self.source, self.target, self.send, self.recv, self.axis, self.same = source, target, send, recv, axis, same
        self.count = target.shape[0]
        self.rank = lax.axis_index(axis)

    def device(self, to):
        if self.axis == "tensor":
            return (lax.axis_index("dp"), to)
        return (to, lax.axis_index("tensor"))

    def copy(self, r):
        to = lax.rem(self.rank + r, self.count)
        return pltpu.make_async_remote_copy(
            src_ref=self.source if self.same else self.source.at[to],
            dst_ref=self.target.at[self.rank], send_sem=self.send.at[r - 1],
            recv_sem=self.recv.at[r - 1], device_id=self.device(to), device_id_type=MESH_ID,
        )

    def start(self):
        for r in range(1, self.count):
            self.copy(r).start()

    def arrive(self):
        for r in range(1, self.count):
            origin = lax.rem(self.rank + self.count - r, self.count)
            pltpu.make_async_remote_copy(
                src_ref=self.target.at[origin], dst_ref=self.target.at[origin], send_sem=self.send.at[r - 1],
                recv_sem=self.recv.at[r - 1], device_id=self.device(origin), device_id_type=MESH_ID,
            ).wait_recv()

    def sent(self):
        for r in range(1, self.count):
            self.copy(r).wait_send()


def pair_sems(count):
    return [pltpu.SemaphoreType.DMA((count,))] * 2


def call(kernel, name, number, out_shape, in_specs, out_specs, scratch, limit, flops=0, bytes_accessed=0):
    return pl.pallas_call(
        kernel, out_shape=out_shape, in_specs=in_specs, out_specs=out_specs, scratch_shapes=scratch,
        compiler_params=pltpu.CompilerParams(collective_id=number, has_side_effects=True, vmem_limit_bytes=limit << 10),
        cost_estimate=pl.CostEstimate(flops=flops, bytes_accessed=bytes_accessed, transcendentals=0),
        name=name,
    )


def loads(pairs, sems):
    copies = [pltpu.make_async_copy(a, b, sems.at[i]) for i, (a, b) in enumerate(pairs)]
    for copy in copies:
        copy.start()
    return copies


class Replicas:
    COUNT = RING * RING - 1 + 9

    def __init__(self, own, buf, send, recv, local):
        self.own, self.buf, self.send, self.recv = own, buf, send, recv
        self.keep = pltpu.make_async_copy(own, buf.at[lax.axis_index("tensor"), :, self.columns_of(buf)], local)
        self.rank, self.dp = lax.axis_index("tensor"), lax.axis_index("dp")
        self.x, self.core = lax.div(self.dp, 2), lax.rem(self.dp, 2)
        self.blocks = buf.shape[0]
        self.share = buf.shape[2] // (2 * RING)

    @staticmethod
    def columns_of(buf):
        share = buf.shape[2] // (2 * RING)
        return pl.ds(pl.multiple_of(lax.axis_index("dp") * share, share), share)

    def member(self, dx, other):
        core = 1 - self.core if other else self.core
        return lax.rem(self.x + dx + RING, RING) * 2 + core

    def columns(self, member):
        return pl.ds(pl.multiple_of(member * self.share, self.share), self.share)

    def piece(self, member, part):
        first, count = {0: (0, self.blocks), 1: (0, self.blocks // 2), -1: (self.blocks // 2, self.blocks // 2)}[part]
        return self.buf.at[pl.ds(first, count), :, self.columns(member)]

    def copy(self, number, ref, device):
        return pltpu.make_async_remote_copy(
            src_ref=ref, dst_ref=ref, send_sem=self.send.at[number], recv_sem=self.recv.at[number],
            device_id=device, device_id_type=MESH_ID,
        )

    def first(self):
        count = self.blocks
        self.outgoing = []
        self.keep.start()
        for r in range(1, count):
            self.outgoing.append(pltpu.make_async_remote_copy(
                src_ref=self.own, dst_ref=self.buf.at[self.rank, :, self.columns(self.dp)],
                send_sem=self.send.at[r - 1], recv_sem=self.recv.at[r - 1],
                device_id=(self.dp, lax.rem(self.rank + r, count)), device_id_type=MESH_ID,
            ))
            self.outgoing[-1].start()

    def go(self, number, member, part, dx, other):
        self.outgoing.append(self.copy(self.blocks - 1 + number, self.piece(member, part), (self.member(dx, other), self.rank)))
        self.outgoing[-1].start()

    def come(self, number, member, part):
        self.copy(self.blocks - 1 + number, self.piece(member, part), (self.dp, self.rank)).wait_recv()

    def second(self):
        for r in range(1, self.blocks):
            ref = self.buf.at[lax.rem(self.rank + self.blocks - r, self.blocks), :, self.columns(self.dp)]
            self.copy(r - 1, ref, (self.dp, self.rank)).wait_recv()
        self.keep.wait()
        self.go(0, self.dp, 0, 1, False)
        self.go(1, self.dp, 0, -1, False)
        self.go(4, self.dp, 0, 0, True)

    def third(self):
        for number, way in ((0, 1), (1, -1)):
            member = self.member(-way, False)
            self.come(number, member, 0)
            self.go(2 + number, member, way, way, False)
            self.go(5 + number, member, 0, 0, True)

    def fourth(self):
        for number, way in ((0, 1), (1, -1)):
            member = self.member(2, False)
            self.come(2 + number, member, way)
            self.go(7 + number, member, way, 0, True)

    def finish(self):
        self.come(4, self.member(0, True), 0)
        for number, way in ((0, 1), (1, -1)):
            self.come(5 + number, self.member(-way, True), 0)
            self.come(7 + number, self.member(2, True), way)
        for copy in self.outgoing:
            copy.wait_send()


def near_members():
    x, core = lax.div(lax.axis_index("dp"), 2), lax.rem(lax.axis_index("dp"), 2)
    return [lax.rem(x + 1, RING) * 2 + core, lax.rem(x + RING - 1, RING) * 2 + core, x * 2 + 1 - core]


def attend(qkv, key_rows, wide_ref, log_ref, parts_ref, tokens, todo):
    length = qkv.shape[1]
    allowed = causal(Q_ROWS)
    query, value = slice(0, HD), slice(2 * HD, 3 * HD)
    for block in range(length // Q_ROWS):
        first = block * Q_ROWS
        columns = slice(first, first + Q_ROWS)
        scaled = qkv[query, columns] * ATTN_SCALE
        near = dot(key_rows[columns, :], scaled, ((1,), (0,)))
        near = jnp.where(allowed, near, -1e30)
        largest = jnp.max(near, axis=0, keepdims=True)
        if block:
            far = dot(key_rows[:first, :], scaled, ((1,), (0,)))
            largest = jnp.maximum(largest, jnp.max(far, axis=0, keepdims=True))
        near = jnp.exp(near - largest)
        total = jnp.sum(near, axis=0, keepdims=True)
        context = dot(qkv[value, columns], near.astype(BF16), ((1,), (0,)))
        if block:
            far = jnp.exp(far - largest)
            total = total + jnp.sum(far, axis=0, keepdims=True)
            context = context + dot(qkv[value, :first], far.astype(BF16), ((1,), (0,)))
        context = context / total
        wide_ref[:, columns] = context
        log_ref[:, columns] = largest + jnp.log(total)
        low = context.astype(BF16)
        for part in range(Q_ROWS // tokens):
            parts_ref[first // tokens + part] = low[:, part * tokens : (part + 1) * tokens]
        for task in todo.get(block, ()):
            task()


class RingSum:
    COUNT = 15

    def __init__(self, half, near, far, total, send, recv):
        self.half, self.near, self.far, self.total, self.send, self.recv = half, near, far, total, send, recv
        self.rank, dp = lax.axis_index("tensor"), lax.axis_index("dp")
        self.x, self.core = lax.div(dp, 2), lax.rem(dp, 2)
        self.chunk = total.shape[1] // RING if near is None else near.shape[1]
        self.outgoing = []

    def device(self, dx, other=False):
        core = 1 - self.core if other else self.core
        return (lax.rem(self.x + dx + RING, RING) * 2 + core, self.rank)

    def rows(self, dx, part=0):
        at, half = lax.rem(self.x + dx + RING, RING) * self.chunk, self.chunk // 2
        at = pl.multiple_of(at + (half if part == -1 else 0), half)
        return pl.ds(at, half if part else self.chunk)

    def copy(self, number, source, target, device):
        return pltpu.make_async_remote_copy(
            src_ref=source, dst_ref=target, send_sem=self.send.at[number], recv_sem=self.recv.at[number],
            device_id=device, device_id_type=MESH_ID,
        )

    def go(self, *args):
        self.outgoing.append(self.copy(*args))
        self.outgoing[-1].start()

    def come(self, number, target):
        self.copy(number, target, target, self.device(0, True)).wait_recv()

    def first(self):
        for i, way in ((0, 1), (1, -1)):
            self.go(i, self.half.at[self.rows(2, way)], self.far.at[i], self.device(way))

    def part(self, way, which):
        half = self.chunk // 2
        return self.near.at[0 if way == 1 else 1, pl.ds(0 if which == 1 else half, half)]

    def early(self):
        for i, way in ((0, 1), (1, -1)):
            self.go(13 + i, self.half.at[self.rows(way, -way)], self.part(way, -way), self.device(way))

    def second(self):
        for i, way in ((0, 1), (1, -1)):
            self.come(i, self.far.at[i])
            at = self.rows(way, way)
            self.half[at, :] = self.half[at, :] + self.far[i]
            self.go(2 + i, self.half.at[at], self.part(way, way), self.device(way))

    def own_sum(self):
        for i, way in ((0, 1), (1, -1)):
            self.come(13 + i, self.part(way, -way))
            self.come(2 + i, self.part(way, way))
        own = self.half[self.rows(0), :].astype(F32) + self.near[0].astype(F32) + self.near[1].astype(F32)
        return own.astype(BF16)

    def third(self):
        ref = self.total.at[self.core, self.rows(0)]
        for i, way in ((0, 1), (1, -1)):
            self.go(4 + i, ref, ref, self.device(way))
        self.go(8, ref, ref, self.device(0, True))

    def fourth(self):
        for i, way in ((0, 1), (1, -1)):
            ref = self.total.at[self.core, self.rows(-way)]
            self.come(4 + i, ref)
            part = self.total.at[self.core, self.rows(-way, way)]
            self.go(6 + i, part, part, self.device(way))
            self.go(9 + i, ref, ref, self.device(0, True))

    def fifth(self):
        for i, way in ((0, 1), (1, -1)):
            ref = self.total.at[self.core, self.rows(2, way)]
            self.come(6 + i, ref)
            self.go(11 + i, ref, ref, self.device(0, True))

    def finish(self):
        self.come(8, self.total.at[1 - self.core, self.rows(0)])
        for i, way in ((0, 1), (1, -1)):
            self.come(9 + i, self.total.at[1 - self.core, self.rows(-way)])
            self.come(11 + i, self.total.at[1 - self.core, self.rows(2, way)])
        self.sent()

    def sent(self):
        for copy in self.outgoing:
            copy.wait_send()


GROUPS = (
    ((0, 0), (0, 1), (0, 3), (1, 0), (3, 0)),
    ((1, 1), (1, 3), (3, 1), (3, 3), (2, 0), (0, 2)),
    ((2, 1), (2, 3), (1, 2), (3, 2), (2, 2)),
)
MOST = 6 * CAP
CHUNK = 32


def front_kernel(
    x_in, gain_in, gain_two_in, query_in, keyval_in, out_w_in, cot_in, cosine_in, sine_in, routes_in, router_in, gateup_in, down_in,
    normed_out, qkv_out, wide_ref, log_ref, context_ref, query_out, residual_ref,
    combined_out, chunk_out, grad_residual_ref, grad_att_ref, small_ref, grad_context_ref,
    x_ref, gain_one_ref, gain_two_ref, cosine_ref, sine_ref, own_w, local_w, pair_w, qkv, key_rows, context_parts,
    normed_ref, router_ref, routes_ref, own_cot,
    buf, weights, buf2, cot, gateup, down, out_w, pick, gate_wide, note_wide, arrived, grad_acts, hidden, grad_slots,
    acts, grad_hidden, grad_rows, landing, far, near, notes, told, own_gates, gate_parts, gate_told,
    sems_a, sems_b, sems_c, sems_d, sems_e, sems_f, pair_a, pair_b, pair_c, pair_d, pair_e, pair_f, free, local_sems, load_sems, late_sems,
):
    combined, parts = buf, weights
    (send_a, recv_a), (send_b, recv_b), (send_c, recv_c) = pair_a, pair_b, pair_c
    (send_d, recv_d), (send_e, recv_e), (send_f, recv_f) = pair_d, pair_e, pair_f
    tokens, width = x_ref.shape
    rank = lax.axis_index("tensor")
    z, y = position()
    half = HD // 2
    copies = loads(
        [
            (x_in, x_ref), (gain_in, gain_one_ref), (out_w_in, own_w.at[:HD]), (query_in, own_w.at[HD:]),
            (routes_in, routes_ref.at[rank]), (cosine_in, cosine_ref), (sine_in, sine_ref), (gain_two_in, gain_two_ref),
            (router_in, router_ref), (cot_in, own_cot),
        ],
        load_sems,
    )
    count = RING * RING
    length = count * tokens
    local_experts, ff = down.shape[0], down.shape[1]
    late = loads([(gateup_in, gateup), (down_in, down)], late_sems)
    dp = lax.axis_index("dp")
    core = lax.rem(dp, 2)
    sibling = (dp + 1 - 2 * core, rank)
    pair_copies = []
    for part in range(2):
        column = pl.multiple_of(part * KV_HEADS * HD + z * 2 * HD, 2 * HD)
        copy = pltpu.make_async_copy(keyval_in.at[:, pl.ds(column, 2 * HD)], pair_w.at[part], local_sems.at[part])
        copy.start()
        pair_copies.append(copy)
    cot_copy = pltpu.make_async_copy(cot_in, cot.at[pl.ds(pl.multiple_of(rank * tokens, tokens), tokens)], local_sems.at[2])
    cot_copy.start()
    copies[0].wait()
    copies[1].wait()
    own_rows = pl.ds(pl.multiple_of(rank * tokens, tokens), tokens)
    inputs = x_ref[...].astype(F32)
    buf[rank] = (inputs * rms_scale(inputs) * gain_one_ref[...].reshape(1, width).astype(F32)).astype(BF16)
    greet(others("tensor", RING * RING), near_members())
    main = Gather(buf, *sems_a)
    main.stage(0)
    for copy in copies[2:5]:
        copy.wait()
    share = Replicas.columns_of(weights)
    of_out = Replicas(own_w.at[pl.ds(0, HD), share], weights.at[:, pl.ds(0, HD)], *sems_b, local_sems.at[3])
    of_query = Replicas(own_w.at[pl.ds(HD, HD), share], weights.at[:, pl.ds(HD, HD)], *sems_c, local_sems.at[1])
    of_out.first()
    tell = Exchange(routes_ref.at[rank], routes_ref, *sems_f, same=True)
    tell.start()
    for copy in pair_copies + copies[5:]:
        copy.wait()
    odd = lax.rem(lax.div(rank, 2), 2)
    local_w[:HD] = own_w[HD:]
    for part in range(2):
        tall = pair_w[part].T.astype(F32)
        local_w[HD * (part + 1) : HD * (part + 2)] = jnp.where(odd == 0, tall[:HD], tall[HD:]).astype(BF16)
    ids = lax.broadcasted_iota(jnp.int32, (EXPERTS, tokens), 0)
    slot_ids = lax.broadcasted_iota(jnp.int32, (CAP, tokens), 0).astype(F32)
    before = lax.broadcasted_iota(jnp.int32, (tokens, tokens), 0) < lax.broadcasted_iota(jnp.int32, (tokens, tokens), 1)
    upper = jnp.where(before, 1.0, 0.0).astype(BF16)
    pos = main.pos

    def named_of(block):
        routes = routes_ref[block]
        hits = ids == routes[0:1]
        for k in range(1, TOP):
            hits = hits | (ids == routes[k : k + 1])
        return hits


    groups, place = [], 0
    for group in GROUPS:
        members = []
        for dz, dy in group:
            members.append((place, joined(shifted(shifted(pos, 0, dz), 1, dy))))
            place += 1
        groups.append(members)
    every = [member for members in groups for member in members]
    pairs_of = [[members[i : i + 2] for i in range(0, len(members), 2)] for members in groups]
    wide = local_experts * CAP
    pair_number = {}
    for pairs in pairs_of:
        for pair in pairs:
            pair_number[pair[0][0]] = len(pair_number)
    def make_picks(pairs):
        for pair in pairs:
            number = pair_number[pair[0][0]]
            if len(pair) == 2:
                pick[number, :wide, tokens:] = jnp.zeros((wide, tokens), BF16)
                pick[number, wide:, :tokens] = jnp.zeros((wide, tokens), BF16)
            for i, (_, block) in enumerate(pair):
                named = jnp.where(named_of(block), 1.0, 0.0)
                places = dot(named.astype(BF16), upper, ((1,), (0,)))
                for e in range(local_experts):
                    mine = ids == rank * local_experts + e
                    hit = jnp.sum(jnp.where(mine, named, 0.0), axis=0, keepdims=True)
                    at = jnp.sum(jnp.where(mine, places, 0.0), axis=0, keepdims=True)
                    at = jnp.where(hit > 0.5, at, -1.0)
                    first = i * wide + e * CAP
                    pick[number, first : first + CAP, i * tokens : (i + 1) * tokens] = jnp.where(slot_ids == at, 1.0, 0.0).astype(BF16)


    def project(dz, dy):
        block = joined(shifted(shifted(pos, 0, dz), 1, dy))
        columns = pl.ds(pl.multiple_of(block * tokens, tokens), tokens)
        made = dot(local_w[...], buf[block], ((1,), (1,)))
        cosine, sine = cosine_ref[:, columns], sine_ref[:, columns]
        rows = []
        for first in (0, HD):
            rows += rotate(made[first : first + half], made[first + half : first + HD], cosine, sine)
        rows.append(made[2 * HD :])
        qkv[:, columns] = jnp.concatenate(rows, axis=0).astype(BF16)

    project(0, 0)
    main.stage(1)
    main.stage(2)
    of_out.second()
    of_query.first()
    main.arrive_stage(0)
    for offset in ((0, 1), (0, 3), (1, 0), (3, 0)):
        project(*offset)
    tell.arrive()
    main.stage(3)
    main.stage(4)
    make_picks(pairs_of[0])
    of_out.third()
    of_query.second()
    cot_copy.wait()
    back = Gather(cot, *sems_d)
    main.arrive_stage(1)
    main.arrive_stage(2)
    for offset in ((1, 1), (1, 3), (3, 1), (3, 3), (2, 0), (0, 2)):
        project(*offset)
    main.stage(5)
    back.stage(0)
    make_picks(pairs_of[1])
    main.arrive_stage(3)
    main.arrive_stage(4)
    of_out.fourth()
    of_query.third()
    for offset in ((2, 1), (2, 3), (1, 2), (3, 2)):
        project(*offset)
    main.arrive_stage(5)
    project(2, 2)
    make_picks(pairs_of[2])
    normed_copy = pltpu.make_async_copy(buf, normed_out, local_sems.at[5])
    normed_copy.start()
    qkv_copy = pltpu.make_async_copy(qkv, qkv_out, local_sems.at[6])
    qkv_copy.start()
    key_rows[...] = qkv[HD : 2 * HD].T
    swap_context = Exchange(context_parts, context_ref, *sems_e)
    todo = {2: [lambda: back.stage(1)], 3: [lambda: back.stage(2)], 5: [of_query.fourth], 6: [lambda: back.stage(3)]}
    attend(qkv, key_rows, wide_ref, log_ref, context_parts, tokens, todo)
    swap_context.start()
    context_ref[rank] = context_parts[rank]
    main.finish()
    of_out.finish()
    of_query.finish()
    query_copy = pltpu.make_async_copy(weights.at[:, pl.ds(HD, HD)], query_out, local_sems.at[7])
    query_copy.start()
    out_copy = pltpu.make_async_copy(weights.at[:, pl.ds(0, HD)], out_w, local_sems.at[4])
    out_copy.start()
    back.stage(4)
    swap_context.arrive()
    back.stage(5)
    context = context_ref[...].reshape(HEADS * HD, tokens)
    attention = dot(context, weights[:, :HD].reshape(HEADS * HD, width), ((0,), (0,)))
    residual = x_ref[...].astype(F32) + RES_SCALE * attention
    residual_ref[...] = residual
    normed_ref[...] = (residual * rms_scale(residual) * gain_two_ref[...].reshape(1, width).astype(F32)).astype(BF16)
    buf2[own_rows, :] = normed_ref[...]
    gather = Gather(buf2, send_a, recv_a)
    gather.stage(0)
    router = router_ref[...]
    named = named_of(rank)
    logits = jnp.where(named, dot(router, normed_ref[...], ((1,), (1,))), -1e30)
    powers = jnp.where(named, jnp.exp(logits - jnp.max(logits, axis=0, keepdims=True)), 0.0)
    own_gates[...] = powers / jnp.sum(powers, axis=0, keepdims=True)
    gate_parts[...] = jnp.zeros_like(gate_parts)
    for i in range(count):
        gate_parts[i, :local_experts] = own_gates[i * local_experts : (i + 1) * local_experts]
    tell_gates = Exchange(gate_parts, gate_told, send_f, recv_f)
    tell_gates.start()
    gate_told[rank] = gate_parts[rank]

    def chosen_of(pair):
        rows = len(pair) * wide
        return pick[pair_number[pair[0][0]], :rows, : len(pair) * tokens]

    back.finish()

    def spread(made, pair, target):
        for i, (at, _) in enumerate(pair):
            for e in range(local_experts):
                first = i * wide + e * CAP
                target[e, at * CAP : (at + 1) * CAP] = made[first : first + CAP]

    def joint(ref, pair, at):
        return jnp.concatenate([ref[e, i * CAP : (i + 1) * CAP] for i in at for e in range(local_experts)], axis=0)

    for pairs in pairs_of:
        for pair in pairs:
            rows = [cot[pl.ds(pl.multiple_of(block * tokens, tokens), tokens), :] for _, block in pair]
            spread(dot(chosen_of(pair), jnp.concatenate(rows, axis=0), ((1,), (0,))).astype(BF16), pair, grad_slots)
    gather.stage(1)
    gather.stage(2)
    for copy in late:
        copy.wait()
    for e in range(local_experts):
        for first in range(0, count * CAP, 256):
            at = slice(first, first + 256)
            grad_hidden[e, at] = dot(grad_slots[e, at], down[e], ((1,), (1,))).astype(BF16)
    for copy in (normed_copy, qkv_copy, query_copy, out_copy):
        copy.wait()
    tell_gates.arrive()
    for pairs in pairs_of:
        for pair in pairs:
            for i, (at, block) in enumerate(pair):
                chosen = chosen_of(pair)[i * wide : (i + 1) * wide, i * tokens : (i + 1) * tokens].astype(F32)
                for e in range(local_experts):
                    column = jnp.sum(chosen[e * CAP : (e + 1) * CAP] * gate_told[block, e : e + 1], axis=1, keepdims=True)
                    gate_wide[e, at * CAP : (at + 1) * CAP] = jnp.broadcast_to(column, (CAP, 128))

    def work(number, between=()):
        pairs, base, rows = pairs_of[number], groups[number][0][0] * CAP, len(groups[number]) * CAP
        first = groups[number][0][0]
        for pair in pairs:
            blocks = jnp.concatenate([buf2[pl.ds(pl.multiple_of(block * tokens, tokens), tokens), :] for _, block in pair], axis=0)
            spread(dot(chosen_of(pair), blocks, ((1,), (0,))).astype(BF16), pair, arrived)

        def one(e):
            acts[:rows] = dot(arrived[e, base : base + rows], gateup[e], ((1,), (0,)))

            @pl.loop(0, rows // CHUNK)
            def _(c):
                at = pl.ds(pl.multiple_of(c * CHUNK, CHUNK), CHUNK)
                out = pl.ds(pl.multiple_of(base + c * CHUNK, CHUNK), CHUNK)
                column = gate_wide[e, out]
                note = jnp.zeros((CHUNK, 128), F32)
                for k in range(0, ff, 128):
                    gate, up = acts[at, k : k + 128], acts[at, ff + k : ff + k + 128]
                    sigmoid = 0.5 + 0.5 * jnp.tanh(0.5 * gate)
                    silu = gate * sigmoid
                    made = silu * up
                    raw = RES_SCALE * grad_hidden[e, out, k : k + 128].astype(F32)
                    note = note + made * raw
                    back = column * raw
                    hidden[e, out, k : k + 128] = (column * made).astype(BF16)
                    grad_acts[e, out, k : k + 128] = (back * up * (sigmoid + silu * (1.0 - sigmoid))).astype(BF16)
                    grad_acts[e, out, ff + k : ff + k + 128] = (back * silu).astype(BF16)
                note_wide[e, out] = note

        for e in range(local_experts):
            one(e)
            if e == 0:
                for task in between:
                    task()
    def rows_back(number):
        pairs, base, rows = pairs_of[number], groups[number][0][0] * CAP, len(groups[number]) * CAP
        first = groups[number][0][0]
        for e in range(local_experts):
            grad_rows[e, :rows] = dot(grad_acts[e, base : base + rows], gateup[e], ((1,), (1,))).astype(BF16)
        for pair in pairs:
            back = joint(grad_rows, pair, [at - first for at, _ in pair])
            made = dot(chosen_of(pair), back, ((0,), (0,))).astype(BF16)
            for i, (_, block) in enumerate(pair):
                parts[block] = made[i * tokens : (i + 1) * tokens]

    def outcome(number):
        pairs, base, rows = pairs_of[number], groups[number][0][0] * CAP, len(groups[number]) * CAP
        first = groups[number][0][0]

        @pl.loop(0, local_experts)
        def _(e):
            grad_rows[e, :rows] = dot(hidden[e, base : base + rows], down[e], ((1,), (0,))).astype(BF16)

        for pair in pairs:
            chosen = chosen_of(pair)
            made = dot(chosen, joint(grad_rows, pair, [at - first for at, _ in pair]), ((0,), (0,))).astype(BF16)
            for i, (at, block) in enumerate(pair):
                combined[block] = made[i * tokens : (i + 1) * tokens]

    def report(number):
        for pair in pairs_of[number]:
            chosen = chosen_of(pair)
            for i, (at, block) in enumerate(pair):
                for e in range(local_experts):
                    begin = i * wide + e * CAP
                    hits = chosen[begin : begin + CAP, i * tokens : (i + 1) * tokens].astype(F32)
                    column = jnp.sum(note_wide[e, at * CAP : (at + 1) * CAP], axis=1, keepdims=True)
                    notes[block, e : e + 1] = jnp.sum(hits * column, axis=0, keepdims=True)

    gather.arrive_stage(0)
    work(0, [lambda: gather.stage(3), lambda: gather.stage(4)])
    gather.arrive_stage(1)
    gather.arrive_stage(2)
    work(1, [lambda: gather.stage(5)])
    rows_back(1)
    for stage in (3, 4, 5):
        gather.arrive_stage(stage)
    work(2)
    rows_back(2)

    gather.finish()
    pl.semaphore_signal(free, inc=1, device_id=sibling, device_id_type=MESH_ID)
    scatter = Scatter(parts, landing, send_b, recv_b)
    quarter = (width // RING, ff // RING)
    chunk = sum(quarter)
    x = lax.div(dp, 2)
    gifts = []

    def rows_of(c):
        return pl.ds(pl.multiple_of(c * chunk, chunk), chunk)

    def gift(number, c):
        return pltpu.make_async_remote_copy(
            src_ref=cot.at[rows_of(c)], dst_ref=buf2.at[rows_of(c)],
            send_sem=send_d.at[number], recv_sem=recv_d.at[number], device_id=sibling, device_id_type=MESH_ID,
        )

    def made_of(e, c):
        first = pl.ds(pl.multiple_of(c * quarter[0], quarter[0]), quarter[0])
        second = pl.ds(pl.multiple_of(c * quarter[1], quarter[1]), quarter[1])
        upper_rows = dot(arrived[e, :, first], grad_acts[e], ((0,), (0,)))
        return upper_rows, RES_SCALE * dot(hidden[e, :, second], grad_slots[e], ((0,), (0,)))

    def give(number, c):
        at = c * chunk
        upper_rows, lower_rows = made_of(1 - core, c)
        cot[pl.ds(pl.multiple_of(at, quarter[1]), quarter[0]), :] = upper_rows.astype(BF16)
        cot[pl.ds(pl.multiple_of(at + quarter[0], quarter[1]), quarter[1]), :] = lower_rows.astype(BF16)
        if number == 0:
            pl.semaphore_wait(free, 1)
        gifts.append(gift(number, c))
        gifts[-1].start()

    def keep(number, c):
        upper_rows, lower_rows = made_of(core, c)
        gift(number, c).wait_recv()
        first = pl.ds(pl.multiple_of(c * chunk, quarter[1]), quarter[0])
        second = pl.ds(pl.multiple_of(c * chunk + quarter[0], quarter[1]), quarter[1])
        buf2[first, :] = (upper_rows + buf2[first, :].astype(F32)).astype(BF16)
        buf2[second, :] = (lower_rows + buf2[second, :].astype(F32)).astype(BF16)

    ring = RingSum(buf2, near, far, None, send_e, recv_e)
    order = [lax.rem(x + dx, RING) for dx in (2, 1, 3, 0)]
    give(0, order[0])
    for stage in (5, 4, 2):
        scatter.stage(stage)
    keep(0, order[0])
    ring.first()
    scatter.stage(3)
    give(1, order[1])
    give(2, order[2])
    keep(1, order[1])
    keep(2, order[2])
    ring.early()
    scatter.stage(1)
    for number in range(3):
        report(number)
    swap = Exchange(notes, told, send_c, recv_c)
    swap.start()
    told[rank] = notes[rank]
    give(3, order[3])
    keep(3, order[3])
    ring.second()
    rows_back(0)
    scatter.stage(0)
    outcome(2)
    outcome(1)
    outcome(0)
    combined_copy = pltpu.make_async_copy(combined, combined_out, local_sems.at[0])
    combined_copy.start()
    swap.arrive()
    gates = own_gates[...]
    grads = jnp.concatenate([told[i, :local_experts] for i in range(count)], axis=0)
    grad_logits = (gates * (grads - jnp.sum(gates * grads, axis=0, keepdims=True))).astype(BF16)
    normed = normed_ref[...]
    small_ref[...] = jnp.zeros_like(small_ref)
    small_ref[:EXPERTS] = dot(grad_logits, normed, ((1,), (0,)))
    from_router = dot(grad_logits, router, ((0,), (0,)))
    gain = gain_two_ref[...].reshape(1, width).astype(F32)
    middle = tokens // 2
    grad_gain = jnp.zeros((1, width), F32)
    for place, back in enumerate(scatter.result()):
        at = slice(place * middle, (place + 1) * middle)
        residual = residual_ref[at]
        scale = rms_scale(residual)
        grad_normed = from_router[at] + back
        grad_norm, part = norm_back(residual, scale, gain, grad_normed)
        grad_gain = grad_gain + part[None]
        grad_residual = own_cot[at].astype(F32) + grad_norm
        grad_residual_ref[at] = grad_residual
        grad_att_ref[at] = (RES_SCALE * grad_residual).astype(BF16)
    small_ref[EXPERTS : EXPERTS + 1] = grad_gain
    grad_context_ref[...] = dot(out_w[...].reshape(HEADS * HD, width), grad_att_ref[...], ((1,), (1,))).astype(BF16).reshape(HEADS, HD, tokens)
    scatter.finish()
    swap.sent()
    swap_context.sent()
    tell.sent()
    tell_gates.sent()
    chunk_out[...] = ring.own_sum()
    for copy in gifts:
        copy.wait_send()
    ring.sent()
    combined_copy.wait()


def front(x, gain, gain_two, w_query, w_keyval, w_out, cotangent, cosine, sine, routes, router, w_gateup, w_down):
    tokens, width = x.shape
    count = RING * RING
    length = tokens * count
    local_experts, ff = w_down.shape[:2]
    rows = count * CAP
    sem_counts = (
        Torus.COUNT, Replicas.COUNT, Replicas.COUNT, Torus.COUNT, count - 1, count - 1,
        Torus.COUNT, Torus.COUNT, count - 1, RING, RingSum.COUNT, count - 1,
    )
    pairs = len(sem_counts)

    def kernel(*refs):
        cut = len(refs) - 2 * pairs - 4
        sems = refs[cut : cut + 2 * pairs]
        front_kernel(*refs[:cut], *[sems[2 * i : 2 * i + 2] for i in range(pairs)], *refs[cut + 2 * pairs :])

    shape = jax.ShapeDtypeStruct
    vmem = pltpu.VMEM
    block = vmem((count, tokens, width), BF16)
    flat = vmem((length, width), BF16)
    note = vmem((count, 8, tokens), F32)
    semaphores = [one for n in sem_counts for one in pair_sems(n)]
    return call(
        kernel, "front", 1,
        (
            shape((count, tokens, width), BF16), shape((3 * HD, length), BF16), shape((HD, length), F32),
            shape((1, length), F32), shape((count, HD, tokens), BF16), shape((count, HD, width), BF16), shape((tokens, width), F32),
            shape((count, tokens, width), BF16), shape(((width + ff) // RING, width), BF16),
            shape((tokens, width), F32), shape((tokens, width), BF16), shape((EXPERTS + 8, width), F32),
            shape((HEADS, HD, tokens), BF16),
        ),
        [anywhere()] * 13,
        [anywhere(), anywhere(), whole(), whole(), whole(), anywhere(), whole(), anywhere()] + [whole()] * 5,
        [
            vmem(x.shape, BF16), vmem(gain.shape, BF16), vmem(gain.shape, BF16), vmem(cosine.shape, F32), vmem(sine.shape, F32),
            vmem((2 * HD, width), BF16), vmem((3 * HD, width), BF16), vmem((2, width, 2 * HD), BF16), vmem((3 * HD, length), BF16),
            vmem((length, HD), BF16), vmem((count, HD, tokens), BF16),
            vmem(x.shape, BF16), vmem(router.shape, BF16), vmem((count, *routes.shape), jnp.int32), vmem(x.shape, BF16),
            block, block, flat, flat, vmem(w_gateup.shape, BF16), vmem(w_down.shape, BF16), vmem((HEADS, HD, width), BF16),
            vmem((9, 2 * local_experts * CAP, 2 * tokens), BF16),
            vmem((local_experts, rows, 128), F32), vmem((local_experts, rows, 128), F32), vmem((local_experts, rows, width), BF16),
            vmem((local_experts, rows, 2 * ff), BF16), vmem((local_experts, rows, ff), BF16), vmem((local_experts, rows, width), BF16),
            vmem((MOST, 2 * ff), F32), vmem((local_experts, rows, ff), BF16), vmem((local_experts, MOST, width), BF16),
            vmem(((count - 1) * tokens, width), BF16), vmem((2, (width + ff) // 8, width), BF16), vmem((2, (width + ff) // 4, width), BF16),
            note, note, vmem((EXPERTS, tokens), F32), note, note,
            *semaphores, pltpu.SemaphoreType.REGULAR, pltpu.SemaphoreType.DMA((8,)), pltpu.SemaphoreType.DMA((10,)),
            pltpu.SemaphoreType.DMA((2,)),
        ],
        65400, flops=2 * 9 * rows * width * ff * local_experts + 2 * length * (3 * HD * width + length * HD * 2), bytes_accessed=40 << 20,
    )(x, gain, gain_two, w_query, w_keyval, w_out, cotangent, cosine, sine, routes, router, w_gateup, w_down)


SMALL = 384


def backward_kernel(
    qkv_in, grad_in, wide_in, log_in, cosine_in, sine_in, normed_in, context_in, grad_att_in, combined_in, residual_in, chunk_in,
    small_in, x_in, gain_in, grad_residual_in, weights_in, keyval_in,
    block_ref, input_ref, query_ref, out_ref, keyval_ref, small_out, gain_out, gateup_out, down_out,
    qkv_ref, grad_ref, wide_ref, log_ref, cosine_ref, sine_ref, normed, context_ref, grad_att_ref, combined, residual_ref,
    small_ref, x_ref, gain_ref, grad_residual_ref, query_all, keyval_all,
    grad_parts, parts_out, parts_back, grad, query_rows, key_rows, value_rows, grad_rows, grad_query, grad_key, grad_value,
    wide_grad, out_parts, out_land, combined_land, total,
    weight, give, pair_land, kv_own, mine, land, summed, small_parts, small_land, small_sum, small_dp, gather_buf,
    gain_sum, gain_dp, gain_land, back_pairs, out_mine, out_dp, out_all,
    send_a, recv_a, send_b, recv_b, send_c, recv_c, send_d, recv_d, send_e, recv_e, send_f, recv_f, send_g, recv_g,
    send_h, recv_h, send_i, recv_i, send_j, recv_j, send_k, recv_k, send_l, recv_l, send_n, recv_n,
    send_m, recv_m, send_q, recv_q, send_p, recv_p, sems, out_sems,
):
    count, _, tokens = grad_ref.shape
    length, width = count * tokens, normed.shape[1]
    dps = land.shape[0]
    rank, dp = lax.axis_index("tensor"), lax.axis_index("dp")
    order = (
        (grad_in, grad_ref), (chunk_in, total.at[lax.rem(dp, 2), pl.ds(pl.multiple_of(lax.div(dp, 2) * chunk_in.shape[0], chunk_in.shape[0]), chunk_in.shape[0])]), (small_in, small_ref), (qkv_in, qkv_ref), (context_in, context_ref),
        (grad_att_in, grad_att_ref), (combined_in, combined), (wide_in, wide_ref), (log_in, log_ref), (cosine_in, cosine_ref),
        (sine_in, sine_ref), (normed_in, normed), (residual_in, residual_ref), (x_in, x_ref), (gain_in, gain_ref),
        (grad_residual_in, grad_residual_ref), (weights_in, query_all), (keyval_in, keyval_all),
    )
    copies = loads(order, sems)
    odd = lax.rem(rank, 2)
    partner = rank + 1 - 2 * odd
    greet(others("tensor", count), others("dp", dps), [(p, partner) for p in others("dp", dps)])
    copies[0].wait()
    swap = Exchange(grad_ref, grad_parts, send_a, recv_a)
    swap.start()
    copies[1].wait()
    ring = RingSum(None, None, None, total, send_e, recv_e)
    ring.third()
    copies[2].wait()
    for i in range(count):
        small_parts[i, :, :256] = small_ref[8 * (i // 4) : 8 * (i // 4) + 8, 256 * (i % 4) : 256 * (i % 4) + 256]
        small_parts[i, :, 256:] = small_ref[32:40, 128 * (i // 2) : 128 * (i // 2) + 128]
    small = Exchange(small_parts, small_land, send_f, recv_f)
    small.start()
    small_land[rank] = small_parts[rank]
    copies[3].wait()
    query, key, value = slice(0, HD), slice(HD, 2 * HD), slice(2 * HD, 3 * HD)
    query_rows[...] = qkv_ref[query].T
    key_rows[...] = qkv_ref[key].T
    value_rows[...] = qkv_ref[value].T
    scatter = Scatter(out_parts, out_land, send_c, recv_c)
    copies[4].wait()
    copies[5].wait()
    grad_att = grad_att_ref[...]
    for part in range(count):
        out_parts[part] = dot(context_ref[part], grad_att, ((1,), (0,))).astype(BF16)
    for stage in (5, 4, 2):
        scatter.stage(stage)
    combine = Scatter(combined, combined_land, send_d, recv_d)
    grad_parts[rank] = grad_ref[rank]
    for copy in copies[7:11]:
        copy.wait()
    swap.arrive()
    for part in range(count):
        grad[:, part * tokens : (part + 1) * tokens] = grad_parts[part]
    grad_rows[...] = grad[...].T
    second_small = Exchange(small_sum.at[0], small_dp, send_g, recv_g, "dp", same=True)
    allowed = causal(Q_ROWS)
    blocks = length // Q_ROWS

    def combine_leaves():
        copies[6].wait()
        for stage in (5, 4, 2):
            combine.stage(stage)

    def small_dps():
        small.arrive()
        small_sum[0] = jnp.sum(small_land[...], axis=0)
        second_small.start()
        small_dp[dp] = small_sum[0]

    def small_again():
        second_small.arrive()
        small_sum[1] = jnp.sum(small_dp[...], axis=0)
        third.start()
        small_out[rank] = small_sum[1]

    third = Exchange(small_sum.at[1], small_out, send_h, recv_h, same=True)
    plan = {0: [combine_leaves], 2: [lambda: scatter.stage(3)], 3: [small_dps], 6: [lambda: scatter.stage(1)], 7: [ring.fourth]}
    for block in reversed(range(blocks)):
        first = block * Q_ROWS
        columns = slice(first, first + Q_ROWS)
        scaled = qkv_ref[query, columns] * ATTN_SCALE
        logs = log_ref[:, columns]
        grad_block = grad[:, columns]
        inner = jnp.sum(grad_block.astype(F32) * wide_ref[:, columns], axis=0, keepdims=True)
        wide_total = jnp.zeros((HD, Q_ROWS), F32)
        spans = [(columns, True)]
        if block:
            spans.append((slice(0, first), False))
        for keys, close in spans:
            weights = jnp.exp(dot(key_rows[keys, :], scaled, ((1,), (0,))) - logs)
            if close:
                weights = jnp.where(allowed, weights, 0.0)
            grad_weights = dot(value_rows[keys, :], grad_block, ((1,), (0,)))
            grad_scores = (weights * (grad_weights - inner)).astype(BF16)
            wide_total = wide_total + dot(qkv_ref[key, keys], grad_scores, ((1,), (0,)))
            key_part = dot(grad_scores, query_rows[columns, :], ((1,), (0,)))
            value_part = dot(weights.astype(BF16), grad_rows[columns, :], ((1,), (0,)))
            if block == blocks - 1:
                grad_key[keys, :] = key_part
                grad_value[keys, :] = value_part
            else:
                grad_key[keys, :] += key_part
                grad_value[keys, :] += value_part
        grad_query[:, columns] = wide_total * ATTN_SCALE
        for task in plan.get(blocks - 1 - block, ()):
            task()
    middle = HD // 2
    cosine, sine = cosine_ref[...], -sine_ref[...]
    for place, wide in enumerate((grad_query[...], grad_key[...].T * ATTN_SCALE)):
        rows = rotate(wide[:middle], wide[middle:], cosine, sine)
        wide_grad[place * HD : (place + 1) * HD] = jnp.concatenate(rows, axis=0).astype(BF16)
    wide_grad[2 * HD :] = grad_value[...].T.astype(BF16)
    for part in range(count):
        parts_out[part] = wide_grad[:, part * tokens : (part + 1) * tokens]
    back = Exchange(parts_out, parts_back, send_b, recv_b)
    back.start()
    parts_back[rank] = parts_out[rank]
    for copy in copies[11:]:
        copy.wait()
    weight[...] = dot(wide_grad[...], normed[...], ((1,), (0,)))
    column = width // dps
    kept = weight[pl.ds(pl.multiple_of(HD + HD * odd, HD), HD), :]
    for j, rows in enumerate((weight[:HD], kept)):
        low = rows.astype(BF16)
        for i in range(dps):
            mine[i, j * HD : (j + 1) * HD] = low[:, i * column : (i + 1) * column]
    dp_first = Exchange(mine, land, send_i, recv_i, "dp")
    dp_first.start()
    low = weight[pl.ds(pl.multiple_of(HD + HD * (1 - odd), HD), HD), :].astype(BF16)
    for i in range(dps):
        give[i] = low[:, i * column : (i + 1) * column]

    def across(r):
        to = lax.rem(dp + r, dps)
        return pltpu.make_async_remote_copy(
            src_ref=give.at[to], dst_ref=pair_land.at[dp], send_sem=send_p.at[r], recv_sem=recv_p.at[r],
            device_id=(to, partner), device_id_type=MESH_ID,
        )

    def across_here(r):
        at = pair_land.at[lax.rem(dp + dps - r, dps)]
        return pltpu.make_async_remote_copy(
            src_ref=at, dst_ref=at, send_sem=send_p.at[r], recv_sem=recv_p.at[r],
            device_id=(dp, partner), device_id_type=MESH_ID,
        )

    for r in range(dps):
        across(r).start()
    land[dp] = mine[dp]
    scatter.stage(0)
    small_again()
    combine.stage(3)
    out_sum = jnp.concatenate(scatter.result(), axis=0).astype(BF16)
    for i in range(dps):
        out_mine[i] = out_sum[:, i * column : (i + 1) * column]
    out_first = Exchange(out_mine, out_dp, send_m, recv_m, "dp")

    back.arrive()
    share = HEADS // KV_HEADS
    for head in range(KV_HEADS):
        for part in range(2):
            at = slice((part + 1) * HD, (part + 2) * HD)
            both = sum(parts_back[head * share + i, at].astype(F32) for i in range(share))
            back_pairs[part * KV_HEADS + head] = both.astype(BF16)
    queries_back = parts_back[:, :HD].reshape(HEADS * HD, tokens)
    grad_normed = dot(queries_back, query_all[...].reshape(HEADS * HD, width), ((0,), (0,)))
    grad_normed = grad_normed + dot(back_pairs[...].reshape(2 * KV_HEADS * HD, tokens), keyval_all[...], ((0,), (1,)))
    inputs = x_ref[...].astype(F32)
    grad_norm, grad_gain = norm_back(inputs, rms_scale(inputs), gain_ref[...].reshape(1, width).astype(F32), grad_normed)
    input_ref[...] = grad_residual_ref[...] + grad_norm
    grad_gain = grad_gain[None]
    for i in range(gain_sum.shape[1]):
        gain_sum[0, i : i + 1] = grad_gain[:, 128 * i : 128 * i + 128]

    dp_first.arrive()
    for r in range(dps):
        across_here(r).wait_recv()
    both = jnp.sum(land[...].astype(F32), axis=0)
    kv_own[...] = (both[HD:] + jnp.sum(pair_land[...].astype(F32), axis=0)).astype(BF16)
    replicas = Replicas(kv_own, gather_buf, send_n, recv_n, out_sems.at[0])
    replicas.first()
    summed[dp] = both[:HD].astype(BF16)
    dp_second = Exchange(summed.at[dp], summed, send_j, recv_j, "dp", same=True)
    dp_second.start()
    gain_first = Exchange(gain_sum.at[0], gain_dp, send_k, recv_k, "dp", same=True)
    gain_first.start()
    gain_dp[dp] = gain_sum[0]
    out_first.start()
    out_dp[dp] = out_mine[dp]
    ring.fifth()
    combine.stage(1)
    replicas.second()
    gain_first.arrive()
    gain_sum[1] = jnp.sum(gain_dp[...], axis=0)
    gain_second = Exchange(gain_sum.at[1], gain_land, send_l, recv_l, same=True)
    gain_second.start()
    gain_land[rank] = gain_sum[1]
    ring.finish()
    outs = []
    per = chunk_in.shape[0]
    for c in range(RING):
        down_rows = per - width // RING
        outs.append(pltpu.make_async_copy(total.at[:, pl.ds(c * per, width // RING)], gateup_out.at[:, pl.ds(c * (width // RING), width // RING)], out_sems.at[1 + c]))
        outs.append(pltpu.make_async_copy(total.at[:, pl.ds(c * per + width // RING, down_rows)], down_out.at[:, pl.ds(c * down_rows, down_rows)], out_sems.at[1 + RING + c]))
    for copy in outs:
        copy.start()
    out_first.arrive()
    out_all[dp] = jnp.sum(out_dp[...].astype(F32), axis=0).astype(BF16)
    out_second = Exchange(out_all.at[dp], out_all, send_q, recv_q, "dp", same=True)
    out_second.start()
    dp_second.arrive()
    for i in range(dps):
        query_ref[:, i * column : (i + 1) * column] = summed[i]
    combine.stage(0)
    replicas.third()
    replicas.fourth()
    rows = block_ref.shape[0] // 2
    for place, value_half in enumerate(combine.result()):
        at = slice(place * rows, (place + 1) * rows)
        block_ref[at] = (residual_ref[at] + RES_SCALE * value_half).astype(BF16)
    out_second.arrive()
    for i in range(dps):
        out_ref[:, i * column : (i + 1) * column] = out_all[i]
    third.arrive()
    gain_second.arrive()
    gain_out[...] = jnp.sum(gain_land[...], axis=0)
    replicas.finish()
    for i in range(count):
        base = (i % 2) * KV_HEADS * HD + (i // 2) * HD
        keyval_ref[base : base + HD, :] = gather_buf[i]
    for r in range(dps):
        across(r).wait_send()
    for each in (swap, back, small, second_small, third, dp_first, dp_second, gain_first, gain_second, out_first, out_second):
        each.sent()
    scatter.finish()
    combine.finish()
    for copy in outs:
        copy.wait()


def backward(
    qkv, grad_context, wide, logs, cosine, sine, normed, context, grad_att, combined, residual, chunk, small,
    x, gain, grad_residual, weights, w_keyval, dps,
):
    count, _, tokens = grad_context.shape
    length, width = normed.shape
    shape = jax.ShapeDtypeStruct
    vmem = pltpu.VMEM
    low = vmem((length, HD), BF16)
    wide_rows = vmem((length, HD), F32)
    column = width // dps
    rows = RING * chunk.shape[0]
    small_shape, gain_shape = (8, SMALL), (8, 128)
    operands = (
        qkv, grad_context, wide, logs, cosine, sine, normed, context, grad_att, combined, residual, chunk, small,
        x, gain, grad_residual, weights, w_keyval,
    )
    held = [vmem(o.shape, o.dtype) for o in operands]
    held[16] = vmem((count, HD, width), BF16)
    del held[11]
    three = vmem((dps, 2 * HD, column), BF16)
    return call(
        backward_kernel, "backward", 4,
        (
            shape((tokens, width), BF16), shape((tokens, width), F32), shape((HD, width), BF16), shape((HD, width), BF16),
            shape((count * HD, width), BF16), shape((count, *small_shape), F32), shape(gain_shape, F32),
            shape((2, width, width), BF16), shape((2, rows - width, width), BF16),
        ),
        [anywhere()] * len(operands), [whole()] * 7 + [anywhere()] * 2,
        [
            *held,
            vmem((count, HD, tokens), BF16), vmem(qkv_parts(count, tokens), BF16), vmem(qkv_parts(count, tokens), BF16),
            vmem((HD, length), BF16), low, low, low, low, vmem((HD, length), F32), wide_rows, wide_rows,
            vmem((3 * HD, length), BF16), vmem((count, HD, width), BF16), vmem(((count - 1) * HD, width), BF16),
            vmem(((count - 1) * tokens, width), BF16),
            vmem((2, rows, width), BF16),
            vmem((3 * HD, width), F32), vmem((dps, HD, column), BF16), vmem((dps, HD, column), BF16), vmem((HD, column), BF16),
            three, three, vmem((dps, HD, column), BF16),
            vmem((count, *small_shape), F32), vmem((count, *small_shape), F32), vmem((2, *small_shape), F32),
            vmem((dps, *small_shape), F32), vmem((count, HD, width), BF16),
            vmem((2, *gain_shape), F32), vmem((dps, *gain_shape), F32), vmem((count, *gain_shape), F32), vmem((2 * KV_HEADS, HD, tokens), BF16), *([vmem((dps, HD, column), BF16)] * 3),
            *pair_sems(count - 1), *pair_sems(count - 1), *pair_sems(Torus.COUNT), *pair_sems(Torus.COUNT),
            *pair_sems(RingSum.COUNT), *pair_sems(count - 1), *pair_sems(dps - 1), *pair_sems(count - 1),
            *pair_sems(dps - 1), *pair_sems(dps - 1), *pair_sems(dps - 1), *pair_sems(count - 1),
            *pair_sems(Replicas.COUNT), *pair_sems(dps - 1), *pair_sems(dps - 1), *pair_sems(dps),
            pltpu.SemaphoreType.DMA((len(operands),)), pltpu.SemaphoreType.DMA((1 + 2 * RING,)),
        ],
        65400, flops=2 * length * length * HD * 5, bytes_accessed=30 << 20,
    )(*operands)


def qkv_parts(count, tokens):
    return (count, 3 * HD, tokens)


def polish_kernel(
    gateup_ref, down_ref, keyval_ref, query_ref, out_ref, block_ref, input_ref, small_ref, gain_ref,
    gateup_out, down_out, keyval_out, query_out, out_out, block_out, input_out, router_out, gain_two_out, gain_one_out,
):
    gateup_out[...] = gateup_ref[...].astype(F32)
    down_out[...] = down_ref[...].astype(F32)
    keyval_out[...] = keyval_ref[...].T.astype(F32)

    @pl.when(pl.program_id(0) == 0)
    def _():
        query_out[...] = query_ref[...].astype(F32)
        out_out[...] = out_ref[...].astype(F32)
        block_out[...] = block_ref[...]
        input_out[...] = input_ref[...]
        for i in range(small_ref.shape[0]):
            router_out[8 * (i // 4) : 8 * (i // 4) + 8, 256 * (i % 4) : 256 * (i % 4) + 256] = small_ref[i, :, :256]
        for i in range(gain_two_out.shape[0]):
            gain_two_out[i : i + 1] = small_ref[2 * i, :1, 256:]
        gain_one_out[...] = gain_ref[...]


def polish(gateup, down, keyval, query, out, block, grad_input, small, gain):
    steps = 4
    experts_here, width, wide = gateup.shape
    ff = down.shape[1]
    per = steps // experts_here
    pairs = keyval.shape[0]
    shape = jax.ShapeDtypeStruct
    gateup_spec = pl.BlockSpec((1, width // per, wide), lambda i: (i // per, i % per, 0))
    down_spec = pl.BlockSpec((1, ff // per, width), lambda i: (i // per, i % per, 0))

    def once(dims):
        return pl.BlockSpec(dims, lambda i: (0,) * len(dims))

    rest = [query.shape, out.shape, block.shape, grad_input.shape]
    return pl.pallas_call(
        polish_kernel, grid=(steps,),
        out_shape=(
            shape(gateup.shape, F32), shape(down.shape, F32), shape((width, pairs), F32), shape(query.shape, F32),
            shape(out.shape, F32), shape(block.shape, BF16), shape(grad_input.shape, F32), shape((EXPERTS, width), F32),
            shape(gain.shape, F32), shape(gain.shape, F32),
        ),
        in_specs=[
            gateup_spec, down_spec, pl.BlockSpec((pairs, width // steps), lambda i: (0, i)),
            *[once(dims) for dims in rest], once(small.shape), once(gain.shape),
        ],
        out_specs=[
            gateup_spec, down_spec, pl.BlockSpec((width // steps, pairs), lambda i: (i, 0)),
            *[once(dims) for dims in rest], once((EXPERTS, width)), once(gain.shape), once(gain.shape),
        ],
        compiler_params=pltpu.CompilerParams(vmem_limit_bytes=65400 << 10),
        name="polish",
    )(gateup, down, keyval, query, out, block, grad_input, small, gain)


def shards(
    block_input, attn_gain, w_query, w_keyval, w_out, ffn_gain, w_router, w_gateup, w_down, routes, cotangent,
):
    tokens, width = block_input.shape
    length = tokens * lax.axis_size("tensor")
    cosine, sine = rope_tables(length, HD)
    (
        normed_one_all, qkv, wide_out, logs, context, query_all, residual, combined, chunk, grad_residual, grad_attention, small,
        grad_context,
    ) = front(
        block_input, attn_gain, ffn_gain, w_query.T, w_keyval, w_out, cotangent, cosine, sine, routes.T, w_router.T, w_gateup, w_down
    )
    block_out, grad_input, grad_query_w, grad_w_out, grad_keyval, small, gain_one, grad_w_gateup, grad_w_down = backward(
        qkv, grad_context, wide_out, logs, cosine, sine, normed_one_all.reshape(length, width), context, grad_attention,
        combined, residual, chunk, small, block_input, attn_gain, grad_residual, query_all, w_keyval, lax.axis_size("dp"),
    )
    grad_w_gateup, grad_w_down, grad_keyval, grad_query_w, grad_w_out, block_out, grad_input, routers, gain_two, gain_one = polish(
        grad_w_gateup, grad_w_down, grad_keyval, grad_query_w, grad_w_out, block_out, grad_input, small, gain_one
    )
    return (
        block_out,
        grad_input,
        gain_one.reshape(width),
        grad_query_w.T,
        grad_keyval,
        grad_w_out,
        gain_two.reshape(width),
        routers.T,
        grad_w_gateup,
        grad_w_down,
    )


def solution(mesh):
    rows = P(("dp", "tensor"), None)
    in_specs = (
        rows, P(), P(None, "tensor"), P(), P("tensor", None), P(), P(),
        P("tensor", None, None), P("tensor", None, None), rows, rows,
    )
    out_specs = (
        rows, rows, P(), P(None, "tensor"), P(), P("tensor", None), P(), P(),
        P("tensor", None, None), P("tensor", None, None),
    )
    return jax.shard_map(shards, mesh=mesh, in_specs=in_specs, out_specs=out_specs, check_vma=False)
```
